256 devices in a mesh: dom: 128 (over x, z, y), rep: 2 (over core).
Axes of the slice: x: 4, y: 4, z: 8, core: 2. Of those that a mesh axis runs over, the one named last changes fastest.
Arguments:
- entity_table: bfloat16 [131072, 800], P('dom'), may hold values from -3 to 3
- entity_state: float32 [131072], P('dom'), may hold values from 0.02 to 0.2
- relation_phase: float32 [16384, 400], P(('dom', 'rep')), may hold values from -3.140625 to 3.140625
- relation_state: float32 [16384], P(('dom', 'rep')), may hold values from 0.02 to 0.2
- want_rows: int32 [256, 2, 128, 8], P(('dom', 'rep')), may hold values from 0 to 1023
- want_count: int32 [256, 2, 128], P(('dom', 'rep')), may hold values from 2 to 8, as said below
- head_slot: int32 [256, 2, 128], P(('dom', 'rep')), may hold values from 0 to 1023, as said below
- tail_slot: int32 [256, 2, 128], P(('dom', 'rep')), may hold values from 0 to 1023, as said below
- negative_slot: int32 [256, 2, 2, 16], P(('dom', 'rep')), may hold values from 0 to 1023, as said below
- relation_ids: int32 [256, 2, 128], P(('dom', 'rep')), may hold values from 0 to 63
Outputs:
- new_entity_table: bfloat16 [131072, 800], P('dom')
- new_entity_state: float32 [131072], P('dom')
- new_relation_phase: float32 [16384, 400], P(('dom', 'rep'))
- new_relation_state: float32 [16384], P(('dom', 'rep'))
The draws below stay inside these ranges and needn't reach their ends.
Inputs may be any that keep to these rules, and one draw needn't show every extreme that they name: `want_rows`: each list names rows of its owner's partition; only the first want_count entries of a list are ever named by a slot. `want_count`: a trainer asks an owner for 8 rows at most; in every step one or two owners, drawn from the seed, receive exactly 8 rows from every trainer, and one trainer, drawn from the seed, asks every owner for exactly 8 rows. `head_slot`: a slot is below the sum of the trainer's want_count in that step. `tail_slot`: a slot is below the sum of the trainer's want_count in that step. `negative_slot`: a slot is below the sum of the trainer's want_count in that step.
All inputs are finite; a program needn't handle non-finite values.
Results may differ from the reference program's by a relative error of at most 0.0031.
Values may be sent and summed in bfloat16 or wider, within the bound.
No kernel may reach another device: no remote copies, remote signals or barrier semaphores. Data moves between devices by JAX's collectives and lax.ppermute only.
A program may use at most 64 MiB of HBM per device.

```python
import math
import jax
import jax.numpy as jnp
from jax import lax

DIM = 400
ENT_DEV = 1024
REL_DEV = 64
TRIPLES_DEV = 128
NEG = 16
CAP = 8
STEPS = 2
TRAINERS = 256
ENTITIES = 131072
RELATIONS = 16384
GROUPS = 2
N_DOM = 128


def count_table(key):
    hot_key, base_key, full_key = jax.random.split(key, 3)
    hot_owners = jax.random.randint(hot_key, (STEPS, 2), 0, N_DOM, dtype=jnp.int32)
    owner_ids = jnp.arange(N_DOM, dtype=jnp.int32)
    is_hot = jnp.any(owner_ids[None, :, None] == hot_owners[:, None, :], axis=-1)
    base_counts = jax.random.randint(base_key, (TRAINERS, STEPS, N_DOM), max(1, CAP // 4), 3 * CAP // 4 + 1, dtype=jnp.int32)
    full_trainer = jax.random.randint(full_key, (STEPS,), 0, TRAINERS, dtype=jnp.int32)
    trainer_ids = jnp.arange(TRAINERS, dtype=jnp.int32)
    is_full = (trainer_ids[:, None] == full_trainer[None, :])[:, :, None]
    return jnp.where(is_hot[None] | is_full, CAP, base_counts).astype(jnp.int32)


def slot_totals(key):
    return jnp.sum(count_table(key), axis=-1, dtype=jnp.int32)


def place_last(key, slots, totals):
    length = slots.shape[2]
    where_key = jax.random.fold_in(key, 7)
    spot = jax.random.randint(where_key, (TRAINERS, STEPS, 1), 0, length, dtype=jnp.int32)
    positions = jnp.arange(length, dtype=jnp.int32)[None, None, :]
    return jnp.where(positions == spot, totals[:, :, None] - 1, slots).astype(jnp.int32)


def draw_want_count(key, part):
    counts = count_table(key)
    return counts


def draw_head_slot(key, part):
    totals = slot_totals(key)
    key = jax.random.fold_in(key, 2)
    slots = jax.random.randint(key, (TRAINERS, STEPS, TRIPLES_DEV), 0, totals[:, :, None], dtype=jnp.int32)
    return place_last(key, slots, totals)


def draw_tail_slot(key, part):
    totals = slot_totals(key)
    key = jax.random.fold_in(key, 3)
    slots = jax.random.randint(key, (TRAINERS, STEPS, TRIPLES_DEV), 0, totals[:, :, None], dtype=jnp.int32)
    return place_last(key, slots, totals)


def draw_negative_slot(key, part):
    totals = slot_totals(key)
    key = jax.random.fold_in(key, 4)
    slots = jax.random.randint(key, (TRAINERS, STEPS, GROUPS * NEG), 0, totals[:, :, None], dtype=jnp.int32)
    return place_last(key, slots, totals).reshape(TRAINERS, STEPS, GROUPS, NEG)


def touch_ends(result, rng, smallest, high):
    extent = result.shape
    index_at = [jax.random.randint(jax.random.fold_in(rng, axis), (), 0, extent[axis]) for axis in range(len(extent))]
    result = result.at[tuple(index_at)].set(smallest)
    longest = extent.index(max(extent))
    index_at[longest] = (index_at[longest] + 1) % extent[longest]
    return result.at[tuple(index_at)].set(high)


def shard_levels(stream_key, dims, pieces, least, top_value):
    level = 1.0
    for axis_at, blocks in pieces:
        steps = jax.random.uniform(jax.random.fold_in(jax.random.fold_in(stream_key, 6), axis_at), (blocks,), jnp.float32, least / len(pieces), top_value / len(pieces))
        level = level * jnp.repeat(jnp.exp(steps), dims[axis_at] // blocks).reshape((-1,) + (1,) * (len(dims) - 1 - axis_at))
    return level


def noise(rng, extent, scale, limit, pieces=(), held_as=jnp.bfloat16):
    result = jax.random.normal(rng, extent, jnp.float32) * scale
    if len(pieces) > 0:
        result = shard_levels(rng, extent, pieces, -0.22, 0.18) * result
    return jnp.clip(result, min=-limit, max=limit).astype(held_as)


def setup_inputs(seed: int = 0) -> dict:
    key_list = jax.random.split(jax.random.key(seed), 11)
    entity_table = noise(key_list[0], (ENTITIES, 2 * DIM), 0.5, 3.0, ((0, 128),))
    entity_state = jnp.clip(jnp.exp(math.log(0.2) - 2.3025851 * jax.random.uniform(key_list[1], (ENTITIES,), jnp.float32) ** shard_levels(key_list[1], (ENTITIES,), ((0, 128),), -0.2, 0.2)), 0.02, 0.2)
    relation_phase = jnp.clip(jax.random.uniform(key_list[2], (RELATIONS, DIM), jnp.float32, -3.140625, 3.140625), -3.140625, 3.140625)
    relation_state = jnp.clip(jnp.exp(math.log(0.2) - 2.3025851 * jax.random.uniform(key_list[3], (RELATIONS,), jnp.float32) ** shard_levels(key_list[3], (RELATIONS,), ((0, 256),), -0.2, 0.2)), 0.02, 0.2)
    want_rows = touch_ends(jax.random.randint(key_list[4], (TRAINERS, STEPS, N_DOM, CAP), 0, ENT_DEV), jax.random.fold_in(key_list[4], 1), 0, ENT_DEV - 1).astype(jnp.int32)
    want_count = draw_want_count(jax.random.fold_in(key_list[10], 71), 0)
    head_slot = draw_head_slot(jax.random.fold_in(key_list[10], 71), 0)
    tail_slot = draw_tail_slot(jax.random.fold_in(key_list[10], 71), 0)
    negative_slot = draw_negative_slot(jax.random.fold_in(key_list[10], 71), 0)
    relation_ids = touch_ends(jax.random.randint(key_list[9], (TRAINERS, STEPS, TRIPLES_DEV), 0, REL_DEV), jax.random.fold_in(key_list[9], 1), 0, REL_DEV - 1).astype(jnp.int32)
    return dict(entity_table=entity_table, entity_state=entity_state, relation_phase=relation_phase, relation_state=relation_state, want_rows=want_rows, want_count=want_count, head_slot=head_slot, tail_slot=tail_slot, negative_slot=negative_slot, relation_ids=relation_ids)


learn_rate = 0.5
smoothing = 0.25
epsilon = 1e-10
margin_rate = 0.26

def slot_place(slot_ids, counts, slot_cap):
    running = jnp.cumsum(counts, dtype=jnp.int32)
    passed = (slot_ids[..., None] >= running).astype(jnp.int32)
    owner_index = lax.optimization_barrier(jnp.sum(passed, axis=-1, dtype=jnp.int32))
    before = lax.optimization_barrier(jnp.sum(passed * counts, axis=-1, dtype=jnp.int32))
    return (owner_index * slot_cap + slot_ids - before).astype(jnp.int32)

def distance(rot_real, rot_imag, target):
    half_width = rot_real.shape[-1]
    diff_real = rot_real - target[..., :half_width]
    diff_imag = rot_imag - target[..., half_width:]
    return lax.optimization_barrier(jnp.sum(jnp.sqrt(diff_real * diff_real + diff_imag * diff_imag + smoothing), axis=-1))

def pair_loss(head_rows, tail_rows, negatives, phase_rows):
    half_width = phase_rows.shape[-1]
    cosine = jnp.cos(phase_rows)
    sine_part = jnp.sin(phase_rows)
    rot_real = head_rows[:, :half_width] * cosine - head_rows[:, half_width:] * sine_part
    rot_imag = head_rows[:, :half_width] * sine_part + head_rows[:, half_width:] * cosine
    margin = margin_rate * half_width
    positive = margin - 0.25 * distance(rot_real, rot_imag, tail_rows)
    blocks = negatives.shape[0]
    neg_count = negatives.shape[1]
    block_real = rot_real.reshape(blocks, -1, 1, half_width)
    block_imag = rot_imag.reshape(blocks, -1, 1, half_width)
    negative = margin - 0.25 * distance(block_real, block_imag, negatives[:, None])
    return -jnp.sum(jax.nn.log_sigmoid(positive)) - jnp.sum(jax.nn.log_sigmoid(-negative)) / neg_count

def adagrad(values, accumulator, gradient):
    fresh_state = accumulator + lax.optimization_barrier(jnp.mean(gradient * gradient, axis=-1))
    stepped = values.astype(jnp.float32) - learn_rate * gradient / (jnp.sqrt(fresh_state)[:, None] + epsilon)
    return (stepped, fresh_state)

def reference(entity_table, entity_state, relation_phase, relation_state, want_rows, want_count, head_slot, tail_slot, negative_slot, relation_ids):
    row_width = 2 * DIM
    entities_now = entity_table
    entity_acc = entity_state
    phase_tables = relation_phase.reshape(TRAINERS, REL_DEV, DIM)
    phase_states = relation_state.reshape(TRAINERS, REL_DEV)
    owner_base = jnp.arange(N_DOM, dtype=jnp.int32)[:, None] * ENT_DEV
    for step_index in range(STEPS):

        def trainer(grad_table, inputs):
            asked_rows, counts, head_at, tail_at, negative_at, relation_rows, phase_table, phase_state = inputs
            global_ids = (owner_base + asked_rows).reshape(-1).astype(jnp.int32)
            pulled = jnp.take(entities_now, global_ids, axis=0)
            head_pos = slot_place(head_at, counts, CAP)
            tail_pos = slot_place(tail_at, counts, CAP)
            negative_pos = slot_place(negative_at, counts, CAP)
            head_rows = jnp.take(pulled, head_pos, axis=0).astype(jnp.float32)
            tail_rows = jnp.take(pulled, tail_pos, axis=0).astype(jnp.float32)
            negatives = jnp.take(pulled, negative_pos, axis=0).astype(jnp.float32)
            phase_rows = jnp.take(phase_table, relation_rows, axis=0)
            loss_value, pullback = jax.vjp(pair_loss, head_rows, tail_rows, negatives, phase_rows)
            grad_head, grad_tail, grad_negative, grad_phase = pullback(jnp.ones_like(loss_value))
            padded = jnp.zeros((N_DOM * CAP, row_width), jnp.float32)
            padded = padded.at[head_pos].add(grad_head)
            padded = padded.at[tail_pos].add(grad_tail)
            padded = padded.at[negative_pos.reshape(-1)].add(grad_negative.reshape(-1, row_width))
            grad_table = grad_table.at[global_ids].add(padded)
            phase_grad = jnp.zeros((REL_DEV, DIM), jnp.float32).at[relation_rows].add(grad_phase)
            new_phase, new_state = adagrad(phase_table, phase_state, phase_grad)
            return (grad_table, (new_phase, new_state))
        inputs = (want_rows[:, step_index], want_count[:, step_index], head_slot[:, step_index], tail_slot[:, step_index], negative_slot[:, step_index], relation_ids[:, step_index], phase_tables, phase_states)
        grad_table, (phase_tables, phase_states) = lax.scan(trainer, jnp.zeros((ENTITIES, row_width), jnp.float32), inputs)
        stepped, entity_acc = adagrad(entities_now, entity_acc, grad_table)
        entities_now = stepped.astype(jnp.bfloat16)
    return (entities_now, entity_acc, phase_tables.reshape(RELATIONS, DIM), phase_states.reshape(RELATIONS))
```

```python
import functools

import jax
import jax.numpy as jnp
from jax import lax
from jax.experimental import pallas as pl
from jax.experimental.pallas import tpu as pltpu
from jax.sharding import PartitionSpec as P

learn_rate = 0.5
smoothing = 0.25
epsilon = 1e-10
margin_rate = 0.26

LANES = 128
VMEM_LIMIT = 48 * 1024 * 1024


def slot_place(slot_ids, counts, slot_cap):
    running = jnp.cumsum(counts, dtype=jnp.int32)
    passed = (slot_ids[..., None] >= running).astype(jnp.int32)
    owner_index = jnp.sum(passed, axis=-1, dtype=jnp.int32)
    before = jnp.sum(passed * counts, axis=-1, dtype=jnp.int32)
    return owner_index * slot_cap + slot_ids - before


def call(kernel, out_shape, name, flops=0, nbytes=0, **kwargs):
    return pl.pallas_call(
        kernel,
        out_shape=out_shape,
        name=name,
        cost_estimate=pl.CostEstimate(flops=flops, bytes_accessed=nbytes, transcendentals=0),
        compiler_params=pltpu.CompilerParams(vmem_limit_bytes=VMEM_LIMIT),
        **kwargs,
    )


def diagonal():
    down = lax.broadcasted_iota(jnp.int32, (LANES, LANES), 0)
    across = lax.broadcasted_iota(jnp.int32, (LANES, LANES), 1)
    return down == across


def to_column(row):
    spread = jnp.broadcast_to(row, (LANES, LANES))
    return jnp.sum(jnp.where(diagonal(), spread, 0.0), axis=1, keepdims=True)


def to_row(column):
    spread = jnp.broadcast_to(column, (LANES, LANES))
    return jnp.sum(jnp.where(diagonal(), spread, 0.0), axis=0, keepdims=True)


def one_hot_rows(column, width):
    lanes = lax.broadcasted_iota(jnp.int32, (column.shape[0], width), 1)
    return jnp.where(lanes == column, 1.0, 0.0).astype(jnp.bfloat16)


def one_hot_columns(row, first, height):
    down = lax.broadcasted_iota(jnp.int32, (height, row.shape[1]), 0) + first
    return jnp.where(down == row, 1.0, 0.0).astype(jnp.bfloat16)


def dot(left, right):
    return jnp.dot(left, right, preferred_element_type=jnp.float32)


def split3(values):
    high = values.astype(jnp.bfloat16)
    rest = values - high.astype(jnp.float32)
    middle = rest.astype(jnp.bfloat16)
    low = (rest - middle.astype(jnp.float32)).astype(jnp.bfloat16)
    return high, middle, low


def gather_rows(wanted_ref, table_ref, offered_ref):
    table_rows = table_ref.shape[0]
    blocks = wanted_ref.shape[0]
    step = 2
    for start in range(0, blocks, step):
        columns = [
            to_column(wanted_ref[block : block + 1, :].astype(jnp.float32)).astype(jnp.int32)
            for block in range(start, start + step)
        ]
        chosen = one_hot_rows(jnp.concatenate(columns, axis=0), table_rows)
        rows = pl.ds(start * LANES, step * LANES)
        offered_ref[rows, :] = dot(chosen, table_ref[...]).astype(jnp.bfloat16)


def offer_kernel(wanted_ref, table_ref, offered_ref):
    gather_rows(wanted_ref, table_ref, offered_ref)


def own_sum_kernel(asked_ref, arrived_ref, total_ref):
    rows = total_ref.shape[0]
    step = 256
    asked = asked_ref[...]
    for first in range(0, rows, step):
        chosen = one_hot_columns(asked, first, step)
        total_ref[first : first + step, :] = dot(chosen, arrived_ref[...])


def update_kernel(
    has_next,
    asked_ref,
    arrived_ref,
    own_ref,
    table_ref,
    state_ref,
    *rest,
):
    if has_next:
        wanted_ref, new_table_ref, new_state_ref, offered_ref = rest
    else:
        new_table_ref, new_state_ref = rest
    rows, width = table_ref.shape
    step = 256
    asked = asked_ref[...]
    for first in range(0, rows, step):
        chosen = one_hot_columns(asked, first, step)
        gradient = own_ref[first : first + step, :] + dot(chosen, arrived_ref[...])
        mean_square = jnp.sum(gradient * gradient, axis=1, keepdims=True) / width
        fresh = []
        for block in range(first // LANES, (first + step) // LANES):
            old = to_column(state_ref[block : block + 1, :])
            at = block * LANES - first
            new = old + mean_square[at : at + LANES, :]
            new_state_ref[block : block + 1, :] = to_row(new)
            fresh.append(new)
        rate = learn_rate / (jnp.sqrt(jnp.concatenate(fresh, axis=0)) + epsilon)
        values = table_ref[first : first + step, :].astype(jnp.float32)
        new_table_ref[first : first + step, :] = (values - gradient * rate).astype(jnp.bfloat16)
    if has_next:
        gather_rows(wanted_ref, new_table_ref, offered_ref)


def sigmoid(value):
    tail = jnp.exp(-jnp.abs(value))
    return jnp.where(value >= 0, 1.0, tail) / (1.0 + tail)


def trainer_kernel(
    blocks,
    negatives,
    pulled_ref,
    place_ref,
    spot_ref,
    cosine_ref,
    sine_ref,
    padded_ref,
    phase_grad_ref,
    head_ref,
    tail_ref,
    negative_ref,
    rot_real_ref,
    rot_imag_ref,
    tail_real_ref,
    tail_imag_ref,
    neg_real_ref,
    neg_imag_ref,
    rot_real_grad_ref,
    rot_imag_grad_ref,
    tail_real_grad_ref,
    tail_imag_grad_ref,
    neg_real_grad_ref,
    neg_imag_grad_ref,
    grads_ref,
):
    slots, width = pulled_ref.shape
    half = width // 2
    triples = cosine_ref.shape[0]
    neg_rows = blocks * negatives
    margin = margin_rate * half

    pulled = pulled_ref[...]
    head_ref[...] = dot(one_hot_rows(place_ref[:, 0:1], slots), pulled)
    tail_ref[...] = dot(one_hot_rows(place_ref[:, 1:2], slots), pulled)
    negative_ref[...] = dot(one_hot_rows(place_ref[:neg_rows, 2:3], slots), pulled)

    cosine = cosine_ref[...]
    sine = sine_ref[...]
    head_real = head_ref[:, :half]
    head_imag = head_ref[:, half:]
    rot_real_ref[...] = head_real * cosine - head_imag * sine
    rot_imag_ref[...] = head_real * sine + head_imag * cosine
    tail_real_ref[...] = tail_ref[:, :half]
    tail_imag_ref[...] = tail_ref[:, half:]
    neg_real_ref[...] = negative_ref[:, :half]
    neg_imag_ref[...] = negative_ref[:, half:]
    neg_real_grad_ref[...] = jnp.zeros_like(neg_real_grad_ref)
    neg_imag_grad_ref[...] = jnp.zeros_like(neg_imag_grad_ref)

    group = 8
    per_block = triples // blocks

    def pair(real, imag, other_real, other_imag):
        diff_real = real - other_real
        diff_imag = imag - other_imag
        square = diff_real * diff_real + diff_imag * diff_imag + smoothing
        inverse = lax.rsqrt(square)
        distance = jnp.sum(square * inverse, axis=1, keepdims=True)
        return distance, diff_real * inverse, diff_imag * inverse

    def chunk(index, carry):
        rows = pl.ds(pl.multiple_of(index * group, group), group)
        first = (index * group) // per_block * negatives
        real = rot_real_ref[rows, :]
        imag = rot_imag_ref[rows, :]
        distance, unit_real, unit_imag = pair(
            real, imag, tail_real_ref[rows, :], tail_imag_ref[rows, :]
        )
        weight = 0.25 * sigmoid(0.25 * distance - margin)
        total_real = weight * unit_real
        total_imag = weight * unit_imag
        tail_real_grad_ref[rows, :] = -total_real
        tail_imag_grad_ref[rows, :] = -total_imag
        for n in range(negatives):
            distance, unit_real, unit_imag = pair(
                real,
                imag,
                neg_real_ref[pl.ds(first + n, 1), :],
                neg_imag_ref[pl.ds(first + n, 1), :],
            )
            weight = (-0.25 / negatives) * sigmoid(margin - 0.25 * distance)
            unit_real = weight * unit_real
            unit_imag = weight * unit_imag
            total_real += unit_real
            total_imag += unit_imag
            neg_real_grad_ref[first + n] -= unit_real
            neg_imag_grad_ref[first + n] -= unit_imag
        rot_real_grad_ref[rows, :] = total_real
        rot_imag_grad_ref[rows, :] = total_imag
        return carry

    lax.fori_loop(0, triples // group, chunk, 0)

    real_grad = rot_real_grad_ref[...]
    imag_grad = rot_imag_grad_ref[...]
    phase_grad_ref[...] = imag_grad * rot_real_ref[...] - real_grad * rot_imag_ref[...]

    def put(first, rows, real, imag):
        high = jnp.concatenate([real, imag], axis=1)
        rounded = high.astype(jnp.bfloat16)
        grads_ref[first : first + rows, :] = rounded
        low = (high - rounded.astype(jnp.float32)).astype(jnp.bfloat16)
        grads_ref[3 * triples + first : 3 * triples + first + rows, :] = low

    put(
        0,
        triples,
        real_grad * cosine + imag_grad * sine,
        imag_grad * cosine - real_grad * sine,
    )
    put(triples, triples, tail_real_grad_ref[...], tail_imag_grad_ref[...])
    spare = jnp.zeros((triples - neg_rows, half), jnp.float32)
    put(
        2 * triples,
        triples,
        jnp.concatenate([jnp.sum(neg_real_grad_ref[...], axis=1), spare], axis=0),
        jnp.concatenate([jnp.sum(neg_imag_grad_ref[...], axis=1), spare], axis=0),
    )
    step = 256
    spots = [spot_ref[index : index + 1, :] for index in range(3)]
    for first in range(0, slots, step):
        chosen = [one_hot_columns(spot, first, step) for spot in spots]
        chosen = jnp.concatenate(chosen + chosen, axis=1)
        padded_ref[first : first + step, :] = dot(chosen, grads_ref[...]).astype(jnp.bfloat16)


def relation_kernel(spot_ref, grad_ref, phase_ref, state_ref, new_phase_ref, new_state_ref):
    relations, half = phase_ref.shape
    chosen = one_hot_columns(spot_ref[3:4, :], 0, relations)
    high, middle, low = split3(grad_ref[...])
    gradient = dot(chosen, high) + dot(chosen, middle) + dot(chosen, low)
    mean_square = jnp.sum(gradient * gradient, axis=1, keepdims=True) / half
    fresh = state_ref[...] + mean_square
    new_state_ref[...] = fresh
    new_phase_ref[...] = phase_ref[...] - learn_rate * gradient / (jnp.sqrt(fresh) + epsilon)


def shape(dims, dtype):
    return jax.ShapeDtypeStruct(dims, dtype)


def local(
    entity_table,
    entity_state,
    relation_phase,
    relation_state,
    want_rows,
    want_count,
    head_slot,
    tail_slot,
    negative_slot,
    relation_ids,
):
    steps, owners, cap = want_rows.shape[1:]
    rows, width = entity_table.shape
    half = width // 2
    blocks, negatives = negative_slot.shape[2:]
    triples = head_slot.shape[2]
    slots = owners * cap
    relations = relation_phase.shape[0]
    table_bytes = 2 * rows * width

    asked = jnp.transpose(want_rows[0], (1, 0, 2)).reshape(owners, steps * cap)
    asked = lax.all_to_all(asked, "dom", split_axis=0, concat_axis=0, tiled=True)
    asked = jnp.transpose(asked.reshape(owners, steps, cap), (1, 0, 2))
    asked = asked.reshape(steps, slots // LANES, LANES)
    asked_other = lax.ppermute(asked, "rep", [(0, 1), (1, 0)])
    ask_row = asked.reshape(steps, 1, slots)
    ask_row_other = asked_other.reshape(steps, 1, slots)

    spots = []
    for step in range(steps):
        counts = want_count[0, step]
        neg = slot_place(negative_slot[0, step].reshape(-1), counts, cap)
        spare = jnp.full((triples - neg.shape[0],), -1, jnp.int32)
        spots.append(
            jnp.stack(
                [
                    slot_place(head_slot[0, step], counts, cap),
                    slot_place(tail_slot[0, step], counts, cap),
                    jnp.concatenate([neg, spare]),
                    relation_ids[0, step],
                ]
            )
        )

    table = entity_table
    state = entity_state.reshape(rows // LANES, LANES)
    phase = relation_phase
    phase_state = relation_state[:, None]
    offered = call(
        offer_kernel,
        shape((slots, width), jnp.bfloat16),
        "offer",
        flops=2 * slots * rows * width,
        nbytes=2 * table_bytes,
    )(asked[0], table)
    f32 = jnp.float32
    for step in range(steps):
        pulled = lax.all_to_all(
            offered.reshape(owners, cap, width), "dom", split_axis=0, concat_axis=0, tiled=True
        ).reshape(slots, width)
        relation_span = jnp.arange(relations, dtype=jnp.int32)
        selector = (relation_ids[0, step][:, None] == relation_span[None, :]).astype(f32)
        phase_rows = jnp.dot(selector, phase, precision=lax.Precision.HIGHEST)
        padded, phase_grad = call(
            functools.partial(trainer_kernel, blocks, negatives),
            (shape((slots, width), jnp.bfloat16), shape((triples, half), f32)),
            "trainer",
            flops=2 * slots * (9 * triples) * width,
            nbytes=2 * table_bytes,
            scratch_shapes=[
                pltpu.VMEM((triples, width), f32),
                pltpu.VMEM((triples, width), f32),
                pltpu.VMEM((blocks * negatives, width), f32),
                pltpu.VMEM((triples, half), f32),
                pltpu.VMEM((triples, half), f32),
                pltpu.VMEM((triples, half), f32),
                pltpu.VMEM((triples, half), f32),
                pltpu.VMEM((blocks * negatives, half), f32),
                pltpu.VMEM((blocks * negatives, half), f32),
                pltpu.VMEM((triples, half), f32),
                pltpu.VMEM((triples, half), f32),
                pltpu.VMEM((triples, half), f32),
                pltpu.VMEM((triples, half), f32),
                pltpu.VMEM((blocks * negatives, 8, half), f32),
                pltpu.VMEM((blocks * negatives, 8, half), f32),
                pltpu.VMEM((6 * triples, width), jnp.bfloat16),
            ],
        )(pulled, spots[step].T, spots[step], jnp.cos(phase_rows), jnp.sin(phase_rows))
        arrived = lax.all_to_all(
            padded.reshape(owners, cap, width), "dom", split_axis=0, concat_axis=0, tiled=True
        ).reshape(slots, width)
        phase, phase_state = call(
            relation_kernel,
            (shape((relations, half), f32), shape((relations, 1), f32)),
            "relation",
            flops=6 * triples * relations * half,
            nbytes=4 * triples * half,
        )(spots[step], phase_grad, phase, phase_state)
        arrived_other = lax.ppermute(arrived, "rep", [(0, 1), (1, 0)])
        own = call(
            own_sum_kernel,
            shape((rows, width), f32),
            "own_sum",
            flops=2 * slots * rows * width,
            nbytes=3 * table_bytes,
        )(ask_row[step], arrived)
        has_next = step + 1 < steps
        outputs = [
            shape((rows, width), jnp.bfloat16),
            shape((rows // LANES, LANES), f32),
        ]
        operands = [ask_row_other[step], arrived_other, own, table, state]
        if has_next:
            outputs.append(shape((slots, width), jnp.bfloat16))
            operands.append(asked[step + 1])
        results = call(
            functools.partial(update_kernel, has_next),
            tuple(outputs),
            "update",
            flops=2 * slots * rows * width * (1 + has_next),
            nbytes=6 * table_bytes,
        )(*operands)
        table, state = results[:2]
        if has_next:
            offered = results[2]
    return (table, state.reshape(rows), phase, phase_state[:, 0])


def solution(mesh):
    placed = (
        P("dom", None),
        P("dom"),
        P(("dom", "rep"), None),
        P(("dom", "rep")),
        P(("dom", "rep"), None, None, None),
        P(("dom", "rep"), None, None),
        P(("dom", "rep"), None, None),
        P(("dom", "rep"), None, None),
        P(("dom", "rep"), None, None, None),
        P(("dom", "rep"), None, None),
    )
    return jax.shard_map(
        local,
        mesh=mesh,
        in_specs=placed,
        out_specs=(P("dom", None), P("dom"), P(("dom", "rep"), None), P(("dom", "rep"))),
        check_vma=False,
    )
```

```python
import functools

import jax
import jax.numpy as jnp
from jax import lax
from jax.experimental import pallas as pl
from jax.experimental.pallas import tpu as pltpu
from jax.sharding import PartitionSpec as P

learn_rate = 0.5
smoothing = 0.25
epsilon = 1e-10
margin_rate = 0.26

LANES = 128
VMEM_LIMIT = 20 * 1024 * 1024


def slot_place(slot_ids, counts, slot_cap):
    running = jnp.cumsum(counts, dtype=jnp.int32)
    passed = (slot_ids[..., None] >= running).astype(jnp.int32)
    owner_index = jnp.sum(passed, axis=-1, dtype=jnp.int32)
    before = jnp.sum(passed * counts, axis=-1, dtype=jnp.int32)
    return owner_index * slot_cap + slot_ids - before


def call(kernel, out_shape, name, flops=0, nbytes=0, **kwargs):
    return pl.pallas_call(
        kernel,
        out_shape=out_shape,
        name=name,
        cost_estimate=pl.CostEstimate(flops=flops, bytes_accessed=nbytes, transcendentals=0),
        compiler_params=pltpu.CompilerParams(vmem_limit_bytes=VMEM_LIMIT),
        **kwargs,
    )


def diagonal():
    down = lax.broadcasted_iota(jnp.int32, (LANES, LANES), 0)
    across = lax.broadcasted_iota(jnp.int32, (LANES, LANES), 1)
    return down == across


def to_column(row):
    spread = jnp.broadcast_to(row, (LANES, LANES))
    return jnp.sum(jnp.where(diagonal(), spread, 0.0), axis=1, keepdims=True)


def to_row(column):
    spread = jnp.broadcast_to(column, (LANES, LANES))
    return jnp.sum(jnp.where(diagonal(), spread, 0.0), axis=0, keepdims=True)


def one_hot_rows(column, width):
    lanes = lax.broadcasted_iota(jnp.int32, (column.shape[0], width), 1)
    return jnp.where(lanes == column, 1.0, 0.0).astype(jnp.bfloat16)


def one_hot_columns(row, first, height):
    down = lax.broadcasted_iota(jnp.int32, (height, row.shape[1]), 0) + first
    return jnp.where(down == row, 1.0, 0.0).astype(jnp.bfloat16)


def dot(left, right):
    return jnp.dot(left, right, preferred_element_type=jnp.float32)


def turned(values):
    width = values.shape[1]
    down = lax.broadcasted_iota(jnp.int32, (width, width), 0)
    across = lax.broadcasted_iota(jnp.int32, (width, width), 1)
    unit = jnp.where(down == across, 1.0, 0.0).astype(jnp.bfloat16)
    product = lax.dot_general(
        unit, values, (((1,), (1,)), ((), ())), preferred_element_type=jnp.float32
    )
    return product.astype(jnp.bfloat16)


def split3(values):
    high = values.astype(jnp.bfloat16)
    rest = values - high.astype(jnp.float32)
    middle = rest.astype(jnp.bfloat16)
    low = (rest - middle.astype(jnp.float32)).astype(jnp.bfloat16)
    return high, middle, low


def gather_rows(wanted_ref, table_ref, offered_ref):
    table_rows = table_ref.shape[0]
    blocks = wanted_ref.shape[0]
    step = 2
    for start in range(0, blocks, step):
        columns = [
            to_column(wanted_ref[block : block + 1, :].astype(jnp.float32)).astype(jnp.int32)
            for block in range(start, start + step)
        ]
        chosen = one_hot_rows(jnp.concatenate(columns, axis=0), table_rows)
        rows = pl.ds(start * LANES, step * LANES)
        offered_ref[rows, :] = dot(chosen, table_ref[...]).astype(jnp.bfloat16)


def offer_kernel(wanted_ref, table_ref, offered_ref):
    gather_rows(wanted_ref, table_ref, offered_ref)


def own_sum_kernel(asked_ref, arrived_ref, total_ref):
    rows = total_ref.shape[0]
    step = 256
    asked = asked_ref[...]
    for first in range(0, rows, step):
        chosen = one_hot_columns(asked, first, step)
        total_ref[first : first + step, :] = dot(chosen, arrived_ref[...])


def update_kernel(
    has_next,
    asked_ref,
    arrived_ref,
    own_ref,
    table_ref,
    state_ref,
    *rest,
):
    if has_next:
        wanted_ref, new_table_ref, new_state_ref, offered_ref = rest
    else:
        new_table_ref, new_state_ref = rest
    rows, width = table_ref.shape
    step = 256
    asked = asked_ref[...]
    for first in range(0, rows, step):
        chosen = one_hot_columns(asked, first, step)
        gradient = own_ref[first : first + step, :] + dot(chosen, arrived_ref[...])
        gradient = gradient[:, :width]
        mean_square = jnp.sum(gradient * gradient, axis=1, keepdims=True) / width
        fresh = []
        for block in range(first // LANES, (first + step) // LANES):
            old = to_column(state_ref[block : block + 1, :])
            at = block * LANES - first
            new = old + mean_square[at : at + LANES, :]
            new_state_ref[block : block + 1, :] = to_row(new)
            fresh.append(new)
        rate = learn_rate / (jnp.sqrt(jnp.concatenate(fresh, axis=0)) + epsilon)
        values = table_ref[first : first + step, :].astype(jnp.float32)
        stepped = (values - gradient * rate).astype(jnp.bfloat16)
        if has_next:
            new_table_ref[first : first + step, :] = stepped
        else:
            new_table_ref[:, first : first + step] = turned(stepped)
    if has_next:
        gather_rows(wanted_ref, new_table_ref, offered_ref)


def sigmoid(value):
    tail = jnp.exp(-jnp.abs(value))
    return jnp.where(value >= 0, 1.0, tail) / (1.0 + tail)


def trainer_kernel(
    blocks,
    negatives,
    pulled_ref,
    place_ref,
    spot_ref,
    cosine_ref,
    sine_ref,
    padded_ref,
    phase_grad_ref,
    read_ref,
    rot_real_ref,
    rot_imag_ref,
    tail_real_ref,
    tail_imag_ref,
    neg_real_ref,
    neg_imag_ref,
    rot_real_grad_ref,
    rot_imag_grad_ref,
    tail_real_grad_ref,
    tail_imag_grad_ref,
    neg_real_grad_ref,
    neg_imag_grad_ref,
    grads_ref,
):
    slots, width = pulled_ref.shape
    half = width // 2
    triples = cosine_ref.shape[0]
    neg_rows = blocks * negatives
    margin = margin_rate * half

    pulled = pulled_ref[...]
    places = [place_ref[:, 0:1], place_ref[:, 1:2], place_ref[:neg_rows, 2:3]]
    read_ref[...] = dot(one_hot_rows(jnp.concatenate(places, axis=0), slots), pulled)
    head_ref = read_ref.at[:triples, :]
    tail_ref = read_ref.at[triples : 2 * triples, :]
    negative_ref = read_ref.at[2 * triples :, :]

    cosine = cosine_ref[...]
    sine = sine_ref[...]
    head_real = head_ref[:, :half]
    head_imag = head_ref[:, half:]
    rot_real_ref[...] = head_real * cosine - head_imag * sine
    rot_imag_ref[...] = head_real * sine + head_imag * cosine
    tail_real_ref[...] = tail_ref[:, :half]
    tail_imag_ref[...] = tail_ref[:, half:]
    neg_real_ref[...] = negative_ref[:, :half]
    neg_imag_ref[...] = negative_ref[:, half:]
    neg_real_grad_ref[...] = jnp.zeros_like(neg_real_grad_ref)
    neg_imag_grad_ref[...] = jnp.zeros_like(neg_imag_grad_ref)

    group = 8
    per_block = triples // blocks

    def pair(real, imag, other_real, other_imag):
        diff_real = real - other_real
        diff_imag = imag - other_imag
        square = diff_real * diff_real + diff_imag * diff_imag + smoothing
        inverse = lax.rsqrt(square)
        distance = jnp.sum(square * inverse, axis=1, keepdims=True)
        return distance, diff_real * inverse, diff_imag * inverse

    def chunk(index, carry):
        rows = pl.ds(pl.multiple_of(index * group, group), group)
        first = (index * group) // per_block * negatives
        real = rot_real_ref[rows, :]
        imag = rot_imag_ref[rows, :]
        distance, unit_real, unit_imag = pair(
            real, imag, tail_real_ref[rows, :], tail_imag_ref[rows, :]
        )
        weight = 0.25 * sigmoid(0.25 * distance - margin)
        total_real = weight * unit_real
        total_imag = weight * unit_imag
        tail_real_grad_ref[rows, :] = -total_real
        tail_imag_grad_ref[rows, :] = -total_imag
        for n in range(negatives):
            distance, unit_real, unit_imag = pair(
                real,
                imag,
                neg_real_ref[pl.ds(first + n, 1), :],
                neg_imag_ref[pl.ds(first + n, 1), :],
            )
            weight = (-0.25 / negatives) * sigmoid(margin - 0.25 * distance)
            unit_real = weight * unit_real
            unit_imag = weight * unit_imag
            total_real += unit_real
            total_imag += unit_imag
            neg_real_grad_ref[first + n] -= unit_real
            neg_imag_grad_ref[first + n] -= unit_imag
        rot_real_grad_ref[rows, :] = total_real
        rot_imag_grad_ref[rows, :] = total_imag
        return carry

    lax.fori_loop(0, triples // group, chunk, 0)

    real_grad = rot_real_grad_ref[...]
    imag_grad = rot_imag_grad_ref[...]
    phase_grad_ref[...] = imag_grad * rot_real_ref[...] - real_grad * rot_imag_ref[...]

    grads_ref[:, width:] = jnp.zeros_like(grads_ref[:, width:])

    def put(first, rows, real, imag):
        high = jnp.concatenate([real, imag], axis=1)
        rounded = high.astype(jnp.bfloat16)
        grads_ref[first : first + rows, :width] = rounded
        low = (high - rounded.astype(jnp.float32)).astype(jnp.bfloat16)
        grads_ref[3 * triples + first : 3 * triples + first + rows, :width] = low

    put(
        0,
        triples,
        real_grad * cosine + imag_grad * sine,
        imag_grad * cosine - real_grad * sine,
    )
    put(triples, triples, tail_real_grad_ref[...], tail_imag_grad_ref[...])
    spare = jnp.zeros((triples - neg_rows, half), jnp.float32)
    put(
        2 * triples,
        triples,
        jnp.concatenate([jnp.sum(neg_real_grad_ref[...], axis=1), spare], axis=0),
        jnp.concatenate([jnp.sum(neg_imag_grad_ref[...], axis=1), spare], axis=0),
    )
    step = 256
    spots = [spot_ref[index : index + 1, :] for index in range(3)]
    for first in range(0, slots, step):
        chosen = [one_hot_columns(spot, first, step) for spot in spots]
        chosen = jnp.concatenate(chosen + chosen, axis=1)
        padded_ref[first : first + step, :] = dot(chosen, grads_ref[...]).astype(jnp.bfloat16)


def relation_kernel(spot_ref, grad_ref, phase_ref, state_ref, new_phase_ref, new_state_ref):
    relations, half = phase_ref.shape
    chosen = one_hot_columns(spot_ref[3:4, :], 0, relations)
    high, middle, low = split3(grad_ref[...])
    gradient = dot(chosen, high) + dot(chosen, middle) + dot(chosen, low)
    mean_square = jnp.sum(gradient * gradient, axis=1, keepdims=True) / half
    fresh = state_ref[...] + mean_square
    new_state_ref[...] = fresh
    new_phase_ref[...] = phase_ref[...] - learn_rate * gradient / (jnp.sqrt(fresh) + epsilon)


def shape(dims, dtype):
    return jax.ShapeDtypeStruct(dims, dtype)


def local(
    entity_table,
    entity_state,
    relation_phase,
    relation_state,
    want_rows,
    want_count,
    head_slot,
    tail_slot,
    negative_slot,
    relation_ids,
):
    steps, owners, cap = want_rows.shape[1:]
    rows, width = entity_table.shape
    half = width // 2
    wide = -(-width // LANES) * LANES
    blocks, negatives = negative_slot.shape[2:]
    triples = head_slot.shape[2]
    slots = owners * cap
    relations = relation_phase.shape[0]
    table_bytes = 2 * rows * width

    asked = jnp.transpose(want_rows[0], (1, 0, 2)).reshape(owners, steps * cap)
    asked = lax.all_to_all(asked, "dom", split_axis=0, concat_axis=0, tiled=True)
    asked = jnp.transpose(asked.reshape(owners, steps, cap), (1, 0, 2))
    asked = asked.reshape(steps, slots // LANES, LANES)
    asked_other = lax.ppermute(asked, "rep", [(0, 1), (1, 0)])
    ask_row = asked.reshape(steps, 1, slots)
    ask_row_other = asked_other.reshape(steps, 1, slots)

    spots = []
    for step in range(steps):
        counts = want_count[0, step]
        neg = slot_place(negative_slot[0, step].reshape(-1), counts, cap)
        spare = jnp.full((triples - neg.shape[0],), -1, jnp.int32)
        spots.append(
            jnp.stack(
                [
                    slot_place(head_slot[0, step], counts, cap),
                    slot_place(tail_slot[0, step], counts, cap),
                    jnp.concatenate([neg, spare]),
                    relation_ids[0, step],
                ]
            )
        )

    table = entity_table
    state = entity_state.reshape(rows // LANES, LANES)
    phase = relation_phase
    phase_state = relation_state[:, None]
    offered = call(
        offer_kernel,
        shape((slots, width), jnp.bfloat16),
        "offer",
        flops=2 * slots * rows * width,
        nbytes=2 * table_bytes,
    )(asked[0], table)
    f32 = jnp.float32
    for step in range(steps):
        pulled = lax.all_to_all(
            offered.reshape(owners, cap, width), "dom", split_axis=0, concat_axis=0, tiled=True
        ).reshape(slots, width)
        relation_span = jnp.arange(relations, dtype=jnp.int32)
        selector = (relation_ids[0, step][:, None] == relation_span[None, :]).astype(f32)
        phase_rows = jnp.dot(selector, phase, precision=lax.Precision.HIGHEST)
        padded, phase_grad = call(
            functools.partial(trainer_kernel, blocks, negatives),
            (shape((slots, wide), jnp.bfloat16), shape((triples, half), f32)),
            "trainer",
            flops=2 * slots * (9 * triples) * width,
            nbytes=2 * table_bytes,
            scratch_shapes=[
                pltpu.VMEM((2 * triples + blocks * negatives, width), f32),
                pltpu.VMEM((triples, half), f32),
                pltpu.VMEM((triples, half), f32),
                pltpu.VMEM((triples, half), f32),
                pltpu.VMEM((triples, half), f32),
                pltpu.VMEM((blocks * negatives, half), f32),
                pltpu.VMEM((blocks * negatives, half), f32),
                pltpu.VMEM((triples, half), f32),
                pltpu.VMEM((triples, half), f32),
                pltpu.VMEM((triples, half), f32),
                pltpu.VMEM((triples, half), f32),
                pltpu.VMEM((blocks * negatives, 8, half), f32),
                pltpu.VMEM((blocks * negatives, 8, half), f32),
                pltpu.VMEM((6 * triples, wide), jnp.bfloat16),
            ],
        )(pulled, spots[step].T, spots[step], jnp.cos(phase_rows), jnp.sin(phase_rows))
        arrived = lax.all_to_all(
            padded.reshape(owners, cap, wide), "dom", split_axis=0, concat_axis=0, tiled=True
        ).reshape(slots, wide)
        phase, phase_state = call(
            relation_kernel,
            (shape((relations, half), f32), shape((relations, 1), f32)),
            "relation",
            flops=6 * triples * relations * half,
            nbytes=4 * triples * half,
        )(spots[step], phase_grad, phase, phase_state)
        arrived_other = lax.ppermute(arrived, "rep", [(0, 1), (1, 0)])
        own = call(
            own_sum_kernel,
            shape((rows, wide), f32),
            "own_sum",
            flops=2 * slots * rows * width,
            nbytes=3 * table_bytes,
        )(ask_row[step], arrived)
        has_next = step + 1 < steps
        outputs = [
            shape((rows, width) if has_next else (width, rows), jnp.bfloat16),
            shape((rows // LANES, LANES), f32),
        ]
        operands = [ask_row_other[step], arrived_other, own, table, state]
        if has_next:
            outputs.append(shape((slots, width), jnp.bfloat16))
            operands.append(asked[step + 1])
        results = call(
            functools.partial(update_kernel, has_next),
            tuple(outputs),
            "update",
            flops=2 * slots * rows * width * (1 + has_next),
            nbytes=6 * table_bytes,
        )(*operands)
        table, state = results[:2]
        if has_next:
            offered = results[2]
    return (table.T, state.reshape(rows), phase, phase_state[:, 0])


def solution(mesh):
    placed = (
        P("dom", None),
        P("dom"),
        P(("dom", "rep"), None),
        P(("dom", "rep")),
        P(("dom", "rep"), None, None, None),
        P(("dom", "rep"), None, None),
        P(("dom", "rep"), None, None),
        P(("dom", "rep"), None, None),
        P(("dom", "rep"), None, None, None),
        P(("dom", "rep"), None, None),
    )
    return jax.shard_map(
        local,
        mesh=mesh,
        in_specs=placed,
        out_specs=(P("dom", None), P("dom"), P(("dom", "rep"), None), P(("dom", "rep"))),
        check_vma=False,
    )
```

```python
import functools

import jax
import jax.numpy as jnp
from jax import lax
from jax.experimental import pallas as pl
from jax.experimental.pallas import tpu as pltpu
from jax.sharding import PartitionSpec as P

learn_rate = 0.5
smoothing = 0.25
epsilon = 1e-10
margin_rate = 0.26

LANES = 128
VMEM_LIMIT = 20 * 1024 * 1024


def slot_place(slot_ids, counts, slot_cap):
    running = jnp.cumsum(counts, dtype=jnp.int32)
    passed = (slot_ids[..., None] >= running).astype(jnp.int32)
    owner_index = jnp.sum(passed, axis=-1, dtype=jnp.int32)
    before = jnp.sum(passed * counts, axis=-1, dtype=jnp.int32)
    return owner_index * slot_cap + slot_ids - before


def call(kernel, out_shape, name, flops=0, nbytes=0, **kwargs):
    return pl.pallas_call(
        kernel,
        out_shape=out_shape,
        name=name,
        cost_estimate=pl.CostEstimate(flops=flops, bytes_accessed=nbytes, transcendentals=0),
        compiler_params=pltpu.CompilerParams(vmem_limit_bytes=VMEM_LIMIT),
        **kwargs,
    )


def diagonal():
    down = lax.broadcasted_iota(jnp.int32, (LANES, LANES), 0)
    across = lax.broadcasted_iota(jnp.int32, (LANES, LANES), 1)
    return down == across


def to_column(row):
    spread = jnp.broadcast_to(row, (LANES, LANES))
    return jnp.sum(jnp.where(diagonal(), spread, 0.0), axis=1, keepdims=True)


def to_row(column):
    spread = jnp.broadcast_to(column, (LANES, LANES))
    return jnp.sum(jnp.where(diagonal(), spread, 0.0), axis=0, keepdims=True)


def one_hot_rows(column, width):
    lanes = lax.broadcasted_iota(jnp.int32, (column.shape[0], width), 1)
    return jnp.where(lanes == column, 1.0, 0.0).astype(jnp.bfloat16)


def one_hot_columns(row, first, height):
    down = lax.broadcasted_iota(jnp.int32, (height, row.shape[1]), 0) + first
    return jnp.where(down == row, 1.0, 0.0).astype(jnp.bfloat16)


def dot(left, right):
    return jnp.dot(left, right, preferred_element_type=jnp.float32)


def turned(values):
    width = values.shape[1]
    down = lax.broadcasted_iota(jnp.int32, (width, width), 0)
    across = lax.broadcasted_iota(jnp.int32, (width, width), 1)
    unit = jnp.where(down == across, 1.0, 0.0).astype(jnp.bfloat16)
    product = lax.dot_general(
        unit, values, (((1,), (1,)), ((), ())), preferred_element_type=jnp.float32
    )
    return product.astype(jnp.bfloat16)


def split3(values):
    high = values.astype(jnp.bfloat16)
    rest = values - high.astype(jnp.float32)
    middle = rest.astype(jnp.bfloat16)
    low = (rest - middle.astype(jnp.float32)).astype(jnp.bfloat16)
    return high, middle, low


def gather_rows(wanted_ref, table_ref, offered_ref):
    table_rows = table_ref.shape[0]
    blocks = wanted_ref.shape[0]
    step = 2
    for start in range(0, blocks, step):
        columns = [
            to_column(wanted_ref[block : block + 1, :].astype(jnp.float32)).astype(jnp.int32)
            for block in range(start, start + step)
        ]
        chosen = one_hot_rows(jnp.concatenate(columns, axis=0), table_rows)
        rows = pl.ds(start * LANES, step * LANES)
        offered_ref[rows, :] = dot(chosen, table_ref[...]).astype(jnp.bfloat16)


def offer_kernel(wanted_ref, table_ref, offered_ref):
    gather_rows(wanted_ref, table_ref, offered_ref)


def own_sum_kernel(asked_ref, arrived_ref, total_ref):
    rows = total_ref.shape[0]
    step = 256
    asked = asked_ref[...]
    for first in range(0, rows, step):
        chosen = one_hot_columns(asked, first, step)
        total_ref[first : first + step, :] = dot(chosen, arrived_ref[...])


def adagrad_block(gradient, first, table_ref, state_ref, new_state_ref):
    step, width = gradient.shape
    mean_square = jnp.sum(gradient * gradient, axis=1, keepdims=True) / width
    fresh = []
    for block in range(first // LANES, (first + step) // LANES):
        old = to_column(state_ref[block : block + 1, :])
        at = block * LANES - first
        new = old + mean_square[at : at + LANES, :]
        new_state_ref[block : block + 1, :] = to_row(new)
        fresh.append(new)
    rate = learn_rate / (jnp.sqrt(jnp.concatenate(fresh, axis=0)) + epsilon)
    values = table_ref[first : first + step, :].astype(jnp.float32)
    return (values - gradient * rate).astype(jnp.bfloat16)


def update_kernel(
    has_next,
    asked_ref,
    arrived_ref,
    own_ref,
    table_ref,
    state_ref,
    *rest,
):
    if has_next:
        wanted_ref, new_table_ref, new_state_ref, offered_ref = rest
    else:
        new_table_ref, new_state_ref = rest
    rows, width = table_ref.shape
    step = 256
    asked = asked_ref[...]
    for first in range(0, rows, step):
        chosen = one_hot_columns(asked, first, step)
        gradient = own_ref[first : first + step, :] + dot(chosen, arrived_ref[...])
        gradient = gradient[:, :width]
        stepped = adagrad_block(gradient, first, table_ref, state_ref, new_state_ref)
        if has_next:
            new_table_ref[first : first + step, :] = stepped
        else:
            new_table_ref[:, first : first + step] = turned(stepped)
    if has_next:
        gather_rows(wanted_ref, new_table_ref, offered_ref)


def sigmoid(value):
    tail = jnp.exp(-jnp.abs(value))
    return jnp.where(value >= 0, 1.0, tail) / (1.0 + tail)


def trainer_core(
    blocks,
    negatives,
    width,
    pulled,
    place_ref,
    spot_ref,
    cosine_ref,
    sine_ref,
    padded_ref,
    phase_grad_ref,
    read_ref,
    rot_real_ref,
    rot_imag_ref,
    tail_real_ref,
    tail_imag_ref,
    neg_real_ref,
    neg_imag_ref,
    rot_real_grad_ref,
    rot_imag_grad_ref,
    tail_real_grad_ref,
    tail_imag_grad_ref,
    neg_real_grad_ref,
    neg_imag_grad_ref,
    grads_ref,
):
    slots = pulled.shape[0]
    half = width // 2
    triples = cosine_ref.shape[0]
    neg_rows = blocks * negatives
    margin = margin_rate * half

    places = [place_ref[:, 0:1], place_ref[:, 1:2], place_ref[:neg_rows, 2:3]]
    read_ref[...] = dot(one_hot_rows(jnp.concatenate(places, axis=0), slots), pulled)
    head_ref = read_ref.at[:triples, :]
    tail_ref = read_ref.at[triples : 2 * triples, :]
    negative_ref = read_ref.at[2 * triples :, :]

    cosine = cosine_ref[...]
    sine = sine_ref[...]
    head_real = head_ref[:, :half]
    head_imag = head_ref[:, half:width]
    rot_real_ref[...] = head_real * cosine - head_imag * sine
    rot_imag_ref[...] = head_real * sine + head_imag * cosine
    tail_real_ref[...] = tail_ref[:, :half]
    tail_imag_ref[...] = tail_ref[:, half:width]
    neg_real_ref[...] = negative_ref[:, :half]
    neg_imag_ref[...] = negative_ref[:, half:width]
    neg_real_grad_ref[...] = jnp.zeros_like(neg_real_grad_ref)
    neg_imag_grad_ref[...] = jnp.zeros_like(neg_imag_grad_ref)

    group = 8
    per_block = triples // blocks

    def pair(real, imag, other_real, other_imag):
        diff_real = real - other_real
        diff_imag = imag - other_imag
        square = diff_real * diff_real + diff_imag * diff_imag + smoothing
        inverse = lax.rsqrt(square)
        distance = jnp.sum(square * inverse, axis=1, keepdims=True)
        return distance, diff_real * inverse, diff_imag * inverse

    def chunk(index, carry):
        rows = pl.ds(pl.multiple_of(index * group, group), group)
        first = (index * group) // per_block * negatives
        real = rot_real_ref[rows, :]
        imag = rot_imag_ref[rows, :]
        distance, unit_real, unit_imag = pair(
            real, imag, tail_real_ref[rows, :], tail_imag_ref[rows, :]
        )
        weight = 0.25 * sigmoid(0.25 * distance - margin)
        total_real = weight * unit_real
        total_imag = weight * unit_imag
        tail_real_grad_ref[rows, :] = -total_real
        tail_imag_grad_ref[rows, :] = -total_imag
        for n in range(negatives):
            distance, unit_real, unit_imag = pair(
                real,
                imag,
                neg_real_ref[pl.ds(first + n, 1), :],
                neg_imag_ref[pl.ds(first + n, 1), :],
            )
            weight = (-0.25 / negatives) * sigmoid(margin - 0.25 * distance)
            unit_real = weight * unit_real
            unit_imag = weight * unit_imag
            total_real += unit_real
            total_imag += unit_imag
            neg_real_grad_ref[first + n] -= unit_real
            neg_imag_grad_ref[first + n] -= unit_imag
        rot_real_grad_ref[rows, :] = total_real
        rot_imag_grad_ref[rows, :] = total_imag
        return carry

    lax.fori_loop(0, triples // group, chunk, 0)

    real_grad = rot_real_grad_ref[...]
    imag_grad = rot_imag_grad_ref[...]
    phase_grad_ref[...] = imag_grad * rot_real_ref[...] - real_grad * rot_imag_ref[...]

    grads_ref[:, width:] = jnp.zeros_like(grads_ref[:, width:])

    def put(first, rows, real, imag):
        high = jnp.concatenate([real, imag], axis=1)
        rounded = high.astype(jnp.bfloat16)
        grads_ref[first : first + rows, :width] = rounded
        low = (high - rounded.astype(jnp.float32)).astype(jnp.bfloat16)
        grads_ref[3 * triples + first : 3 * triples + first + rows, :width] = low

    put(
        0,
        triples,
        real_grad * cosine + imag_grad * sine,
        imag_grad * cosine - real_grad * sine,
    )
    put(triples, triples, tail_real_grad_ref[...], tail_imag_grad_ref[...])
    spare = jnp.zeros((triples - neg_rows, half), jnp.float32)
    put(
        2 * triples,
        triples,
        jnp.concatenate([jnp.sum(neg_real_grad_ref[...], axis=1), spare], axis=0),
        jnp.concatenate([jnp.sum(neg_imag_grad_ref[...], axis=1), spare], axis=0),
    )
    spots = [spot_ref[index : index + 1, :] for index in range(3)]
    for first in range(0, slots, 256):
        step = min(256, slots - first)
        chosen = [one_hot_columns(spot, first, step) for spot in spots]
        chosen = jnp.concatenate(chosen + chosen, axis=1)
        padded_ref[first : first + step, :] = dot(chosen, grads_ref[...]).astype(jnp.bfloat16)


def trainer_kernel(blocks, negatives, pulled_ref, *refs):
    trainer_core(blocks, negatives, pulled_ref.shape[1], pulled_ref[...], *refs)


def trainer_scratch(triples, neg_rows, width, wide, read_width):
    half = width // 2
    return (
        [pltpu.VMEM((2 * triples + neg_rows, read_width), jnp.float32)]
        + [pltpu.VMEM((triples, half), jnp.float32)] * 4
        + [pltpu.VMEM((neg_rows, half), jnp.float32)] * 2
        + [pltpu.VMEM((triples, half), jnp.float32)] * 4
        + [pltpu.VMEM((neg_rows, 8, half), jnp.float32)] * 2
        + [pltpu.VMEM((6 * triples, wide), jnp.bfloat16)]
    )


def relation_kernel(spot_ref, grad_ref, phase_ref, state_ref, new_phase_ref, new_state_ref):
    relations, half = phase_ref.shape
    chosen = one_hot_columns(spot_ref[3:4, :], 0, relations)
    high, middle, low = split3(grad_ref[...])
    gradient = dot(chosen, high) + dot(chosen, middle) + dot(chosen, low)
    mean_square = jnp.sum(gradient * gradient, axis=1, keepdims=True) / half
    fresh = state_ref[...] + mean_square
    new_state_ref[...] = fresh
    new_phase_ref[...] = phase_ref[...] - learn_rate * gradient / (jnp.sqrt(fresh) + epsilon)


def shape(dims, dtype):
    return jax.ShapeDtypeStruct(dims, dtype)


def full_steps(
    entity_table,
    entity_state,
    relation_phase,
    relation_state,
    want_rows,
    want_count,
    head_slot,
    tail_slot,
    negative_slot,
    relation_ids,
):
    steps, owners, cap = want_rows.shape[1:]
    rows, width = entity_table.shape
    half = width // 2
    wide = -(-width // LANES) * LANES
    blocks, negatives = negative_slot.shape[2:]
    triples = head_slot.shape[2]
    slots = owners * cap
    relations = relation_phase.shape[0]
    table_bytes = 2 * rows * width

    asked = jnp.transpose(want_rows[0], (1, 0, 2)).reshape(owners, steps * cap)
    asked = lax.all_to_all(asked, "dom", split_axis=0, concat_axis=0, tiled=True)
    asked = jnp.transpose(asked.reshape(owners, steps, cap), (1, 0, 2))
    asked = asked.reshape(steps, slots // LANES, LANES)
    asked_other = lax.ppermute(asked, "rep", [(0, 1), (1, 0)])
    ask_row = asked.reshape(steps, 1, slots)
    ask_row_other = asked_other.reshape(steps, 1, slots)

    spots = []
    for step in range(steps):
        counts = want_count[0, step]
        neg = slot_place(negative_slot[0, step].reshape(-1), counts, cap)
        spare = jnp.full((triples - neg.shape[0],), -1, jnp.int32)
        spots.append(
            jnp.stack(
                [
                    slot_place(head_slot[0, step], counts, cap),
                    slot_place(tail_slot[0, step], counts, cap),
                    jnp.concatenate([neg, spare]),
                    relation_ids[0, step],
                ]
            )
        )

    table = entity_table
    state = entity_state.reshape(rows // LANES, LANES)
    phase = relation_phase
    phase_state = relation_state[:, None]
    offered = call(
        offer_kernel,
        shape((slots, width), jnp.bfloat16),
        "offer",
        flops=2 * slots * rows * width,
        nbytes=2 * table_bytes,
    )(asked[0], table)
    f32 = jnp.float32
    for step in range(steps):
        pulled = lax.all_to_all(
            offered.reshape(owners, cap, width), "dom", split_axis=0, concat_axis=0, tiled=True
        ).reshape(slots, width)
        relation_span = jnp.arange(relations, dtype=jnp.int32)
        selector = (relation_ids[0, step][:, None] == relation_span[None, :]).astype(f32)
        phase_rows = jnp.dot(selector, phase, precision=lax.Precision.HIGHEST)
        padded, phase_grad = call(
            functools.partial(trainer_kernel, blocks, negatives),
            (shape((slots, wide), jnp.bfloat16), shape((triples, half), f32)),
            "trainer",
            flops=2 * slots * (9 * triples) * width,
            nbytes=2 * table_bytes,
            scratch_shapes=trainer_scratch(triples, blocks * negatives, width, wide, width),
        )(pulled, spots[step].T, spots[step], jnp.cos(phase_rows), jnp.sin(phase_rows))
        arrived = lax.all_to_all(
            padded.reshape(owners, cap, wide), "dom", split_axis=0, concat_axis=0, tiled=True
        ).reshape(slots, wide)
        phase, phase_state = call(
            relation_kernel,
            (shape((relations, half), f32), shape((relations, 1), f32)),
            "relation",
            flops=6 * triples * relations * half,
            nbytes=4 * triples * half,
        )(spots[step], phase_grad, phase, phase_state)
        arrived_other = lax.ppermute(arrived, "rep", [(0, 1), (1, 0)])
        own = call(
            own_sum_kernel,
            shape((rows, wide), f32),
            "own_sum",
            flops=2 * slots * rows * width,
            nbytes=3 * table_bytes,
        )(ask_row[step], arrived)
        has_next = step + 1 < steps
        outputs = [
            shape((rows, width) if has_next else (width, rows), jnp.bfloat16),
            shape((rows // LANES, LANES), f32),
        ]
        operands = [ask_row_other[step], arrived_other, own, table, state]
        if has_next:
            outputs.append(shape((slots, width), jnp.bfloat16))
            operands.append(asked[step + 1])
        results = call(
            functools.partial(update_kernel, has_next),
            tuple(outputs),
            "update",
            flops=2 * slots * rows * width * (1 + has_next),
            nbytes=6 * table_bytes,
        )(*operands)
        table, state = results[:2]
        if has_next:
            offered = results[2]
    return (table.T, state.reshape(rows), phase, phase_state[:, 0])


DIRECT = 5
LINE = 4
LENT = 32
PIECES = 8


def iota(dims, axis):
    return lax.broadcasted_iota(jnp.int32, dims, axis)


def as_bf16(mask):
    return jnp.where(mask, 1.0, 0.0).astype(jnp.bfloat16)


def places(width):
    full, rest = divmod(width, LANES)
    whole = [divmod(index, full) for index in range(DIRECT * full)]
    share = LANES // rest
    groups = [list(range(first, min(first + share, DIRECT))) for first in range(0, DIRECT, share)]
    return full, rest, whole, groups


def packed_width(width):
    full, rest, whole, groups = places(width)
    return -(-(len(whole) + len(groups)) // PIECES) * LANES


def stack_tile(position):
    tile, piece = divmod(position, PIECES)
    return slice(piece * LANES, (piece + 1) * LANES), slice(tile * LANES, (tile + 1) * LANES)


def spread(width, rows_ref, stack_ref, mark):
    full, rest, whole, groups = places(width)
    for position, (row, tile) in enumerate(whole):
        stack_ref[stack_tile(position)] = rows_ref[
            row * LANES : (row + 1) * LANES, tile * LANES : (tile + 1) * LANES
        ]
    last = len(whole) + len(groups) - 1
    for index, group in enumerate(groups):
        position = len(whole) + index
        total = jnp.zeros((LANES, LANES), jnp.float32)
        for row in group:
            tail = rows_ref[row * LANES : (row + 1) * LANES, full * LANES : (full + 1) * LANES]
            tail = tail.astype(jnp.float32)
            shift = rest * (row - group[0])
            total = total + (pltpu.roll(tail, shift, 1) if shift else tail)
        if position == last and mark is not None:
            total = jnp.where(iota((LANES, LANES), 1) == LANES - 1, mark, total)
        stack_ref[stack_tile(position)] = total.astype(jnp.bfloat16)
    for position in range(last + 1, stack_ref.shape[1] // LANES * PIECES):
        stack_ref[stack_tile(position)] = jnp.zeros((LANES, LANES), jnp.bfloat16)


def gather_up(width, stack_ref, rows_ref):
    full, rest, whole, groups = places(width)
    for position, (row, tile) in enumerate(whole):
        rows_ref[row * LANES : (row + 1) * LANES, tile * LANES : (tile + 1) * LANES] = stack_ref[
            stack_tile(position)
        ]
    for index, group in enumerate(groups):
        tails = stack_ref[stack_tile(len(whole) + index)].astype(jnp.float32)
        for row in group:
            shift = rest * (row - group[0])
            tail = pltpu.roll(tails, LANES - shift, 1) if shift else tails
            tail = jnp.where(iota((LANES, LANES), 1) < rest, tail, 0.0)
            rows_ref[row * LANES : (row + 1) * LANES, full * LANES : (full + 1) * LANES] = (
                tail.astype(jnp.bfloat16)
            )


def read_mark(width, stack_ref):
    full, rest, whole, groups = places(width)
    tile = stack_ref[stack_tile(len(whole) + len(groups) - 1)].astype(jnp.float32)
    tile = jnp.where(iota((LANES, LANES), 1) == LANES - 1, tile, 0.0)
    return jnp.max(jnp.max(tile, axis=1, keepdims=True), axis=0, keepdims=True)


PART = LANES // 4


def fold(stack_ref, packed_ref):
    size = PART * PIECES
    down, across = iota((size, size), 0), iota((size, size), 1)
    turn = as_bf16(across == (down % PIECES) * PART + down // PIECES)
    for part in range(LANES // PART):
        pieces = [
            stack_ref[piece * LANES + part * PART : piece * LANES + (part + 1) * PART, :]
            for piece in range(PIECES)
        ]
        packed_ref[part * size : (part + 1) * size, :] = dot(
            turn, jnp.concatenate(pieces, axis=0)
        ).astype(jnp.bfloat16)


def unfold(packed_ref, stack_ref):
    size = PART * PIECES
    down, across = iota((size, size), 0), iota((size, size), 1)
    turn = as_bf16(across == (down % PART) * PIECES + down // PART)
    for part in range(LANES // PART):
        block = dot(turn, packed_ref[part * size : (part + 1) * size, :]).astype(jnp.bfloat16)
        for piece in range(PIECES):
            stack_ref[piece * LANES + part * PART : piece * LANES + (part + 1) * PART, :] = block[
                piece * PART : (piece + 1) * PART, :
            ]


def route_kernel(
    rows,
    want_ref,
    count_ref,
    head_ref,
    tail_ref,
    neg_ref,
    relation_ref,
    ask_ref,
    place_ref,
    spot_ref,
):
    steps, cap, owners = want_ref.shape
    f32 = jnp.float32
    down, across = iota((LANES, LANES), 0), iota((LANES, LANES), 1)
    same_line = down // LINE == across // LINE
    line_mat = as_bf16(same_line)
    line_before = as_bf16(same_line & (down < across))
    upto = as_bf16(down <= across)
    owner = iota((1, LANES), 1).astype(f32)
    y_at = iota((1, LANES), 1) % LINE
    slot_number = iota((cap, LANES), 0).astype(f32)
    none = jnp.zeros((cap - 3, LANES), f32)
    asks = []
    for step in range(steps):
        count = count_ref[step : step + 1, :].astype(f32)
        ends = dot(jnp.broadcast_to(count, (cap, LANES)).astype(jnp.bfloat16), upto)[0:1, :]
        begins = ends - count
        seen = jnp.zeros((cap, LANES), f32)
        uses = []
        for ref in (head_ref, tail_ref, neg_ref):
            slot = to_column(ref[step : step + 1, :].astype(f32))
            owned = (slot >= begins) & (slot < ends)
            within = slot - jnp.sum(jnp.where(owned, begins, 0.0), axis=1, keepdims=True)
            seen += dot(as_bf16(slot_number == to_row(within)), as_bf16(owned))
            uses.append((owned, within))
        used = seen > 0.5
        ranks = [jnp.zeros((1, LANES), f32)]
        for slot in range(cap):
            ranks.append(ranks[-1] + jnp.where(used[slot : slot + 1, :], 1.0, 0.0))
        total = ranks.pop()
        rank = jnp.concatenate(ranks, axis=0)
        over = jnp.maximum(total - DIRECT, 0.0)
        free = DIRECT - jnp.minimum(total, DIRECT)
        pair = jnp.concatenate([over, free, total, none], axis=0).astype(jnp.bfloat16)
        before = dot(pair, line_before)
        whole = dot(pair, line_mat)
        lost = jnp.max(
            jnp.where(whole[0:1, :] > whole[1:2, :], 1.0, 0.0), axis=1, keepdims=True
        )
        turn = before[0:1, :] + rank - DIRECT
        side = jnp.concatenate([before[1:2, :], free, total, none], axis=0).astype(jnp.bfloat16)
        at_slot = rank
        at_owner = jnp.broadcast_to(owner, (cap, LANES))
        code = jnp.zeros((cap, LANES), f32)
        for far in range(1, LINE):
            mover = as_bf16(same_line & (down % LINE == (across + far) % LINE))
            moved = dot(side, mover)
            hit = used & (rank >= DIRECT) & (turn >= moved[0:1, :])
            hit = hit & (turn < moved[0:1, :] + moved[1:2, :])
            slot = moved[2:3, :] + turn - moved[0:1, :]
            other = owner + ((y_at + far) % LINE - y_at).astype(f32)
            at_slot = jnp.where(hit, slot, at_slot)
            at_owner = jnp.where(hit, other, at_owner)
            code = jnp.where(hit, rows * (far * cap + slot), code)
        want = want_ref[step].astype(f32)
        for place in range(cap):
            chosen = used & (rank == place)
            value = want + 1.0 if place < DIRECT else want + code + 1.0
            row = jnp.sum(jnp.where(chosen, value, 0.0), axis=0, keepdims=True) - 1.0
            if place == cap - 1:
                row = jnp.where(lost > 0.5, -2.0, row)
            asks.append(row)
        where_at = at_slot * owners + at_owner
        put = jnp.full((LANES, LANES), -1.0, f32)
        spots = []
        for index, (owned, within) in enumerate(uses):
            table = jnp.zeros((LANES, LANES), f32)
            for slot in range(cap):
                table = jnp.where(within == slot, where_at[slot : slot + 1, :], table)
            found = jnp.sum(jnp.where(owned, table, 0.0), axis=1, keepdims=True)
            found = jnp.where(within < 0, -1.0, found)
            put = jnp.where(across == index, found, put)
            spots.append(to_row(found))
        place_ref[step] = put.astype(jnp.int32)
        spots.append(relation_ref[step : step + 1, :].astype(f32))
        spots.append(jnp.zeros((8 - len(spots), LANES), f32))
        spot_ref[step] = jnp.concatenate(spots, axis=0).astype(jnp.int32)
    asks.append(jnp.zeros((LANES - len(asks), LANES), f32))
    ask_ref[...] = jnp.transpose(jnp.concatenate(asks, axis=0)).astype(jnp.int32)


def fill_lent(tag_ref, step, table_ref, lent_ref):
    rows, width = table_ref.shape
    wide = lent_ref.shape[1] - LANES
    row, slot, trainer = (tag_ref[:, 3 * step + index : 3 * step + index + 1] for index in range(3))
    chosen = one_hot_rows(row.astype(jnp.int32), rows)
    lent_ref[:, wide - LANES : wide] = jnp.zeros((LANES, LANES), jnp.bfloat16)
    lent_ref[:, :width] = dot(chosen, table_ref[...]).astype(jnp.bfloat16)
    lanes = iota((LANES, LANES), 1)
    tags = jnp.where(lanes == 0, slot, jnp.where(lanes == 1, trainer, 0.0))
    lent_ref[:, wide:] = tags.astype(jnp.bfloat16)


def collect_kernel(
    steps, cap, ask_ref, table_ref, plan_ref, tag_ref, flag_ref, lent_ref
):
    rows = table_ref.shape[0]
    f32 = jnp.float32
    asked = jnp.transpose(ask_ref[...].astype(f32))[: steps * cap, :]
    down, across = iota((LANES, LANES), 0), iota((LANES, LANES), 1)
    earlier = as_bf16(down < across)
    trainer = iota((1, LANES), 1).astype(f32)
    flag = jnp.zeros((1, 1), f32)
    tags = jnp.full((LANES, LANES), -1.0, f32)
    lent_rows = []
    extra = cap - DIRECT
    for step in range(steps):
        codes = asked[step * cap + DIRECT : (step + 1) * cap, :].astype(jnp.int32)
        flag = jnp.maximum(
            flag,
            jnp.max(
                jnp.where(codes[extra - 1 : extra, :] == -2, 1.0, 0.0), axis=1, keepdims=True
            ),
        )
        valid = codes >= 0
        row = jnp.where(valid, codes % rows, 0).astype(f32)
        place = jnp.where(valid, codes // rows, 0)
        far = place // cap
        slot = (place % cap).astype(f32)
        masks = [
            jnp.where(valid & (far == distance), 1.0, 0.0) for distance in range(1, LINE)
        ]
        stacked = jnp.concatenate(
            masks + [jnp.zeros((16 - extra * (LINE - 1), LANES), f32)], axis=0
        )
        before = dot(stacked.astype(jnp.bfloat16), earlier)
        totals = jnp.sum(stacked, axis=1, keepdims=True)
        targets = [jnp.full((1, LANES), -1.0, f32) for entry in range(extra)]
        for index in range(LINE - 1):
            offset = jnp.zeros((1, 1), f32)
            for entry in range(extra):
                line = index * extra + entry
                at = before[line : line + 1, :] + offset + index * LENT
                targets[entry] = jnp.where(masks[index][entry : entry + 1, :] > 0.5, at, targets[entry])
                offset = offset + totals[line : line + 1, :]
            flag = jnp.maximum(flag, jnp.where(offset > LENT, 1.0, 0.0))
        sums = [jnp.zeros((LANES, 1), f32) for index in range(3)]
        for entry in range(extra):
            chosen = down.astype(f32) == targets[entry]
            values = (row[entry : entry + 1, :], slot[entry : entry + 1, :], trainer)
            for index, value in enumerate(values):
                picked = jnp.where(chosen, value + 1.0, 0.0)
                sums[index] += jnp.sum(picked, axis=1, keepdims=True)
        for index in range(3):
            tags = jnp.where(across == 3 * step + index, sums[index] - 1.0, tags)
        lent_rows.append(to_row(sums[0] - 1.0))
    lent_rows.append(jnp.full((8 - steps, LANES), -1.0, f32))
    plan_ref[...] = jnp.concatenate([asked] + lent_rows, axis=0).astype(jnp.int32)
    tag_ref[...] = tags
    flag_ref[...] = jnp.broadcast_to(flag, flag_ref.shape)
    fill_lent(tag_ref, 0, table_ref, lent_ref)


def direct_kernel(step, cap, plan_ref, table_ref, rows_ref):
    rows, width = table_ref.shape
    rows_ref[:, rows_ref.shape[1] - LANES :] = jnp.zeros((rows_ref.shape[0], LANES), jnp.bfloat16)
    for first in range(0, DIRECT, 2):
        last = min(first + 2, DIRECT)
        columns = [
            to_column(plan_ref[step * cap + slot : step * cap + slot + 1, :].astype(jnp.float32))
            for slot in range(first, last)
        ]
        chosen = one_hot_rows(jnp.concatenate(columns, axis=0).astype(jnp.int32), rows)
        rows_ref[first * LANES : last * LANES, :width] = dot(chosen, table_ref[...]).astype(
            jnp.bfloat16
        )


def pack_kernel(
    width, rows_ref, flag_ref, one_ref, two_ref, three_ref, packed_ref, tag_ref, lent_ref, full_ref, stack_ref
):
    wide = rows_ref.shape[1]
    lent_ref[3 * LENT :, :] = jnp.zeros((LANES - 3 * LENT, wide), jnp.bfloat16)
    tags = []
    for index, ref in enumerate((one_ref, two_ref, three_ref)):
        lent_ref[index * LENT : (index + 1) * LENT, :] = ref[:, :wide]
        tag = ref[:, wide : wide + LANES].astype(jnp.float32)
        tags.append(tag[:, 0:1] * LANES + tag[:, 1:2])
    tags.append(jnp.full((LANES - 3 * LENT, 1), -1.0, jnp.float32))
    tag = to_row(jnp.concatenate(tags, axis=0)).astype(jnp.int32)
    tag_ref[...] = jnp.broadcast_to(tag, tag_ref.shape)
    for slot in range(DIRECT):
        block = slice(slot * LANES, (slot + 1) * LANES)
        lent = dot(one_hot_columns(tag, slot * LANES, LANES), lent_ref[...])
        full_ref[block, :] = (rows_ref[block, :].astype(jnp.float32) + lent).astype(jnp.bfloat16)
    spread(width, full_ref, stack_ref, flag_ref[0:1, :])
    fold(stack_ref, packed_ref)


def short_trainer_kernel(
    blocks,
    negatives,
    width,
    pulled_ref,
    place_ref,
    spot_ref,
    cosine_ref,
    sine_ref,
    packed_ref,
    phase_grad_ref,
    flag_ref,
    rows_ref,
    stack_ref,
    *scratch,
):
    unfold(pulled_ref, stack_ref)
    gather_up(width, stack_ref, rows_ref)
    flag_ref[...] = jnp.broadcast_to(read_mark(width, stack_ref), flag_ref.shape)
    trainer_core(
        blocks,
        negatives,
        width,
        rows_ref[...],
        place_ref,
        spot_ref,
        cosine_ref,
        sine_ref,
        rows_ref,
        phase_grad_ref,
        *scratch,
    )
    spread(width, rows_ref, stack_ref, None)
    fold(stack_ref, packed_ref)


def return_kernel(width, arrived_ref, tag_ref, rows_ref, lent_ref, stack_ref):
    unfold(arrived_ref, stack_ref)
    gather_up(width, stack_ref, rows_ref)
    tag = to_column(tag_ref[0:1, :].astype(jnp.float32)).astype(jnp.int32)
    chosen = one_hot_rows(tag, rows_ref.shape[0])
    lent_ref[...] = dot(chosen, rows_ref[...]).astype(jnp.bfloat16)


def sum_kernel(
    step, cap, width, plan_ref, other_plan_ref, rows_ref, arrived_ref, total_ref, stack_ref, other_ref
):
    unfold(arrived_ref, stack_ref)
    gather_up(width, stack_ref, other_ref)

    def asked(ref):
        rows = [ref[step * cap + slot : step * cap + slot + 1, :] for slot in range(DIRECT)]
        return jnp.concatenate(rows, axis=1)

    own, other = asked(plan_ref), asked(other_plan_ref)
    for first in range(0, total_ref.shape[0], 256):
        total_ref[first : first + 256, :] = dot(
            one_hot_columns(own, first, 256), rows_ref[...]
        ) + dot(one_hot_columns(other, first, 256), other_ref[...])


def short_update_kernel(
    step,
    cap,
    has_next,
    steps,
    plan_ref,
    other_plan_ref,
    total_ref,
    back_ref,
    other_back_ref,
    table_ref,
    state_ref,
    tag_ref,
    new_table_ref,
    new_state_ref,
    *rest,
):
    if has_next:
        lent_ref, first_ref, second_ref = rest
    else:
        first_ref, second_ref = rest
    rows, width = table_ref.shape
    for ref, source in ((first_ref, back_ref), (second_ref, other_back_ref)):
        ref[: 3 * LENT, :] = source[...]
        ref[3 * LENT :, :] = jnp.zeros((LANES - 3 * LENT, ref.shape[1]), jnp.bfloat16)
    line = steps * cap + step
    own, other = plan_ref[line : line + 1, :], other_plan_ref[line : line + 1, :]
    size = 256
    for first in range(0, rows, size):
        lent = dot(one_hot_columns(own, first, size), first_ref[...]) + dot(
            one_hot_columns(other, first, size), second_ref[...]
        )
        gradient = (total_ref[first : first + size, :] + lent)[:, :width]
        stepped = adagrad_block(gradient, first, table_ref, state_ref, new_state_ref)
        if has_next:
            new_table_ref[first : first + size, :] = stepped
        else:
            new_table_ref[:, first : first + size] = turned(stepped)
    if has_next:
        fill_lent(tag_ref, step + 1, new_table_ref, lent_ref)


def line_pairs(owners, far):
    return [
        (owner, owner // LINE * LINE + (owner % LINE + far) % LINE) for owner in range(owners)
    ]


def short_steps(
    entity_table,
    entity_state,
    relation_phase,
    relation_state,
    want_rows,
    want_count,
    head_slot,
    tail_slot,
    negative_slot,
    relation_ids,
):
    steps, owners, cap = want_rows.shape[1:]
    rows, width = entity_table.shape
    half = width // 2
    wide = -(-width // LANES) * LANES
    blocks, negatives = negative_slot.shape[2:]
    triples = head_slot.shape[2]
    relations = relation_phase.shape[0]
    direct = DIRECT * LANES
    packed_rows = PIECES * LANES
    packed = packed_width(width)
    f32, i32, bf16 = jnp.float32, jnp.int32, jnp.bfloat16

    neg = negative_slot[0].reshape(steps, blocks * negatives)
    neg = jnp.pad(neg, ((0, 0), (0, LANES - blocks * negatives)), constant_values=-1)
    asked, place, spots = call(
        functools.partial(route_kernel, rows),
        (
            shape((LANES, LANES), i32),
            shape((steps, LANES, LANES), i32),
            shape((steps, 8, LANES), i32),
        ),
        "route",
        nbytes=1 << 20,
    )(
        jnp.transpose(want_rows[0], (0, 2, 1)),
        want_count[0],
        head_slot[0],
        tail_slot[0],
        neg,
        relation_ids[0],
    )
    asked = lax.all_to_all(asked, "dom", split_axis=0, concat_axis=0, tiled=True)
    plan, tags, flag, lent = call(
        functools.partial(collect_kernel, steps, cap),
        (
            shape((steps * cap + 8, LANES), i32),
            shape((LANES, LANES), f32),
            shape((8, LANES), f32),
            shape((LANES, wide + LANES), bf16),
        ),
        "collect",
        nbytes=4 << 20,
    )(asked, entity_table)
    swap = [(0, 1), (1, 0)]
    other_plan = lax.ppermute(plan, "rep", swap)
    forth = [line_pairs(owners, far) for far in range(1, LINE)]
    back = [[(target, source) for source, target in pairs] for pairs in forth]

    table = entity_table
    state = entity_state.reshape(rows // LANES, LANES)
    phase = relation_phase
    phase_state = relation_state[:, None]
    spoiled = None
    for step in range(steps):
        has_next = step + 1 < steps
        loans = [
            lax.ppermute(lent[index * LENT : (index + 1) * LENT], "dom", forth[index])
            for index in range(LINE - 1)
        ]
        sent = call(
            functools.partial(direct_kernel, step, cap),
            shape((direct, wide), bf16),
            "direct",
            flops=2 * direct * rows * width,
            nbytes=4 * rows * width,
        )(plan, table)
        offered, loan_tag = call(
            functools.partial(pack_kernel, width),
            (shape((packed_rows, packed), bf16), shape((8, LANES), i32)),
            "pack",
            nbytes=4 * rows * width,
            scratch_shapes=[
                pltpu.VMEM((LANES, wide), bf16),
                pltpu.VMEM((direct, wide), bf16),
                pltpu.VMEM((packed_rows, packed), bf16),
            ],
        )(sent, flag, *loans)
        pulled = lax.all_to_all(
            offered.reshape(owners, PIECES, packed), "dom", split_axis=0, concat_axis=0, tiled=True
        ).reshape(packed_rows, packed)
        relation_span = jnp.arange(relations, dtype=i32)
        selector = (relation_ids[0, step][:, None] == relation_span[None, :]).astype(f32)
        phase_rows = jnp.dot(selector, phase, precision=lax.Precision.HIGHEST)
        padded, phase_grad, seen = call(
            functools.partial(short_trainer_kernel, blocks, negatives, width),
            (
                shape((packed_rows, packed), bf16),
                shape((triples, half), f32),
                shape((8, LANES), f32),
            ),
            "trainer",
            flops=2 * direct * (9 * triples) * width,
            nbytes=4 * rows * width,
            scratch_shapes=[
                pltpu.VMEM((direct, wide), bf16),
                pltpu.VMEM((packed_rows, packed), bf16),
            ]
            + trainer_scratch(triples, blocks * negatives, width, wide, wide),
        )(pulled, place[step], spots[step], jnp.cos(phase_rows), jnp.sin(phase_rows))
        if step == 0:
            spoiled = jnp.maximum(seen, lax.ppermute(seen, "rep", swap))
        arrived = lax.all_to_all(
            padded.reshape(owners, PIECES, packed), "dom", split_axis=0, concat_axis=0, tiled=True
        ).reshape(packed_rows, packed)
        phase, phase_state = call(
            relation_kernel,
            (shape((relations, half), f32), shape((relations, 1), f32)),
            "relation",
            flops=6 * triples * relations * half,
            nbytes=4 * triples * half,
        )(spots[step], phase_grad, phase, phase_state)
        arrived_other = lax.ppermute(arrived, "rep", swap)
        got, dues = call(
            functools.partial(return_kernel, width),
            (shape((direct, wide), bf16), shape((LANES, wide), bf16)),
            "give_back",
            flops=2 * LANES * direct * wide,
            nbytes=4 * rows * width,
            scratch_shapes=[pltpu.VMEM((packed_rows, packed), bf16)],
        )(arrived, loan_tag)
        dues = jnp.concatenate(
            [
                lax.ppermute(dues[index * LENT : (index + 1) * LENT], "dom", back[index])
                for index in range(LINE - 1)
            ],
            axis=0,
        )
        dues_other = lax.ppermute(dues, "rep", swap)
        total = call(
            functools.partial(sum_kernel, step, cap, width),
            shape((rows, wide), f32),
            "sum",
            flops=4 * direct * rows * width,
            nbytes=8 * rows * width,
            scratch_shapes=[
                pltpu.VMEM((packed_rows, packed), bf16),
                pltpu.VMEM((direct, wide), bf16),
            ],
        )(plan, other_plan, got, arrived_other)
        outputs = [
            shape((rows, width) if has_next else (width, rows), bf16),
            shape((rows // LANES, LANES), f32),
        ]
        if has_next:
            outputs.append(shape((LANES, wide + LANES), bf16))
        results = call(
            functools.partial(short_update_kernel, step, cap, has_next, steps),
            tuple(outputs),
            "update",
            flops=4 * LANES * rows * width,
            nbytes=12 * rows * width,
            scratch_shapes=[pltpu.VMEM((LANES, wide), bf16)] * 2,
        )(plan, other_plan, total, dues, dues_other, table, state, tags)
        table, state = results[:2]
        if has_next:
            lent = results[2]
    return (table.T, state.reshape(rows), phase, phase_state[:, 0]), jnp.max(spoiled) > 0.5


def local(*arrays):
    results, spoiled = short_steps(*arrays)
    return lax.cond(spoiled, lambda: full_steps(*arrays), lambda: results)


def solution(mesh):
    placed = (
        P("dom", None),
        P("dom"),
        P(("dom", "rep"), None),
        P(("dom", "rep")),
        P(("dom", "rep"), None, None, None),
        P(("dom", "rep"), None, None),
        P(("dom", "rep"), None, None),
        P(("dom", "rep"), None, None),
        P(("dom", "rep"), None, None, None),
        P(("dom", "rep"), None, None),
    )
    return jax.shard_map(
        local,
        mesh=mesh,
        in_specs=placed,
        out_specs=(P("dom", None), P("dom"), P(("dom", "rep"), None), P(("dom", "rep"))),
        check_vma=False,
    )
```

```python
import functools

import jax
import jax.numpy as jnp
from jax import lax
from jax.experimental import pallas as pl
from jax.experimental.pallas import tpu as pltpu
from jax.sharding import PartitionSpec as P

learn_rate = 0.5
smoothing = 0.25
epsilon = 1e-10
margin_rate = 0.26

LANES = 128
VMEM_LIMIT = 20 * 1024 * 1024


def slot_place(slot_ids, counts, slot_cap):
    running = jnp.cumsum(counts, dtype=jnp.int32)
    passed = (slot_ids[..., None] >= running).astype(jnp.int32)
    owner_index = jnp.sum(passed, axis=-1, dtype=jnp.int32)
    before = jnp.sum(passed * counts, axis=-1, dtype=jnp.int32)
    return owner_index * slot_cap + slot_ids - before


def call(kernel, out_shape, name, flops=0, nbytes=0, **kwargs):
    return pl.pallas_call(
        kernel,
        out_shape=out_shape,
        name=name,
        cost_estimate=pl.CostEstimate(flops=flops, bytes_accessed=nbytes, transcendentals=0),
        compiler_params=pltpu.CompilerParams(vmem_limit_bytes=VMEM_LIMIT),
        **kwargs,
    )


def diagonal():
    down = lax.broadcasted_iota(jnp.int32, (LANES, LANES), 0)
    across = lax.broadcasted_iota(jnp.int32, (LANES, LANES), 1)
    return down == across


def to_column(row):
    spread = jnp.broadcast_to(row, (LANES, LANES))
    return jnp.sum(jnp.where(diagonal(), spread, 0.0), axis=1, keepdims=True)


def to_row(column):
    spread = jnp.broadcast_to(column, (LANES, LANES))
    return jnp.sum(jnp.where(diagonal(), spread, 0.0), axis=0, keepdims=True)


def one_hot_rows(column, width):
    lanes = lax.broadcasted_iota(jnp.int32, (column.shape[0], width), 1)
    return jnp.where(lanes == column, 1.0, 0.0).astype(jnp.bfloat16)


def one_hot_columns(row, first, height):
    down = lax.broadcasted_iota(jnp.int32, (height, row.shape[1]), 0) + first
    return jnp.where(down == row, 1.0, 0.0).astype(jnp.bfloat16)


def dot(left, right):
    return jnp.dot(left, right, preferred_element_type=jnp.float32)


def turn_into(values, ref, first):
    rows, width = values.shape
    for start in range(0, width, 256):
        size = min(256, width - start)
        down = lax.broadcasted_iota(jnp.int32, (size, size), 0)
        across = lax.broadcasted_iota(jnp.int32, (size, size), 1)
        unit = jnp.where(down == across, 1.0, 0.0).astype(jnp.bfloat16)
        product = lax.dot_general(
            unit,
            values[:, start : start + size],
            (((1,), (1,)), ((), ())),
            preferred_element_type=jnp.float32,
        )
        ref[start : start + size, first : first + rows] = product.astype(jnp.bfloat16)


def split3(values):
    high = values.astype(jnp.bfloat16)
    rest = values - high.astype(jnp.float32)
    middle = rest.astype(jnp.bfloat16)
    low = (rest - middle.astype(jnp.float32)).astype(jnp.bfloat16)
    return high, middle, low


def gather_rows(wanted_ref, table_ref, offered_ref):
    table_rows = table_ref.shape[0]
    blocks = wanted_ref.shape[0]
    step = 2
    for start in range(0, blocks, step):
        columns = [
            to_column(wanted_ref[block : block + 1, :].astype(jnp.float32)).astype(jnp.int32)
            for block in range(start, start + step)
        ]
        chosen = one_hot_rows(jnp.concatenate(columns, axis=0), table_rows)
        rows = pl.ds(start * LANES, step * LANES)
        offered_ref[rows, :] = dot(chosen, table_ref[...]).astype(jnp.bfloat16)


def offer_kernel(wanted_ref, table_ref, offered_ref):
    gather_rows(wanted_ref, table_ref, offered_ref)


def own_sum_kernel(asked_ref, arrived_ref, total_ref):
    rows = total_ref.shape[0]
    step = 256
    asked = asked_ref[...]
    for first in range(0, rows, step):
        chosen = one_hot_columns(asked, first, step)
        total_ref[first : first + step, :] = dot(chosen, arrived_ref[...])


def adagrad_block(gradient, first, table_ref, state_ref, new_state_ref):
    step, width = gradient.shape
    mean_square = jnp.sum(gradient * gradient, axis=1, keepdims=True) / width
    fresh = []
    for block in range(first // LANES, (first + step) // LANES):
        old = to_column(state_ref[block : block + 1, :])
        at = block * LANES - first
        new = old + mean_square[at : at + LANES, :]
        new_state_ref[block : block + 1, :] = to_row(new)
        fresh.append(new)
    rate = learn_rate / (jnp.sqrt(jnp.concatenate(fresh, axis=0)) + epsilon)
    values = table_ref[first : first + step, :].astype(jnp.float32)
    return (values - gradient * rate).astype(jnp.bfloat16)


def update_kernel(
    has_next,
    asked_ref,
    arrived_ref,
    own_ref,
    table_ref,
    state_ref,
    *rest,
):
    if has_next:
        wanted_ref, new_table_ref, new_state_ref, offered_ref = rest
    else:
        new_table_ref, new_state_ref = rest
    rows, width = table_ref.shape
    step = 256
    asked = asked_ref[...]
    for first in range(0, rows, step):
        chosen = one_hot_columns(asked, first, step)
        gradient = own_ref[first : first + step, :] + dot(chosen, arrived_ref[...])
        gradient = gradient[:, :width]
        stepped = adagrad_block(gradient, first, table_ref, state_ref, new_state_ref)
        if has_next:
            new_table_ref[first : first + step, :] = stepped
        else:
            turn_into(stepped, new_table_ref, first)
    if has_next:
        gather_rows(wanted_ref, new_table_ref, offered_ref)


def sigmoid(value):
    tail = jnp.exp(-jnp.abs(value))
    return jnp.where(value >= 0, 1.0, tail) / (1.0 + tail)


def trainer_core(
    blocks,
    negatives,
    width,
    pulled,
    spot_ref,
    cosine_ref,
    sine_ref,
    padded_ref,
    put_phase_grad,
    read_ref,
    rot_real_ref,
    rot_imag_ref,
    tail_real_ref,
    tail_imag_ref,
    neg_real_ref,
    neg_imag_ref,
    rot_real_grad_ref,
    rot_imag_grad_ref,
    tail_real_grad_ref,
    tail_imag_grad_ref,
    neg_real_grad_ref,
    neg_imag_grad_ref,
    grads_ref,
):
    slots = pulled.shape[0]
    half = width // 2
    triples = cosine_ref.shape[0]
    neg_rows = blocks * negatives
    margin = margin_rate * half

    places = [
        to_column(spot_ref[index : index + 1, :].astype(jnp.float32)).astype(jnp.int32)
        for index in range(3)
    ]
    places[2] = places[2][:neg_rows]
    read_ref[...] = dot(one_hot_rows(jnp.concatenate(places, axis=0), slots), pulled)
    head_ref = read_ref.at[:triples, :]
    tail_ref = read_ref.at[triples : 2 * triples, :]
    negative_ref = read_ref.at[2 * triples :, :]

    cosine = cosine_ref[...]
    sine = sine_ref[...]
    head_real = head_ref[:, :half]
    head_imag = head_ref[:, half:width]
    rot_real_ref[...] = head_real * cosine - head_imag * sine
    rot_imag_ref[...] = head_real * sine + head_imag * cosine
    tail_real_ref[...] = tail_ref[:, :half]
    tail_imag_ref[...] = tail_ref[:, half:width]
    neg_real_ref[...] = negative_ref[:, :half]
    neg_imag_ref[...] = negative_ref[:, half:width]
    neg_real_grad_ref[...] = jnp.zeros_like(neg_real_grad_ref)
    neg_imag_grad_ref[...] = jnp.zeros_like(neg_imag_grad_ref)

    group = 8
    per_block = triples // blocks

    def pair(real, imag, other_real, other_imag):
        diff_real = real - other_real
        diff_imag = imag - other_imag
        square = diff_real * diff_real + diff_imag * diff_imag + smoothing
        inverse = lax.rsqrt(square)
        distance = jnp.sum(square * inverse, axis=1, keepdims=True)
        return distance, diff_real * inverse, diff_imag * inverse

    def chunk(index, carry):
        rows = pl.ds(pl.multiple_of(index * group, group), group)
        first = (index * group) // per_block * negatives
        real = rot_real_ref[rows, :]
        imag = rot_imag_ref[rows, :]
        distance, unit_real, unit_imag = pair(
            real, imag, tail_real_ref[rows, :], tail_imag_ref[rows, :]
        )
        weight = 0.25 * sigmoid(0.25 * distance - margin)
        total_real = weight * unit_real
        total_imag = weight * unit_imag
        tail_real_grad_ref[rows, :] = -total_real
        tail_imag_grad_ref[rows, :] = -total_imag
        for n in range(negatives):
            distance, unit_real, unit_imag = pair(
                real,
                imag,
                neg_real_ref[pl.ds(first + n, 1), :],
                neg_imag_ref[pl.ds(first + n, 1), :],
            )
            weight = (-0.25 / negatives) * sigmoid(margin - 0.25 * distance)
            unit_real = weight * unit_real
            unit_imag = weight * unit_imag
            total_real += unit_real
            total_imag += unit_imag
            neg_real_grad_ref[first + n] -= unit_real
            neg_imag_grad_ref[first + n] -= unit_imag
        rot_real_grad_ref[rows, :] = total_real
        rot_imag_grad_ref[rows, :] = total_imag
        return carry

    lax.fori_loop(0, triples // group, chunk, 0)

    real_grad = rot_real_grad_ref[...]
    imag_grad = rot_imag_grad_ref[...]
    put_phase_grad(imag_grad * rot_real_ref[...] - real_grad * rot_imag_ref[...])

    grads_ref[:, width:] = jnp.zeros_like(grads_ref[:, width:])

    def put(first, rows, real, imag):
        high = jnp.concatenate([real, imag], axis=1)
        rounded = high.astype(jnp.bfloat16)
        grads_ref[first : first + rows, :width] = rounded
        low = (high - rounded.astype(jnp.float32)).astype(jnp.bfloat16)
        grads_ref[3 * triples + first : 3 * triples + first + rows, :width] = low

    put(
        0,
        triples,
        real_grad * cosine + imag_grad * sine,
        imag_grad * cosine - real_grad * sine,
    )
    put(triples, triples, tail_real_grad_ref[...], tail_imag_grad_ref[...])
    spare = jnp.zeros((triples - neg_rows, half), jnp.float32)
    put(
        2 * triples,
        triples,
        jnp.concatenate([jnp.sum(neg_real_grad_ref[...], axis=1), spare], axis=0),
        jnp.concatenate([jnp.sum(neg_imag_grad_ref[...], axis=1), spare], axis=0),
    )
    spots = [spot_ref[index : index + 1, :] for index in range(3)]
    for first in range(0, slots, 256):
        step = min(256, slots - first)
        chosen = [one_hot_columns(spot, first, step) for spot in spots]
        chosen = jnp.concatenate(chosen + chosen, axis=1)
        padded_ref[first : first + step, :] = dot(chosen, grads_ref[...]).astype(jnp.bfloat16)


def trainer_kernel(
    blocks,
    negatives,
    pulled_ref,
    spot_ref,
    cosine_ref,
    sine_ref,
    padded_ref,
    phase_grad_ref,
    *scratch,
):
    def put_phase_grad(value):
        phase_grad_ref[...] = value

    trainer_core(
        blocks,
        negatives,
        pulled_ref.shape[1],
        pulled_ref[...],
        spot_ref,
        cosine_ref,
        sine_ref,
        padded_ref,
        put_phase_grad,
        *scratch,
    )


def trainer_scratch(triples, neg_rows, width, wide, read_width):
    half = width // 2
    return (
        [pltpu.VMEM((2 * triples + neg_rows, read_width), jnp.float32)]
        + [pltpu.VMEM((triples, half), jnp.float32)] * 4
        + [pltpu.VMEM((neg_rows, half), jnp.float32)] * 2
        + [pltpu.VMEM((triples, half), jnp.float32)] * 4
        + [pltpu.VMEM((neg_rows, 8, half), jnp.float32)] * 2
        + [pltpu.VMEM((6 * triples, wide), jnp.bfloat16)]
    )


def relation_kernel(spot_ref, grad_ref, phase_ref, state_ref, new_phase_ref, new_state_ref):
    relations, half = phase_ref.shape
    chosen = one_hot_columns(spot_ref[3:4, :], 0, relations)
    high, middle, low = split3(grad_ref[...])
    gradient = dot(chosen, high) + dot(chosen, middle) + dot(chosen, low)
    gradient = gradient[:, :half]
    mean_square = jnp.sum(gradient * gradient, axis=1, keepdims=True) / half
    fresh = state_ref[...] + mean_square
    new_state_ref[...] = fresh
    new_phase_ref[...] = phase_ref[...] - learn_rate * gradient / (jnp.sqrt(fresh) + epsilon)


def short_relation_kernel(
    spot_ref, grad_ref, phase_ref, state_ref, new_phase_ref, new_state_ref, row_ref, flag_ref
):
    relation_kernel(spot_ref, grad_ref, phase_ref, state_ref, new_phase_ref, new_state_ref)
    relations = phase_ref.shape[0]
    spare = jnp.zeros((LANES - relations, 1), jnp.float32)
    row = to_row(jnp.concatenate([new_state_ref[...], spare], axis=0))
    row_ref[...] = row[:, :relations]
    last = grad_ref.shape[1] - 1
    mark = jnp.max(grad_ref[:, last : last + 1], axis=0, keepdims=True)
    flag_ref[...] = jnp.broadcast_to(mark, flag_ref.shape)


def shape(dims, dtype):
    return jax.ShapeDtypeStruct(dims, dtype)


def full_steps(
    entity_table,
    entity_state,
    relation_phase,
    relation_state,
    want_rows,
    want_count,
    head_slot,
    tail_slot,
    negative_slot,
    relation_ids,
):
    steps, owners, cap = want_rows.shape[1:]
    rows, width = entity_table.shape
    half = width // 2
    wide = -(-width // LANES) * LANES
    blocks, negatives = negative_slot.shape[2:]
    triples = head_slot.shape[2]
    slots = owners * cap
    relations = relation_phase.shape[0]
    table_bytes = 2 * rows * width

    asked = jnp.transpose(want_rows[0], (1, 0, 2)).reshape(owners, steps * cap)
    asked = lax.all_to_all(asked, "dom", split_axis=0, concat_axis=0, tiled=True)
    asked = jnp.transpose(asked.reshape(owners, steps, cap), (1, 0, 2))
    asked = asked.reshape(steps, slots // LANES, LANES)
    asked_other = lax.ppermute(asked, "rep", [(0, 1), (1, 0)])
    ask_row = asked.reshape(steps, 1, slots)
    ask_row_other = asked_other.reshape(steps, 1, slots)

    spots = []
    for step in range(steps):
        counts = want_count[0, step]
        neg = slot_place(negative_slot[0, step].reshape(-1), counts, cap)
        spare = jnp.full((triples - neg.shape[0],), -1, jnp.int32)
        spots.append(
            jnp.stack(
                [
                    slot_place(head_slot[0, step], counts, cap),
                    slot_place(tail_slot[0, step], counts, cap),
                    jnp.concatenate([neg, spare]),
                    relation_ids[0, step],
                ]
            )
        )

    table = entity_table
    state = entity_state.reshape(rows // LANES, LANES)
    phase = relation_phase
    phase_state = relation_state[:, None]
    offered = call(
        offer_kernel,
        shape((slots, width), jnp.bfloat16),
        "offer",
        flops=2 * slots * rows * width,
        nbytes=2 * table_bytes,
    )(asked[0], table)
    f32 = jnp.float32
    for step in range(steps):
        pulled = lax.all_to_all(
            offered.reshape(owners, cap, width), "dom", split_axis=0, concat_axis=0, tiled=True
        ).reshape(slots, width)
        relation_span = jnp.arange(relations, dtype=jnp.int32)
        selector = (relation_ids[0, step][:, None] == relation_span[None, :]).astype(f32)
        phase_rows = jnp.dot(selector, phase, precision=lax.Precision.HIGHEST)
        padded, phase_grad = call(
            functools.partial(trainer_kernel, blocks, negatives),
            (shape((slots, wide), jnp.bfloat16), shape((triples, half), f32)),
            "trainer",
            flops=2 * slots * (9 * triples) * width,
            nbytes=2 * table_bytes,
            scratch_shapes=trainer_scratch(triples, blocks * negatives, width, wide, width),
        )(pulled, spots[step], jnp.cos(phase_rows), jnp.sin(phase_rows))
        arrived = lax.all_to_all(
            padded.reshape(owners, cap, wide), "dom", split_axis=0, concat_axis=0, tiled=True
        ).reshape(slots, wide)
        phase, phase_state = call(
            relation_kernel,
            (shape((relations, half), f32), shape((relations, 1), f32)),
            "relation",
            flops=6 * triples * relations * half,
            nbytes=4 * triples * half,
        )(spots[step], phase_grad, phase, phase_state)
        arrived_other = lax.ppermute(arrived, "rep", [(0, 1), (1, 0)])
        own = call(
            own_sum_kernel,
            shape((rows, wide), f32),
            "own_sum",
            flops=2 * slots * rows * width,
            nbytes=3 * table_bytes,
        )(ask_row[step], arrived)
        has_next = step + 1 < steps
        outputs = [
            shape((rows, width) if has_next else (width, rows), jnp.bfloat16),
            shape((rows // LANES, LANES), f32),
        ]
        operands = [ask_row_other[step], arrived_other, own, table, state]
        if has_next:
            outputs.append(shape((slots, width), jnp.bfloat16))
            operands.append(asked[step + 1])
        results = call(
            functools.partial(update_kernel, has_next),
            tuple(outputs),
            "update",
            flops=2 * slots * rows * width * (1 + has_next),
            nbytes=6 * table_bytes,
        )(*operands)
        table, state = results[:2]
        if has_next:
            offered = results[2]
    return (table.T, state.reshape(rows), phase, phase_state[:, 0])


DIRECT = 5
LINE = 4
LENT = 32
PIECES = 8


def iota(dims, axis):
    return lax.broadcasted_iota(jnp.int32, dims, axis)


def as_bf16(mask):
    return jnp.where(mask, 1.0, 0.0).astype(jnp.bfloat16)


def places(width):
    full, rest = divmod(width, LANES)
    whole = [divmod(index, full) for index in range(DIRECT * full)]
    share = LANES // rest
    groups = [list(range(first, min(first + share, DIRECT))) for first in range(0, DIRECT, share)]
    return full, rest, whole, groups


def packed_width(width):
    full, rest, whole, groups = places(width)
    return -(-(len(whole) + len(groups)) // PIECES) * LANES


def stack_tile(position):
    tile, piece = divmod(position, PIECES)
    return slice(piece * LANES, (piece + 1) * LANES), slice(tile * LANES, (tile + 1) * LANES)


def spread(width, rows_ref, stack_ref, mark):
    full, rest, whole, groups = places(width)
    for position, (row, tile) in enumerate(whole):
        stack_ref[stack_tile(position)] = rows_ref[
            row * LANES : (row + 1) * LANES, tile * LANES : (tile + 1) * LANES
        ]
    last = len(whole) + len(groups) - 1
    for index, group in enumerate(groups):
        position = len(whole) + index
        total = jnp.zeros((LANES, LANES), jnp.float32)
        for row in group:
            tail = rows_ref[row * LANES : (row + 1) * LANES, full * LANES : (full + 1) * LANES]
            tail = tail.astype(jnp.float32)
            shift = rest * (row - group[0])
            total = total + (pltpu.roll(tail, shift, 1) if shift else tail)
        if position == last and mark is not None:
            total = jnp.where(iota((LANES, LANES), 1) == LANES - 1, mark, total)
        stack_ref[stack_tile(position)] = total.astype(jnp.bfloat16)
    for position in range(last + 1, stack_ref.shape[1] // LANES * PIECES):
        stack_ref[stack_tile(position)] = jnp.zeros((LANES, LANES), jnp.bfloat16)


def gather_up(width, stack_ref, rows_ref):
    full, rest, whole, groups = places(width)
    for position, (row, tile) in enumerate(whole):
        rows_ref[row * LANES : (row + 1) * LANES, tile * LANES : (tile + 1) * LANES] = stack_ref[
            stack_tile(position)
        ]
    for index, group in enumerate(groups):
        tails = stack_ref[stack_tile(len(whole) + index)].astype(jnp.float32)
        for row in group:
            shift = rest * (row - group[0])
            tail = pltpu.roll(tails, LANES - shift, 1) if shift else tails
            tail = jnp.where(iota((LANES, LANES), 1) < rest, tail, 0.0)
            rows_ref[row * LANES : (row + 1) * LANES, full * LANES : (full + 1) * LANES] = (
                tail.astype(jnp.bfloat16)
            )


def read_mark(width, stack_ref):
    full, rest, whole, groups = places(width)
    tile = stack_ref[stack_tile(len(whole) + len(groups) - 1)].astype(jnp.float32)
    tile = jnp.where(iota((LANES, LANES), 1) == LANES - 1, tile, 0.0)
    return jnp.max(jnp.max(tile, axis=1, keepdims=True), axis=0, keepdims=True)


PART = LANES // 4


def fold(stack_ref, packed_ref):
    size = PART * PIECES
    down, across = iota((size, size), 0), iota((size, size), 1)
    turn = as_bf16(across == (down % PIECES) * PART + down // PIECES)
    for part in range(LANES // PART):
        pieces = [
            stack_ref[piece * LANES + part * PART : piece * LANES + (part + 1) * PART, :]
            for piece in range(PIECES)
        ]
        packed_ref[part * size : (part + 1) * size, :] = dot(
            turn, jnp.concatenate(pieces, axis=0)
        ).astype(jnp.bfloat16)


def unfold(packed_ref, stack_ref):
    size = PART * PIECES
    down, across = iota((size, size), 0), iota((size, size), 1)
    turn = as_bf16(across == (down % PART) * PIECES + down // PART)
    for part in range(LANES // PART):
        block = dot(turn, packed_ref[part * size : (part + 1) * size, :]).astype(jnp.bfloat16)
        for piece in range(PIECES):
            stack_ref[piece * LANES + part * PART : piece * LANES + (part + 1) * PART, :] = block[
                piece * PART : (piece + 1) * PART, :
            ]


def route_kernel(
    rows,
    want_ref,
    count_ref,
    head_ref,
    tail_ref,
    neg_ref,
    relation_ref,
    ask_ref,
    *spot_refs,
):
    steps, cap, owners = want_ref.shape
    f32 = jnp.float32
    down, across = iota((LANES, LANES), 0), iota((LANES, LANES), 1)
    same_line = down // LINE == across // LINE
    line_mat = as_bf16(same_line)
    line_before = as_bf16(same_line & (down < across))
    upto = as_bf16(down <= across)
    owner = iota((1, LANES), 1).astype(f32)
    y_at = iota((1, LANES), 1) % LINE
    slot_number = iota((cap, LANES), 0).astype(f32)
    none = jnp.zeros((cap - 3, LANES), f32)
    asks = []
    for step in range(steps):
        count = count_ref[step : step + 1, :].astype(f32)
        ends = dot(jnp.broadcast_to(count, (cap, LANES)).astype(jnp.bfloat16), upto)[0:1, :]
        begins = ends - count
        seen = jnp.zeros((cap, LANES), f32)
        uses = []
        for ref in (head_ref, tail_ref, neg_ref):
            slot = to_column(ref[step : step + 1, :].astype(f32))
            owned = (slot >= begins) & (slot < ends)
            within = slot - jnp.sum(jnp.where(owned, begins, 0.0), axis=1, keepdims=True)
            seen += dot(as_bf16(slot_number == to_row(within)), as_bf16(owned))
            uses.append((owned, within))
        used = seen > 0.5
        ranks = [jnp.zeros((1, LANES), f32)]
        for slot in range(cap):
            ranks.append(ranks[-1] + jnp.where(used[slot : slot + 1, :], 1.0, 0.0))
        total = ranks.pop()
        rank = jnp.concatenate(ranks, axis=0)
        over = jnp.maximum(total - DIRECT, 0.0)
        free = DIRECT - jnp.minimum(total, DIRECT)
        pair = jnp.concatenate([over, free, total, none], axis=0).astype(jnp.bfloat16)
        before = dot(pair, line_before)
        whole = dot(pair, line_mat)
        lost = jnp.max(
            jnp.where(whole[0:1, :] > whole[1:2, :], 1.0, 0.0), axis=1, keepdims=True
        )
        turn = before[0:1, :] + rank - DIRECT
        side = jnp.concatenate([before[1:2, :], free, total, none], axis=0).astype(jnp.bfloat16)
        at_slot = rank
        at_owner = jnp.broadcast_to(owner, (cap, LANES))
        code = jnp.zeros((cap, LANES), f32)
        for far in range(1, LINE):
            mover = as_bf16(same_line & (down % LINE == (across + far) % LINE))
            moved = dot(side, mover)
            hit = used & (rank >= DIRECT) & (turn >= moved[0:1, :])
            hit = hit & (turn < moved[0:1, :] + moved[1:2, :])
            slot = moved[2:3, :] + turn - moved[0:1, :]
            other = owner + ((y_at + far) % LINE - y_at).astype(f32)
            at_slot = jnp.where(hit, slot, at_slot)
            at_owner = jnp.where(hit, other, at_owner)
            code = jnp.where(hit, rows * (far * cap + slot), code)
        want = want_ref[step].astype(f32)
        for place in range(cap):
            chosen = used & (rank == place)
            value = want + 1.0 if place < DIRECT else want + code + 1.0
            row = jnp.sum(jnp.where(chosen, value, 0.0), axis=0, keepdims=True) - 1.0
            if place == cap - 1:
                row = jnp.where(lost > 0.5, -2.0, row)
            asks.append(row)
        where_at = at_slot * owners + at_owner
        spots = []
        for owned, within in uses:
            table = jnp.zeros((LANES, LANES), f32)
            for slot in range(cap):
                table = jnp.where(within == slot, where_at[slot : slot + 1, :], table)
            found = jnp.sum(jnp.where(owned, table, 0.0), axis=1, keepdims=True)
            found = jnp.where(within < 0, -1.0, found)
            spots.append(to_row(found))
        spots.append(relation_ref[step : step + 1, :].astype(f32))
        spots.append(jnp.zeros((8 - len(spots), LANES), f32))
        spot_refs[step][...] = jnp.concatenate(spots, axis=0).astype(jnp.int32)
    asks.append(jnp.zeros((LANES - len(asks), LANES), f32))
    ask_ref[...] = jnp.transpose(jnp.concatenate(asks, axis=0)).astype(jnp.int32)


def fill_lent(tag_ref, step, table_ref, lent_ref):
    rows, width = table_ref.shape
    wide = lent_ref.shape[1] - LANES
    row, slot, trainer = (tag_ref[:, 3 * step + index : 3 * step + index + 1] for index in range(3))
    chosen = one_hot_rows(row.astype(jnp.int32), rows)
    lent_ref[:, wide - LANES : wide] = jnp.zeros((LANES, LANES), jnp.bfloat16)
    lent_ref[:, :width] = dot(chosen, table_ref[...]).astype(jnp.bfloat16)
    lanes = iota((LANES, LANES), 1)
    tags = jnp.where(lanes == 0, slot, jnp.where(lanes == 1, trainer, 0.0))
    lent_ref[:, wide:] = tags.astype(jnp.bfloat16)


def collect_kernel(
    steps, cap, ask_ref, table_ref, plan_ref, tag_ref, flag_ref, lent_ref
):
    rows = table_ref.shape[0]
    f32 = jnp.float32
    asked = jnp.transpose(ask_ref[...].astype(f32))[: steps * cap, :]
    down, across = iota((LANES, LANES), 0), iota((LANES, LANES), 1)
    earlier = as_bf16(down < across)
    trainer = iota((1, LANES), 1).astype(f32)
    flag = jnp.zeros((1, 1), f32)
    tags = jnp.full((LANES, LANES), -1.0, f32)
    lent_rows = []
    extra = cap - DIRECT
    for step in range(steps):
        codes = asked[step * cap + DIRECT : (step + 1) * cap, :].astype(jnp.int32)
        flag = jnp.maximum(
            flag,
            jnp.max(
                jnp.where(codes[extra - 1 : extra, :] == -2, 1.0, 0.0), axis=1, keepdims=True
            ),
        )
        valid = codes >= 0
        row = jnp.where(valid, codes % rows, 0).astype(f32)
        place = jnp.where(valid, codes // rows, 0)
        far = place // cap
        slot = (place % cap).astype(f32)
        masks = [
            jnp.where(valid & (far == distance), 1.0, 0.0) for distance in range(1, LINE)
        ]
        stacked = jnp.concatenate(
            masks + [jnp.zeros((16 - extra * (LINE - 1), LANES), f32)], axis=0
        )
        before = dot(stacked.astype(jnp.bfloat16), earlier)
        totals = jnp.sum(stacked, axis=1, keepdims=True)
        targets = [jnp.full((1, LANES), -1.0, f32) for entry in range(extra)]
        for index in range(LINE - 1):
            offset = jnp.zeros((1, 1), f32)
            for entry in range(extra):
                line = index * extra + entry
                at = before[line : line + 1, :] + offset + index * LENT
                targets[entry] = jnp.where(masks[index][entry : entry + 1, :] > 0.5, at, targets[entry])
                offset = offset + totals[line : line + 1, :]
            flag = jnp.maximum(flag, jnp.where(offset > LENT, 1.0, 0.0))
        sums = [jnp.zeros((LANES, 1), f32) for index in range(3)]
        for entry in range(extra):
            chosen = down.astype(f32) == targets[entry]
            values = (row[entry : entry + 1, :], slot[entry : entry + 1, :], trainer)
            for index, value in enumerate(values):
                picked = jnp.where(chosen, value + 1.0, 0.0)
                sums[index] += jnp.sum(picked, axis=1, keepdims=True)
        for index in range(3):
            tags = jnp.where(across == 3 * step + index, sums[index] - 1.0, tags)
        lent_rows.append(to_row(sums[0] - 1.0))
    lent_rows.append(jnp.full((8 - steps, LANES), -1.0, f32))
    plan_ref[...] = jnp.concatenate([asked] + lent_rows, axis=0).astype(jnp.int32)
    tag_ref[...] = tags
    flag_ref[...] = jnp.broadcast_to(flag, flag_ref.shape)
    fill_lent(tag_ref, 0, table_ref, lent_ref)


def direct_kernel(step, cap, plan_ref, table_ref, rows_ref):
    rows, width = table_ref.shape
    rows_ref[:, rows_ref.shape[1] - LANES :] = jnp.zeros((rows_ref.shape[0], LANES), jnp.bfloat16)
    for first in range(0, DIRECT, 2):
        last = min(first + 2, DIRECT)
        columns = [
            to_column(plan_ref[step * cap + slot : step * cap + slot + 1, :].astype(jnp.float32))
            for slot in range(first, last)
        ]
        chosen = one_hot_rows(jnp.concatenate(columns, axis=0).astype(jnp.int32), rows)
        rows_ref[first * LANES : last * LANES, :width] = dot(chosen, table_ref[...]).astype(
            jnp.bfloat16
        )


def pack_kernel(
    width, rows_ref, flag_ref, one_ref, two_ref, three_ref, packed_ref, tag_ref, lent_ref, full_ref, stack_ref
):
    wide = rows_ref.shape[1]
    lent_ref[3 * LENT :, :] = jnp.zeros((LANES - 3 * LENT, wide), jnp.bfloat16)
    tags = []
    for index, ref in enumerate((one_ref, two_ref, three_ref)):
        lent_ref[index * LENT : (index + 1) * LENT, :] = ref[:, :wide]
        tag = ref[:, wide : wide + LANES].astype(jnp.float32)
        tags.append(tag[:, 0:1] * LANES + tag[:, 1:2])
    tags.append(jnp.full((LANES - 3 * LENT, 1), -1.0, jnp.float32))
    tag = to_row(jnp.concatenate(tags, axis=0)).astype(jnp.int32)
    tag_ref[...] = jnp.broadcast_to(tag, tag_ref.shape)
    for slot in range(DIRECT):
        block = slice(slot * LANES, (slot + 1) * LANES)
        lent = dot(one_hot_columns(tag, slot * LANES, LANES), lent_ref[...])
        full_ref[block, :] = (rows_ref[block, :].astype(jnp.float32) + lent).astype(jnp.bfloat16)
    spread(width, full_ref, stack_ref, flag_ref[0:1, :])
    fold(stack_ref, packed_ref)


def short_trainer_kernel(
    blocks,
    negatives,
    width,
    pulled_ref,
    spot_ref,
    cosine_ref,
    sine_ref,
    packed_ref,
    phase_grad_ref,
    rows_ref,
    stack_ref,
    held_ref,
    copied,
    *scratch,
):
    unfold(pulled_ref, stack_ref)
    gather_up(width, stack_ref, rows_ref)
    mark = read_mark(width, stack_ref)
    sending = pltpu.make_async_copy(held_ref, phase_grad_ref, copied)

    def put_phase_grad(value):
        last = iota((held_ref.shape[0], LANES), 1) == LANES - 1
        held_ref[:, held_ref.shape[1] - LANES :] = jnp.where(last, mark, 0.0)
        held_ref[:, : value.shape[1]] = value
        sending.start()

    trainer_core(
        blocks,
        negatives,
        width,
        rows_ref[...],
        spot_ref,
        cosine_ref,
        sine_ref,
        rows_ref,
        put_phase_grad,
        *scratch,
    )
    spread(width, rows_ref, stack_ref, None)
    fold(stack_ref, packed_ref)
    sending.wait()


def return_kernel(width, arrived_ref, tag_ref, rows_ref, lent_ref, stack_ref):
    unfold(arrived_ref, stack_ref)
    gather_up(width, stack_ref, rows_ref)
    tag = to_column(tag_ref[0:1, :].astype(jnp.float32)).astype(jnp.int32)
    chosen = one_hot_rows(tag, rows_ref.shape[0])
    lent_ref[...] = dot(chosen, rows_ref[...]).astype(jnp.bfloat16)


def add_direct(step, cap, plan_ref, rows_ref, total_ref, before_ref):
    rows = [plan_ref[step * cap + slot : step * cap + slot + 1, :] for slot in range(DIRECT)]
    asked = jnp.concatenate(rows, axis=1)
    for first in range(0, total_ref.shape[0], 256):
        block = dot(one_hot_columns(asked, first, 256), rows_ref[...])
        if before_ref is not None:
            block = before_ref[first : first + 256, :] + block
        total_ref[first : first + 256, :] = block


def short_own_kernel(step, cap, plan_ref, rows_ref, total_ref):
    add_direct(step, cap, plan_ref, rows_ref, total_ref, None)


def short_other_kernel(
    step, cap, width, plan_ref, before_ref, arrived_ref, total_ref, stack_ref, other_ref
):
    unfold(arrived_ref, stack_ref)
    gather_up(width, stack_ref, other_ref)
    add_direct(step, cap, plan_ref, other_ref, total_ref, before_ref)


def short_update_kernel(
    step,
    cap,
    has_next,
    steps,
    plan_ref,
    other_plan_ref,
    total_ref,
    back_ref,
    other_back_ref,
    table_ref,
    state_ref,
    tag_ref,
    new_table_ref,
    new_state_ref,
    *rest,
):
    if has_next:
        lent_ref, first_ref, second_ref = rest
    else:
        first_ref, second_ref = rest
    rows, width = table_ref.shape
    for ref, source in ((first_ref, back_ref), (second_ref, other_back_ref)):
        ref[: 3 * LENT, :] = source[...]
        ref[3 * LENT :, :] = jnp.zeros((LANES - 3 * LENT, ref.shape[1]), jnp.bfloat16)
    line = steps * cap + step
    own, other = plan_ref[line : line + 1, :], other_plan_ref[line : line + 1, :]
    size = 256
    for first in range(0, rows, size):
        lent = dot(one_hot_columns(own, first, size), first_ref[...]) + dot(
            one_hot_columns(other, first, size), second_ref[...]
        )
        gradient = (total_ref[first : first + size, :] + lent)[:, :width]
        stepped = adagrad_block(gradient, first, table_ref, state_ref, new_state_ref)
        if has_next:
            new_table_ref[first : first + size, :] = stepped
        else:
            turn_into(stepped, new_table_ref, first)
    if has_next:
        fill_lent(tag_ref, step + 1, new_table_ref, lent_ref)


def line_pairs(owners, far):
    return [
        (owner, owner // LINE * LINE + (owner % LINE + far) % LINE) for owner in range(owners)
    ]


def short_steps(
    entity_table,
    entity_state,
    relation_phase,
    relation_state,
    want_rows,
    want_count,
    head_slot,
    tail_slot,
    negative_slot,
    relation_ids,
):
    steps, owners, cap = want_rows.shape[1:]
    rows, width = entity_table.shape
    half = width // 2
    wide = -(-width // LANES) * LANES
    blocks, negatives = negative_slot.shape[2:]
    triples = head_slot.shape[2]
    relations = relation_phase.shape[0]
    direct = DIRECT * LANES
    packed_rows = PIECES * LANES
    packed = packed_width(width)
    half_wide = -(-(half + 1) // LANES) * LANES
    f32, i32, bf16 = jnp.float32, jnp.int32, jnp.bfloat16

    neg = negative_slot[0].reshape(steps, blocks * negatives)
    neg = jnp.pad(neg, ((0, 0), (0, LANES - blocks * negatives)), constant_values=-1)
    asked, *spots = call(
        functools.partial(route_kernel, rows),
        (shape((LANES, LANES), i32),) + (shape((8, LANES), i32),) * steps,
        "route",
        nbytes=1 << 20,
    )(
        jnp.transpose(want_rows[0], (0, 2, 1)),
        want_count[0],
        head_slot[0],
        tail_slot[0],
        neg,
        relation_ids[0],
    )
    asked = lax.all_to_all(asked, "dom", split_axis=0, concat_axis=0, tiled=True)
    plan, tags, flag, lent = call(
        functools.partial(collect_kernel, steps, cap),
        (
            shape((steps * cap + 8, LANES), i32),
            shape((LANES, LANES), f32),
            shape((8, LANES), f32),
            shape((LANES, wide + LANES), bf16),
        ),
        "collect",
        nbytes=4 << 20,
    )(asked, entity_table)
    swap = [(0, 1), (1, 0)]
    other_plan = lax.ppermute(plan, "rep", swap)
    forth = [line_pairs(owners, far) for far in range(1, LINE)]
    back = [[(target, source) for source, target in pairs] for pairs in forth]

    table = entity_table
    state = entity_state.reshape(rows // LANES, LANES)
    phase = relation_phase
    phase_state = relation_state[:, None]
    relation = call(
        short_relation_kernel,
        (
            shape((relations, half), f32),
            shape((relations, 1), f32),
            shape((1, relations), f32),
            shape((8, LANES), f32),
        ),
        "relation",
        flops=6 * triples * relations * half,
        nbytes=4 * triples * half,
    )
    for step in range(steps):
        has_next = step + 1 < steps
        loans = [
            lax.ppermute(lent[index * LENT : (index + 1) * LENT], "dom", forth[index])
            for index in range(LINE - 1)
        ]
        sent = call(
            functools.partial(direct_kernel, step, cap),
            shape((direct, wide), bf16),
            "direct",
            flops=2 * direct * rows * width,
            nbytes=4 * rows * width,
        )(plan, table)
        offered, loan_tag = call(
            functools.partial(pack_kernel, width),
            (shape((packed_rows, packed), bf16), shape((8, LANES), i32)),
            "pack",
            nbytes=4 * rows * width,
            scratch_shapes=[
                pltpu.VMEM((LANES, wide), bf16),
                pltpu.VMEM((direct, wide), bf16),
                pltpu.VMEM((packed_rows, packed), bf16),
            ],
        )(sent, flag, *loans)
        if step > 0:
            offered, phase_grad = lax.optimization_barrier((offered, phase_grad))
            phase, phase_state, state_row, seen = relation(
                spots[step - 1], phase_grad, phase, phase_state
            )
            if step == 1:
                seen = jnp.maximum(seen, lax.ppermute(seen, "rep", swap))
                phase, spoiled = lax.optimization_barrier((phase, jnp.max(seen)))
        pulled = lax.all_to_all(
            offered.reshape(owners, PIECES, packed), "dom", split_axis=0, concat_axis=0, tiled=True
        ).reshape(packed_rows, packed)
        relation_span = jnp.arange(relations, dtype=i32)
        selector = (relation_ids[0, step][:, None] == relation_span[None, :]).astype(f32)
        phase_rows = jnp.dot(selector, phase, precision=lax.Precision.HIGHEST)
        padded, phase_grad = call(
            functools.partial(short_trainer_kernel, blocks, negatives, width),
            (shape((packed_rows, packed), bf16), shape((triples, half_wide), f32)),
            "trainer",
            flops=2 * direct * (9 * triples) * width,
            nbytes=4 * rows * width,
            out_specs=(pl.BlockSpec(memory_space=pltpu.VMEM), pl.BlockSpec(memory_space=pl.ANY)),
            scratch_shapes=[
                pltpu.VMEM((direct, wide), bf16),
                pltpu.VMEM((packed_rows, packed), bf16),
                pltpu.VMEM((triples, half_wide), f32),
                pltpu.SemaphoreType.DMA,
            ]
            + trainer_scratch(triples, blocks * negatives, width, wide, wide),
        )(pulled, spots[step], jnp.cos(phase_rows), jnp.sin(phase_rows))
        arrived = lax.all_to_all(
            padded.reshape(owners, PIECES, packed), "dom", split_axis=0, concat_axis=0, tiled=True
        ).reshape(packed_rows, packed)
        arrived_other = lax.ppermute(arrived, "rep", swap)
        got, dues = call(
            functools.partial(return_kernel, width),
            (shape((direct, wide), bf16), shape((LANES, wide), bf16)),
            "give_back",
            flops=2 * LANES * direct * wide,
            nbytes=4 * rows * width,
            scratch_shapes=[pltpu.VMEM((packed_rows, packed), bf16)],
        )(arrived, loan_tag)
        dues = [
            lax.ppermute(dues[index * LENT : (index + 1) * LENT], "dom", back[index])
            for index in range(LINE - 1)
        ]
        total = call(
            functools.partial(short_own_kernel, step, cap),
            shape((rows, wide), f32),
            "sum_own",
            flops=2 * direct * rows * width,
            nbytes=6 * rows * width,
        )(plan, got)
        dues, total = lax.optimization_barrier((dues, total))
        dues = jnp.concatenate(dues, axis=0)
        dues_other = lax.ppermute(dues, "rep", swap)
        total = call(
            functools.partial(short_other_kernel, step, cap, width),
            shape((rows, wide), f32),
            "sum_other",
            flops=2 * direct * rows * width,
            nbytes=10 * rows * width,
            scratch_shapes=[
                pltpu.VMEM((packed_rows, packed), bf16),
                pltpu.VMEM((direct, wide), bf16),
            ],
        )(other_plan, total, arrived_other)
        outputs = [
            shape((rows, width) if has_next else (width, rows), bf16),
            shape((rows // LANES, LANES), f32),
        ]
        if has_next:
            outputs.append(shape((LANES, wide + LANES), bf16))
        results = call(
            functools.partial(short_update_kernel, step, cap, has_next, steps),
            tuple(outputs),
            "update",
            flops=4 * LANES * rows * width,
            nbytes=12 * rows * width,
            scratch_shapes=[pltpu.VMEM((LANES, wide), bf16)] * 2,
        )(plan, other_plan, total, dues, dues_other, table, state, tags)
        table, state = results[:2]
        if has_next:
            lent = results[2]
    phase, phase_state, state_row, seen = relation(spots[-1], phase_grad, phase, phase_state)
    return (table.T, state.reshape(rows), phase, state_row.reshape(relations)), spoiled > 0.5


def local(*arrays):
    results, spoiled = short_steps(*arrays)
    return lax.cond(spoiled, lambda: full_steps(*arrays), lambda: results)


def solution(mesh):
    placed = (
        P("dom", None),
        P("dom"),
        P(("dom", "rep"), None),
        P(("dom", "rep")),
        P(("dom", "rep"), None, None, None),
        P(("dom", "rep"), None, None),
        P(("dom", "rep"), None, None),
        P(("dom", "rep"), None, None),
        P(("dom", "rep"), None, None, None),
        P(("dom", "rep"), None, None),
    )
    return jax.shard_map(
        local,
        mesh=mesh,
        in_specs=placed,
        out_specs=(P("dom", None), P("dom"), P(("dom", "rep"), None), P(("dom", "rep"))),
        check_vma=False,
    )
```

```python
import functools

import jax
import jax.numpy as jnp
from jax import lax
from jax.experimental import pallas as pl
from jax.experimental.pallas import tpu as pltpu
from jax.sharding import PartitionSpec as P

learn_rate = 0.5
smoothing = 0.25
epsilon = 1e-10
margin_rate = 0.26

LANES = 128
VMEM_LIMIT = 20 * 1024 * 1024


def slot_place(slot_ids, counts, slot_cap):
    running = jnp.cumsum(counts, dtype=jnp.int32)
    passed = (slot_ids[..., None] >= running).astype(jnp.int32)
    owner_index = jnp.sum(passed, axis=-1, dtype=jnp.int32)
    before = jnp.sum(passed * counts, axis=-1, dtype=jnp.int32)
    return owner_index * slot_cap + slot_ids - before


def call(kernel, out_shape, name, flops=0, nbytes=0, **kwargs):
    return pl.pallas_call(
        kernel,
        out_shape=out_shape,
        name=name,
        cost_estimate=pl.CostEstimate(flops=flops, bytes_accessed=nbytes, transcendentals=0),
        compiler_params=pltpu.CompilerParams(vmem_limit_bytes=VMEM_LIMIT),
        **kwargs,
    )


def diagonal():
    down = lax.broadcasted_iota(jnp.int32, (LANES, LANES), 0)
    across = lax.broadcasted_iota(jnp.int32, (LANES, LANES), 1)
    return down == across


def to_column(row):
    spread = jnp.broadcast_to(row, (LANES, LANES))
    return jnp.sum(jnp.where(diagonal(), spread, 0.0), axis=1, keepdims=True)


def to_row(column):
    spread = jnp.broadcast_to(column, (LANES, LANES))
    return jnp.sum(jnp.where(diagonal(), spread, 0.0), axis=0, keepdims=True)


def one_hot_rows(column, width):
    lanes = lax.broadcasted_iota(jnp.int32, (column.shape[0], width), 1)
    return jnp.where(lanes == column, 1.0, 0.0).astype(jnp.bfloat16)


def one_hot_columns(row, first, height):
    down = lax.broadcasted_iota(jnp.int32, (height, row.shape[1]), 0) + first
    return jnp.where(down == row, 1.0, 0.0).astype(jnp.bfloat16)


def dot(left, right):
    return jnp.dot(left, right, preferred_element_type=jnp.float32)


def turn_into(values, ref, first):
    rows, width = values.shape
    for start in range(0, width, 256):
        size = min(256, width - start)
        down = lax.broadcasted_iota(jnp.int32, (size, size), 0)
        across = lax.broadcasted_iota(jnp.int32, (size, size), 1)
        unit = jnp.where(down == across, 1.0, 0.0).astype(jnp.bfloat16)
        product = lax.dot_general(
            unit,
            values[:, start : start + size],
            (((1,), (1,)), ((), ())),
            preferred_element_type=jnp.float32,
        )
        ref[start : start + size, first : first + rows] = product.astype(jnp.bfloat16)


def split3(values):
    high = values.astype(jnp.bfloat16)
    rest = values - high.astype(jnp.float32)
    middle = rest.astype(jnp.bfloat16)
    low = (rest - middle.astype(jnp.float32)).astype(jnp.bfloat16)
    return high, middle, low


def gather_rows(wanted_ref, table_ref, offered_ref):
    table_rows = table_ref.shape[0]
    blocks = wanted_ref.shape[0]
    step = 2
    for start in range(0, blocks, step):
        columns = [
            to_column(wanted_ref[block : block + 1, :].astype(jnp.float32)).astype(jnp.int32)
            for block in range(start, start + step)
        ]
        chosen = one_hot_rows(jnp.concatenate(columns, axis=0), table_rows)
        rows = pl.ds(start * LANES, step * LANES)
        offered_ref[rows, :] = dot(chosen, table_ref[...]).astype(jnp.bfloat16)


def offer_kernel(wanted_ref, table_ref, offered_ref):
    gather_rows(wanted_ref, table_ref, offered_ref)


def own_sum_kernel(asked_ref, arrived_ref, total_ref):
    rows = total_ref.shape[0]
    step = 256
    asked = asked_ref[...]
    for first in range(0, rows, step):
        chosen = one_hot_columns(asked, first, step)
        total_ref[first : first + step, :] = dot(chosen, arrived_ref[...])


def adagrad_block(gradient, first, values, state_ref, new_state_ref):
    step, width = gradient.shape
    mean_square = jnp.sum(gradient * gradient, axis=1, keepdims=True) / width
    fresh = []
    for block in range(first // LANES, (first + step) // LANES):
        old = to_column(state_ref[block : block + 1, :])
        at = block * LANES - first
        new = old + mean_square[at : at + LANES, :]
        new_state_ref[block : block + 1, :] = to_row(new)
        fresh.append(new)
    rate = learn_rate / (jnp.sqrt(jnp.concatenate(fresh, axis=0)) + epsilon)
    return (values - gradient * rate).astype(jnp.bfloat16)


def update_kernel(
    has_next,
    asked_ref,
    arrived_ref,
    own_ref,
    table_ref,
    state_ref,
    *rest,
):
    if has_next:
        wanted_ref, new_table_ref, new_state_ref, offered_ref = rest
    else:
        new_table_ref, new_state_ref = rest
    rows, width = table_ref.shape
    step = 256
    asked = asked_ref[...]
    for first in range(0, rows, step):
        chosen = one_hot_columns(asked, first, step)
        gradient = own_ref[first : first + step, :] + dot(chosen, arrived_ref[...])
        gradient = gradient[:, :width]
        values = table_ref[first : first + step, :].astype(jnp.float32)
        stepped = adagrad_block(gradient, first, values, state_ref, new_state_ref)
        if has_next:
            new_table_ref[first : first + step, :] = stepped
        else:
            turn_into(stepped, new_table_ref, first)
    if has_next:
        gather_rows(wanted_ref, new_table_ref, offered_ref)


def sigmoid(value):
    tail = jnp.exp(-jnp.abs(value))
    return jnp.where(value >= 0, 1.0, tail) / (1.0 + tail)


def trainer_core(
    blocks,
    negatives,
    width,
    pulled,
    spot_ref,
    cosine_ref,
    sine_ref,
    padded_ref,
    put_phase_grad,
    read_ref,
    rot_real_ref,
    rot_imag_ref,
    tail_real_ref,
    tail_imag_ref,
    neg_real_ref,
    neg_imag_ref,
    rot_real_grad_ref,
    rot_imag_grad_ref,
    tail_real_grad_ref,
    tail_imag_grad_ref,
    neg_real_grad_ref,
    neg_imag_grad_ref,
    grads_ref,
):
    slots = pulled.shape[0]
    half = width // 2
    triples = cosine_ref.shape[0]
    neg_rows = blocks * negatives
    margin = margin_rate * half

    places = [
        to_column(spot_ref[index : index + 1, :].astype(jnp.float32)).astype(jnp.int32)
        for index in range(3)
    ]
    places[2] = places[2][:neg_rows]
    read_ref[...] = dot(one_hot_rows(jnp.concatenate(places, axis=0), slots), pulled)
    head_ref = read_ref.at[:triples, :]
    tail_ref = read_ref.at[triples : 2 * triples, :]
    negative_ref = read_ref.at[2 * triples :, :]

    cosine = cosine_ref[...]
    sine = sine_ref[...]
    head_real = head_ref[:, :half]
    head_imag = head_ref[:, half:width]
    rot_real_ref[...] = head_real * cosine - head_imag * sine
    rot_imag_ref[...] = head_real * sine + head_imag * cosine
    tail_real_ref[...] = tail_ref[:, :half]
    tail_imag_ref[...] = tail_ref[:, half:width]
    neg_real_ref[...] = negative_ref[:, :half]
    neg_imag_ref[...] = negative_ref[:, half:width]
    neg_real_grad_ref[...] = jnp.zeros_like(neg_real_grad_ref)
    neg_imag_grad_ref[...] = jnp.zeros_like(neg_imag_grad_ref)

    group = 8
    per_block = triples // blocks

    def pair(real, imag, other_real, other_imag):
        diff_real = real - other_real
        diff_imag = imag - other_imag
        square = diff_real * diff_real + diff_imag * diff_imag + smoothing
        inverse = lax.rsqrt(square)
        distance = jnp.sum(square * inverse, axis=1, keepdims=True)
        return distance, diff_real * inverse, diff_imag * inverse

    def chunk(index, carry):
        rows = pl.ds(pl.multiple_of(index * group, group), group)
        first = (index * group) // per_block * negatives
        real = rot_real_ref[rows, :]
        imag = rot_imag_ref[rows, :]
        distance, unit_real, unit_imag = pair(
            real, imag, tail_real_ref[rows, :], tail_imag_ref[rows, :]
        )
        weight = 0.25 * sigmoid(0.25 * distance - margin)
        total_real = weight * unit_real
        total_imag = weight * unit_imag
        tail_real_grad_ref[rows, :] = -total_real
        tail_imag_grad_ref[rows, :] = -total_imag
        for n in range(negatives):
            distance, unit_real, unit_imag = pair(
                real,
                imag,
                neg_real_ref[pl.ds(first + n, 1), :],
                neg_imag_ref[pl.ds(first + n, 1), :],
            )
            weight = (-0.25 / negatives) * sigmoid(margin - 0.25 * distance)
            unit_real = weight * unit_real
            unit_imag = weight * unit_imag
            total_real += unit_real
            total_imag += unit_imag
            neg_real_grad_ref[first + n] -= unit_real
            neg_imag_grad_ref[first + n] -= unit_imag
        rot_real_grad_ref[rows, :] = total_real
        rot_imag_grad_ref[rows, :] = total_imag
        return carry

    lax.fori_loop(0, triples // group, chunk, 0)

    real_grad = rot_real_grad_ref[...]
    imag_grad = rot_imag_grad_ref[...]
    put_phase_grad(imag_grad * rot_real_ref[...] - real_grad * rot_imag_ref[...])

    grads_ref[:, width:] = jnp.zeros_like(grads_ref[:, width:])

    def put(first, rows, real, imag):
        value = jnp.concatenate([real, imag], axis=1)
        grads_ref[first : first + rows, :width] = value.astype(jnp.bfloat16)

    put(
        0,
        triples,
        real_grad * cosine + imag_grad * sine,
        imag_grad * cosine - real_grad * sine,
    )
    put(triples, triples, tail_real_grad_ref[...], tail_imag_grad_ref[...])
    spare = jnp.zeros((triples - neg_rows, half), jnp.float32)
    put(
        2 * triples,
        triples,
        jnp.concatenate([jnp.sum(neg_real_grad_ref[...], axis=1), spare], axis=0),
        jnp.concatenate([jnp.sum(neg_imag_grad_ref[...], axis=1), spare], axis=0),
    )
    spots = [spot_ref[index : index + 1, :] for index in range(3)]
    for first in range(0, slots, 256):
        step = min(256, slots - first)
        chosen = [one_hot_columns(spot, first, step) for spot in spots]
        chosen = jnp.concatenate(chosen, axis=1)
        padded_ref[first : first + step, :] = dot(chosen, grads_ref[...]).astype(jnp.bfloat16)


def trainer_kernel(
    blocks,
    negatives,
    pulled_ref,
    spot_ref,
    cosine_ref,
    sine_ref,
    padded_ref,
    phase_grad_ref,
    *scratch,
):
    def put_phase_grad(value):
        phase_grad_ref[...] = value

    trainer_core(
        blocks,
        negatives,
        pulled_ref.shape[1],
        pulled_ref[...],
        spot_ref,
        cosine_ref,
        sine_ref,
        padded_ref,
        put_phase_grad,
        *scratch,
    )


def trainer_scratch(triples, neg_rows, width, wide, read_width):
    half = width // 2
    return (
        [pltpu.VMEM((2 * triples + neg_rows, read_width), jnp.float32)]
        + [pltpu.VMEM((triples, half), jnp.float32)] * 4
        + [pltpu.VMEM((neg_rows, half), jnp.float32)] * 2
        + [pltpu.VMEM((triples, half), jnp.float32)] * 4
        + [pltpu.VMEM((neg_rows, 8, half), jnp.float32)] * 2
        + [pltpu.VMEM((3 * triples, wide), jnp.bfloat16)]
    )


def relation_kernel(spot_ref, grad_ref, phase_ref, state_ref, new_phase_ref, new_state_ref):
    relations, half = phase_ref.shape
    chosen = one_hot_columns(spot_ref[3:4, :], 0, relations)
    high, middle, low = split3(grad_ref[...])
    gradient = dot(chosen, high) + dot(chosen, middle) + dot(chosen, low)
    gradient = gradient[:, :half]
    mean_square = jnp.sum(gradient * gradient, axis=1, keepdims=True) / half
    fresh = state_ref[...] + mean_square
    new_state_ref[...] = fresh
    new_phase_ref[...] = phase_ref[...] - learn_rate * gradient / (jnp.sqrt(fresh) + epsilon)


def short_relation_kernel(
    spot_ref,
    grad_ref,
    phase_ref,
    state_ref,
    new_phase_ref,
    new_state_ref,
    row_ref,
    flag_ref,
    held_ref,
    copied,
):
    relation_kernel(spot_ref, grad_ref, phase_ref, state_ref, held_ref, new_state_ref)
    sending = pltpu.make_async_copy(held_ref, new_phase_ref, copied)
    sending.start()
    relations = phase_ref.shape[0]
    spare = jnp.zeros((LANES - relations, 1), jnp.float32)
    row = to_row(jnp.concatenate([new_state_ref[...], spare], axis=0))
    row_ref[...] = row[:, :relations]
    last = grad_ref.shape[1] - 1
    mark = jnp.max(grad_ref[:, last : last + 1], axis=0, keepdims=True)
    flag_ref[...] = jnp.broadcast_to(mark, flag_ref.shape)
    sending.wait()


def shape(dims, dtype):
    return jax.ShapeDtypeStruct(dims, dtype)


def full_steps(
    entity_table,
    entity_state,
    relation_phase,
    relation_state,
    want_rows,
    want_count,
    head_slot,
    tail_slot,
    negative_slot,
    relation_ids,
):
    steps, owners, cap = want_rows.shape[1:]
    rows, width = entity_table.shape
    half = width // 2
    wide = -(-width // LANES) * LANES
    blocks, negatives = negative_slot.shape[2:]
    triples = head_slot.shape[2]
    slots = owners * cap
    relations = relation_phase.shape[0]
    table_bytes = 2 * rows * width

    asked = jnp.transpose(want_rows[0], (1, 0, 2)).reshape(owners, steps * cap)
    asked = lax.all_to_all(asked, "dom", split_axis=0, concat_axis=0, tiled=True)
    asked = jnp.transpose(asked.reshape(owners, steps, cap), (1, 0, 2))
    asked = asked.reshape(steps, slots // LANES, LANES)
    asked_other = lax.ppermute(asked, "rep", [(0, 1), (1, 0)])
    ask_row = asked.reshape(steps, 1, slots)
    ask_row_other = asked_other.reshape(steps, 1, slots)

    spots = []
    for step in range(steps):
        counts = want_count[0, step]
        neg = slot_place(negative_slot[0, step].reshape(-1), counts, cap)
        spare = jnp.full((triples - neg.shape[0],), -1, jnp.int32)
        spots.append(
            jnp.stack(
                [
                    slot_place(head_slot[0, step], counts, cap),
                    slot_place(tail_slot[0, step], counts, cap),
                    jnp.concatenate([neg, spare]),
                    relation_ids[0, step],
                ]
            )
        )

    table = entity_table
    state = entity_state.reshape(rows // LANES, LANES)
    phase = relation_phase
    phase_state = relation_state[:, None]
    offered = call(
        offer_kernel,
        shape((slots, width), jnp.bfloat16),
        "offer",
        flops=2 * slots * rows * width,
        nbytes=2 * table_bytes,
    )(asked[0], table)
    f32 = jnp.float32
    for step in range(steps):
        pulled = lax.all_to_all(
            offered.reshape(owners, cap, width), "dom", split_axis=0, concat_axis=0, tiled=True
        ).reshape(slots, width)
        relation_span = jnp.arange(relations, dtype=jnp.int32)
        selector = (relation_ids[0, step][:, None] == relation_span[None, :]).astype(f32)
        phase_rows = jnp.dot(selector, phase, precision=lax.Precision.HIGHEST)
        padded, phase_grad = call(
            functools.partial(trainer_kernel, blocks, negatives),
            (shape((slots, wide), jnp.bfloat16), shape((triples, half), f32)),
            "trainer",
            flops=2 * slots * (9 * triples) * width,
            nbytes=2 * table_bytes,
            scratch_shapes=trainer_scratch(triples, blocks * negatives, width, wide, width),
        )(pulled, spots[step], jnp.cos(phase_rows), jnp.sin(phase_rows))
        arrived = lax.all_to_all(
            padded.reshape(owners, cap, wide), "dom", split_axis=0, concat_axis=0, tiled=True
        ).reshape(slots, wide)
        phase, phase_state = call(
            relation_kernel,
            (shape((relations, half), f32), shape((relations, 1), f32)),
            "relation",
            flops=6 * triples * relations * half,
            nbytes=4 * triples * half,
        )(spots[step], phase_grad, phase, phase_state)
        arrived_other = lax.ppermute(arrived, "rep", [(0, 1), (1, 0)])
        own = call(
            own_sum_kernel,
            shape((rows, wide), f32),
            "own_sum",
            flops=2 * slots * rows * width,
            nbytes=3 * table_bytes,
        )(ask_row[step], arrived)
        has_next = step + 1 < steps
        outputs = [
            shape((rows, width) if has_next else (width, rows), jnp.bfloat16),
            shape((rows // LANES, LANES), f32),
        ]
        operands = [ask_row_other[step], arrived_other, own, table, state]
        if has_next:
            outputs.append(shape((slots, width), jnp.bfloat16))
            operands.append(asked[step + 1])
        results = call(
            functools.partial(update_kernel, has_next),
            tuple(outputs),
            "update",
            flops=2 * slots * rows * width * (1 + has_next),
            nbytes=6 * table_bytes,
        )(*operands)
        table, state = results[:2]
        if has_next:
            offered = results[2]
    return (table.T, state.reshape(rows), phase, phase_state[:, 0])


DIRECT = 5
LINE = 4
LENT = 32
PIECES = 8


def iota(dims, axis):
    return lax.broadcasted_iota(jnp.int32, dims, axis)


def as_bf16(mask):
    return jnp.where(mask, 1.0, 0.0).astype(jnp.bfloat16)


def places(width):
    full, rest = divmod(width, LANES)
    whole = [divmod(index, full) for index in range(DIRECT * full)]
    share = LANES // rest
    groups = [list(range(first, min(first + share, DIRECT))) for first in range(0, DIRECT, share)]
    return full, rest, whole, groups


def packed_width(width):
    full, rest, whole, groups = places(width)
    return -(-(len(whole) + len(groups)) // PIECES) * LANES


def stack_tile(position):
    tile, piece = divmod(position, PIECES)
    return slice(piece * LANES, (piece + 1) * LANES), slice(tile * LANES, (tile + 1) * LANES)


def spread(width, rows_ref, stack_ref, mark):
    full, rest, whole, groups = places(width)
    for position, (row, tile) in enumerate(whole):
        stack_ref[stack_tile(position)] = rows_ref[
            row * LANES : (row + 1) * LANES, tile * LANES : (tile + 1) * LANES
        ]
    last = len(whole) + len(groups) - 1
    for index, group in enumerate(groups):
        position = len(whole) + index
        total = jnp.zeros((LANES, LANES), jnp.float32)
        for row in group:
            tail = rows_ref[row * LANES : (row + 1) * LANES, full * LANES : (full + 1) * LANES]
            tail = tail.astype(jnp.float32)
            shift = rest * (row - group[0])
            total = total + (pltpu.roll(tail, shift, 1) if shift else tail)
        if position == last and mark is not None:
            total = jnp.where(iota((LANES, LANES), 1) == LANES - 1, mark, total)
        stack_ref[stack_tile(position)] = total.astype(jnp.bfloat16)
    for position in range(last + 1, stack_ref.shape[1] // LANES * PIECES):
        stack_ref[stack_tile(position)] = jnp.zeros((LANES, LANES), jnp.bfloat16)


def gather_up(width, stack_ref, rows_ref):
    full, rest, whole, groups = places(width)
    for position, (row, tile) in enumerate(whole):
        rows_ref[row * LANES : (row + 1) * LANES, tile * LANES : (tile + 1) * LANES] = stack_ref[
            stack_tile(position)
        ]
    for index, group in enumerate(groups):
        tails = stack_ref[stack_tile(len(whole) + index)].astype(jnp.float32)
        for row in group:
            shift = rest * (row - group[0])
            tail = pltpu.roll(tails, LANES - shift, 1) if shift else tails
            tail = jnp.where(iota((LANES, LANES), 1) < rest, tail, 0.0)
            rows_ref[row * LANES : (row + 1) * LANES, full * LANES : (full + 1) * LANES] = (
                tail.astype(jnp.bfloat16)
            )


def read_mark(width, stack_ref):
    full, rest, whole, groups = places(width)
    tile = stack_ref[stack_tile(len(whole) + len(groups) - 1)].astype(jnp.float32)
    tile = jnp.where(iota((LANES, LANES), 1) == LANES - 1, tile, 0.0)
    return jnp.max(jnp.max(tile, axis=1, keepdims=True), axis=0, keepdims=True)


PART = LANES // 4


def fold(stack_ref, packed_ref, done=None):
    size = PART * PIECES
    down, across = iota((size, size), 0), iota((size, size), 1)
    turn = as_bf16(across == (down % PIECES) * PART + down // PIECES)
    for part in range(LANES // PART):
        pieces = [
            stack_ref[piece * LANES + part * PART : piece * LANES + (part + 1) * PART, :]
            for piece in range(PIECES)
        ]
        packed_ref[part * size : (part + 1) * size, :] = dot(
            turn, jnp.concatenate(pieces, axis=0)
        ).astype(jnp.bfloat16)
        if done is not None:
            done(part, pl.ds(part * size, size))


def unfold(packed_ref, stack_ref):
    size = PART * PIECES
    down, across = iota((size, size), 0), iota((size, size), 1)
    turn = as_bf16(across == (down % PART) * PIECES + down // PART)
    for part in range(LANES // PART):
        block = dot(turn, packed_ref[part * size : (part + 1) * size, :]).astype(jnp.bfloat16)
        for piece in range(PIECES):
            stack_ref[piece * LANES + part * PART : piece * LANES + (part + 1) * PART, :] = block[
                piece * PART : (piece + 1) * PART, :
            ]


def route_kernel(
    rows,
    want_ref,
    count_ref,
    head_ref,
    tail_ref,
    neg_ref,
    relation_ref,
    ask_ref,
    *spot_refs,
):
    steps, cap, owners = want_ref.shape
    f32 = jnp.float32
    down, across = iota((LANES, LANES), 0), iota((LANES, LANES), 1)
    same_line = down // LINE == across // LINE
    line_mat = as_bf16(same_line)
    line_before = as_bf16(same_line & (down < across))
    upto = as_bf16(down <= across)
    owner = iota((1, LANES), 1).astype(f32)
    y_at = iota((1, LANES), 1) % LINE
    slot_number = iota((cap, LANES), 0).astype(f32)
    none = jnp.zeros((cap - 3, LANES), f32)
    asks = []
    for step in range(steps):
        count = count_ref[step : step + 1, :].astype(f32)
        ends = dot(jnp.broadcast_to(count, (cap, LANES)).astype(jnp.bfloat16), upto)[0:1, :]
        begins = ends - count
        seen = jnp.zeros((cap, LANES), f32)
        uses = []
        slots = [to_column(ref[step : step + 1, :].astype(f32)) for ref in (head_ref, tail_ref)]
        slots.append(jnp.full((LANES, 1), -1.0, f32))
        blocks, negatives = neg_ref.shape[1:]
        for block in range(blocks):
            row = neg_ref[step, block : block + 1, :].astype(f32) + 1.0
            here = iota((LANES, negatives), 0) - block * negatives == iota((LANES, negatives), 1)
            slots[2] += jnp.sum(jnp.where(here, row, 0.0), axis=1, keepdims=True)
        for slot in slots:
            owned = (slot >= begins) & (slot < ends)
            within = slot - jnp.sum(jnp.where(owned, begins, 0.0), axis=1, keepdims=True)
            seen += dot(as_bf16(slot_number == to_row(within)), as_bf16(owned))
            uses.append((owned, within))
        used = seen > 0.5
        ranks = [jnp.zeros((1, LANES), f32)]
        for slot in range(cap):
            ranks.append(ranks[-1] + jnp.where(used[slot : slot + 1, :], 1.0, 0.0))
        total = ranks.pop()
        rank = jnp.concatenate(ranks, axis=0)
        over = jnp.maximum(total - DIRECT, 0.0)
        free = DIRECT - jnp.minimum(total, DIRECT)
        pair = jnp.concatenate([over, free, total, none], axis=0).astype(jnp.bfloat16)
        before = dot(pair, line_before)
        whole = dot(pair, line_mat)
        lost = jnp.max(
            jnp.where(whole[0:1, :] > whole[1:2, :], 1.0, 0.0), axis=1, keepdims=True
        )
        turn = before[0:1, :] + rank - DIRECT
        side = jnp.concatenate([before[1:2, :], free, total, none], axis=0).astype(jnp.bfloat16)
        at_slot = rank
        at_owner = jnp.broadcast_to(owner, (cap, LANES))
        code = jnp.zeros((cap, LANES), f32)
        for far in range(1, LINE):
            mover = as_bf16(same_line & (down % LINE == (across + far) % LINE))
            moved = dot(side, mover)
            hit = used & (rank >= DIRECT) & (turn >= moved[0:1, :])
            hit = hit & (turn < moved[0:1, :] + moved[1:2, :])
            slot = moved[2:3, :] + turn - moved[0:1, :]
            other = owner + ((y_at + far) % LINE - y_at).astype(f32)
            at_slot = jnp.where(hit, slot, at_slot)
            at_owner = jnp.where(hit, other, at_owner)
            code = jnp.where(hit, rows * (far * cap + slot), code)
        want = want_ref[step].astype(f32)
        for place in range(cap):
            chosen = used & (rank == place)
            value = want + 1.0 if place < DIRECT else want + code + 1.0
            row = jnp.sum(jnp.where(chosen, value, 0.0), axis=0, keepdims=True) - 1.0
            if place == cap - 1:
                row = jnp.where(lost > 0.5, -2.0, row)
            asks.append(row)
        where_at = at_slot * owners + at_owner
        spots = []
        for owned, within in uses:
            table = jnp.zeros((LANES, LANES), f32)
            for slot in range(cap):
                table = jnp.where(within == slot, where_at[slot : slot + 1, :], table)
            found = jnp.sum(jnp.where(owned, table, 0.0), axis=1, keepdims=True)
            found = jnp.where(within < 0, -1.0, found)
            spots.append(to_row(found))
        spots.append(relation_ref[step : step + 1, :].astype(f32))
        spots.append(jnp.zeros((8 - len(spots), LANES), f32))
        spot_refs[step][...] = jnp.concatenate(spots, axis=0).astype(jnp.int32)
    asks.append(jnp.zeros((LANES - len(asks), LANES), f32))
    ask_ref[...] = jnp.transpose(jnp.concatenate(asks, axis=0)).astype(jnp.int32)


def table_dims(table_ref, across):
    return table_ref.shape[::-1] if across else table_ref.shape


def pick_rows(chosen, table_ref, across):
    axis = 1 if across else 0
    return lax.dot_general(
        chosen,
        table_ref[...],
        (((1,), (axis,)), ((), ())),
        preferred_element_type=jnp.float32,
    )


def table_block(table_ref, first, size, across):
    if not across:
        return table_ref[first : first + size, :].astype(jnp.float32)
    width = table_ref.shape[0]
    unit = as_bf16(iota((size, size), 0) == iota((size, size), 1))
    return lax.dot_general(
        unit,
        table_ref[:, first : first + size],
        (((1,), (1,)), ((), ())),
        preferred_element_type=jnp.float32,
    )


def fill_lent(tag_ref, step, table_ref, lent_ref, across):
    rows, width = table_dims(table_ref, across)
    wide = lent_ref.shape[1] - LANES
    row, slot, trainer = (tag_ref[:, 3 * step + index : 3 * step + index + 1] for index in range(3))
    chosen = one_hot_rows(row.astype(jnp.int32), rows)
    lent_ref[:, wide - LANES : wide] = jnp.zeros((LANES, LANES), jnp.bfloat16)
    lent_ref[:, :width] = pick_rows(chosen, table_ref, across).astype(jnp.bfloat16)
    lanes = iota((LANES, LANES), 1)
    tags = jnp.where(lanes == 0, slot, jnp.where(lanes == 1, trainer, 0.0))
    lent_ref[:, wide:] = tags.astype(jnp.bfloat16)


def collect_kernel(
    steps, cap, ask_ref, table_ref, plan_ref, tag_ref, flag_ref, lent_ref
):
    rows = table_ref.shape[1]
    f32 = jnp.float32
    asked = jnp.transpose(ask_ref[...].astype(f32))[: steps * cap, :]
    down, across = iota((LANES, LANES), 0), iota((LANES, LANES), 1)
    earlier = as_bf16(down < across)
    trainer = iota((1, LANES), 1).astype(f32)
    flag = jnp.zeros((1, 1), f32)
    tags = jnp.full((LANES, LANES), -1.0, f32)
    lent_rows = []
    extra = cap - DIRECT
    for step in range(steps):
        codes = asked[step * cap + DIRECT : (step + 1) * cap, :].astype(jnp.int32)
        flag = jnp.maximum(
            flag,
            jnp.max(
                jnp.where(codes[extra - 1 : extra, :] == -2, 1.0, 0.0), axis=1, keepdims=True
            ),
        )
        valid = codes >= 0
        row = jnp.where(valid, codes % rows, 0).astype(f32)
        place = jnp.where(valid, codes // rows, 0)
        far = place // cap
        slot = (place % cap).astype(f32)
        masks = [
            jnp.where(valid & (far == distance), 1.0, 0.0) for distance in range(1, LINE)
        ]
        stacked = jnp.concatenate(
            masks + [jnp.zeros((16 - extra * (LINE - 1), LANES), f32)], axis=0
        )
        before = dot(stacked.astype(jnp.bfloat16), earlier)
        totals = jnp.sum(stacked, axis=1, keepdims=True)
        targets = [jnp.full((1, LANES), -1.0, f32) for entry in range(extra)]
        for index in range(LINE - 1):
            offset = jnp.zeros((1, 1), f32)
            for entry in range(extra):
                line = index * extra + entry
                at = before[line : line + 1, :] + offset + index * LENT
                targets[entry] = jnp.where(masks[index][entry : entry + 1, :] > 0.5, at, targets[entry])
                offset = offset + totals[line : line + 1, :]
            flag = jnp.maximum(flag, jnp.where(offset > LENT, 1.0, 0.0))
        sums = [jnp.zeros((LANES, 1), f32) for index in range(3)]
        for entry in range(extra):
            chosen = down.astype(f32) == targets[entry]
            values = (row[entry : entry + 1, :], slot[entry : entry + 1, :], trainer)
            for index, value in enumerate(values):
                picked = jnp.where(chosen, value + 1.0, 0.0)
                sums[index] += jnp.sum(picked, axis=1, keepdims=True)
        for index in range(3):
            tags = jnp.where(across == 3 * step + index, sums[index] - 1.0, tags)
        lent_rows.append(to_row(sums[0] - 1.0))
    lent_rows.append(jnp.full((8 - steps, LANES), -1.0, f32))
    plan_ref[...] = jnp.concatenate([asked] + lent_rows, axis=0).astype(jnp.int32)
    tag_ref[...] = tags
    flag_ref[...] = jnp.broadcast_to(flag, flag_ref.shape)
    fill_lent(tag_ref, 0, table_ref, lent_ref, True)


def direct_kernel(step, cap, across, plan_ref, table_ref, rows_ref):
    rows, width = table_dims(table_ref, across)
    rows_ref[:, rows_ref.shape[1] - LANES :] = jnp.zeros((rows_ref.shape[0], LANES), jnp.bfloat16)
    for first in range(0, DIRECT, 2):
        last = min(first + 2, DIRECT)
        columns = [
            to_column(plan_ref[step * cap + slot : step * cap + slot + 1, :].astype(jnp.float32))
            for slot in range(first, last)
        ]
        chosen = one_hot_rows(jnp.concatenate(columns, axis=0).astype(jnp.int32), rows)
        rows_ref[first * LANES : last * LANES, :width] = pick_rows(
            chosen, table_ref, across
        ).astype(jnp.bfloat16)


def pack_kernel(
    width,
    rows_ref,
    flag_ref,
    one_ref,
    two_ref,
    three_ref,
    packed_ref,
    tag_ref,
    lent_ref,
    full_ref,
    stack_ref,
    held_ref,
    copied,
):
    wide = rows_ref.shape[1]
    lent_ref[3 * LENT :, :] = jnp.zeros((LANES - 3 * LENT, wide), jnp.bfloat16)
    tags = []
    for index, ref in enumerate((one_ref, two_ref, three_ref)):
        lent_ref[index * LENT : (index + 1) * LENT, :] = ref[:, :wide]
        tag = ref[:, wide : wide + LANES].astype(jnp.float32)
        tags.append(tag[:, 0:1] * LANES + tag[:, 1:2])
    tags.append(jnp.full((LANES - 3 * LENT, 1), -1.0, jnp.float32))
    tag = to_row(jnp.concatenate(tags, axis=0)).astype(jnp.int32)
    tag_ref[...] = jnp.broadcast_to(tag, tag_ref.shape)
    for slot in range(DIRECT):
        block = slice(slot * LANES, (slot + 1) * LANES)
        lent = dot(one_hot_columns(tag, slot * LANES, LANES), lent_ref[...])
        full_ref[block, :] = (rows_ref[block, :].astype(jnp.float32) + lent).astype(jnp.bfloat16)
    spread(width, full_ref, stack_ref, flag_ref[0:1, :])
    copies = []

    def send(part, rows):
        copies.append(
            pltpu.make_async_copy(held_ref.at[rows, :], packed_ref.at[rows, :], copied.at[part])
        )
        copies[-1].start()

    fold(stack_ref, held_ref, send)
    for copy in copies:
        copy.wait()


def short_trainer_kernel(
    blocks,
    negatives,
    width,
    pulled_ref,
    spot_ref,
    cosine_ref,
    sine_ref,
    packed_ref,
    phase_grad_ref,
    rows_ref,
    stack_ref,
    held_ref,
    copied,
    *scratch,
):
    unfold(pulled_ref, stack_ref)
    gather_up(width, stack_ref, rows_ref)
    mark = read_mark(width, stack_ref)
    sending = pltpu.make_async_copy(held_ref, phase_grad_ref, copied)

    def put_phase_grad(value):
        last = iota((held_ref.shape[0], LANES), 1) == LANES - 1
        held_ref[:, held_ref.shape[1] - LANES :] = jnp.where(last, mark, 0.0)
        held_ref[:, : value.shape[1]] = value
        sending.start()

    trainer_core(
        blocks,
        negatives,
        width,
        rows_ref[...],
        spot_ref,
        cosine_ref,
        sine_ref,
        rows_ref,
        put_phase_grad,
        *scratch,
    )
    spread(width, rows_ref, stack_ref, None)
    fold(stack_ref, packed_ref)
    sending.wait()


def return_kernel(width, arrived_ref, tag_ref, rows_ref, lent_ref, stack_ref):
    unfold(arrived_ref, stack_ref)
    gather_up(width, stack_ref, rows_ref)
    tag = to_column(tag_ref[0:1, :].astype(jnp.float32)).astype(jnp.int32)
    chosen = one_hot_rows(tag, rows_ref.shape[0])
    lent_ref[...] = dot(chosen, rows_ref[...]).astype(jnp.bfloat16)


def sum_kernel(
    step, cap, width, plan_ref, other_plan_ref, rows_ref, arrived_ref, total_ref, stack_ref, other_ref
):
    unfold(arrived_ref, stack_ref)
    gather_up(width, stack_ref, other_ref)

    def asked(ref):
        rows = [ref[step * cap + slot : step * cap + slot + 1, :] for slot in range(DIRECT)]
        return jnp.concatenate(rows, axis=1)

    own, other = asked(plan_ref), asked(other_plan_ref)
    for first in range(0, total_ref.shape[0], 256):
        total_ref[first : first + 256, :] = dot(
            one_hot_columns(own, first, 256), rows_ref[...]
        ) + dot(one_hot_columns(other, first, 256), other_ref[...])


def short_update_kernel(
    step,
    cap,
    has_next,
    steps,
    plan_ref,
    other_plan_ref,
    total_ref,
    back_ref,
    other_back_ref,
    table_ref,
    state_ref,
    tag_ref,
    new_table_ref,
    new_state_ref,
    *rest,
):
    if has_next:
        lent_ref, first_ref, second_ref = rest
    else:
        first_ref, second_ref = rest
    rows, width = table_dims(table_ref, step == 0)
    for ref, source in ((first_ref, back_ref), (second_ref, other_back_ref)):
        ref[: 3 * LENT, :] = source[...]
        ref[3 * LENT :, :] = jnp.zeros((LANES - 3 * LENT, ref.shape[1]), jnp.bfloat16)
    line = steps * cap + step
    own, other = plan_ref[line : line + 1, :], other_plan_ref[line : line + 1, :]
    size = 256
    for first in range(0, rows, size):
        lent = dot(one_hot_columns(own, first, size), first_ref[...]) + dot(
            one_hot_columns(other, first, size), second_ref[...]
        )
        gradient = (total_ref[first : first + size, :] + lent)[:, :width]
        values = table_block(table_ref, first, size, step == 0)
        stepped = adagrad_block(gradient, first, values, state_ref, new_state_ref)
        if has_next:
            new_table_ref[first : first + size, :] = stepped
        else:
            turn_into(stepped, new_table_ref, first)
    if has_next:
        fill_lent(tag_ref, step + 1, new_table_ref, lent_ref, False)


def line_pairs(owners, far):
    return [
        (owner, owner // LINE * LINE + (owner % LINE + far) % LINE) for owner in range(owners)
    ]


def short_steps(
    entity_table,
    entity_state,
    relation_phase,
    relation_state,
    want_rows,
    want_count,
    head_slot,
    tail_slot,
    negative_slot,
    relation_ids,
):
    steps, owners, cap = want_rows.shape[1:]
    rows, width = entity_table.shape
    half = width // 2
    wide = -(-width // LANES) * LANES
    blocks, negatives = negative_slot.shape[2:]
    triples = head_slot.shape[2]
    relations = relation_phase.shape[0]
    direct = DIRECT * LANES
    packed_rows = PIECES * LANES
    packed = packed_width(width)
    half_wide = -(-(half + 1) // LANES) * LANES
    f32, i32, bf16 = jnp.float32, jnp.int32, jnp.bfloat16

    asked, *spots = call(
        functools.partial(route_kernel, rows),
        (shape((LANES, LANES), i32),) + (shape((8, LANES), i32),) * steps,
        "route",
        nbytes=1 << 20,
    )(
        jnp.transpose(want_rows[0], (0, 2, 1)),
        want_count[0],
        head_slot[0],
        tail_slot[0],
        negative_slot[0],
        relation_ids[0],
    )
    asked = lax.all_to_all(asked, "dom", split_axis=0, concat_axis=0, tiled=True)
    plan, tags, flag, lent = call(
        functools.partial(collect_kernel, steps, cap),
        (
            shape((steps * cap + 8, LANES), i32),
            shape((LANES, LANES), f32),
            shape((8, LANES), f32),
            shape((LANES, wide + LANES), bf16),
        ),
        "collect",
        nbytes=4 << 20,
    )(asked, entity_table.T)
    swap = [(0, 1), (1, 0)]
    other_plan = lax.ppermute(plan, "rep", swap)
    forth = [line_pairs(owners, far) for far in range(1, LINE)]
    back = [[(target, source) for source, target in pairs] for pairs in forth]

    table = entity_table.T
    state = entity_state.reshape(rows // LANES, LANES)
    phase = relation_phase
    phase_state = relation_state[:, None]
    relation = call(
        short_relation_kernel,
        (
            shape((relations, half), f32),
            shape((relations, 1), f32),
            shape((1, relations), f32),
            shape((8, LANES), f32),
        ),
        "relation",
        flops=6 * triples * relations * half,
        nbytes=4 * triples * half,
        out_specs=(pl.BlockSpec(memory_space=pltpu.HBM),)
        + (pl.BlockSpec(memory_space=pltpu.VMEM),) * 3,
        scratch_shapes=[pltpu.VMEM((relations, half), f32), pltpu.SemaphoreType.DMA],
    )
    for step in range(steps):
        has_next = step + 1 < steps
        loans = [
            lax.ppermute(lent[index * LENT : (index + 1) * LENT], "dom", forth[index])
            for index in range(LINE - 1)
        ]
        sent = call(
            functools.partial(direct_kernel, step, cap, step == 0),
            shape((direct, wide), bf16),
            "direct",
            flops=2 * direct * rows * width,
            nbytes=4 * rows * width,
        )(plan, table)
        offered, loan_tag = call(
            functools.partial(pack_kernel, width),
            (shape((packed_rows, packed), bf16), shape((8, LANES), i32)),
            "pack",
            nbytes=4 * rows * width,
            out_specs=(pl.BlockSpec(memory_space=pltpu.HBM), pl.BlockSpec(memory_space=pltpu.VMEM)),
            scratch_shapes=[
                pltpu.VMEM((LANES, wide), bf16),
                pltpu.VMEM((direct, wide), bf16),
                pltpu.VMEM((packed_rows, packed), bf16),
                pltpu.VMEM((packed_rows, packed), bf16),
                pltpu.SemaphoreType.DMA((LANES // PART,)),
            ],
        )(sent, flag, *loans)
        if step > 0:
            offered, phase_grad = lax.optimization_barrier((offered, phase_grad))
            phase, phase_state, state_row, seen = relation(
                spots[step - 1], phase_grad, phase, phase_state
            )
            if step == 1:
                seen = jnp.maximum(seen, lax.ppermute(seen, "rep", swap))
                phase, spoiled = lax.optimization_barrier((phase, jnp.max(seen)))
        pulled = lax.all_to_all(
            offered.reshape(owners, PIECES, packed), "dom", split_axis=0, concat_axis=0, tiled=True
        ).reshape(packed_rows, packed)
        relation_span = jnp.arange(relations, dtype=i32)
        selector = (relation_ids[0, step][:, None] == relation_span[None, :]).astype(f32)
        phase_rows = jnp.dot(selector, phase, precision=lax.Precision.HIGHEST)
        padded, phase_grad = call(
            functools.partial(short_trainer_kernel, blocks, negatives, width),
            (shape((packed_rows, packed), bf16), shape((triples, half_wide), f32)),
            "trainer",
            flops=2 * direct * (9 * triples) * width,
            nbytes=4 * rows * width,
            out_specs=(pl.BlockSpec(memory_space=pltpu.VMEM), pl.BlockSpec(memory_space=pltpu.HBM)),
            scratch_shapes=[
                pltpu.VMEM((direct, wide), bf16),
                pltpu.VMEM((packed_rows, packed), bf16),
                pltpu.VMEM((triples, half_wide), f32),
                pltpu.SemaphoreType.DMA,
            ]
            + trainer_scratch(triples, blocks * negatives, width, wide, wide),
        )(pulled, spots[step], jnp.cos(phase_rows), jnp.sin(phase_rows))
        arrived = lax.all_to_all(
            padded.reshape(owners, PIECES, packed), "dom", split_axis=0, concat_axis=0, tiled=True
        ).reshape(packed_rows, packed)
        arrived_other = lax.ppermute(arrived, "rep", swap)
        got, dues = call(
            functools.partial(return_kernel, width),
            (shape((direct, wide), bf16), shape((LANES, wide), bf16)),
            "give_back",
            flops=2 * LANES * direct * wide,
            nbytes=4 * rows * width,
            scratch_shapes=[pltpu.VMEM((packed_rows, packed), bf16)],
        )(arrived, loan_tag)
        dues = [
            lax.ppermute(dues[index * LENT : (index + 1) * LENT], "dom", back[index])
            for index in range(LINE - 1)
        ]
        total = call(
            functools.partial(sum_kernel, step, cap, width),
            shape((rows, wide), f32),
            "sum",
            flops=4 * direct * rows * width,
            nbytes=8 * rows * width,
            scratch_shapes=[
                pltpu.VMEM((packed_rows, packed), bf16),
                pltpu.VMEM((direct, wide), bf16),
            ],
        )(plan, other_plan, got, arrived_other)
        dues, total = lax.optimization_barrier((dues, total))
        dues = jnp.concatenate(dues, axis=0)
        dues_other = lax.ppermute(dues, "rep", swap)
        outputs = [
            shape((rows, width) if has_next else (width, rows), bf16),
            shape((rows // LANES, LANES), f32),
        ]
        if has_next:
            outputs.append(shape((LANES, wide + LANES), bf16))
        results = call(
            functools.partial(short_update_kernel, step, cap, has_next, steps),
            tuple(outputs),
            "update",
            flops=4 * LANES * rows * width,
            nbytes=12 * rows * width,
            scratch_shapes=[pltpu.VMEM((LANES, wide), bf16)] * 2,
        )(plan, other_plan, total, dues, dues_other, table, state, tags)
        table, state = results[:2]
        if has_next:
            lent = results[2]
    phase, phase_state, state_row, seen = relation(spots[-1], phase_grad, phase, phase_state)
    return (table.T, state.reshape(rows), phase, state_row.reshape(relations)), spoiled > 0.5


def local(*arrays):
    results, spoiled = short_steps(*arrays)
    return lax.cond(spoiled, lambda: full_steps(*arrays), lambda: results)


def solution(mesh):
    placed = (
        P("dom", None),
        P("dom"),
        P(("dom", "rep"), None),
        P(("dom", "rep")),
        P(("dom", "rep"), None, None, None),
        P(("dom", "rep"), None, None),
        P(("dom", "rep"), None, None),
        P(("dom", "rep"), None, None),
        P(("dom", "rep"), None, None, None),
        P(("dom", "rep"), None, None),
    )
    return jax.shard_map(
        local,
        mesh=mesh,
        in_specs=placed,
        out_specs=(P("dom", None), P("dom"), P(("dom", "rep"), None), P(("dom", "rep"))),
        check_vma=False,
    )
```

```python
import functools

import jax
import jax.numpy as jnp
from jax import lax
from jax.experimental import pallas as pl
from jax.experimental.pallas import tpu as pltpu
from jax.sharding import PartitionSpec as P

learn_rate = 0.5
smoothing = 0.25
epsilon = 1e-10
margin_rate = 0.26

LANES = 128
VMEM_LIMIT = 20 * 1024 * 1024


def slot_place(slot_ids, counts, slot_cap):
    running = jnp.cumsum(counts, dtype=jnp.int32)
    passed = (slot_ids[..., None] >= running).astype(jnp.int32)
    owner_index = jnp.sum(passed, axis=-1, dtype=jnp.int32)
    before = jnp.sum(passed * counts, axis=-1, dtype=jnp.int32)
    return owner_index * slot_cap + slot_ids - before


def call(kernel, out_shape, name, flops=0, nbytes=0, **kwargs):
    return pl.pallas_call(
        kernel,
        out_shape=out_shape,
        name=name,
        cost_estimate=pl.CostEstimate(flops=flops, bytes_accessed=nbytes, transcendentals=0),
        compiler_params=pltpu.CompilerParams(vmem_limit_bytes=VMEM_LIMIT),
        **kwargs,
    )


def diagonal():
    down = lax.broadcasted_iota(jnp.int32, (LANES, LANES), 0)
    across = lax.broadcasted_iota(jnp.int32, (LANES, LANES), 1)
    return down == across


def to_column(row):
    spread = jnp.broadcast_to(row, (LANES, LANES))
    return jnp.sum(jnp.where(diagonal(), spread, 0.0), axis=1, keepdims=True)


def to_row(column):
    spread = jnp.broadcast_to(column, (LANES, LANES))
    return jnp.sum(jnp.where(diagonal(), spread, 0.0), axis=0, keepdims=True)


def one_hot_rows(column, width):
    lanes = lax.broadcasted_iota(jnp.int32, (column.shape[0], width), 1)
    return jnp.where(lanes == column, 1.0, 0.0).astype(jnp.bfloat16)


def one_hot_columns(row, first, height):
    down = lax.broadcasted_iota(jnp.int32, (height, row.shape[1]), 0) + first
    return jnp.where(down == row, 1.0, 0.0).astype(jnp.bfloat16)


def dot(left, right):
    return jnp.dot(left, right, preferred_element_type=jnp.float32)


def turn_into(values, ref, first):
    rows, width = values.shape
    for start in range(0, width, 256):
        size = min(256, width - start)
        down = lax.broadcasted_iota(jnp.int32, (size, size), 0)
        across = lax.broadcasted_iota(jnp.int32, (size, size), 1)
        unit = jnp.where(down == across, 1.0, 0.0).astype(jnp.bfloat16)
        product = lax.dot_general(
            unit,
            values[:, start : start + size],
            (((1,), (1,)), ((), ())),
            preferred_element_type=jnp.float32,
        )
        ref[start : start + size, first : first + rows] = product.astype(jnp.bfloat16)


def split3(values):
    high = values.astype(jnp.bfloat16)
    rest = values - high.astype(jnp.float32)
    middle = rest.astype(jnp.bfloat16)
    low = (rest - middle.astype(jnp.float32)).astype(jnp.bfloat16)
    return high, middle, low


def gather_rows(wanted_ref, table_ref, offered_ref):
    table_rows = table_ref.shape[0]
    blocks = wanted_ref.shape[0]
    step = 2
    for start in range(0, blocks, step):
        columns = [
            to_column(wanted_ref[block : block + 1, :].astype(jnp.float32)).astype(jnp.int32)
            for block in range(start, start + step)
        ]
        chosen = one_hot_rows(jnp.concatenate(columns, axis=0), table_rows)
        rows = pl.ds(start * LANES, step * LANES)
        offered_ref[rows, :] = dot(chosen, table_ref[...]).astype(jnp.bfloat16)


def offer_kernel(wanted_ref, table_ref, offered_ref):
    gather_rows(wanted_ref, table_ref, offered_ref)


def own_sum_kernel(asked_ref, arrived_ref, total_ref):
    rows = total_ref.shape[0]
    step = 256
    asked = asked_ref[...]
    for first in range(0, rows, step):
        chosen = one_hot_columns(asked, first, step)
        total_ref[first : first + step, :] = dot(chosen, arrived_ref[...])


def adagrad_block(gradient, first, values, state_ref, new_state_ref):
    step, width = gradient.shape
    mean_square = jnp.sum(gradient * gradient, axis=1, keepdims=True) / width
    fresh = []
    for block in range(first // LANES, (first + step) // LANES):
        old = to_column(state_ref[block : block + 1, :])
        at = block * LANES - first
        new = old + mean_square[at : at + LANES, :]
        new_state_ref[block : block + 1, :] = to_row(new)
        fresh.append(new)
    rate = learn_rate / (jnp.sqrt(jnp.concatenate(fresh, axis=0)) + epsilon)
    return (values - gradient * rate).astype(jnp.bfloat16)


def update_kernel(
    has_next,
    asked_ref,
    arrived_ref,
    own_ref,
    table_ref,
    state_ref,
    *rest,
):
    if has_next:
        wanted_ref, new_table_ref, new_state_ref, offered_ref = rest
    else:
        new_table_ref, new_state_ref = rest
    rows, width = table_ref.shape
    step = 256
    asked = asked_ref[...]
    for first in range(0, rows, step):
        chosen = one_hot_columns(asked, first, step)
        gradient = own_ref[first : first + step, :] + dot(chosen, arrived_ref[...])
        gradient = gradient[:, :width]
        values = table_ref[first : first + step, :].astype(jnp.float32)
        stepped = adagrad_block(gradient, first, values, state_ref, new_state_ref)
        if has_next:
            new_table_ref[first : first + step, :] = stepped
        else:
            turn_into(stepped, new_table_ref, first)
    if has_next:
        gather_rows(wanted_ref, new_table_ref, offered_ref)


def sigmoid(value):
    tail = jnp.exp(-jnp.abs(value))
    return jnp.where(value >= 0, 1.0, tail) / (1.0 + tail)


def trainer_core(
    blocks,
    negatives,
    width,
    pulled,
    spot_ref,
    cosine_ref,
    sine_ref,
    padded_ref,
    put_phase_grad,
    read_ref,
    rot_real_ref,
    rot_imag_ref,
    tail_real_ref,
    tail_imag_ref,
    neg_real_ref,
    neg_imag_ref,
    rot_real_grad_ref,
    rot_imag_grad_ref,
    tail_real_grad_ref,
    tail_imag_grad_ref,
    neg_real_grad_ref,
    neg_imag_grad_ref,
    grads_ref,
):
    slots = pulled.shape[0]
    half = width // 2
    triples = cosine_ref.shape[0]
    neg_rows = blocks * negatives
    margin = margin_rate * half

    places = [
        to_column(spot_ref[index : index + 1, :].astype(jnp.float32)).astype(jnp.int32)
        for index in range(3)
    ]
    places[2] = places[2][:neg_rows]
    read_ref[...] = dot(one_hot_rows(jnp.concatenate(places, axis=0), slots), pulled)
    head_ref = read_ref.at[:triples, :]
    tail_ref = read_ref.at[triples : 2 * triples, :]
    negative_ref = read_ref.at[2 * triples :, :]

    cosine = cosine_ref[...]
    sine = sine_ref[...]
    head_real = head_ref[:, :half]
    head_imag = head_ref[:, half:width]
    rot_real_ref[...] = head_real * cosine - head_imag * sine
    rot_imag_ref[...] = head_real * sine + head_imag * cosine
    tail_real_ref[...] = tail_ref[:, :half]
    tail_imag_ref[...] = tail_ref[:, half:width]
    neg_real_ref[...] = negative_ref[:, :half]
    neg_imag_ref[...] = negative_ref[:, half:width]
    neg_real_grad_ref[...] = jnp.zeros_like(neg_real_grad_ref)
    neg_imag_grad_ref[...] = jnp.zeros_like(neg_imag_grad_ref)

    group = 8
    per_block = triples // blocks

    def pair(real, imag, other_real, other_imag):
        diff_real = real - other_real
        diff_imag = imag - other_imag
        square = diff_real * diff_real + diff_imag * diff_imag + smoothing
        inverse = lax.rsqrt(square)
        distance = jnp.sum(square * inverse, axis=1, keepdims=True)
        return distance, diff_real * inverse, diff_imag * inverse

    def chunk(index, carry):
        rows = pl.ds(pl.multiple_of(index * group, group), group)
        first = (index * group) // per_block * negatives
        real = rot_real_ref[rows, :]
        imag = rot_imag_ref[rows, :]
        distance, unit_real, unit_imag = pair(
            real, imag, tail_real_ref[rows, :], tail_imag_ref[rows, :]
        )
        weight = 0.25 * sigmoid(0.25 * distance - margin)
        total_real = weight * unit_real
        total_imag = weight * unit_imag
        tail_real_grad_ref[rows, :] = -total_real
        tail_imag_grad_ref[rows, :] = -total_imag
        for n in range(negatives):
            distance, unit_real, unit_imag = pair(
                real,
                imag,
                neg_real_ref[pl.ds(first + n, 1), :],
                neg_imag_ref[pl.ds(first + n, 1), :],
            )
            weight = (-0.25 / negatives) * sigmoid(margin - 0.25 * distance)
            unit_real = weight * unit_real
            unit_imag = weight * unit_imag
            total_real += unit_real
            total_imag += unit_imag
            neg_real_grad_ref[first + n] -= unit_real
            neg_imag_grad_ref[first + n] -= unit_imag
        rot_real_grad_ref[rows, :] = total_real
        rot_imag_grad_ref[rows, :] = total_imag
        return carry

    lax.fori_loop(0, triples // group, chunk, 0)

    real_grad = rot_real_grad_ref[...]
    imag_grad = rot_imag_grad_ref[...]
    put_phase_grad(imag_grad * rot_real_ref[...] - real_grad * rot_imag_ref[...])

    grads_ref[:, width:] = jnp.zeros_like(grads_ref[:, width:])

    def put(first, rows, real, imag):
        value = jnp.concatenate([real, imag], axis=1)
        grads_ref[first : first + rows, :width] = value.astype(jnp.bfloat16)

    put(
        0,
        triples,
        real_grad * cosine + imag_grad * sine,
        imag_grad * cosine - real_grad * sine,
    )
    put(triples, triples, tail_real_grad_ref[...], tail_imag_grad_ref[...])
    spare = jnp.zeros((triples - neg_rows, half), jnp.float32)
    put(
        2 * triples,
        triples,
        jnp.concatenate([jnp.sum(neg_real_grad_ref[...], axis=1), spare], axis=0),
        jnp.concatenate([jnp.sum(neg_imag_grad_ref[...], axis=1), spare], axis=0),
    )
    spots = [spot_ref[index : index + 1, :] for index in range(3)]
    for first in range(0, slots, 256):
        step = min(256, slots - first)
        chosen = [one_hot_columns(spot, first, step) for spot in spots]
        chosen = jnp.concatenate(chosen, axis=1)
        padded_ref[first : first + step, :] = dot(chosen, grads_ref[...]).astype(jnp.bfloat16)


def trainer_kernel(
    blocks,
    negatives,
    pulled_ref,
    spot_ref,
    cosine_ref,
    sine_ref,
    padded_ref,
    phase_grad_ref,
    *scratch,
):
    def put_phase_grad(value):
        phase_grad_ref[...] = value

    trainer_core(
        blocks,
        negatives,
        pulled_ref.shape[1],
        pulled_ref[...],
        spot_ref,
        cosine_ref,
        sine_ref,
        padded_ref,
        put_phase_grad,
        *scratch,
    )


def trainer_scratch(triples, neg_rows, width, wide, read_width):
    half = width // 2
    return (
        [pltpu.VMEM((2 * triples + neg_rows, read_width), jnp.float32)]
        + [pltpu.VMEM((triples, half), jnp.float32)] * 4
        + [pltpu.VMEM((neg_rows, half), jnp.float32)] * 2
        + [pltpu.VMEM((triples, half), jnp.float32)] * 4
        + [pltpu.VMEM((neg_rows, 8, half), jnp.float32)] * 2
        + [pltpu.VMEM((3 * triples, wide), jnp.bfloat16)]
    )


def relation_kernel(spot_ref, grad_ref, phase_ref, state_ref, new_phase_ref, new_state_ref):
    relations, half = phase_ref.shape
    chosen = one_hot_columns(spot_ref[3:4, :], 0, relations)
    high, middle, low = split3(grad_ref[...])
    gradient = dot(chosen, high) + dot(chosen, middle) + dot(chosen, low)
    gradient = gradient[:, :half]
    mean_square = jnp.sum(gradient * gradient, axis=1, keepdims=True) / half
    fresh = state_ref[...] + mean_square
    new_state_ref[...] = fresh
    new_phase_ref[...] = phase_ref[...] - learn_rate * gradient / (jnp.sqrt(fresh) + epsilon)


def short_relation_kernel(
    spot_ref,
    grad_ref,
    phase_ref,
    state_ref,
    new_phase_ref,
    new_state_ref,
    row_ref,
    flag_ref,
):
    relation_kernel(spot_ref, grad_ref, phase_ref, state_ref, new_phase_ref, new_state_ref)
    relations = phase_ref.shape[0]
    spare = jnp.zeros((LANES - relations, 1), jnp.float32)
    row = to_row(jnp.concatenate([new_state_ref[...], spare], axis=0))
    row_ref[...] = row[:, :relations]
    last = grad_ref.shape[1] - 1
    mark = jnp.max(grad_ref[:, last : last + 1], axis=0, keepdims=True)
    flag_ref[...] = jnp.broadcast_to(mark, flag_ref.shape)


def shape(dims, dtype):
    return jax.ShapeDtypeStruct(dims, dtype)


def full_steps(
    entity_table,
    entity_state,
    relation_phase,
    relation_state,
    want_rows,
    want_count,
    head_slot,
    tail_slot,
    negative_slot,
    relation_ids,
):
    steps, owners, cap = want_rows.shape[1:]
    rows, width = entity_table.shape
    half = width // 2
    wide = -(-width // LANES) * LANES
    blocks, negatives = negative_slot.shape[2:]
    triples = head_slot.shape[2]
    slots = owners * cap
    relations = relation_phase.shape[0]
    table_bytes = 2 * rows * width

    asked = jnp.transpose(want_rows[0], (1, 0, 2)).reshape(owners, steps * cap)
    asked = lax.all_to_all(asked, "dom", split_axis=0, concat_axis=0, tiled=True)
    asked = jnp.transpose(asked.reshape(owners, steps, cap), (1, 0, 2))
    asked = asked.reshape(steps, slots // LANES, LANES)
    asked_other = lax.ppermute(asked, "rep", [(0, 1), (1, 0)])
    ask_row = asked.reshape(steps, 1, slots)
    ask_row_other = asked_other.reshape(steps, 1, slots)

    spots = []
    for step in range(steps):
        counts = want_count[0, step]
        neg = slot_place(negative_slot[0, step].reshape(-1), counts, cap)
        spare = jnp.full((triples - neg.shape[0],), -1, jnp.int32)
        spots.append(
            jnp.stack(
                [
                    slot_place(head_slot[0, step], counts, cap),
                    slot_place(tail_slot[0, step], counts, cap),
                    jnp.concatenate([neg, spare]),
                    relation_ids[0, step],
                ]
            )
        )

    table = entity_table
    state = entity_state.reshape(rows // LANES, LANES)
    phase = relation_phase
    phase_state = relation_state[:, None]
    offered = call(
        offer_kernel,
        shape((slots, width), jnp.bfloat16),
        "offer",
        flops=2 * slots * rows * width,
        nbytes=2 * table_bytes,
    )(asked[0], table)
    f32 = jnp.float32
    for step in range(steps):
        pulled = lax.all_to_all(
            offered.reshape(owners, cap, width), "dom", split_axis=0, concat_axis=0, tiled=True
        ).reshape(slots, width)
        relation_span = jnp.arange(relations, dtype=jnp.int32)
        selector = (relation_ids[0, step][:, None] == relation_span[None, :]).astype(f32)
        phase_rows = jnp.dot(selector, phase, precision=lax.Precision.HIGHEST)
        padded, phase_grad = call(
            functools.partial(trainer_kernel, blocks, negatives),
            (shape((slots, wide), jnp.bfloat16), shape((triples, half), f32)),
            "trainer",
            flops=2 * slots * (9 * triples) * width,
            nbytes=2 * table_bytes,
            scratch_shapes=trainer_scratch(triples, blocks * negatives, width, wide, width),
        )(pulled, spots[step], jnp.cos(phase_rows), jnp.sin(phase_rows))
        arrived = lax.all_to_all(
            padded.reshape(owners, cap, wide), "dom", split_axis=0, concat_axis=0, tiled=True
        ).reshape(slots, wide)
        phase, phase_state = call(
            relation_kernel,
            (shape((relations, half), f32), shape((relations, 1), f32)),
            "relation",
            flops=6 * triples * relations * half,
            nbytes=4 * triples * half,
        )(spots[step], phase_grad, phase, phase_state)
        arrived_other = lax.ppermute(arrived, "rep", [(0, 1), (1, 0)])
        own = call(
            own_sum_kernel,
            shape((rows, wide), f32),
            "own_sum",
            flops=2 * slots * rows * width,
            nbytes=3 * table_bytes,
        )(ask_row[step], arrived)
        has_next = step + 1 < steps
        outputs = [
            shape((rows, width) if has_next else (width, rows), jnp.bfloat16),
            shape((rows // LANES, LANES), f32),
        ]
        operands = [ask_row_other[step], arrived_other, own, table, state]
        if has_next:
            outputs.append(shape((slots, width), jnp.bfloat16))
            operands.append(asked[step + 1])
        results = call(
            functools.partial(update_kernel, has_next),
            tuple(outputs),
            "update",
            flops=2 * slots * rows * width * (1 + has_next),
            nbytes=6 * table_bytes,
        )(*operands)
        table, state = results[:2]
        if has_next:
            offered = results[2]
    return (table.T, state.reshape(rows), phase, phase_state[:, 0])


DIRECT = 5
LINE = 4
LENT = 32
PIECES = 8


def iota(dims, axis):
    return lax.broadcasted_iota(jnp.int32, dims, axis)


def as_bf16(mask):
    return jnp.where(mask, 1.0, 0.0).astype(jnp.bfloat16)


def places(width):
    full, rest = divmod(width, LANES)
    whole = [divmod(index, full) for index in range(DIRECT * full)]
    share = LANES // rest
    groups = [list(range(first, min(first + share, DIRECT))) for first in range(0, DIRECT, share)]
    return full, rest, whole, groups


def packed_width(width):
    full, rest, whole, groups = places(width)
    return -(-(len(whole) + len(groups)) // PIECES) * LANES


def stack_tile(position):
    tile, piece = divmod(position, PIECES)
    return slice(piece * LANES, (piece + 1) * LANES), slice(tile * LANES, (tile + 1) * LANES)


def spread(width, rows_ref, stack_ref, mark):
    full, rest, whole, groups = places(width)
    for position, (row, tile) in enumerate(whole):
        stack_ref[stack_tile(position)] = rows_ref[
            row * LANES : (row + 1) * LANES, tile * LANES : (tile + 1) * LANES
        ]
    last = len(whole) + len(groups) - 1
    for index, group in enumerate(groups):
        position = len(whole) + index
        total = jnp.zeros((LANES, LANES), jnp.float32)
        for row in group:
            tail = rows_ref[row * LANES : (row + 1) * LANES, full * LANES : (full + 1) * LANES]
            tail = tail.astype(jnp.float32)
            shift = rest * (row - group[0])
            total = total + (pltpu.roll(tail, shift, 1) if shift else tail)
        if position == last and mark is not None:
            total = jnp.where(iota((LANES, LANES), 1) == LANES - 1, mark, total)
        stack_ref[stack_tile(position)] = total.astype(jnp.bfloat16)
    for position in range(last + 1, stack_ref.shape[1] // LANES * PIECES):
        stack_ref[stack_tile(position)] = jnp.zeros((LANES, LANES), jnp.bfloat16)


def gather_up(width, stack_ref, rows_ref):
    full, rest, whole, groups = places(width)
    for position, (row, tile) in enumerate(whole):
        rows_ref[row * LANES : (row + 1) * LANES, tile * LANES : (tile + 1) * LANES] = stack_ref[
            stack_tile(position)
        ]
    for index, group in enumerate(groups):
        tails = stack_ref[stack_tile(len(whole) + index)].astype(jnp.float32)
        for row in group:
            shift = rest * (row - group[0])
            tail = pltpu.roll(tails, LANES - shift, 1) if shift else tails
            tail = jnp.where(iota((LANES, LANES), 1) < rest, tail, 0.0)
            rows_ref[row * LANES : (row + 1) * LANES, full * LANES : (full + 1) * LANES] = (
                tail.astype(jnp.bfloat16)
            )


def read_mark(width, stack_ref):
    full, rest, whole, groups = places(width)
    tile = stack_ref[stack_tile(len(whole) + len(groups) - 1)].astype(jnp.float32)
    tile = jnp.where(iota((LANES, LANES), 1) == LANES - 1, tile, 0.0)
    return jnp.max(jnp.max(tile, axis=1, keepdims=True), axis=0, keepdims=True)


PART = LANES // 4


def fold(stack_ref, packed_ref, done=None):
    size = PART * PIECES
    down, across = iota((size, size), 0), iota((size, size), 1)
    turn = as_bf16(across == (down % PIECES) * PART + down // PIECES)
    for part in range(LANES // PART):
        pieces = [
            stack_ref[piece * LANES + part * PART : piece * LANES + (part + 1) * PART, :]
            for piece in range(PIECES)
        ]
        packed_ref[part * size : (part + 1) * size, :] = dot(
            turn, jnp.concatenate(pieces, axis=0)
        ).astype(jnp.bfloat16)
        if done is not None:
            done(part, pl.ds(part * size, size))


def unfold(packed_ref, stack_ref):
    size = PART * PIECES
    down, across = iota((size, size), 0), iota((size, size), 1)
    turn = as_bf16(across == (down % PART) * PIECES + down // PART)
    for part in range(LANES // PART):
        block = dot(turn, packed_ref[part * size : (part + 1) * size, :]).astype(jnp.bfloat16)
        for piece in range(PIECES):
            stack_ref[piece * LANES + part * PART : piece * LANES + (part + 1) * PART, :] = block[
                piece * PART : (piece + 1) * PART, :
            ]


def route_kernel(
    rows,
    want_ref,
    count_ref,
    head_ref,
    tail_ref,
    neg_ref,
    relation_ref,
    ask_ref,
    *spot_refs,
):
    steps, cap, owners = want_ref.shape
    f32 = jnp.float32
    down, across = iota((LANES, LANES), 0), iota((LANES, LANES), 1)
    same_line = down // LINE == across // LINE
    line_mat = as_bf16(same_line)
    line_before = as_bf16(same_line & (down < across))
    upto = as_bf16(down <= across)
    owner = iota((1, LANES), 1).astype(f32)
    y_at = iota((1, LANES), 1) % LINE
    slot_number = iota((cap, LANES), 0).astype(f32)
    none = jnp.zeros((cap - 3, LANES), f32)
    asks = []
    for step in range(steps):
        count = count_ref[step : step + 1, :].astype(f32)
        ends = dot(jnp.broadcast_to(count, (cap, LANES)).astype(jnp.bfloat16), upto)[0:1, :]
        begins = ends - count
        seen = jnp.zeros((cap, LANES), f32)
        uses = []
        slots = [to_column(ref[step : step + 1, :].astype(f32)) for ref in (head_ref, tail_ref)]
        slots.append(jnp.full((LANES, 1), -1.0, f32))
        blocks, negatives = neg_ref.shape[1:]
        for block in range(blocks):
            row = neg_ref[step, block : block + 1, :].astype(f32) + 1.0
            here = iota((LANES, negatives), 0) - block * negatives == iota((LANES, negatives), 1)
            slots[2] += jnp.sum(jnp.where(here, row, 0.0), axis=1, keepdims=True)
        for slot in slots:
            owned = (slot >= begins) & (slot < ends)
            within = slot - jnp.sum(jnp.where(owned, begins, 0.0), axis=1, keepdims=True)
            seen += dot(as_bf16(slot_number == to_row(within)), as_bf16(owned))
            uses.append((owned, within))
        used = seen > 0.5
        ranks = [jnp.zeros((1, LANES), f32)]
        for slot in range(cap):
            ranks.append(ranks[-1] + jnp.where(used[slot : slot + 1, :], 1.0, 0.0))
        total = ranks.pop()
        rank = jnp.concatenate(ranks, axis=0)
        over = jnp.maximum(total - DIRECT, 0.0)
        free = DIRECT - jnp.minimum(total, DIRECT)
        pair = jnp.concatenate([over, free, total, none], axis=0).astype(jnp.bfloat16)
        before = dot(pair, line_before)
        whole = dot(pair, line_mat)
        lost = jnp.max(
            jnp.where(whole[0:1, :] > whole[1:2, :], 1.0, 0.0), axis=1, keepdims=True
        )
        turn = before[0:1, :] + rank - DIRECT
        side = jnp.concatenate([before[1:2, :], free, total, none], axis=0).astype(jnp.bfloat16)
        at_slot = rank
        at_owner = jnp.broadcast_to(owner, (cap, LANES))
        code = jnp.zeros((cap, LANES), f32)
        for far in range(1, LINE):
            mover = as_bf16(same_line & (down % LINE == (across + far) % LINE))
            moved = dot(side, mover)
            hit = used & (rank >= DIRECT) & (turn >= moved[0:1, :])
            hit = hit & (turn < moved[0:1, :] + moved[1:2, :])
            slot = moved[2:3, :] + turn - moved[0:1, :]
            other = owner + ((y_at + far) % LINE - y_at).astype(f32)
            at_slot = jnp.where(hit, slot, at_slot)
            at_owner = jnp.where(hit, other, at_owner)
            code = jnp.where(hit, rows * (far * cap + slot), code)
        want = want_ref[step].astype(f32)
        for place in range(cap):
            chosen = used & (rank == place)
            value = want + 1.0 if place < DIRECT else want + code + 1.0
            row = jnp.sum(jnp.where(chosen, value, 0.0), axis=0, keepdims=True) - 1.0
            if place == cap - 1:
                row = jnp.where(lost > 0.5, -2.0, row)
            asks.append(row)
        where_at = at_slot * owners + at_owner
        spots = []
        for owned, within in uses:
            table = jnp.zeros((LANES, LANES), f32)
            for slot in range(cap):
                table = jnp.where(within == slot, where_at[slot : slot + 1, :], table)
            found = jnp.sum(jnp.where(owned, table, 0.0), axis=1, keepdims=True)
            found = jnp.where(within < 0, -1.0, found)
            spots.append(to_row(found))
        spots.append(relation_ref[step : step + 1, :].astype(f32))
        spots.append(jnp.zeros((8 - len(spots), LANES), f32))
        spot_refs[step][...] = jnp.concatenate(spots, axis=0).astype(jnp.int32)
    asks.append(jnp.zeros((LANES - len(asks), LANES), f32))
    ask_ref[...] = jnp.transpose(jnp.concatenate(asks, axis=0)).astype(jnp.int32)


def fill_lent(tag_ref, step, table_ref, lent_ref):
    rows, width = table_ref.shape
    wide = lent_ref.shape[1] - LANES
    row, slot, trainer = (tag_ref[:, 3 * step + index : 3 * step + index + 1] for index in range(3))
    chosen = one_hot_rows(row.astype(jnp.int32), rows)
    lent_ref[:, wide - LANES : wide] = jnp.zeros((LANES, LANES), jnp.bfloat16)
    lent_ref[:, :width] = dot(chosen, table_ref[...]).astype(jnp.bfloat16)
    lanes = iota((LANES, LANES), 1)
    tags = jnp.where(lanes == 0, slot, jnp.where(lanes == 1, trainer, 0.0))
    lent_ref[:, wide:] = tags.astype(jnp.bfloat16)


def collect_kernel(
    steps, cap, ask_ref, table_ref, plan_ref, tag_ref, flag_ref, lent_ref
):
    rows = table_ref.shape[0]
    f32 = jnp.float32
    asked = jnp.transpose(ask_ref[...].astype(f32))[: steps * cap, :]
    down, across = iota((LANES, LANES), 0), iota((LANES, LANES), 1)
    earlier = as_bf16(down < across)
    trainer = iota((1, LANES), 1).astype(f32)
    flag = jnp.zeros((1, 1), f32)
    tags = jnp.full((LANES, LANES), -1.0, f32)
    lent_rows = []
    extra = cap - DIRECT
    for step in range(steps):
        codes = asked[step * cap + DIRECT : (step + 1) * cap, :].astype(jnp.int32)
        flag = jnp.maximum(
            flag,
            jnp.max(
                jnp.where(codes[extra - 1 : extra, :] == -2, 1.0, 0.0), axis=1, keepdims=True
            ),
        )
        valid = codes >= 0
        row = jnp.where(valid, codes % rows, 0).astype(f32)
        place = jnp.where(valid, codes // rows, 0)
        far = place // cap
        slot = (place % cap).astype(f32)
        masks = [
            jnp.where(valid & (far == distance), 1.0, 0.0) for distance in range(1, LINE)
        ]
        stacked = jnp.concatenate(
            masks + [jnp.zeros((16 - extra * (LINE - 1), LANES), f32)], axis=0
        )
        before = dot(stacked.astype(jnp.bfloat16), earlier)
        totals = jnp.sum(stacked, axis=1, keepdims=True)
        targets = [jnp.full((1, LANES), -1.0, f32) for entry in range(extra)]
        for index in range(LINE - 1):
            offset = jnp.zeros((1, 1), f32)
            for entry in range(extra):
                line = index * extra + entry
                at = before[line : line + 1, :] + offset + index * LENT
                targets[entry] = jnp.where(masks[index][entry : entry + 1, :] > 0.5, at, targets[entry])
                offset = offset + totals[line : line + 1, :]
            flag = jnp.maximum(flag, jnp.where(offset > LENT, 1.0, 0.0))
        sums = [jnp.zeros((LANES, 1), f32) for index in range(3)]
        for entry in range(extra):
            chosen = down.astype(f32) == targets[entry]
            values = (row[entry : entry + 1, :], slot[entry : entry + 1, :], trainer)
            for index, value in enumerate(values):
                picked = jnp.where(chosen, value + 1.0, 0.0)
                sums[index] += jnp.sum(picked, axis=1, keepdims=True)
        for index in range(3):
            tags = jnp.where(across == 3 * step + index, sums[index] - 1.0, tags)
        lent_rows.append(to_row(sums[0] - 1.0))
    lent_rows.append(jnp.full((8 - steps, LANES), -1.0, f32))
    plan_ref[...] = jnp.concatenate([asked] + lent_rows, axis=0).astype(jnp.int32)
    tag_ref[...] = tags
    flag_ref[...] = jnp.broadcast_to(flag, flag_ref.shape)
    fill_lent(tag_ref, 0, table_ref, lent_ref)


def direct_kernel(step, cap, plan_ref, table_ref, rows_ref):
    rows, width = table_ref.shape
    rows_ref[:, rows_ref.shape[1] - LANES :] = jnp.zeros((rows_ref.shape[0], LANES), jnp.bfloat16)
    for first in range(0, DIRECT, 2):
        last = min(first + 2, DIRECT)
        columns = [
            to_column(plan_ref[step * cap + slot : step * cap + slot + 1, :].astype(jnp.float32))
            for slot in range(first, last)
        ]
        chosen = one_hot_rows(jnp.concatenate(columns, axis=0).astype(jnp.int32), rows)
        rows_ref[first * LANES : last * LANES, :width] = dot(chosen, table_ref[...]).astype(
            jnp.bfloat16
        )


def pack_kernel(
    width,
    rows_ref,
    flag_ref,
    one_ref,
    two_ref,
    three_ref,
    packed_ref,
    tag_ref,
    lent_ref,
    full_ref,
    stack_ref,
    held_ref,
    copied,
):
    wide = rows_ref.shape[1]
    lent_ref[3 * LENT :, :] = jnp.zeros((LANES - 3 * LENT, wide), jnp.bfloat16)
    tags = []
    for index, ref in enumerate((one_ref, two_ref, three_ref)):
        lent_ref[index * LENT : (index + 1) * LENT, :] = ref[:, :wide]
        tag = ref[:, wide : wide + LANES].astype(jnp.float32)
        tags.append(tag[:, 0:1] * LANES + tag[:, 1:2])
    tags.append(jnp.full((LANES - 3 * LENT, 1), -1.0, jnp.float32))
    tag = to_row(jnp.concatenate(tags, axis=0)).astype(jnp.int32)
    tag_ref[...] = jnp.broadcast_to(tag, tag_ref.shape)
    for slot in range(DIRECT):
        block = slice(slot * LANES, (slot + 1) * LANES)
        lent = dot(one_hot_columns(tag, slot * LANES, LANES), lent_ref[...])
        full_ref[block, :] = (rows_ref[block, :].astype(jnp.float32) + lent).astype(jnp.bfloat16)
    spread(width, full_ref, stack_ref, flag_ref[0:1, :])
    copies = []

    def send(part, rows):
        copies.append(
            pltpu.make_async_copy(held_ref.at[rows, :], packed_ref.at[rows, :], copied.at[part])
        )
        copies[-1].start()

    fold(stack_ref, held_ref, send)
    for copy in copies:
        copy.wait()


def short_trainer_kernel(
    blocks,
    negatives,
    width,
    pulled_ref,
    spot_ref,
    cosine_ref,
    sine_ref,
    packed_ref,
    phase_grad_ref,
    rows_ref,
    stack_ref,
    held_ref,
    copied,
    *scratch,
):
    unfold(pulled_ref, stack_ref)
    gather_up(width, stack_ref, rows_ref)
    mark = read_mark(width, stack_ref)
    sending = pltpu.make_async_copy(held_ref, phase_grad_ref, copied)

    def put_phase_grad(value):
        last = iota((held_ref.shape[0], LANES), 1) == LANES - 1
        held_ref[:, held_ref.shape[1] - LANES :] = jnp.where(last, mark, 0.0)
        held_ref[:, : value.shape[1]] = value
        sending.start()

    trainer_core(
        blocks,
        negatives,
        width,
        rows_ref[...],
        spot_ref,
        cosine_ref,
        sine_ref,
        rows_ref,
        put_phase_grad,
        *scratch,
    )
    spread(width, rows_ref, stack_ref, None)
    fold(stack_ref, packed_ref)
    sending.wait()


def return_kernel(width, arrived_ref, tag_ref, rows_ref, lent_ref, stack_ref):
    unfold(arrived_ref, stack_ref)
    gather_up(width, stack_ref, rows_ref)
    tag = to_column(tag_ref[0:1, :].astype(jnp.float32)).astype(jnp.int32)
    chosen = one_hot_rows(tag, rows_ref.shape[0])
    lent_ref[...] = dot(chosen, rows_ref[...]).astype(jnp.bfloat16)


def sum_kernel(
    step, cap, width, plan_ref, other_plan_ref, rows_ref, arrived_ref, total_ref, stack_ref, other_ref
):
    unfold(arrived_ref, stack_ref)
    gather_up(width, stack_ref, other_ref)

    def asked(ref):
        rows = [ref[step * cap + slot : step * cap + slot + 1, :] for slot in range(DIRECT)]
        return jnp.concatenate(rows, axis=1)

    own, other = asked(plan_ref), asked(other_plan_ref)
    for first in range(0, total_ref.shape[0], 256):
        total_ref[first : first + 256, :] = dot(
            one_hot_columns(own, first, 256), rows_ref[...]
        ) + dot(one_hot_columns(other, first, 256), other_ref[...])


def short_update_kernel(
    step,
    cap,
    has_next,
    steps,
    plan_ref,
    other_plan_ref,
    total_ref,
    back_ref,
    other_back_ref,
    table_ref,
    state_ref,
    tag_ref,
    new_table_ref,
    new_state_ref,
    *rest,
):
    if has_next:
        lent_ref, first_ref, second_ref = rest
    else:
        first_ref, second_ref = rest
    rows, width = table_ref.shape
    for ref, source in ((first_ref, back_ref), (second_ref, other_back_ref)):
        ref[: 3 * LENT, :] = source[...]
        ref[3 * LENT :, :] = jnp.zeros((LANES - 3 * LENT, ref.shape[1]), jnp.bfloat16)
    line = steps * cap + step
    own, other = plan_ref[line : line + 1, :], other_plan_ref[line : line + 1, :]
    size = 256
    for first in range(0, rows, size):
        lent = dot(one_hot_columns(own, first, size), first_ref[...]) + dot(
            one_hot_columns(other, first, size), second_ref[...]
        )
        gradient = (total_ref[first : first + size, :] + lent)[:, :width]
        values = table_ref[first : first + size, :].astype(jnp.float32)
        stepped = adagrad_block(gradient, first, values, state_ref, new_state_ref)
        if has_next:
            new_table_ref[first : first + size, :] = stepped
        else:
            turn_into(stepped, new_table_ref, first)
    if has_next:
        fill_lent(tag_ref, step + 1, new_table_ref, lent_ref)


def line_pairs(owners, far):
    return [
        (owner, owner // LINE * LINE + (owner % LINE + far) % LINE) for owner in range(owners)
    ]


def short_steps(
    entity_table,
    entity_state,
    relation_phase,
    relation_state,
    want_rows,
    want_count,
    head_slot,
    tail_slot,
    negative_slot,
    relation_ids,
):
    steps, owners, cap = want_rows.shape[1:]
    rows, width = entity_table.shape
    half = width // 2
    wide = -(-width // LANES) * LANES
    blocks, negatives = negative_slot.shape[2:]
    triples = head_slot.shape[2]
    relations = relation_phase.shape[0]
    direct = DIRECT * LANES
    packed_rows = PIECES * LANES
    packed = packed_width(width)
    half_wide = -(-(half + 1) // LANES) * LANES
    f32, i32, bf16 = jnp.float32, jnp.int32, jnp.bfloat16

    asked, *spots = call(
        functools.partial(route_kernel, rows),
        (shape((LANES, LANES), i32),) + (shape((8, LANES), i32),) * steps,
        "route",
        nbytes=1 << 20,
    )(
        jnp.transpose(want_rows[0], (0, 2, 1)),
        want_count[0],
        head_slot[0],
        tail_slot[0],
        negative_slot[0],
        relation_ids[0],
    )
    asked = lax.all_to_all(asked, "dom", split_axis=0, concat_axis=0, tiled=True)
    plan, tags, flag, lent = call(
        functools.partial(collect_kernel, steps, cap),
        (
            shape((steps * cap + 8, LANES), i32),
            shape((LANES, LANES), f32),
            shape((8, LANES), f32),
            shape((LANES, wide + LANES), bf16),
        ),
        "collect",
        nbytes=4 << 20,
    )(asked, entity_table)
    swap = [(0, 1), (1, 0)]
    other_plan = lax.ppermute(plan, "rep", swap)
    forth = [line_pairs(owners, far) for far in range(1, LINE)]
    back = [[(target, source) for source, target in pairs] for pairs in forth]

    table = entity_table
    state = entity_state.reshape(rows // LANES, LANES)
    phase = relation_phase
    phase_state = relation_state[:, None]
    relation = call(
        short_relation_kernel,
        (
            shape((relations, half), f32),
            shape((relations, 1), f32),
            shape((1, relations), f32),
            shape((8, LANES), f32),
        ),
        "relation",
        flops=6 * triples * relations * half,
        nbytes=4 * triples * half,
    )
    for step in range(steps):
        has_next = step + 1 < steps
        loans = [
            lax.ppermute(lent[index * LENT : (index + 1) * LENT], "dom", forth[index])
            for index in range(LINE - 1)
        ]
        sent = call(
            functools.partial(direct_kernel, step, cap),
            shape((direct, wide), bf16),
            "direct",
            flops=2 * direct * rows * width,
            nbytes=4 * rows * width,
        )(plan, table)
        offered, loan_tag = call(
            functools.partial(pack_kernel, width),
            (shape((packed_rows, packed), bf16), shape((8, LANES), i32)),
            "pack",
            nbytes=4 * rows * width,
            out_specs=(pl.BlockSpec(memory_space=pltpu.HBM), pl.BlockSpec(memory_space=pltpu.VMEM)),
            scratch_shapes=[
                pltpu.VMEM((LANES, wide), bf16),
                pltpu.VMEM((direct, wide), bf16),
                pltpu.VMEM((packed_rows, packed), bf16),
                pltpu.VMEM((packed_rows, packed), bf16),
                pltpu.SemaphoreType.DMA((LANES // PART,)),
            ],
        )(sent, flag, *loans)
        if step > 0:
            offered, phase_grad = lax.optimization_barrier((offered, phase_grad))
            phase, phase_state, state_row, seen = relation(
                spots[step - 1], phase_grad, phase, phase_state
            )
            if step == 1:
                seen = jnp.maximum(seen, lax.ppermute(seen, "rep", swap))
                phase, spoiled = lax.optimization_barrier((phase, jnp.max(seen)))
        pulled = lax.all_to_all(
            offered.reshape(owners, PIECES, packed), "dom", split_axis=0, concat_axis=0, tiled=True
        ).reshape(packed_rows, packed)
        relation_span = jnp.arange(relations, dtype=i32)
        selector = (relation_ids[0, step][:, None] == relation_span[None, :]).astype(f32)
        phase_rows = jnp.dot(selector, phase, precision=lax.Precision.HIGHEST)
        padded, phase_grad = call(
            functools.partial(short_trainer_kernel, blocks, negatives, width),
            (shape((packed_rows, packed), bf16), shape((triples, half_wide), f32)),
            "trainer",
            flops=2 * direct * (9 * triples) * width,
            nbytes=4 * rows * width,
            out_specs=(pl.BlockSpec(memory_space=pltpu.VMEM), pl.BlockSpec(memory_space=pltpu.HBM)),
            scratch_shapes=[
                pltpu.VMEM((direct, wide), bf16),
                pltpu.VMEM((packed_rows, packed), bf16),
                pltpu.VMEM((triples, half_wide), f32),
                pltpu.SemaphoreType.DMA,
            ]
            + trainer_scratch(triples, blocks * negatives, width, wide, wide),
        )(pulled, spots[step], jnp.cos(phase_rows), jnp.sin(phase_rows))
        arrived = lax.all_to_all(
            padded.reshape(owners, PIECES, packed), "dom", split_axis=0, concat_axis=0, tiled=True
        ).reshape(packed_rows, packed)
        arrived_other = lax.ppermute(arrived, "rep", swap)
        got, dues = call(
            functools.partial(return_kernel, width),
            (shape((direct, wide), bf16), shape((LANES, wide), bf16)),
            "give_back",
            flops=2 * LANES * direct * wide,
            nbytes=4 * rows * width,
            scratch_shapes=[pltpu.VMEM((packed_rows, packed), bf16)],
        )(arrived, loan_tag)
        dues = [
            lax.ppermute(dues[index * LENT : (index + 1) * LENT], "dom", back[index])
            for index in range(LINE - 1)
        ]
        if not has_next:
            phase, phase_state, state_row, seen = relation(
                spots[step], phase_grad, phase, phase_state
            )
            got, phase, state_row = lax.optimization_barrier((got, phase, state_row))
        total = call(
            functools.partial(sum_kernel, step, cap, width),
            shape((rows, wide), f32),
            "sum",
            flops=4 * direct * rows * width,
            nbytes=8 * rows * width,
            scratch_shapes=[
                pltpu.VMEM((packed_rows, packed), bf16),
                pltpu.VMEM((direct, wide), bf16),
            ],
        )(plan, other_plan, got, arrived_other)
        dues, total = lax.optimization_barrier((dues, total))
        dues = jnp.concatenate(dues, axis=0)
        dues_other = lax.ppermute(dues, "rep", swap)
        outputs = [
            shape((rows, width) if has_next else (width, rows), bf16),
            shape((rows // LANES, LANES), f32),
        ]
        if has_next:
            outputs.append(shape((LANES, wide + LANES), bf16))
        results = call(
            functools.partial(short_update_kernel, step, cap, has_next, steps),
            tuple(outputs),
            "update",
            flops=4 * LANES * rows * width,
            nbytes=12 * rows * width,
            scratch_shapes=[pltpu.VMEM((LANES, wide), bf16)] * 2,
        )(plan, other_plan, total, dues, dues_other, table, state, tags)
        table, state = results[:2]
        if has_next:
            lent = results[2]
    return (table.T, state.reshape(rows), phase, state_row.reshape(relations)), spoiled > 0.5


def local(*arrays):
    results, spoiled = short_steps(*arrays)
    return lax.cond(spoiled, lambda: full_steps(*arrays), lambda: results)


def solution(mesh):
    placed = (
        P("dom", None),
        P("dom"),
        P(("dom", "rep"), None),
        P(("dom", "rep")),
        P(("dom", "rep"), None, None, None),
        P(("dom", "rep"), None, None),
        P(("dom", "rep"), None, None),
        P(("dom", "rep"), None, None),
        P(("dom", "rep"), None, None, None),
        P(("dom", "rep"), None, None),
    )
    return jax.shard_map(
        local,
        mesh=mesh,
        in_specs=placed,
        out_specs=(P("dom", None), P("dom"), P(("dom", "rep"), None), P(("dom", "rep"))),
        check_vma=False,
    )
```

```python
import functools

import jax
import jax.numpy as jnp
from jax import lax
from jax.experimental import pallas as pl
from jax.experimental.pallas import tpu as pltpu
from jax.sharding import PartitionSpec as P

learn_rate = 0.5
smoothing = 0.25
epsilon = 1e-10
margin_rate = 0.26

LANES = 128
VMEM_LIMIT = 20 * 1024 * 1024


def slot_place(slot_ids, counts, slot_cap):
    running = jnp.cumsum(counts, dtype=jnp.int32)
    passed = (slot_ids[..., None] >= running).astype(jnp.int32)
    owner_index = jnp.sum(passed, axis=-1, dtype=jnp.int32)
    before = jnp.sum(passed * counts, axis=-1, dtype=jnp.int32)
    return owner_index * slot_cap + slot_ids - before


def call(kernel, out_shape, name, flops=0, nbytes=0, **kwargs):
    return pl.pallas_call(
        kernel,
        out_shape=out_shape,
        name=name,
        cost_estimate=pl.CostEstimate(flops=flops, bytes_accessed=nbytes, transcendentals=0),
        compiler_params=pltpu.CompilerParams(vmem_limit_bytes=VMEM_LIMIT),
        **kwargs,
    )


def diagonal():
    down = lax.broadcasted_iota(jnp.int32, (LANES, LANES), 0)
    across = lax.broadcasted_iota(jnp.int32, (LANES, LANES), 1)
    return down == across


def to_column(row):
    spread = jnp.broadcast_to(row, (LANES, LANES))
    return jnp.sum(jnp.where(diagonal(), spread, 0.0), axis=1, keepdims=True)


def to_row(column):
    spread = jnp.broadcast_to(column, (LANES, LANES))
    return jnp.sum(jnp.where(diagonal(), spread, 0.0), axis=0, keepdims=True)


def one_hot_rows(column, width):
    lanes = lax.broadcasted_iota(jnp.int32, (column.shape[0], width), 1)
    return jnp.where(lanes == column, 1.0, 0.0).astype(jnp.bfloat16)


def one_hot_columns(row, first, height):
    down = lax.broadcasted_iota(jnp.int32, (height, row.shape[1]), 0) + first
    return jnp.where(down == row, 1.0, 0.0).astype(jnp.bfloat16)


def dot(left, right):
    return jnp.dot(left, right, preferred_element_type=jnp.float32)


def turn_into(values, ref, first):
    rows, width = values.shape
    for start in range(0, width, 256):
        size = min(256, width - start)
        down = lax.broadcasted_iota(jnp.int32, (size, size), 0)
        across = lax.broadcasted_iota(jnp.int32, (size, size), 1)
        unit = jnp.where(down == across, 1.0, 0.0).astype(jnp.bfloat16)
        product = lax.dot_general(
            unit,
            values[:, start : start + size],
            (((1,), (1,)), ((), ())),
            preferred_element_type=jnp.float32,
        )
        ref[start : start + size, first : first + rows] = product.astype(jnp.bfloat16)


def split3(values):
    high = values.astype(jnp.bfloat16)
    rest = values - high.astype(jnp.float32)
    middle = rest.astype(jnp.bfloat16)
    low = (rest - middle.astype(jnp.float32)).astype(jnp.bfloat16)
    return high, middle, low


def gather_rows(wanted_ref, table_ref, offered_ref):
    table_rows = table_ref.shape[0]
    blocks = wanted_ref.shape[0]
    step = 2
    for start in range(0, blocks, step):
        columns = [
            to_column(wanted_ref[block : block + 1, :].astype(jnp.float32)).astype(jnp.int32)
            for block in range(start, start + step)
        ]
        chosen = one_hot_rows(jnp.concatenate(columns, axis=0), table_rows)
        rows = pl.ds(start * LANES, step * LANES)
        offered_ref[rows, :] = dot(chosen, table_ref[...]).astype(jnp.bfloat16)


def offer_kernel(wanted_ref, table_ref, offered_ref):
    gather_rows(wanted_ref, table_ref, offered_ref)


def own_sum_kernel(asked_ref, arrived_ref, total_ref):
    rows = total_ref.shape[0]
    step = 256
    asked = asked_ref[...]
    for first in range(0, rows, step):
        chosen = one_hot_columns(asked, first, step)
        total_ref[first : first + step, :] = dot(chosen, arrived_ref[...])


def adagrad_block(gradient, first, values, state_ref, new_state_ref):
    step, width = gradient.shape
    mean_square = jnp.sum(gradient * gradient, axis=1, keepdims=True) / width
    fresh = []
    for block in range(first // LANES, (first + step) // LANES):
        old = to_column(state_ref[block : block + 1, :])
        at = block * LANES - first
        new = old + mean_square[at : at + LANES, :]
        new_state_ref[block : block + 1, :] = to_row(new)
        fresh.append(new)
    rate = learn_rate / (jnp.sqrt(jnp.concatenate(fresh, axis=0)) + epsilon)
    return (values - gradient * rate).astype(jnp.bfloat16)


def update_kernel(
    has_next,
    asked_ref,
    arrived_ref,
    own_ref,
    table_ref,
    state_ref,
    *rest,
):
    if has_next:
        wanted_ref, new_table_ref, new_state_ref, offered_ref = rest
    else:
        new_table_ref, new_state_ref = rest
    rows, width = table_ref.shape
    step = 256
    asked = asked_ref[...]
    for first in range(0, rows, step):
        chosen = one_hot_columns(asked, first, step)
        gradient = own_ref[first : first + step, :] + dot(chosen, arrived_ref[...])
        gradient = gradient[:, :width]
        values = table_ref[first : first + step, :].astype(jnp.float32)
        stepped = adagrad_block(gradient, first, values, state_ref, new_state_ref)
        if has_next:
            new_table_ref[first : first + step, :] = stepped
        else:
            turn_into(stepped, new_table_ref, first)
    if has_next:
        gather_rows(wanted_ref, new_table_ref, offered_ref)


def sigmoid(value):
    tail = jnp.exp(-jnp.abs(value))
    return jnp.where(value >= 0, 1.0, tail) / (1.0 + tail)


def trainer_core(
    blocks,
    negatives,
    width,
    pulled,
    spot_ref,
    cosine_ref,
    sine_ref,
    padded_ref,
    put_phase_grad,
    read_ref,
    rot_real_ref,
    rot_imag_ref,
    tail_real_ref,
    tail_imag_ref,
    neg_real_ref,
    neg_imag_ref,
    rot_real_grad_ref,
    rot_imag_grad_ref,
    tail_real_grad_ref,
    tail_imag_grad_ref,
    neg_real_grad_ref,
    neg_imag_grad_ref,
    grads_ref,
):
    slots = pulled.shape[0]
    half = width // 2
    triples = cosine_ref.shape[0]
    neg_rows = blocks * negatives
    margin = margin_rate * half

    places = [
        to_column(spot_ref[index : index + 1, :].astype(jnp.float32)).astype(jnp.int32)
        for index in range(3)
    ]
    places[2] = places[2][:neg_rows]
    read_ref[...] = dot(one_hot_rows(jnp.concatenate(places, axis=0), slots), pulled)
    head_ref = read_ref.at[:triples, :]
    tail_ref = read_ref.at[triples : 2 * triples, :]
    negative_ref = read_ref.at[2 * triples :, :]

    cosine = cosine_ref[...]
    sine = sine_ref[...]
    head_real = head_ref[:, :half]
    head_imag = head_ref[:, half:width]
    rot_real_ref[...] = head_real * cosine - head_imag * sine
    rot_imag_ref[...] = head_real * sine + head_imag * cosine
    tail_real_ref[...] = tail_ref[:, :half]
    tail_imag_ref[...] = tail_ref[:, half:width]
    neg_real_ref[...] = negative_ref[:, :half]
    neg_imag_ref[...] = negative_ref[:, half:width]
    neg_real_grad_ref[...] = jnp.zeros_like(neg_real_grad_ref)
    neg_imag_grad_ref[...] = jnp.zeros_like(neg_imag_grad_ref)

    group = 8
    per_block = triples // blocks

    def pair(real, imag, other_real, other_imag):
        diff_real = real - other_real
        diff_imag = imag - other_imag
        square = diff_real * diff_real + diff_imag * diff_imag + smoothing
        inverse = lax.rsqrt(square)
        distance = jnp.sum(square * inverse, axis=1, keepdims=True)
        return distance, diff_real * inverse, diff_imag * inverse

    def chunk(index, carry):
        rows = pl.ds(pl.multiple_of(index * group, group), group)
        first = (index * group) // per_block * negatives
        real = rot_real_ref[rows, :]
        imag = rot_imag_ref[rows, :]
        distance, unit_real, unit_imag = pair(
            real, imag, tail_real_ref[rows, :], tail_imag_ref[rows, :]
        )
        weight = 0.25 * sigmoid(0.25 * distance - margin)
        total_real = weight * unit_real
        total_imag = weight * unit_imag
        tail_real_grad_ref[rows, :] = -total_real
        tail_imag_grad_ref[rows, :] = -total_imag
        for n in range(negatives):
            distance, unit_real, unit_imag = pair(
                real,
                imag,
                neg_real_ref[pl.ds(first + n, 1), :],
                neg_imag_ref[pl.ds(first + n, 1), :],
            )
            weight = (-0.25 / negatives) * sigmoid(margin - 0.25 * distance)
            unit_real = weight * unit_real
            unit_imag = weight * unit_imag
            total_real += unit_real
            total_imag += unit_imag
            neg_real_grad_ref[first + n] -= unit_real
            neg_imag_grad_ref[first + n] -= unit_imag
        rot_real_grad_ref[rows, :] = total_real
        rot_imag_grad_ref[rows, :] = total_imag
        return carry

    lax.fori_loop(0, triples // group, chunk, 0)

    real_grad = rot_real_grad_ref[...]
    imag_grad = rot_imag_grad_ref[...]
    put_phase_grad(imag_grad * rot_real_ref[...] - real_grad * rot_imag_ref[...])

    grads_ref[:, width:] = jnp.zeros_like(grads_ref[:, width:])

    def put(first, rows, real, imag):
        value = jnp.concatenate([real, imag], axis=1)
        grads_ref[first : first + rows, :width] = value.astype(jnp.bfloat16)

    put(
        0,
        triples,
        real_grad * cosine + imag_grad * sine,
        imag_grad * cosine - real_grad * sine,
    )
    put(triples, triples, tail_real_grad_ref[...], tail_imag_grad_ref[...])
    partial = neg_rows * group
    put(
        2 * triples,
        partial,
        neg_real_grad_ref[...].reshape(partial, half),
        neg_imag_grad_ref[...].reshape(partial, half),
    )
    spots = [spot_ref[index : index + 1, :] for index in range(2)]
    column = to_column(spot_ref[2:3, :].astype(jnp.float32))
    for first in range(0, partial, LANES):
        down = lax.broadcasted_iota(jnp.int32, (LANES, LANES), 0)
        across = lax.broadcasted_iota(jnp.int32, (LANES, LANES), 1) + first
        repeated = jnp.where(down == across // group, column, 0.0)
        spots.append(jnp.sum(repeated, axis=0, keepdims=True).astype(jnp.int32))
    for first in range(0, slots, 256):
        step = min(256, slots - first)
        chosen = [one_hot_columns(spot, first, step) for spot in spots]
        chosen = jnp.concatenate(chosen, axis=1)
        padded_ref[first : first + step, :] = dot(chosen, grads_ref[...]).astype(jnp.bfloat16)


def trainer_kernel(
    blocks,
    negatives,
    pulled_ref,
    spot_ref,
    cosine_ref,
    sine_ref,
    padded_ref,
    phase_grad_ref,
    *scratch,
):
    def put_phase_grad(value):
        phase_grad_ref[...] = value

    trainer_core(
        blocks,
        negatives,
        pulled_ref.shape[1],
        pulled_ref[...],
        spot_ref,
        cosine_ref,
        sine_ref,
        padded_ref,
        put_phase_grad,
        *scratch,
    )


def trainer_scratch(triples, neg_rows, width, wide, read_width):
    half = width // 2
    return (
        [pltpu.VMEM((2 * triples + neg_rows, read_width), jnp.float32)]
        + [pltpu.VMEM((triples, half), jnp.float32)] * 4
        + [pltpu.VMEM((neg_rows, half), jnp.float32)] * 2
        + [pltpu.VMEM((triples, half), jnp.float32)] * 4
        + [pltpu.VMEM((neg_rows, 8, half), jnp.float32)] * 2
        + [pltpu.VMEM((2 * triples + 8 * neg_rows, wide), jnp.bfloat16)]
    )


def relation_kernel(spot_ref, grad_ref, phase_ref, state_ref, new_phase_ref, new_state_ref):
    relations, half = phase_ref.shape
    chosen = one_hot_columns(spot_ref[3:4, :], 0, relations)
    high, middle, low = split3(grad_ref[...])
    gradient = dot(chosen, high) + dot(chosen, middle) + dot(chosen, low)
    gradient = gradient[:, :half]
    mean_square = jnp.sum(gradient * gradient, axis=1, keepdims=True) / half
    fresh = state_ref[...] + mean_square
    new_state_ref[...] = fresh
    new_phase_ref[...] = phase_ref[...] - learn_rate * gradient / (jnp.sqrt(fresh) + epsilon)


def short_relation_kernel(
    spot_ref,
    grad_ref,
    phase_ref,
    state_ref,
    new_phase_ref,
    new_state_ref,
    row_ref,
    flag_ref,
):
    relation_kernel(spot_ref, grad_ref, phase_ref, state_ref, new_phase_ref, new_state_ref)
    relations = phase_ref.shape[0]
    spare = jnp.zeros((LANES - relations, 1), jnp.float32)
    row = to_row(jnp.concatenate([new_state_ref[...], spare], axis=0))
    row_ref[...] = row[:, :relations]
    last = grad_ref.shape[1] - 1
    mark = jnp.max(grad_ref[:, last : last + 1], axis=0, keepdims=True)
    flag_ref[...] = jnp.broadcast_to(mark, flag_ref.shape)


def shape(dims, dtype):
    return jax.ShapeDtypeStruct(dims, dtype)


def full_steps(
    entity_table,
    entity_state,
    relation_phase,
    relation_state,
    want_rows,
    want_count,
    head_slot,
    tail_slot,
    negative_slot,
    relation_ids,
):
    steps, owners, cap = want_rows.shape[1:]
    rows, width = entity_table.shape
    half = width // 2
    wide = -(-width // LANES) * LANES
    blocks, negatives = negative_slot.shape[2:]
    triples = head_slot.shape[2]
    slots = owners * cap
    relations = relation_phase.shape[0]
    table_bytes = 2 * rows * width

    asked = jnp.transpose(want_rows[0], (1, 0, 2)).reshape(owners, steps * cap)
    asked = lax.all_to_all(asked, "dom", split_axis=0, concat_axis=0, tiled=True)
    asked = jnp.transpose(asked.reshape(owners, steps, cap), (1, 0, 2))
    asked = asked.reshape(steps, slots // LANES, LANES)
    asked_other = lax.ppermute(asked, "rep", [(0, 1), (1, 0)])
    ask_row = asked.reshape(steps, 1, slots)
    ask_row_other = asked_other.reshape(steps, 1, slots)

    spots = []
    for step in range(steps):
        counts = want_count[0, step]
        neg = slot_place(negative_slot[0, step].reshape(-1), counts, cap)
        spare = jnp.full((triples - neg.shape[0],), -1, jnp.int32)
        spots.append(
            jnp.stack(
                [
                    slot_place(head_slot[0, step], counts, cap),
                    slot_place(tail_slot[0, step], counts, cap),
                    jnp.concatenate([neg, spare]),
                    relation_ids[0, step],
                ]
            )
        )

    table = entity_table
    state = entity_state.reshape(rows // LANES, LANES)
    phase = relation_phase
    phase_state = relation_state[:, None]
    offered = call(
        offer_kernel,
        shape((slots, width), jnp.bfloat16),
        "offer",
        flops=2 * slots * rows * width,
        nbytes=2 * table_bytes,
    )(asked[0], table)
    f32 = jnp.float32
    for step in range(steps):
        pulled = lax.all_to_all(
            offered.reshape(owners, cap, width), "dom", split_axis=0, concat_axis=0, tiled=True
        ).reshape(slots, width)
        relation_span = jnp.arange(relations, dtype=jnp.int32)
        selector = (relation_ids[0, step][:, None] == relation_span[None, :]).astype(f32)
        phase_rows = jnp.dot(selector, phase, precision=lax.Precision.HIGHEST)
        padded, phase_grad = call(
            functools.partial(trainer_kernel, blocks, negatives),
            (shape((slots, wide), jnp.bfloat16), shape((triples, half), f32)),
            "trainer",
            flops=2 * slots * (9 * triples) * width,
            nbytes=2 * table_bytes,
            scratch_shapes=trainer_scratch(triples, blocks * negatives, width, wide, width),
        )(pulled, spots[step], jnp.cos(phase_rows), jnp.sin(phase_rows))
        arrived = lax.all_to_all(
            padded.reshape(owners, cap, wide), "dom", split_axis=0, concat_axis=0, tiled=True
        ).reshape(slots, wide)
        phase, phase_state = call(
            relation_kernel,
            (shape((relations, half), f32), shape((relations, 1), f32)),
            "relation",
            flops=6 * triples * relations * half,
            nbytes=4 * triples * half,
        )(spots[step], phase_grad, phase, phase_state)
        arrived_other = lax.ppermute(arrived, "rep", [(0, 1), (1, 0)])
        own = call(
            own_sum_kernel,
            shape((rows, wide), f32),
            "own_sum",
            flops=2 * slots * rows * width,
            nbytes=3 * table_bytes,
        )(ask_row[step], arrived)
        has_next = step + 1 < steps
        outputs = [
            shape((rows, width) if has_next else (width, rows), jnp.bfloat16),
            shape((rows // LANES, LANES), f32),
        ]
        operands = [ask_row_other[step], arrived_other, own, table, state]
        if has_next:
            outputs.append(shape((slots, width), jnp.bfloat16))
            operands.append(asked[step + 1])
        results = call(
            functools.partial(update_kernel, has_next),
            tuple(outputs),
            "update",
            flops=2 * slots * rows * width * (1 + has_next),
            nbytes=6 * table_bytes,
        )(*operands)
        table, state = results[:2]
        if has_next:
            offered = results[2]
    return (table.T, state.reshape(rows), phase, phase_state[:, 0])


DIRECT = 5
LINE = 4
LENT = 32
PIECES = 8


def iota(dims, axis):
    return lax.broadcasted_iota(jnp.int32, dims, axis)


def as_bf16(mask):
    return jnp.where(mask, 1.0, 0.0).astype(jnp.bfloat16)


def places(width):
    full, rest = divmod(width, LANES)
    whole = [divmod(index, full) for index in range(DIRECT * full)]
    share = LANES // rest
    groups = [list(range(first, min(first + share, DIRECT))) for first in range(0, DIRECT, share)]
    return full, rest, whole, groups


def packed_width(width):
    full, rest, whole, groups = places(width)
    return -(-(len(whole) + len(groups)) // PIECES) * LANES


def stack_tile(position):
    tile, piece = divmod(position, PIECES)
    return slice(piece * LANES, (piece + 1) * LANES), slice(tile * LANES, (tile + 1) * LANES)


def spread(width, rows_ref, stack_ref, mark):
    full, rest, whole, groups = places(width)
    for position, (row, tile) in enumerate(whole):
        stack_ref[stack_tile(position)] = rows_ref[
            row * LANES : (row + 1) * LANES, tile * LANES : (tile + 1) * LANES
        ]
    last = len(whole) + len(groups) - 1
    for index, group in enumerate(groups):
        position = len(whole) + index
        total = jnp.zeros((LANES, LANES), jnp.float32)
        for row in group:
            tail = rows_ref[row * LANES : (row + 1) * LANES, full * LANES : (full + 1) * LANES]
            tail = tail.astype(jnp.float32)
            shift = rest * (row - group[0])
            total = total + (pltpu.roll(tail, shift, 1) if shift else tail)
        if position == last and mark is not None:
            total = jnp.where(iota((LANES, LANES), 1) == LANES - 1, mark, total)
        stack_ref[stack_tile(position)] = total.astype(jnp.bfloat16)
    for position in range(last + 1, stack_ref.shape[1] // LANES * PIECES):
        stack_ref[stack_tile(position)] = jnp.zeros((LANES, LANES), jnp.bfloat16)


def gather_up(width, stack_ref, rows_ref):
    full, rest, whole, groups = places(width)
    for position, (row, tile) in enumerate(whole):
        rows_ref[row * LANES : (row + 1) * LANES, tile * LANES : (tile + 1) * LANES] = stack_ref[
            stack_tile(position)
        ]
    for index, group in enumerate(groups):
        tails = stack_ref[stack_tile(len(whole) + index)].astype(jnp.float32)
        for row in group:
            shift = rest * (row - group[0])
            tail = pltpu.roll(tails, LANES - shift, 1) if shift else tails
            tail = jnp.where(iota((LANES, LANES), 1) < rest, tail, 0.0)
            rows_ref[row * LANES : (row + 1) * LANES, full * LANES : (full + 1) * LANES] = (
                tail.astype(jnp.bfloat16)
            )


def read_mark(width, stack_ref):
    full, rest, whole, groups = places(width)
    tile = stack_ref[stack_tile(len(whole) + len(groups) - 1)].astype(jnp.float32)
    tile = jnp.where(iota((LANES, LANES), 1) == LANES - 1, tile, 0.0)
    return jnp.max(jnp.max(tile, axis=1, keepdims=True), axis=0, keepdims=True)


PART = LANES // 4


def fold(stack_ref, packed_ref, done=None):
    size = PART * PIECES
    down, across = iota((size, size), 0), iota((size, size), 1)
    turn = as_bf16(across == (down % PIECES) * PART + down // PIECES)
    for part in range(LANES // PART):
        pieces = [
            stack_ref[piece * LANES + part * PART : piece * LANES + (part + 1) * PART, :]
            for piece in range(PIECES)
        ]
        packed_ref[part * size : (part + 1) * size, :] = dot(
            turn, jnp.concatenate(pieces, axis=0)
        ).astype(jnp.bfloat16)
        if done is not None:
            done(part, pl.ds(part * size, size))


def unfold(packed_ref, stack_ref):
    size = PART * PIECES
    down, across = iota((size, size), 0), iota((size, size), 1)
    turn = as_bf16(across == (down % PART) * PIECES + down // PART)
    for part in range(LANES // PART):
        block = dot(turn, packed_ref[part * size : (part + 1) * size, :]).astype(jnp.bfloat16)
        for piece in range(PIECES):
            stack_ref[piece * LANES + part * PART : piece * LANES + (part + 1) * PART, :] = block[
                piece * PART : (piece + 1) * PART, :
            ]


def route_kernel(
    rows,
    want_ref,
    count_ref,
    head_ref,
    tail_ref,
    neg_ref,
    relation_ref,
    ask_ref,
    *spot_refs,
):
    steps, cap, owners = want_ref.shape
    f32 = jnp.float32
    down, across = iota((LANES, LANES), 0), iota((LANES, LANES), 1)
    same_line = down // LINE == across // LINE
    line_mat = as_bf16(same_line)
    line_before = as_bf16(same_line & (down < across))
    upto = as_bf16(down <= across)
    owner = iota((1, LANES), 1).astype(f32)
    y_at = iota((1, LANES), 1) % LINE
    slot_number = iota((cap, LANES), 0).astype(f32)
    none = jnp.zeros((cap - 3, LANES), f32)
    asks = []
    for step in range(steps):
        count = count_ref[step : step + 1, :].astype(f32)
        ends = dot(jnp.broadcast_to(count, (cap, LANES)).astype(jnp.bfloat16), upto)[0:1, :]
        begins = ends - count
        seen = jnp.zeros((cap, LANES), f32)
        uses = []
        slots = [to_column(ref[step : step + 1, :].astype(f32)) for ref in (head_ref, tail_ref)]
        slots.append(jnp.full((LANES, 1), -1.0, f32))
        blocks, negatives = neg_ref.shape[1:]
        for block in range(blocks):
            row = neg_ref[step, block : block + 1, :].astype(f32) + 1.0
            here = iota((LANES, negatives), 0) - block * negatives == iota((LANES, negatives), 1)
            slots[2] += jnp.sum(jnp.where(here, row, 0.0), axis=1, keepdims=True)
        for slot in slots:
            owned = (slot >= begins) & (slot < ends)
            within = slot - jnp.sum(jnp.where(owned, begins, 0.0), axis=1, keepdims=True)
            seen += dot(as_bf16(slot_number == to_row(within)), as_bf16(owned))
            uses.append((owned, within))
        used = seen > 0.5
        ranks = [jnp.zeros((1, LANES), f32)]
        for slot in range(cap):
            ranks.append(ranks[-1] + jnp.where(used[slot : slot + 1, :], 1.0, 0.0))
        total = ranks.pop()
        rank = jnp.concatenate(ranks, axis=0)
        over = jnp.maximum(total - DIRECT, 0.0)
        free = DIRECT - jnp.minimum(total, DIRECT)
        pair = jnp.concatenate([over, free, total, none], axis=0).astype(jnp.bfloat16)
        before = dot(pair, line_before)
        whole = dot(pair, line_mat)
        lost = jnp.max(
            jnp.where(whole[0:1, :] > whole[1:2, :], 1.0, 0.0), axis=1, keepdims=True
        )
        turn = before[0:1, :] + rank - DIRECT
        side = jnp.concatenate([before[1:2, :], free, total, none], axis=0).astype(jnp.bfloat16)
        at_slot = rank
        at_owner = jnp.broadcast_to(owner, (cap, LANES))
        code = jnp.zeros((cap, LANES), f32)
        for far in range(1, LINE):
            mover = as_bf16(same_line & (down % LINE == (across + far) % LINE))
            moved = dot(side, mover)
            hit = used & (rank >= DIRECT) & (turn >= moved[0:1, :])
            hit = hit & (turn < moved[0:1, :] + moved[1:2, :])
            slot = moved[2:3, :] + turn - moved[0:1, :]
            other = owner + ((y_at + far) % LINE - y_at).astype(f32)
            at_slot = jnp.where(hit, slot, at_slot)
            at_owner = jnp.where(hit, other, at_owner)
            code = jnp.where(hit, rows * (far * cap + slot), code)
        want = want_ref[step].astype(f32)
        for place in range(cap):
            chosen = used & (rank == place)
            value = want + 1.0 if place < DIRECT else want + code + 1.0
            row = jnp.sum(jnp.where(chosen, value, 0.0), axis=0, keepdims=True) - 1.0
            if place == cap - 1:
                row = jnp.where(lost > 0.5, -2.0, row)
            asks.append(row)
        where_at = at_slot * owners + at_owner
        spots = []
        for owned, within in uses:
            table = jnp.zeros((LANES, LANES), f32)
            for slot in range(cap):
                table = jnp.where(within == slot, where_at[slot : slot + 1, :], table)
            found = jnp.sum(jnp.where(owned, table, 0.0), axis=1, keepdims=True)
            found = jnp.where(within < 0, -1.0, found)
            spots.append(to_row(found))
        spots.append(relation_ref[step : step + 1, :].astype(f32))
        spots.append(jnp.zeros((8 - len(spots), LANES), f32))
        spot_refs[step][...] = jnp.concatenate(spots, axis=0).astype(jnp.int32)
    asks.append(jnp.zeros((LANES - len(asks), LANES), f32))
    ask_ref[...] = jnp.transpose(jnp.concatenate(asks, axis=0)).astype(jnp.int32)


def fill_lent(tag_ref, step, table_ref, lent_ref):
    rows, width = table_ref.shape
    wide = lent_ref.shape[1] - LANES
    row, slot, trainer = (tag_ref[:, 3 * step + index : 3 * step + index + 1] for index in range(3))
    chosen = one_hot_rows(row.astype(jnp.int32), rows)
    lent_ref[:, wide - LANES : wide] = jnp.zeros((LANES, LANES), jnp.bfloat16)
    lent_ref[:, :width] = dot(chosen, table_ref[...]).astype(jnp.bfloat16)
    lanes = iota((LANES, LANES), 1)
    tags = jnp.where(lanes == 0, slot, jnp.where(lanes == 1, trainer, 0.0))
    lent_ref[:, wide:] = tags.astype(jnp.bfloat16)


def collect_kernel(
    steps, cap, ask_ref, table_ref, plan_ref, tag_ref, flag_ref, lent_ref
):
    rows = table_ref.shape[0]
    f32 = jnp.float32
    asked = jnp.transpose(ask_ref[...].astype(f32))[: steps * cap, :]
    down, across = iota((LANES, LANES), 0), iota((LANES, LANES), 1)
    earlier = as_bf16(down < across)
    trainer = iota((1, LANES), 1).astype(f32)
    flag = jnp.zeros((1, 1), f32)
    tags = jnp.full((LANES, LANES), -1.0, f32)
    lent_rows = []
    extra = cap - DIRECT
    for step in range(steps):
        codes = asked[step * cap + DIRECT : (step + 1) * cap, :].astype(jnp.int32)
        flag = jnp.maximum(
            flag,
            jnp.max(
                jnp.where(codes[extra - 1 : extra, :] == -2, 1.0, 0.0), axis=1, keepdims=True
            ),
        )
        valid = codes >= 0
        row = jnp.where(valid, codes % rows, 0).astype(f32)
        place = jnp.where(valid, codes // rows, 0)
        far = place // cap
        slot = (place % cap).astype(f32)
        masks = [
            jnp.where(valid & (far == distance), 1.0, 0.0) for distance in range(1, LINE)
        ]
        stacked = jnp.concatenate(
            masks + [jnp.zeros((16 - extra * (LINE - 1), LANES), f32)], axis=0
        )
        before = dot(stacked.astype(jnp.bfloat16), earlier)
        totals = jnp.sum(stacked, axis=1, keepdims=True)
        targets = [jnp.full((1, LANES), -1.0, f32) for entry in range(extra)]
        for index in range(LINE - 1):
            offset = jnp.zeros((1, 1), f32)
            for entry in range(extra):
                line = index * extra + entry
                at = before[line : line + 1, :] + offset + index * LENT
                targets[entry] = jnp.where(masks[index][entry : entry + 1, :] > 0.5, at, targets[entry])
                offset = offset + totals[line : line + 1, :]
            flag = jnp.maximum(flag, jnp.where(offset > LENT, 1.0, 0.0))
        sums = [jnp.zeros((LANES, 1), f32) for index in range(3)]
        for entry in range(extra):
            chosen = down.astype(f32) == targets[entry]
            values = (row[entry : entry + 1, :], slot[entry : entry + 1, :], trainer)
            for index, value in enumerate(values):
                picked = jnp.where(chosen, value + 1.0, 0.0)
                sums[index] += jnp.sum(picked, axis=1, keepdims=True)
        for index in range(3):
            tags = jnp.where(across == 3 * step + index, sums[index] - 1.0, tags)
        lent_rows.append(to_row(sums[0] - 1.0))
    lent_rows.append(jnp.full((8 - steps, LANES), -1.0, f32))
    plan_ref[...] = jnp.concatenate([asked] + lent_rows, axis=0).astype(jnp.int32)
    tag_ref[...] = tags
    flag_ref[...] = jnp.broadcast_to(flag, flag_ref.shape)
    fill_lent(tag_ref, 0, table_ref, lent_ref)


def direct_kernel(step, cap, plan_ref, table_ref, rows_ref):
    rows, width = table_ref.shape
    rows_ref[:, rows_ref.shape[1] - LANES :] = jnp.zeros((rows_ref.shape[0], LANES), jnp.bfloat16)
    for first in range(0, DIRECT, 2):
        last = min(first + 2, DIRECT)
        columns = [
            to_column(plan_ref[step * cap + slot : step * cap + slot + 1, :].astype(jnp.float32))
            for slot in range(first, last)
        ]
        chosen = one_hot_rows(jnp.concatenate(columns, axis=0).astype(jnp.int32), rows)
        rows_ref[first * LANES : last * LANES, :width] = dot(chosen, table_ref[...]).astype(
            jnp.bfloat16
        )


def pack_kernel(
    width,
    rows_ref,
    flag_ref,
    one_ref,
    two_ref,
    three_ref,
    packed_ref,
    tag_ref,
    lent_ref,
    full_ref,
    stack_ref,
    held_ref,
    copied,
):
    wide = rows_ref.shape[1]
    lent_ref[3 * LENT :, :] = jnp.zeros((LANES - 3 * LENT, wide), jnp.bfloat16)
    tags = []
    for index, ref in enumerate((one_ref, two_ref, three_ref)):
        lent_ref[index * LENT : (index + 1) * LENT, :] = ref[:, :wide]
        tag = ref[:, wide : wide + LANES].astype(jnp.float32)
        tags.append(tag[:, 0:1] * LANES + tag[:, 1:2])
    tags.append(jnp.full((LANES - 3 * LENT, 1), -1.0, jnp.float32))
    tag = to_row(jnp.concatenate(tags, axis=0)).astype(jnp.int32)
    tag_ref[...] = jnp.broadcast_to(tag, tag_ref.shape)
    for slot in range(DIRECT):
        block = slice(slot * LANES, (slot + 1) * LANES)
        lent = dot(one_hot_columns(tag, slot * LANES, LANES), lent_ref[...])
        full_ref[block, :] = (rows_ref[block, :].astype(jnp.float32) + lent).astype(jnp.bfloat16)
    spread(width, full_ref, stack_ref, flag_ref[0:1, :])
    copies = []

    def send(part, rows):
        copies.append(
            pltpu.make_async_copy(held_ref.at[rows, :], packed_ref.at[rows, :], copied.at[part])
        )
        copies[-1].start()

    fold(stack_ref, held_ref, send)
    for copy in copies:
        copy.wait()


def short_trainer_kernel(
    blocks,
    negatives,
    width,
    pulled_ref,
    spot_ref,
    cosine_ref,
    sine_ref,
    packed_ref,
    phase_grad_ref,
    rows_ref,
    stack_ref,
    held_ref,
    copied,
    *scratch,
):
    unfold(pulled_ref, stack_ref)
    gather_up(width, stack_ref, rows_ref)
    mark = read_mark(width, stack_ref)
    sending = pltpu.make_async_copy(held_ref, phase_grad_ref, copied)

    def put_phase_grad(value):
        last = iota((held_ref.shape[0], LANES), 1) == LANES - 1
        held_ref[:, held_ref.shape[1] - LANES :] = jnp.where(last, mark, 0.0)
        held_ref[:, : value.shape[1]] = value
        sending.start()

    trainer_core(
        blocks,
        negatives,
        width,
        rows_ref[...],
        spot_ref,
        cosine_ref,
        sine_ref,
        rows_ref,
        put_phase_grad,
        *scratch,
    )
    spread(width, rows_ref, stack_ref, None)
    fold(stack_ref, packed_ref)
    sending.wait()


def return_kernel(width, arrived_ref, tag_ref, rows_ref, lent_ref, stack_ref):
    unfold(arrived_ref, stack_ref)
    gather_up(width, stack_ref, rows_ref)
    tag = to_column(tag_ref[0:1, :].astype(jnp.float32)).astype(jnp.int32)
    chosen = one_hot_rows(tag, rows_ref.shape[0])
    lent_ref[...] = dot(chosen, rows_ref[...]).astype(jnp.bfloat16)


def sum_kernel(
    step, cap, width, plan_ref, other_plan_ref, rows_ref, arrived_ref, total_ref, stack_ref, other_ref
):
    unfold(arrived_ref, stack_ref)
    gather_up(width, stack_ref, other_ref)

    def asked(ref):
        rows = [ref[step * cap + slot : step * cap + slot + 1, :] for slot in range(DIRECT)]
        return jnp.concatenate(rows, axis=1)

    own, other = asked(plan_ref), asked(other_plan_ref)
    for first in range(0, total_ref.shape[0], 256):
        total_ref[first : first + 256, :] = dot(
            one_hot_columns(own, first, 256), rows_ref[...]
        ) + dot(one_hot_columns(other, first, 256), other_ref[...])


def short_update_kernel(
    step,
    cap,
    has_next,
    steps,
    plan_ref,
    other_plan_ref,
    total_ref,
    back_ref,
    other_back_ref,
    table_ref,
    state_ref,
    tag_ref,
    new_table_ref,
    new_state_ref,
    *rest,
):
    if has_next:
        lent_ref, first_ref, second_ref = rest
    else:
        first_ref, second_ref = rest
    rows, width = table_ref.shape
    for ref, source in ((first_ref, back_ref), (second_ref, other_back_ref)):
        ref[: 3 * LENT, :] = source[...]
        ref[3 * LENT :, :] = jnp.zeros((LANES - 3 * LENT, ref.shape[1]), jnp.bfloat16)
    line = steps * cap + step
    own, other = plan_ref[line : line + 1, :], other_plan_ref[line : line + 1, :]
    size = 256
    for first in range(0, rows, size):
        lent = dot(one_hot_columns(own, first, size), first_ref[...]) + dot(
            one_hot_columns(other, first, size), second_ref[...]
        )
        gradient = (total_ref[first : first + size, :] + lent)[:, :width]
        values = table_ref[first : first + size, :].astype(jnp.float32)
        stepped = adagrad_block(gradient, first, values, state_ref, new_state_ref)
        if has_next:
            new_table_ref[first : first + size, :] = stepped
        else:
            turn_into(stepped, new_table_ref, first)
    if has_next:
        fill_lent(tag_ref, step + 1, new_table_ref, lent_ref)


def line_pairs(owners, far):
    return [
        (owner, owner // LINE * LINE + (owner % LINE + far) % LINE) for owner in range(owners)
    ]


def short_steps(
    entity_table,
    entity_state,
    relation_phase,
    relation_state,
    want_rows,
    want_count,
    head_slot,
    tail_slot,
    negative_slot,
    relation_ids,
):
    steps, owners, cap = want_rows.shape[1:]
    rows, width = entity_table.shape
    half = width // 2
    wide = -(-width // LANES) * LANES
    blocks, negatives = negative_slot.shape[2:]
    triples = head_slot.shape[2]
    relations = relation_phase.shape[0]
    direct = DIRECT * LANES
    packed_rows = PIECES * LANES
    packed = packed_width(width)
    half_wide = -(-(half + 1) // LANES) * LANES
    f32, i32, bf16 = jnp.float32, jnp.int32, jnp.bfloat16

    asked, *spots = call(
        functools.partial(route_kernel, rows),
        (shape((LANES, LANES), i32),) + (shape((8, LANES), i32),) * steps,
        "route",
        nbytes=1 << 20,
    )(
        jnp.transpose(want_rows[0], (0, 2, 1)),
        want_count[0],
        head_slot[0],
        tail_slot[0],
        negative_slot[0],
        relation_ids[0],
    )
    asked = lax.all_to_all(asked, "dom", split_axis=0, concat_axis=0, tiled=True)
    plan, tags, flag, lent = call(
        functools.partial(collect_kernel, steps, cap),
        (
            shape((steps * cap + 8, LANES), i32),
            shape((LANES, LANES), f32),
            shape((8, LANES), f32),
            shape((LANES, wide + LANES), bf16),
        ),
        "collect",
        nbytes=4 << 20,
    )(asked, entity_table)
    swap = [(0, 1), (1, 0)]
    other_plan = lax.ppermute(plan, "rep", swap)
    forth = [line_pairs(owners, far) for far in range(1, LINE)]
    back = [[(target, source) for source, target in pairs] for pairs in forth]

    table = entity_table
    state = entity_state.reshape(rows // LANES, LANES)
    phase = relation_phase
    phase_state = relation_state[:, None]
    phase, other_plan = lax.optimization_barrier((phase, other_plan))
    relation = call(
        short_relation_kernel,
        (
            shape((relations, half), f32),
            shape((relations, 1), f32),
            shape((1, relations), f32),
            shape((8, LANES), f32),
        ),
        "relation",
        flops=6 * triples * relations * half,
        nbytes=4 * triples * half,
    )
    for step in range(steps):
        has_next = step + 1 < steps
        loans = [
            lax.ppermute(lent[index * LENT : (index + 1) * LENT], "dom", forth[index])
            for index in range(LINE - 1)
        ]
        sent = call(
            functools.partial(direct_kernel, step, cap),
            shape((direct, wide), bf16),
            "direct",
            flops=2 * direct * rows * width,
            nbytes=4 * rows * width,
        )(plan, table)
        offered, loan_tag = call(
            functools.partial(pack_kernel, width),
            (shape((packed_rows, packed), bf16), shape((8, LANES), i32)),
            "pack",
            nbytes=4 * rows * width,
            out_specs=(pl.BlockSpec(memory_space=pltpu.HBM), pl.BlockSpec(memory_space=pltpu.VMEM)),
            scratch_shapes=[
                pltpu.VMEM((LANES, wide), bf16),
                pltpu.VMEM((direct, wide), bf16),
                pltpu.VMEM((packed_rows, packed), bf16),
                pltpu.VMEM((packed_rows, packed), bf16),
                pltpu.SemaphoreType.DMA((LANES // PART,)),
            ],
        )(sent, flag, *loans)
        if step > 0:
            offered, phase_grad = lax.optimization_barrier((offered, phase_grad))
            phase, phase_state, state_row, seen = relation(
                spots[step - 1], phase_grad, phase, phase_state
            )
            if step == 1:
                seen = jnp.maximum(seen, lax.ppermute(seen, "rep", swap))
                phase, spoiled = lax.optimization_barrier((phase, jnp.max(seen)))
        pulled = lax.all_to_all(
            offered.reshape(owners, PIECES, packed), "dom", split_axis=0, concat_axis=0, tiled=True
        ).reshape(packed_rows, packed)
        relation_span = jnp.arange(relations, dtype=i32)
        selector = (relation_ids[0, step][:, None] == relation_span[None, :]).astype(f32)
        phase_rows = jnp.dot(selector, phase, precision=lax.Precision.HIGHEST)
        padded, phase_grad = call(
            functools.partial(short_trainer_kernel, blocks, negatives, width),
            (shape((packed_rows, packed), bf16), shape((triples, half_wide), f32)),
            "trainer",
            flops=2 * direct * (9 * triples) * width,
            nbytes=4 * rows * width,
            out_specs=(pl.BlockSpec(memory_space=pltpu.VMEM), pl.BlockSpec(memory_space=pltpu.HBM)),
            scratch_shapes=[
                pltpu.VMEM((direct, wide), bf16),
                pltpu.VMEM((packed_rows, packed), bf16),
                pltpu.VMEM((triples, half_wide), f32),
                pltpu.SemaphoreType.DMA,
            ]
            + trainer_scratch(triples, blocks * negatives, width, wide, wide),
        )(pulled, spots[step], jnp.cos(phase_rows), jnp.sin(phase_rows))
        arrived = lax.all_to_all(
            padded.reshape(owners, PIECES, packed), "dom", split_axis=0, concat_axis=0, tiled=True
        ).reshape(packed_rows, packed)
        arrived_other = lax.ppermute(arrived, "rep", swap)
        got, dues = call(
            functools.partial(return_kernel, width),
            (shape((direct, wide), bf16), shape((LANES, wide), bf16)),
            "give_back",
            flops=2 * LANES * direct * wide,
            nbytes=4 * rows * width,
            scratch_shapes=[pltpu.VMEM((packed_rows, packed), bf16)],
        )(arrived, loan_tag)
        dues = [
            lax.ppermute(dues[index * LENT : (index + 1) * LENT], "dom", back[index])
            for index in range(LINE - 1)
        ]
        total = call(
            functools.partial(sum_kernel, step, cap, width),
            shape((rows, wide), f32),
            "sum",
            flops=4 * direct * rows * width,
            nbytes=8 * rows * width,
            scratch_shapes=[
                pltpu.VMEM((packed_rows, packed), bf16),
                pltpu.VMEM((direct, wide), bf16),
            ],
        )(plan, other_plan, got, arrived_other)
        dues, total = lax.optimization_barrier((dues, total))
        dues = jnp.concatenate(dues, axis=0)
        dues_other = lax.ppermute(dues, "rep", swap)
        outputs = [
            shape((rows, width) if has_next else (width, rows), bf16),
            shape((rows // LANES, LANES), f32),
        ]
        if has_next:
            outputs.append(shape((LANES, wide + LANES), bf16))
        results = call(
            functools.partial(short_update_kernel, step, cap, has_next, steps),
            tuple(outputs),
            "update",
            flops=4 * LANES * rows * width,
            nbytes=12 * rows * width,
            scratch_shapes=[pltpu.VMEM((LANES, wide), bf16)] * 2,
        )(plan, other_plan, total, dues, dues_other, table, state, tags)
        table, state = results[:2]
        if has_next:
            lent = results[2]
    phase, phase_state, state_row, seen = relation(spots[-1], phase_grad, phase, phase_state)
    table, spoiled = lax.optimization_barrier((table, spoiled))
    return (table.T, state.reshape(rows), phase, state_row.reshape(relations)), spoiled > 0.5


def local(*arrays):
    results, spoiled = short_steps(*arrays)
    return lax.cond(spoiled, lambda: full_steps(*arrays), lambda: results)


def solution(mesh):
    placed = (
        P("dom", None),
        P("dom"),
        P(("dom", "rep"), None),
        P(("dom", "rep")),
        P(("dom", "rep"), None, None, None),
        P(("dom", "rep"), None, None),
        P(("dom", "rep"), None, None),
        P(("dom", "rep"), None, None),
        P(("dom", "rep"), None, None, None),
        P(("dom", "rep"), None, None),
    )
    return jax.shard_map(
        local,
        mesh=mesh,
        in_specs=placed,
        out_specs=(P("dom", None), P("dom"), P(("dom", "rep"), None), P(("dom", "rep"))),
        check_vma=False,
    )
```

```python
import functools

import jax
import jax.numpy as jnp
from jax import lax
from jax.experimental import pallas as pl
from jax.experimental.pallas import tpu as pltpu
from jax.sharding import PartitionSpec as P

learn_rate = 0.5
smoothing = 0.25
epsilon = 1e-10
margin_rate = 0.26

LANES = 128
VMEM_LIMIT = 20 * 1024 * 1024


def slot_place(slot_ids, counts, slot_cap):
    running = jnp.cumsum(counts, dtype=jnp.int32)
    passed = (slot_ids[..., None] >= running).astype(jnp.int32)
    owner_index = jnp.sum(passed, axis=-1, dtype=jnp.int32)
    before = jnp.sum(passed * counts, axis=-1, dtype=jnp.int32)
    return owner_index * slot_cap + slot_ids - before


def call(kernel, out_shape, name, flops=0, nbytes=0, **kwargs):
    return pl.pallas_call(
        kernel,
        out_shape=out_shape,
        name=name,
        cost_estimate=pl.CostEstimate(flops=flops, bytes_accessed=nbytes, transcendentals=0),
        compiler_params=pltpu.CompilerParams(vmem_limit_bytes=VMEM_LIMIT),
        **kwargs,
    )


def diagonal():
    down = lax.broadcasted_iota(jnp.int32, (LANES, LANES), 0)
    across = lax.broadcasted_iota(jnp.int32, (LANES, LANES), 1)
    return down == across


def to_column(row):
    spread = jnp.broadcast_to(row, (LANES, LANES))
    return jnp.sum(jnp.where(diagonal(), spread, 0.0), axis=1, keepdims=True)


def to_row(column):
    spread = jnp.broadcast_to(column, (LANES, LANES))
    return jnp.sum(jnp.where(diagonal(), spread, 0.0), axis=0, keepdims=True)


def one_hot_rows(column, width):
    lanes = lax.broadcasted_iota(jnp.int32, (column.shape[0], width), 1)
    return jnp.where(lanes == column, 1.0, 0.0).astype(jnp.bfloat16)


def one_hot_columns(row, first, height):
    down = lax.broadcasted_iota(jnp.int32, (height, row.shape[1]), 0) + first
    return jnp.where(down == row, 1.0, 0.0).astype(jnp.bfloat16)


def dot(left, right):
    return jnp.dot(left, right, preferred_element_type=jnp.float32)


def turn_into(values, ref, first):
    rows, width = values.shape
    for start in range(0, width, 256):
        size = min(256, width - start)
        down = lax.broadcasted_iota(jnp.int32, (size, size), 0)
        across = lax.broadcasted_iota(jnp.int32, (size, size), 1)
        unit = jnp.where(down == across, 1.0, 0.0).astype(jnp.bfloat16)
        product = lax.dot_general(
            unit,
            values[:, start : start + size],
            (((1,), (1,)), ((), ())),
            preferred_element_type=jnp.float32,
        )
        ref[start : start + size, first : first + rows] = product.astype(jnp.bfloat16)


def split3(values):
    high = values.astype(jnp.bfloat16)
    rest = values - high.astype(jnp.float32)
    middle = rest.astype(jnp.bfloat16)
    low = (rest - middle.astype(jnp.float32)).astype(jnp.bfloat16)
    return high, middle, low


def gather_rows(wanted_ref, table_ref, offered_ref):
    table_rows = table_ref.shape[0]
    blocks = wanted_ref.shape[0]
    step = 2
    for start in range(0, blocks, step):
        columns = [
            to_column(wanted_ref[block : block + 1, :].astype(jnp.float32)).astype(jnp.int32)
            for block in range(start, start + step)
        ]
        chosen = one_hot_rows(jnp.concatenate(columns, axis=0), table_rows)
        rows = pl.ds(start * LANES, step * LANES)
        offered_ref[rows, :] = dot(chosen, table_ref[...]).astype(jnp.bfloat16)


def offer_kernel(wanted_ref, table_ref, offered_ref):
    gather_rows(wanted_ref, table_ref, offered_ref)


def own_sum_kernel(asked_ref, arrived_ref, total_ref):
    rows = total_ref.shape[0]
    step = 256
    asked = asked_ref[...]
    for first in range(0, rows, step):
        chosen = one_hot_columns(asked, first, step)
        total_ref[first : first + step, :] = dot(chosen, arrived_ref[...])


def adagrad_block(gradient, first, values, state_ref, new_state_ref):
    step, width = gradient.shape
    mean_square = jnp.sum(gradient * gradient, axis=1, keepdims=True) / width
    fresh = []
    for block in range(first // LANES, (first + step) // LANES):
        old = to_column(state_ref[block : block + 1, :])
        at = block * LANES - first
        new = old + mean_square[at : at + LANES, :]
        new_state_ref[block : block + 1, :] = to_row(new)
        fresh.append(new)
    rate = learn_rate / (jnp.sqrt(jnp.concatenate(fresh, axis=0)) + epsilon)
    return (values - gradient * rate).astype(jnp.bfloat16)


def update_kernel(
    has_next,
    asked_ref,
    arrived_ref,
    own_ref,
    table_ref,
    state_ref,
    *rest,
):
    if has_next:
        wanted_ref, new_table_ref, new_state_ref, offered_ref = rest
    else:
        new_table_ref, new_state_ref = rest
    rows, width = table_ref.shape
    step = 256
    asked = asked_ref[...]
    for first in range(0, rows, step):
        chosen = one_hot_columns(asked, first, step)
        gradient = own_ref[first : first + step, :] + dot(chosen, arrived_ref[...])
        gradient = gradient[:, :width]
        values = table_ref[first : first + step, :].astype(jnp.float32)
        stepped = adagrad_block(gradient, first, values, state_ref, new_state_ref)
        if has_next:
            new_table_ref[first : first + step, :] = stepped
        else:
            turn_into(stepped, new_table_ref, first)
    if has_next:
        gather_rows(wanted_ref, new_table_ref, offered_ref)


def sigmoid(value):
    tail = jnp.exp(-jnp.abs(value))
    return jnp.where(value >= 0, 1.0, tail) / (1.0 + tail)


def trainer_core(
    blocks,
    negatives,
    width,
    pulled,
    spot_ref,
    cosine_ref,
    sine_ref,
    padded_ref,
    put_phase_grad,
    read_ref,
    rot_real_ref,
    rot_imag_ref,
    tail_real_ref,
    tail_imag_ref,
    neg_real_ref,
    neg_imag_ref,
    rot_real_grad_ref,
    rot_imag_grad_ref,
    tail_real_grad_ref,
    tail_imag_grad_ref,
    neg_real_grad_ref,
    neg_imag_grad_ref,
    grads_ref,
):
    slots = pulled.shape[0]
    half = width // 2
    triples = cosine_ref.shape[0]
    neg_rows = blocks * negatives
    margin = margin_rate * half

    places = [
        to_column(spot_ref[index : index + 1, :].astype(jnp.float32)).astype(jnp.int32)
        for index in range(3)
    ]
    places[2] = places[2][:neg_rows]
    read_ref[...] = dot(one_hot_rows(jnp.concatenate(places, axis=0), slots), pulled)
    head_ref = read_ref.at[:triples, :]
    tail_ref = read_ref.at[triples : 2 * triples, :]
    negative_ref = read_ref.at[2 * triples :, :]

    cosine = cosine_ref[...]
    sine = sine_ref[...]
    head_real = head_ref[:, :half]
    head_imag = head_ref[:, half:width]
    rot_real_ref[...] = head_real * cosine - head_imag * sine
    rot_imag_ref[...] = head_real * sine + head_imag * cosine
    tail_real_ref[...] = tail_ref[:, :half]
    tail_imag_ref[...] = tail_ref[:, half:width]
    neg_real_ref[...] = negative_ref[:, :half]
    neg_imag_ref[...] = negative_ref[:, half:width]
    neg_real_grad_ref[...] = jnp.zeros_like(neg_real_grad_ref)
    neg_imag_grad_ref[...] = jnp.zeros_like(neg_imag_grad_ref)

    group = 8
    per_block = triples // blocks

    def pair(real, imag, other_real, other_imag):
        diff_real = real - other_real
        diff_imag = imag - other_imag
        square = diff_real * diff_real + diff_imag * diff_imag + smoothing
        inverse = lax.rsqrt(square)
        distance = jnp.sum(square * inverse, axis=1, keepdims=True)
        return distance, inverse, diff_real, diff_imag

    def chunk(index, carry):
        rows = pl.ds(pl.multiple_of(index * group, group), group)
        first = (index * group) // per_block * negatives
        real = rot_real_ref[rows, :]
        imag = rot_imag_ref[rows, :]
        distance, inverse, diff_real, diff_imag = pair(
            real, imag, tail_real_ref[rows, :], tail_imag_ref[rows, :]
        )
        scale = 0.25 * sigmoid(0.25 * distance - margin) * inverse
        total_real = scale * diff_real
        total_imag = scale * diff_imag
        tail_real_grad_ref[rows, :] = -total_real
        tail_imag_grad_ref[rows, :] = -total_imag
        for n in range(negatives):
            distance, inverse, diff_real, diff_imag = pair(
                real,
                imag,
                neg_real_ref[pl.ds(first + n, 1), :],
                neg_imag_ref[pl.ds(first + n, 1), :],
            )
            scale = (-0.25 / negatives) * sigmoid(margin - 0.25 * distance) * inverse
            part_real = scale * diff_real
            part_imag = scale * diff_imag
            total_real += part_real
            total_imag += part_imag
            neg_real_grad_ref[first + n] -= part_real
            neg_imag_grad_ref[first + n] -= part_imag
        rot_real_grad_ref[rows, :] = total_real
        rot_imag_grad_ref[rows, :] = total_imag
        return carry

    lax.fori_loop(0, triples // group, chunk, 0, unroll=4)

    real_grad = rot_real_grad_ref[...]
    imag_grad = rot_imag_grad_ref[...]
    put_phase_grad(imag_grad * rot_real_ref[...] - real_grad * rot_imag_ref[...])

    grads_ref[:, width:] = jnp.zeros_like(grads_ref[:, width:])

    def put(first, rows, real, imag):
        value = jnp.concatenate([real, imag], axis=1)
        grads_ref[first : first + rows, :width] = value.astype(jnp.bfloat16)

    put(
        0,
        triples,
        real_grad * cosine + imag_grad * sine,
        imag_grad * cosine - real_grad * sine,
    )
    put(triples, triples, tail_real_grad_ref[...], tail_imag_grad_ref[...])
    partial = neg_rows * group
    put(
        2 * triples,
        partial,
        neg_real_grad_ref[...].reshape(partial, half),
        neg_imag_grad_ref[...].reshape(partial, half),
    )
    spots = [spot_ref[index : index + 1, :] for index in range(2)]
    column = to_column(spot_ref[2:3, :].astype(jnp.float32))
    for first in range(0, partial, LANES):
        down = lax.broadcasted_iota(jnp.int32, (LANES, LANES), 0)
        across = lax.broadcasted_iota(jnp.int32, (LANES, LANES), 1) + first
        repeated = jnp.where(down == across // group, column, 0.0)
        spots.append(jnp.sum(repeated, axis=0, keepdims=True).astype(jnp.int32))
    for first in range(0, slots, 256):
        step = min(256, slots - first)
        chosen = [one_hot_columns(spot, first, step) for spot in spots]
        chosen = jnp.concatenate(chosen, axis=1)
        padded_ref[first : first + step, :] = dot(chosen, grads_ref[...]).astype(jnp.bfloat16)


def trainer_kernel(
    blocks,
    negatives,
    pulled_ref,
    spot_ref,
    cosine_ref,
    sine_ref,
    padded_ref,
    phase_grad_ref,
    *scratch,
):
    def put_phase_grad(value):
        phase_grad_ref[...] = value

    trainer_core(
        blocks,
        negatives,
        pulled_ref.shape[1],
        pulled_ref[...],
        spot_ref,
        cosine_ref,
        sine_ref,
        padded_ref,
        put_phase_grad,
        *scratch,
    )


def trainer_scratch(triples, neg_rows, width, wide, read_width):
    half = width // 2
    return (
        [pltpu.VMEM((2 * triples + neg_rows, read_width), jnp.float32)]
        + [pltpu.VMEM((triples, half), jnp.float32)] * 4
        + [pltpu.VMEM((neg_rows, half), jnp.float32)] * 2
        + [pltpu.VMEM((triples, half), jnp.float32)] * 4
        + [pltpu.VMEM((neg_rows, 8, half), jnp.float32)] * 2
        + [pltpu.VMEM((2 * triples + 8 * neg_rows, wide), jnp.bfloat16)]
    )


def relation_kernel(spot_ref, grad_ref, phase_ref, state_ref, new_phase_ref, new_state_ref):
    relations, half = phase_ref.shape
    chosen = one_hot_columns(spot_ref[3:4, :], 0, relations)
    high, middle, low = split3(grad_ref[...])
    gradient = dot(chosen, high) + dot(chosen, middle) + dot(chosen, low)
    gradient = gradient[:, :half]
    mean_square = jnp.sum(gradient * gradient, axis=1, keepdims=True) / half
    fresh = state_ref[...] + mean_square
    new_state_ref[...] = fresh
    new_phase_ref[...] = phase_ref[...] - learn_rate * gradient / (jnp.sqrt(fresh) + epsilon)


def put_angles(spot_ref, phase, cosine_ref, sine_ref):
    column = to_column(spot_ref[3:4, :].astype(jnp.float32)).astype(jnp.int32)
    chosen = one_hot_rows(column, phase.shape[0])
    for ref, values in ((cosine_ref, jnp.cos(phase)), (sine_ref, jnp.sin(phase))):
        high, middle, low = split3(values)
        ref[...] = dot(chosen, high) + dot(chosen, middle) + dot(chosen, low)


def short_relation_kernel(
    spot_ref,
    grad_ref,
    phase_ref,
    state_ref,
    next_spot_ref,
    new_phase_ref,
    new_state_ref,
    row_ref,
    flag_ref,
    cosine_ref,
    sine_ref,
):
    relation_kernel(spot_ref, grad_ref, phase_ref, state_ref, new_phase_ref, new_state_ref)
    relations = phase_ref.shape[0]
    spare = jnp.zeros((LANES - relations, 1), jnp.float32)
    row = to_row(jnp.concatenate([new_state_ref[...], spare], axis=0))
    row_ref[...] = row[:, :relations]
    last = grad_ref.shape[1] - 1
    mark = jnp.max(grad_ref[:, last : last + 1], axis=0, keepdims=True)
    flag_ref[...] = jnp.broadcast_to(mark, flag_ref.shape)
    put_angles(next_spot_ref, new_phase_ref[...], cosine_ref, sine_ref)


def shape(dims, dtype):
    return jax.ShapeDtypeStruct(dims, dtype)


def full_steps(
    entity_table,
    entity_state,
    relation_phase,
    relation_state,
    want_rows,
    want_count,
    head_slot,
    tail_slot,
    negative_slot,
    relation_ids,
):
    steps, owners, cap = want_rows.shape[1:]
    rows, width = entity_table.shape
    half = width // 2
    wide = -(-width // LANES) * LANES
    blocks, negatives = negative_slot.shape[2:]
    triples = head_slot.shape[2]
    slots = owners * cap
    relations = relation_phase.shape[0]
    table_bytes = 2 * rows * width

    asked = jnp.transpose(want_rows[0], (1, 0, 2)).reshape(owners, steps * cap)
    asked = lax.all_to_all(asked, "dom", split_axis=0, concat_axis=0, tiled=True)
    asked = jnp.transpose(asked.reshape(owners, steps, cap), (1, 0, 2))
    asked = asked.reshape(steps, slots // LANES, LANES)
    asked_other = lax.ppermute(asked, "rep", [(0, 1), (1, 0)])
    ask_row = asked.reshape(steps, 1, slots)
    ask_row_other = asked_other.reshape(steps, 1, slots)

    spots = []
    for step in range(steps):
        counts = want_count[0, step]
        neg = slot_place(negative_slot[0, step].reshape(-1), counts, cap)
        spare = jnp.full((triples - neg.shape[0],), -1, jnp.int32)
        spots.append(
            jnp.stack(
                [
                    slot_place(head_slot[0, step], counts, cap),
                    slot_place(tail_slot[0, step], counts, cap),
                    jnp.concatenate([neg, spare]),
                    relation_ids[0, step],
                ]
            )
        )

    table = entity_table
    state = entity_state.reshape(rows // LANES, LANES)
    phase = relation_phase
    phase_state = relation_state[:, None]
    offered = call(
        offer_kernel,
        shape((slots, width), jnp.bfloat16),
        "offer",
        flops=2 * slots * rows * width,
        nbytes=2 * table_bytes,
    )(asked[0], table)
    f32 = jnp.float32
    for step in range(steps):
        pulled = lax.all_to_all(
            offered.reshape(owners, cap, width), "dom", split_axis=0, concat_axis=0, tiled=True
        ).reshape(slots, width)
        relation_span = jnp.arange(relations, dtype=jnp.int32)
        selector = (relation_ids[0, step][:, None] == relation_span[None, :]).astype(f32)
        phase_rows = jnp.dot(selector, phase, precision=lax.Precision.HIGHEST)
        padded, phase_grad = call(
            functools.partial(trainer_kernel, blocks, negatives),
            (shape((slots, wide), jnp.bfloat16), shape((triples, half), f32)),
            "trainer",
            flops=2 * slots * (9 * triples) * width,
            nbytes=2 * table_bytes,
            scratch_shapes=trainer_scratch(triples, blocks * negatives, width, wide, width),
        )(pulled, spots[step], jnp.cos(phase_rows), jnp.sin(phase_rows))
        arrived = lax.all_to_all(
            padded.reshape(owners, cap, wide), "dom", split_axis=0, concat_axis=0, tiled=True
        ).reshape(slots, wide)
        phase, phase_state = call(
            relation_kernel,
            (shape((relations, half), f32), shape((relations, 1), f32)),
            "relation",
            flops=6 * triples * relations * half,
            nbytes=4 * triples * half,
        )(spots[step], phase_grad, phase, phase_state)
        arrived_other = lax.ppermute(arrived, "rep", [(0, 1), (1, 0)])
        own = call(
            own_sum_kernel,
            shape((rows, wide), f32),
            "own_sum",
            flops=2 * slots * rows * width,
            nbytes=3 * table_bytes,
        )(ask_row[step], arrived)
        has_next = step + 1 < steps
        outputs = [
            shape((rows, width) if has_next else (width, rows), jnp.bfloat16),
            shape((rows // LANES, LANES), f32),
        ]
        operands = [ask_row_other[step], arrived_other, own, table, state]
        if has_next:
            outputs.append(shape((slots, width), jnp.bfloat16))
            operands.append(asked[step + 1])
        results = call(
            functools.partial(update_kernel, has_next),
            tuple(outputs),
            "update",
            flops=2 * slots * rows * width * (1 + has_next),
            nbytes=6 * table_bytes,
        )(*operands)
        table, state = results[:2]
        if has_next:
            offered = results[2]
    return (table.T, state.reshape(rows), phase, phase_state[:, 0])


DIRECT = 5
LINE = 4
LENT = 32
PIECES = 8


def iota(dims, axis):
    return lax.broadcasted_iota(jnp.int32, dims, axis)


def as_bf16(mask):
    return jnp.where(mask, 1.0, 0.0).astype(jnp.bfloat16)


def places(width):
    full, rest = divmod(width, LANES)
    whole = [divmod(index, full) for index in range(DIRECT * full)]
    share = LANES // rest
    groups = [list(range(first, min(first + share, DIRECT))) for first in range(0, DIRECT, share)]
    return full, rest, whole, groups


def packed_width(width):
    full, rest, whole, groups = places(width)
    return -(-(len(whole) + len(groups)) // PIECES) * LANES


def stack_tile(position):
    tile, piece = divmod(position, PIECES)
    return slice(piece * LANES, (piece + 1) * LANES), slice(tile * LANES, (tile + 1) * LANES)


def spread(width, rows_ref, stack_ref, mark):
    full, rest, whole, groups = places(width)
    for position, (row, tile) in enumerate(whole):
        stack_ref[stack_tile(position)] = rows_ref[
            row * LANES : (row + 1) * LANES, tile * LANES : (tile + 1) * LANES
        ]
    last = len(whole) + len(groups) - 1
    for index, group in enumerate(groups):
        position = len(whole) + index
        total = jnp.zeros((LANES, LANES), jnp.float32)
        for row in group:
            tail = rows_ref[row * LANES : (row + 1) * LANES, full * LANES : (full + 1) * LANES]
            tail = tail.astype(jnp.float32)
            shift = rest * (row - group[0])
            total = total + (pltpu.roll(tail, shift, 1) if shift else tail)
        if position == last and mark is not None:
            total = jnp.where(iota((LANES, LANES), 1) == LANES - 1, mark, total)
        stack_ref[stack_tile(position)] = total.astype(jnp.bfloat16)
    for position in range(last + 1, stack_ref.shape[1] // LANES * PIECES):
        stack_ref[stack_tile(position)] = jnp.zeros((LANES, LANES), jnp.bfloat16)


def gather_up(width, stack_ref, rows_ref):
    full, rest, whole, groups = places(width)
    for position, (row, tile) in enumerate(whole):
        rows_ref[row * LANES : (row + 1) * LANES, tile * LANES : (tile + 1) * LANES] = stack_ref[
            stack_tile(position)
        ]
    for index, group in enumerate(groups):
        tails = stack_ref[stack_tile(len(whole) + index)].astype(jnp.float32)
        for row in group:
            shift = rest * (row - group[0])
            tail = pltpu.roll(tails, LANES - shift, 1) if shift else tails
            tail = jnp.where(iota((LANES, LANES), 1) < rest, tail, 0.0)
            rows_ref[row * LANES : (row + 1) * LANES, full * LANES : (full + 1) * LANES] = (
                tail.astype(jnp.bfloat16)
            )


def read_mark(width, stack_ref):
    full, rest, whole, groups = places(width)
    tile = stack_ref[stack_tile(len(whole) + len(groups) - 1)].astype(jnp.float32)
    tile = jnp.where(iota((LANES, LANES), 1) == LANES - 1, tile, 0.0)
    return jnp.max(jnp.max(tile, axis=1, keepdims=True), axis=0, keepdims=True)


PART = LANES // 4


def fold(stack_ref, packed_ref, done=None):
    size = PART * PIECES
    down, across = iota((size, size), 0), iota((size, size), 1)
    turn = as_bf16(across == (down % PIECES) * PART + down // PIECES)
    for part in range(LANES // PART):
        pieces = [
            stack_ref[piece * LANES + part * PART : piece * LANES + (part + 1) * PART, :]
            for piece in range(PIECES)
        ]
        packed_ref[part * size : (part + 1) * size, :] = dot(
            turn, jnp.concatenate(pieces, axis=0)
        ).astype(jnp.bfloat16)
        if done is not None:
            done(part, pl.ds(part * size, size))


def unfold(packed_ref, stack_ref):
    size = PART * PIECES
    down, across = iota((size, size), 0), iota((size, size), 1)
    turn = as_bf16(across == (down % PART) * PIECES + down // PART)
    for part in range(LANES // PART):
        block = dot(turn, packed_ref[part * size : (part + 1) * size, :]).astype(jnp.bfloat16)
        for piece in range(PIECES):
            stack_ref[piece * LANES + part * PART : piece * LANES + (part + 1) * PART, :] = block[
                piece * PART : (piece + 1) * PART, :
            ]


def route_kernel(
    rows,
    want_ref,
    count_ref,
    head_ref,
    tail_ref,
    neg_ref,
    relation_ref,
    ask_ref,
    *spot_refs,
):
    steps, cap, owners = want_ref.shape
    f32 = jnp.float32
    down, across = iota((LANES, LANES), 0), iota((LANES, LANES), 1)
    same_line = down // LINE == across // LINE
    line_mat = as_bf16(same_line)
    line_before = as_bf16(same_line & (down < across))
    upto = as_bf16(down <= across)
    owner = iota((1, LANES), 1).astype(f32)
    y_at = iota((1, LANES), 1) % LINE
    slot_number = iota((cap, LANES), 0).astype(f32)
    none = jnp.zeros((cap - 3, LANES), f32)
    asks = []
    for step in range(steps):
        count = count_ref[step : step + 1, :].astype(f32)
        ends = dot(jnp.broadcast_to(count, (cap, LANES)).astype(jnp.bfloat16), upto)[0:1, :]
        begins = ends - count
        seen = jnp.zeros((cap, LANES), f32)
        uses = []
        slots = [to_column(ref[step : step + 1, :].astype(f32)) for ref in (head_ref, tail_ref)]
        slots.append(jnp.full((LANES, 1), -1.0, f32))
        blocks, negatives = neg_ref.shape[1:]
        for block in range(blocks):
            row = neg_ref[step, block : block + 1, :].astype(f32) + 1.0
            here = iota((LANES, negatives), 0) - block * negatives == iota((LANES, negatives), 1)
            slots[2] += jnp.sum(jnp.where(here, row, 0.0), axis=1, keepdims=True)
        for slot in slots:
            owned = (slot >= begins) & (slot < ends)
            within = slot - jnp.sum(jnp.where(owned, begins, 0.0), axis=1, keepdims=True)
            seen += dot(as_bf16(slot_number == to_row(within)), as_bf16(owned))
            uses.append((owned, within))
        used = seen > 0.5
        ranks = [jnp.zeros((1, LANES), f32)]
        for slot in range(cap):
            ranks.append(ranks[-1] + jnp.where(used[slot : slot + 1, :], 1.0, 0.0))
        total = ranks.pop()
        rank = jnp.concatenate(ranks, axis=0)
        over = jnp.maximum(total - DIRECT, 0.0)
        free = DIRECT - jnp.minimum(total, DIRECT)
        pair = jnp.concatenate([over, free, total, none], axis=0).astype(jnp.bfloat16)
        before = dot(pair, line_before)
        whole = dot(pair, line_mat)
        lost = jnp.max(
            jnp.where(whole[0:1, :] > whole[1:2, :], 1.0, 0.0), axis=1, keepdims=True
        )
        turn = before[0:1, :] + rank - DIRECT
        side = jnp.concatenate([before[1:2, :], free, total, none], axis=0).astype(jnp.bfloat16)
        at_slot = rank
        at_owner = jnp.broadcast_to(owner, (cap, LANES))
        code = jnp.zeros((cap, LANES), f32)
        for far in range(1, LINE):
            mover = as_bf16(same_line & (down % LINE == (across + far) % LINE))
            moved = dot(side, mover)
            hit = used & (rank >= DIRECT) & (turn >= moved[0:1, :])
            hit = hit & (turn < moved[0:1, :] + moved[1:2, :])
            slot = moved[2:3, :] + turn - moved[0:1, :]
            other = owner + ((y_at + far) % LINE - y_at).astype(f32)
            at_slot = jnp.where(hit, slot, at_slot)
            at_owner = jnp.where(hit, other, at_owner)
            code = jnp.where(hit, rows * (far * cap + slot), code)
        want = want_ref[step].astype(f32)
        for place in range(cap):
            chosen = used & (rank == place)
            value = want + 1.0 if place < DIRECT else want + code + 1.0
            row = jnp.sum(jnp.where(chosen, value, 0.0), axis=0, keepdims=True) - 1.0
            if place == cap - 1:
                row = jnp.where(lost > 0.5, -2.0, row)
            asks.append(row)
        where_at = at_slot * owners + at_owner
        spots = []
        for owned, within in uses:
            table = jnp.zeros((LANES, LANES), f32)
            for slot in range(cap):
                table = jnp.where(within == slot, where_at[slot : slot + 1, :], table)
            found = jnp.sum(jnp.where(owned, table, 0.0), axis=1, keepdims=True)
            found = jnp.where(within < 0, -1.0, found)
            spots.append(to_row(found))
        spots.append(relation_ref[step : step + 1, :].astype(f32))
        spots.append(jnp.zeros((8 - len(spots), LANES), f32))
        spot_refs[step][...] = jnp.concatenate(spots, axis=0).astype(jnp.int32)
    asks.append(jnp.zeros((LANES - len(asks), LANES), f32))
    ask_ref[...] = jnp.transpose(jnp.concatenate(asks, axis=0)).astype(jnp.int32)


def fill_lent(tag_ref, step, table_ref, lent_ref):
    rows, width = table_ref.shape
    wide = lent_ref.shape[1] - LANES
    row, slot, trainer = (tag_ref[:, 3 * step + index : 3 * step + index + 1] for index in range(3))
    chosen = one_hot_rows(row.astype(jnp.int32), rows)
    lent_ref[:, wide - LANES : wide] = jnp.zeros((LANES, LANES), jnp.bfloat16)
    lent_ref[:, :width] = dot(chosen, table_ref[...]).astype(jnp.bfloat16)
    lanes = iota((LANES, LANES), 1)
    tags = jnp.where(lanes == 0, slot, jnp.where(lanes == 1, trainer, 0.0))
    lent_ref[:, wide:] = tags.astype(jnp.bfloat16)


def collect_kernel(
    steps, cap, ask_ref, table_ref, plan_ref, tag_ref, flag_ref, lent_ref
):
    rows = table_ref.shape[0]
    f32 = jnp.float32
    asked = jnp.transpose(ask_ref[...].astype(f32))[: steps * cap, :]
    down, across = iota((LANES, LANES), 0), iota((LANES, LANES), 1)
    earlier = as_bf16(down < across)
    trainer = iota((1, LANES), 1).astype(f32)
    flag = jnp.zeros((1, 1), f32)
    tags = jnp.full((LANES, LANES), -1.0, f32)
    lent_rows = []
    extra = cap - DIRECT
    for step in range(steps):
        codes = asked[step * cap + DIRECT : (step + 1) * cap, :].astype(jnp.int32)
        flag = jnp.maximum(
            flag,
            jnp.max(
                jnp.where(codes[extra - 1 : extra, :] == -2, 1.0, 0.0), axis=1, keepdims=True
            ),
        )
        valid = codes >= 0
        row = jnp.where(valid, codes % rows, 0).astype(f32)
        place = jnp.where(valid, codes // rows, 0)
        far = place // cap
        slot = (place % cap).astype(f32)
        masks = [
            jnp.where(valid & (far == distance), 1.0, 0.0) for distance in range(1, LINE)
        ]
        stacked = jnp.concatenate(
            masks + [jnp.zeros((16 - extra * (LINE - 1), LANES), f32)], axis=0
        )
        before = dot(stacked.astype(jnp.bfloat16), earlier)
        totals = jnp.sum(stacked, axis=1, keepdims=True)
        targets = [jnp.full((1, LANES), -1.0, f32) for entry in range(extra)]
        for index in range(LINE - 1):
            offset = jnp.zeros((1, 1), f32)
            for entry in range(extra):
                line = index * extra + entry
                at = before[line : line + 1, :] + offset + index * LENT
                targets[entry] = jnp.where(masks[index][entry : entry + 1, :] > 0.5, at, targets[entry])
                offset = offset + totals[line : line + 1, :]
            flag = jnp.maximum(flag, jnp.where(offset > LENT, 1.0, 0.0))
        sums = [jnp.zeros((LANES, 1), f32) for index in range(3)]
        for entry in range(extra):
            chosen = down.astype(f32) == targets[entry]
            values = (row[entry : entry + 1, :], slot[entry : entry + 1, :], trainer)
            for index, value in enumerate(values):
                picked = jnp.where(chosen, value + 1.0, 0.0)
                sums[index] += jnp.sum(picked, axis=1, keepdims=True)
        for index in range(3):
            tags = jnp.where(across == 3 * step + index, sums[index] - 1.0, tags)
        lent_rows.append(to_row(sums[0] - 1.0))
    lent_rows.append(jnp.full((8 - steps, LANES), -1.0, f32))
    plan_ref[...] = jnp.concatenate([asked] + lent_rows, axis=0).astype(jnp.int32)
    tag_ref[...] = tags
    flag_ref[...] = jnp.broadcast_to(flag, flag_ref.shape)
    fill_lent(tag_ref, 0, table_ref, lent_ref)


def first_direct_kernel(
    cap, plan_ref, table_ref, spot_ref, phase_ref, rows_ref, cosine_ref, sine_ref
):
    put_angles(spot_ref, phase_ref[...], cosine_ref, sine_ref)
    direct_kernel(0, cap, plan_ref, table_ref, rows_ref)


def direct_kernel(step, cap, plan_ref, table_ref, rows_ref):
    rows, width = table_ref.shape
    rows_ref[:, rows_ref.shape[1] - LANES :] = jnp.zeros((rows_ref.shape[0], LANES), jnp.bfloat16)
    for first in range(0, DIRECT, 2):
        last = min(first + 2, DIRECT)
        columns = [
            to_column(plan_ref[step * cap + slot : step * cap + slot + 1, :].astype(jnp.float32))
            for slot in range(first, last)
        ]
        chosen = one_hot_rows(jnp.concatenate(columns, axis=0).astype(jnp.int32), rows)
        rows_ref[first * LANES : last * LANES, :width] = dot(chosen, table_ref[...]).astype(
            jnp.bfloat16
        )


def pack_kernel(
    width,
    rows_ref,
    flag_ref,
    one_ref,
    two_ref,
    three_ref,
    packed_ref,
    tag_ref,
    lent_ref,
    full_ref,
    stack_ref,
    held_ref,
    copied,
):
    wide = rows_ref.shape[1]
    lent_ref[3 * LENT :, :] = jnp.zeros((LANES - 3 * LENT, wide), jnp.bfloat16)
    tags = []
    for index, ref in enumerate((one_ref, two_ref, three_ref)):
        lent_ref[index * LENT : (index + 1) * LENT, :] = ref[:, :wide]
        tag = ref[:, wide : wide + LANES].astype(jnp.float32)
        tags.append(tag[:, 0:1] * LANES + tag[:, 1:2])
    tags.append(jnp.full((LANES - 3 * LENT, 1), -1.0, jnp.float32))
    tag = to_row(jnp.concatenate(tags, axis=0)).astype(jnp.int32)
    tag_ref[...] = jnp.broadcast_to(tag, tag_ref.shape)
    for slot in range(DIRECT):
        block = slice(slot * LANES, (slot + 1) * LANES)
        lent = dot(one_hot_columns(tag, slot * LANES, LANES), lent_ref[...])
        full_ref[block, :] = (rows_ref[block, :].astype(jnp.float32) + lent).astype(jnp.bfloat16)
    spread(width, full_ref, stack_ref, flag_ref[0:1, :])
    copies = []

    def send(part, rows):
        copies.append(
            pltpu.make_async_copy(held_ref.at[rows, :], packed_ref.at[rows, :], copied.at[part])
        )
        copies[-1].start()

    fold(stack_ref, held_ref, send)
    for copy in copies:
        copy.wait()


def short_trainer_kernel(
    blocks,
    negatives,
    width,
    pulled_ref,
    spot_ref,
    cosine_ref,
    sine_ref,
    packed_ref,
    phase_grad_ref,
    rows_ref,
    stack_ref,
    held_ref,
    copied,
    *scratch,
):
    unfold(pulled_ref, stack_ref)
    gather_up(width, stack_ref, rows_ref)
    mark = read_mark(width, stack_ref)
    sending = pltpu.make_async_copy(held_ref, phase_grad_ref, copied)

    def put_phase_grad(value):
        last = iota((held_ref.shape[0], LANES), 1) == LANES - 1
        held_ref[:, held_ref.shape[1] - LANES :] = jnp.where(last, mark, 0.0)
        held_ref[:, : value.shape[1]] = value
        sending.start()

    trainer_core(
        blocks,
        negatives,
        width,
        rows_ref[...],
        spot_ref,
        cosine_ref,
        sine_ref,
        rows_ref,
        put_phase_grad,
        *scratch,
    )
    spread(width, rows_ref, stack_ref, None)
    fold(stack_ref, packed_ref)
    sending.wait()


def return_kernel(width, arrived_ref, tag_ref, rows_ref, lent_ref, stack_ref):
    unfold(arrived_ref, stack_ref)
    gather_up(width, stack_ref, rows_ref)
    tag = to_column(tag_ref[0:1, :].astype(jnp.float32)).astype(jnp.int32)
    chosen = one_hot_rows(tag, rows_ref.shape[0])
    lent_ref[...] = dot(chosen, rows_ref[...]).astype(jnp.bfloat16)


def sum_kernel(
    step, cap, width, plan_ref, other_plan_ref, rows_ref, arrived_ref, total_ref, stack_ref, other_ref
):
    unfold(arrived_ref, stack_ref)
    gather_up(width, stack_ref, other_ref)

    def asked(ref):
        rows = [ref[step * cap + slot : step * cap + slot + 1, :] for slot in range(DIRECT)]
        return jnp.concatenate(rows, axis=1)

    own, other = asked(plan_ref), asked(other_plan_ref)
    for first in range(0, total_ref.shape[0], 256):
        total_ref[first : first + 256, :] = dot(
            one_hot_columns(own, first, 256), rows_ref[...]
        ) + dot(one_hot_columns(other, first, 256), other_ref[...])


def short_update_kernel(
    step,
    cap,
    has_next,
    steps,
    plan_ref,
    other_plan_ref,
    total_ref,
    back_ref,
    other_back_ref,
    table_ref,
    state_ref,
    *rest,
):
    if has_next:
        tag_ref, new_table_ref, new_state_ref, lent_ref, first_ref, second_ref = rest
    else:
        mark_ref, other_mark_ref, new_table_ref, new_state_ref, flag_ref = rest[:5]
        first_ref, second_ref = rest[5:]
        mark = jnp.max(jnp.maximum(mark_ref[...], other_mark_ref[...]))
        flag_ref[0, 0] = (mark > 0.5).astype(jnp.int32)
    rows, width = table_ref.shape
    for ref, source in ((first_ref, back_ref), (second_ref, other_back_ref)):
        ref[: 3 * LENT, :] = source[...]
        ref[3 * LENT :, :] = jnp.zeros((LANES - 3 * LENT, ref.shape[1]), jnp.bfloat16)
    line = steps * cap + step
    own, other = plan_ref[line : line + 1, :], other_plan_ref[line : line + 1, :]
    size = 256
    for first in range(0, rows, size):
        lent = dot(one_hot_columns(own, first, size), first_ref[...]) + dot(
            one_hot_columns(other, first, size), second_ref[...]
        )
        gradient = (total_ref[first : first + size, :] + lent)[:, :width]
        values = table_ref[first : first + size, :].astype(jnp.float32)
        stepped = adagrad_block(gradient, first, values, state_ref, new_state_ref)
        if has_next:
            new_table_ref[first : first + size, :] = stepped
        else:
            turn_into(stepped, new_table_ref, first)
    if has_next:
        fill_lent(tag_ref, step + 1, new_table_ref, lent_ref)


def line_pairs(owners, far):
    return [
        (owner, owner // LINE * LINE + (owner % LINE + far) % LINE) for owner in range(owners)
    ]


def short_steps(
    entity_table,
    entity_state,
    relation_phase,
    relation_state,
    want_rows,
    want_count,
    head_slot,
    tail_slot,
    negative_slot,
    relation_ids,
):
    steps, owners, cap = want_rows.shape[1:]
    rows, width = entity_table.shape
    half = width // 2
    wide = -(-width // LANES) * LANES
    blocks, negatives = negative_slot.shape[2:]
    triples = head_slot.shape[2]
    relations = relation_phase.shape[0]
    direct = DIRECT * LANES
    packed_rows = PIECES * LANES
    packed = packed_width(width)
    half_wide = -(-(half + 1) // LANES) * LANES
    f32, i32, bf16 = jnp.float32, jnp.int32, jnp.bfloat16

    asked, *spots = call(
        functools.partial(route_kernel, rows),
        (shape((LANES, LANES), i32),) + (shape((8, LANES), i32),) * steps,
        "route",
        nbytes=1 << 20,
    )(
        jnp.transpose(want_rows[0], (0, 2, 1)),
        want_count[0],
        head_slot[0],
        tail_slot[0],
        negative_slot[0],
        relation_ids[0],
    )
    asked = lax.all_to_all(asked, "dom", split_axis=0, concat_axis=0, tiled=True)
    plan, tags, flag, lent = call(
        functools.partial(collect_kernel, steps, cap),
        (
            shape((steps * cap + 8, LANES), i32),
            shape((LANES, LANES), f32),
            shape((8, LANES), f32),
            shape((LANES, wide + LANES), bf16),
        ),
        "collect",
        nbytes=4 << 20,
    )(asked, entity_table)
    swap = [(0, 1), (1, 0)]
    other_plan = lax.ppermute(plan, "rep", swap)
    forth = [line_pairs(owners, far) for far in range(1, LINE)]
    back = [[(target, source) for source, target in pairs] for pairs in forth]

    table = entity_table
    state = entity_state.reshape(rows // LANES, LANES)
    phase = relation_phase
    phase_state = relation_state[:, None]
    relation = call(
        short_relation_kernel,
        (
            shape((relations, half), f32),
            shape((relations, 1), f32),
            shape((1, relations), f32),
            shape((8, LANES), f32),
            shape((triples, half), f32),
            shape((triples, half), f32),
        ),
        "relation",
        flops=6 * triples * relations * half,
        nbytes=4 * triples * half,
    )
    marks = ()
    for step in range(steps):
        has_next = step + 1 < steps
        loans = [
            lax.ppermute(lent[index * LENT : (index + 1) * LENT], "dom", forth[index])
            for index in range(LINE - 1)
        ]
        if step == 0:
            sent, cosine, sine = call(
                functools.partial(first_direct_kernel, cap),
                (shape((direct, wide), bf16),) + (shape((triples, half), f32),) * 2,
                "direct",
                flops=2 * direct * rows * width,
                nbytes=4 * rows * width,
            )(plan, table, spots[0], phase)
        else:
            sent = call(
                functools.partial(direct_kernel, step, cap),
                shape((direct, wide), bf16),
                "direct",
                flops=2 * direct * rows * width,
                nbytes=4 * rows * width,
            )(plan, table)
        offered, loan_tag = call(
            functools.partial(pack_kernel, width),
            (shape((packed_rows, packed), bf16), shape((8, LANES), i32)),
            "pack",
            nbytes=4 * rows * width,
            out_specs=(pl.BlockSpec(memory_space=pltpu.HBM), pl.BlockSpec(memory_space=pltpu.VMEM)),
            scratch_shapes=[
                pltpu.VMEM((LANES, wide), bf16),
                pltpu.VMEM((direct, wide), bf16),
                pltpu.VMEM((packed_rows, packed), bf16),
                pltpu.VMEM((packed_rows, packed), bf16),
                pltpu.SemaphoreType.DMA((LANES // PART,)),
            ],
        )(sent, flag, *loans)
        pulled = lax.all_to_all(
            offered.reshape(owners, PIECES, packed), "dom", split_axis=0, concat_axis=0, tiled=True
        ).reshape(packed_rows, packed)
        padded, phase_grad = call(
            functools.partial(short_trainer_kernel, blocks, negatives, width),
            (shape((packed_rows, packed), bf16), shape((triples, half_wide), f32)),
            "trainer",
            flops=2 * direct * (9 * triples) * width,
            nbytes=4 * rows * width,
            out_specs=(pl.BlockSpec(memory_space=pltpu.VMEM), pl.BlockSpec(memory_space=pltpu.HBM)),
            scratch_shapes=[
                pltpu.VMEM((direct, wide), bf16),
                pltpu.VMEM((packed_rows, packed), bf16),
                pltpu.VMEM((triples, half_wide), f32),
                pltpu.SemaphoreType.DMA,
            ]
            + trainer_scratch(triples, blocks * negatives, width, wide, wide),
        )(pulled, spots[step], cosine, sine)
        arrived = lax.all_to_all(
            padded.reshape(owners, PIECES, packed), "dom", split_axis=0, concat_axis=0, tiled=True
        ).reshape(packed_rows, packed)
        arrived_other = lax.ppermute(arrived, "rep", swap)
        got, dues = call(
            functools.partial(return_kernel, width),
            (shape((direct, wide), bf16), shape((LANES, wide), bf16)),
            "give_back",
            flops=2 * LANES * direct * wide,
            nbytes=4 * rows * width,
            scratch_shapes=[pltpu.VMEM((packed_rows, packed), bf16)],
        )(arrived, loan_tag)
        dues = [
            lax.ppermute(dues[index * LENT : (index + 1) * LENT], "dom", back[index])
            for index in range(LINE - 1)
        ]
        total = call(
            functools.partial(sum_kernel, step, cap, width),
            shape((rows, wide), f32),
            "sum",
            flops=4 * direct * rows * width,
            nbytes=8 * rows * width,
            scratch_shapes=[
                pltpu.VMEM((packed_rows, packed), bf16),
                pltpu.VMEM((direct, wide), bf16),
            ],
        )(plan, other_plan, got, arrived_other)
        dues, total, marks = lax.optimization_barrier((dues, total, marks))
        dues = jnp.concatenate(dues, axis=0)
        dues_other = lax.ppermute(dues, "rep", swap)
        phase, phase_state, state_row, seen, cosine, sine = relation(
            spots[step], phase_grad, phase, phase_state, spots[min(step + 1, steps - 1)]
        )
        dues_other, phase, cosine, sine = lax.optimization_barrier(
            (dues_other, phase, cosine, sine)
        )
        if step == 0:
            marks = (seen, lax.ppermute(seen, "rep", swap))
        outputs = [
            shape((rows, width) if has_next else (width, rows), bf16),
            shape((rows // LANES, LANES), f32),
        ]
        vmem = pl.BlockSpec(memory_space=pltpu.VMEM)
        out_specs = [vmem, vmem]
        operands = [plan, other_plan, total, dues, dues_other, table, state]
        if has_next:
            outputs.append(shape((LANES, wide + LANES), bf16))
            out_specs.append(vmem)
            operands.append(tags)
        else:
            outputs.append(shape((1, 1), i32))
            out_specs.append(pl.BlockSpec(memory_space=pltpu.SMEM))
            operands.extend(marks)
        results = call(
            functools.partial(short_update_kernel, step, cap, has_next, steps),
            tuple(outputs),
            "update",
            flops=4 * LANES * rows * width,
            nbytes=12 * rows * width,
            out_specs=tuple(out_specs),
            scratch_shapes=[pltpu.VMEM((LANES, wide), bf16)] * 2,
        )(*operands)
        table, state = results[:2]
        if has_next:
            lent = results[2]
    spoiled = results[2][0, 0] > 0
    return (table.T, state.reshape(rows), phase, state_row.reshape(relations)), spoiled


def local(*arrays):
    results, spoiled = short_steps(*arrays)
    return lax.cond(spoiled, lambda: full_steps(*arrays), lambda: results)


def solution(mesh):
    placed = (
        P("dom", None),
        P("dom"),
        P(("dom", "rep"), None),
        P(("dom", "rep")),
        P(("dom", "rep"), None, None, None),
        P(("dom", "rep"), None, None),
        P(("dom", "rep"), None, None),
        P(("dom", "rep"), None, None),
        P(("dom", "rep"), None, None, None),
        P(("dom", "rep"), None, None),
    )
    return jax.shard_map(
        local,
        mesh=mesh,
        in_specs=placed,
        out_specs=(P("dom", None), P("dom"), P(("dom", "rep"), None), P(("dom", "rep"))),
        check_vma=False,
    )
```

```python
import functools

import jax
import jax.numpy as jnp
from jax import lax
from jax.experimental import pallas as pl
from jax.experimental.pallas import tpu as pltpu
from jax.sharding import PartitionSpec as P

learn_rate = 0.5
smoothing = 0.25
epsilon = 1e-10
margin_rate = 0.26

LANES = 128
VMEM_LIMIT = 20 * 1024 * 1024


def slot_place(slot_ids, counts, slot_cap):
    running = jnp.cumsum(counts, dtype=jnp.int32)
    passed = (slot_ids[..., None] >= running).astype(jnp.int32)
    owner_index = jnp.sum(passed, axis=-1, dtype=jnp.int32)
    before = jnp.sum(passed * counts, axis=-1, dtype=jnp.int32)
    return owner_index * slot_cap + slot_ids - before


def call(kernel, out_shape, name, flops=0, nbytes=0, **kwargs):
    return pl.pallas_call(
        kernel,
        out_shape=out_shape,
        name=name,
        cost_estimate=pl.CostEstimate(flops=flops, bytes_accessed=nbytes, transcendentals=0),
        compiler_params=pltpu.CompilerParams(vmem_limit_bytes=VMEM_LIMIT),
        **kwargs,
    )


def diagonal():
    down = lax.broadcasted_iota(jnp.int32, (LANES, LANES), 0)
    across = lax.broadcasted_iota(jnp.int32, (LANES, LANES), 1)
    return down == across


def to_column(row):
    spread = jnp.broadcast_to(row, (LANES, LANES))
    return jnp.sum(jnp.where(diagonal(), spread, 0.0), axis=1, keepdims=True)


def to_row(column):
    spread = jnp.broadcast_to(column, (LANES, LANES))
    return jnp.sum(jnp.where(diagonal(), spread, 0.0), axis=0, keepdims=True)


def one_hot_rows(column, width):
    lanes = lax.broadcasted_iota(jnp.int32, (column.shape[0], width), 1)
    return jnp.where(lanes == column, 1.0, 0.0).astype(jnp.bfloat16)


def one_hot_columns(row, first, height):
    down = lax.broadcasted_iota(jnp.int32, (height, row.shape[1]), 0) + first
    return jnp.where(down == row, 1.0, 0.0).astype(jnp.bfloat16)


def dot(left, right):
    return jnp.dot(left, right, preferred_element_type=jnp.float32)


def turn_into(values, ref, first):
    rows, width = values.shape
    for start in range(0, width, 256):
        size = min(256, width - start)
        down = lax.broadcasted_iota(jnp.int32, (size, size), 0)
        across = lax.broadcasted_iota(jnp.int32, (size, size), 1)
        unit = jnp.where(down == across, 1.0, 0.0).astype(jnp.bfloat16)
        product = lax.dot_general(
            unit,
            values[:, start : start + size],
            (((1,), (1,)), ((), ())),
            preferred_element_type=jnp.float32,
        )
        ref[start : start + size, first : first + rows] = product.astype(jnp.bfloat16)


def split3(values):
    high = values.astype(jnp.bfloat16)
    rest = values - high.astype(jnp.float32)
    middle = rest.astype(jnp.bfloat16)
    low = (rest - middle.astype(jnp.float32)).astype(jnp.bfloat16)
    return high, middle, low


def gather_rows(wanted_ref, table_ref, offered_ref):
    table_rows = table_ref.shape[0]
    blocks = wanted_ref.shape[0]
    step = 2
    for start in range(0, blocks, step):
        columns = [
            to_column(wanted_ref[block : block + 1, :].astype(jnp.float32)).astype(jnp.int32)
            for block in range(start, start + step)
        ]
        chosen = one_hot_rows(jnp.concatenate(columns, axis=0), table_rows)
        rows = pl.ds(start * LANES, step * LANES)
        offered_ref[rows, :] = dot(chosen, table_ref[...]).astype(jnp.bfloat16)


def offer_kernel(wanted_ref, table_ref, offered_ref):
    gather_rows(wanted_ref, table_ref, offered_ref)


def own_sum_kernel(asked_ref, arrived_ref, total_ref):
    rows = total_ref.shape[0]
    step = 256
    asked = asked_ref[...]
    for first in range(0, rows, step):
        chosen = one_hot_columns(asked, first, step)
        total_ref[first : first + step, :] = dot(chosen, arrived_ref[...])


def adagrad_block(gradient, first, values, state_ref, new_state_ref):
    step, width = gradient.shape
    mean_square = jnp.sum(gradient * gradient, axis=1, keepdims=True) / width
    fresh = []
    for block in range(first // LANES, (first + step) // LANES):
        old = to_column(state_ref[block : block + 1, :])
        at = block * LANES - first
        new = old + mean_square[at : at + LANES, :]
        new_state_ref[block : block + 1, :] = to_row(new)
        fresh.append(new)
    rate = learn_rate / (jnp.sqrt(jnp.concatenate(fresh, axis=0)) + epsilon)
    return (values - gradient * rate).astype(jnp.bfloat16)


def update_kernel(
    has_next,
    asked_ref,
    arrived_ref,
    own_ref,
    table_ref,
    state_ref,
    *rest,
):
    if has_next:
        wanted_ref, new_table_ref, new_state_ref, offered_ref = rest
    else:
        new_table_ref, new_state_ref = rest
    rows, width = table_ref.shape
    step = 256
    asked = asked_ref[...]
    for first in range(0, rows, step):
        chosen = one_hot_columns(asked, first, step)
        gradient = own_ref[first : first + step, :] + dot(chosen, arrived_ref[...])
        gradient = gradient[:, :width]
        values = table_ref[first : first + step, :].astype(jnp.float32)
        stepped = adagrad_block(gradient, first, values, state_ref, new_state_ref)
        if has_next:
            new_table_ref[first : first + step, :] = stepped
        else:
            turn_into(stepped, new_table_ref, first)
    if has_next:
        gather_rows(wanted_ref, new_table_ref, offered_ref)


def sigmoid(value):
    tail = jnp.exp(-jnp.abs(value))
    return jnp.where(value >= 0, 1.0, tail) / (1.0 + tail)


def trainer_core(
    blocks,
    negatives,
    width,
    pulled,
    spot_ref,
    cosine_ref,
    sine_ref,
    padded_ref,
    put_phase_grad,
    read_ref,
    rot_real_ref,
    rot_imag_ref,
    tail_real_ref,
    tail_imag_ref,
    neg_real_ref,
    neg_imag_ref,
    rot_real_grad_ref,
    rot_imag_grad_ref,
    tail_real_grad_ref,
    tail_imag_grad_ref,
    neg_real_grad_ref,
    neg_imag_grad_ref,
    grads_ref,
):
    slots = pulled.shape[0]
    half = width // 2
    triples = cosine_ref.shape[0]
    neg_rows = blocks * negatives
    margin = margin_rate * half

    places = [
        to_column(spot_ref[index : index + 1, :].astype(jnp.float32)).astype(jnp.int32)
        for index in range(3)
    ]
    places[2] = places[2][:neg_rows]
    read_ref[...] = dot(one_hot_rows(jnp.concatenate(places, axis=0), slots), pulled)
    head_ref = read_ref.at[:triples, :]
    tail_ref = read_ref.at[triples : 2 * triples, :]
    negative_ref = read_ref.at[2 * triples :, :]

    cosine = cosine_ref[...]
    sine = sine_ref[...]
    head_real = head_ref[:, :half]
    head_imag = head_ref[:, half:width]
    rot_real_ref[...] = head_real * cosine - head_imag * sine
    rot_imag_ref[...] = head_real * sine + head_imag * cosine
    tail_real_ref[...] = tail_ref[:, :half]
    tail_imag_ref[...] = tail_ref[:, half:width]
    neg_real_ref[...] = negative_ref[:, :half]
    neg_imag_ref[...] = negative_ref[:, half:width]
    neg_real_grad_ref[...] = jnp.zeros_like(neg_real_grad_ref)
    neg_imag_grad_ref[...] = jnp.zeros_like(neg_imag_grad_ref)

    group = 8
    per_block = triples // blocks

    def pair(real, imag, other_real, other_imag):
        diff_real = real - other_real
        diff_imag = imag - other_imag
        square = diff_real * diff_real + diff_imag * diff_imag + smoothing
        inverse = lax.rsqrt(square)
        distance = jnp.sum(square * inverse, axis=1, keepdims=True)
        return distance, inverse, diff_real, diff_imag

    def chunk(index, carry):
        rows = pl.ds(pl.multiple_of(index * group, group), group)
        first = (index * group) // per_block * negatives
        real = rot_real_ref[rows, :]
        imag = rot_imag_ref[rows, :]
        distance, inverse, diff_real, diff_imag = pair(
            real, imag, tail_real_ref[rows, :], tail_imag_ref[rows, :]
        )
        scale = 0.25 * sigmoid(0.25 * distance - margin) * inverse
        total_real = scale * diff_real
        total_imag = scale * diff_imag
        tail_real_grad_ref[rows, :] = -total_real
        tail_imag_grad_ref[rows, :] = -total_imag
        for n in range(negatives):
            distance, inverse, diff_real, diff_imag = pair(
                real,
                imag,
                neg_real_ref[pl.ds(first + n, 1), :],
                neg_imag_ref[pl.ds(first + n, 1), :],
            )
            scale = (-0.25 / negatives) * sigmoid(margin - 0.25 * distance) * inverse
            part_real = scale * diff_real
            part_imag = scale * diff_imag
            total_real += part_real
            total_imag += part_imag
            neg_real_grad_ref[first + n] -= part_real
            neg_imag_grad_ref[first + n] -= part_imag
        rot_real_grad_ref[rows, :] = total_real
        rot_imag_grad_ref[rows, :] = total_imag
        return carry

    lax.fori_loop(0, triples // group, chunk, 0, unroll=4)

    real_grad = rot_real_grad_ref[...]
    imag_grad = rot_imag_grad_ref[...]
    put_phase_grad(imag_grad * rot_real_ref[...] - real_grad * rot_imag_ref[...])

    grads_ref[:, width:] = jnp.zeros_like(grads_ref[:, width:])

    def put(first, rows, real, imag):
        value = jnp.concatenate([real, imag], axis=1)
        grads_ref[first : first + rows, :width] = value.astype(jnp.bfloat16)

    put(
        0,
        triples,
        real_grad * cosine + imag_grad * sine,
        imag_grad * cosine - real_grad * sine,
    )
    put(triples, triples, tail_real_grad_ref[...], tail_imag_grad_ref[...])
    partial = neg_rows * group
    put(
        2 * triples,
        partial,
        neg_real_grad_ref[...].reshape(partial, half),
        neg_imag_grad_ref[...].reshape(partial, half),
    )
    spots = [spot_ref[index : index + 1, :] for index in range(2)]
    column = to_column(spot_ref[2:3, :].astype(jnp.float32))
    for first in range(0, partial, LANES):
        down = lax.broadcasted_iota(jnp.int32, (LANES, LANES), 0)
        across = lax.broadcasted_iota(jnp.int32, (LANES, LANES), 1) + first
        repeated = jnp.where(down == across // group, column, 0.0)
        spots.append(jnp.sum(repeated, axis=0, keepdims=True).astype(jnp.int32))
    for first in range(0, slots, 256):
        step = min(256, slots - first)
        chosen = [one_hot_columns(spot, first, step) for spot in spots]
        chosen = jnp.concatenate(chosen, axis=1)
        padded_ref[first : first + step, :] = dot(chosen, grads_ref[...]).astype(jnp.bfloat16)


def trainer_kernel(
    blocks,
    negatives,
    pulled_ref,
    spot_ref,
    cosine_ref,
    sine_ref,
    padded_ref,
    phase_grad_ref,
    *scratch,
):
    def put_phase_grad(value):
        phase_grad_ref[...] = value

    trainer_core(
        blocks,
        negatives,
        pulled_ref.shape[1],
        pulled_ref[...],
        spot_ref,
        cosine_ref,
        sine_ref,
        padded_ref,
        put_phase_grad,
        *scratch,
    )


def trainer_scratch(triples, neg_rows, width, wide, read_width):
    half = width // 2
    return (
        [pltpu.VMEM((2 * triples + neg_rows, read_width), jnp.float32)]
        + [pltpu.VMEM((triples, half), jnp.float32)] * 4
        + [pltpu.VMEM((neg_rows, half), jnp.float32)] * 2
        + [pltpu.VMEM((triples, half), jnp.float32)] * 4
        + [pltpu.VMEM((neg_rows, 8, half), jnp.float32)] * 2
        + [pltpu.VMEM((2 * triples + 8 * neg_rows, wide), jnp.bfloat16)]
    )


def relation_kernel(spot_ref, grad_ref, phase_ref, state_ref, new_phase_ref, new_state_ref):
    relations, half = phase_ref.shape
    chosen = one_hot_columns(spot_ref[3:4, :], 0, relations)
    high, middle, low = split3(grad_ref[...])
    gradient = dot(chosen, high) + dot(chosen, middle) + dot(chosen, low)
    gradient = gradient[:, :half]
    mean_square = jnp.sum(gradient * gradient, axis=1, keepdims=True) / half
    fresh = state_ref[...] + mean_square
    new_state_ref[...] = fresh
    new_phase_ref[...] = phase_ref[...] - learn_rate * gradient / (jnp.sqrt(fresh) + epsilon)


def put_angles(spot_ref, phase, cosine_ref, sine_ref):
    column = to_column(spot_ref[3:4, :].astype(jnp.float32)).astype(jnp.int32)
    chosen = one_hot_rows(column, phase.shape[0])
    for ref, values in ((cosine_ref, jnp.cos(phase)), (sine_ref, jnp.sin(phase))):
        high, middle, low = split3(values)
        ref[...] = dot(chosen, high) + dot(chosen, middle) + dot(chosen, low)


def short_relation_kernel(
    has_next,
    spot_ref,
    grad_ref,
    phase_ref,
    state_ref,
    next_spot_ref,
    new_phase_ref,
    new_state_ref,
    *rest,
):
    old_ref, column_ref = rest[-2:]
    relations = phase_ref.shape[0]
    spare = jnp.zeros((1, LANES - relations), jnp.float32)
    row = jnp.concatenate([state_ref[...], spare], axis=1)
    old_ref[...] = to_column(row)[:relations]
    relation_kernel(spot_ref, grad_ref, phase_ref, old_ref, new_phase_ref, column_ref)
    spare = jnp.zeros((LANES - relations, 1), jnp.float32)
    row = to_row(jnp.concatenate([column_ref[...], spare], axis=0))
    new_state_ref[...] = row[:, :relations]
    if has_next:
        flag_ref, cosine_ref, sine_ref = rest[:3]
        last = grad_ref.shape[1] - 1
        mark = jnp.max(grad_ref[:, last : last + 1], axis=0, keepdims=True)
        flag_ref[...] = jnp.broadcast_to(mark, flag_ref.shape)
        put_angles(next_spot_ref, new_phase_ref[...], cosine_ref, sine_ref)


def shape(dims, dtype):
    return jax.ShapeDtypeStruct(dims, dtype)


def full_steps(
    entity_table,
    entity_state,
    relation_phase,
    relation_state,
    want_rows,
    want_count,
    head_slot,
    tail_slot,
    negative_slot,
    relation_ids,
):
    steps, owners, cap = want_rows.shape[1:]
    rows, width = entity_table.shape
    half = width // 2
    wide = -(-width // LANES) * LANES
    blocks, negatives = negative_slot.shape[2:]
    triples = head_slot.shape[2]
    slots = owners * cap
    relations = relation_phase.shape[0]
    table_bytes = 2 * rows * width

    asked = jnp.transpose(want_rows[0], (1, 0, 2)).reshape(owners, steps * cap)
    asked = lax.all_to_all(asked, "dom", split_axis=0, concat_axis=0, tiled=True)
    asked = jnp.transpose(asked.reshape(owners, steps, cap), (1, 0, 2))
    asked = asked.reshape(steps, slots // LANES, LANES)
    asked_other = lax.ppermute(asked, "rep", [(0, 1), (1, 0)])
    ask_row = asked.reshape(steps, 1, slots)
    ask_row_other = asked_other.reshape(steps, 1, slots)

    spots = []
    for step in range(steps):
        counts = want_count[0, step]
        neg = slot_place(negative_slot[0, step].reshape(-1), counts, cap)
        spare = jnp.full((triples - neg.shape[0],), -1, jnp.int32)
        spots.append(
            jnp.stack(
                [
                    slot_place(head_slot[0, step], counts, cap),
                    slot_place(tail_slot[0, step], counts, cap),
                    jnp.concatenate([neg, spare]),
                    relation_ids[0, step],
                ]
            )
        )

    table = entity_table
    state = entity_state.reshape(rows // LANES, LANES)
    phase = relation_phase
    phase_state = relation_state[:, None]
    offered = call(
        offer_kernel,
        shape((slots, width), jnp.bfloat16),
        "offer",
        flops=2 * slots * rows * width,
        nbytes=2 * table_bytes,
    )(asked[0], table)
    f32 = jnp.float32
    for step in range(steps):
        pulled = lax.all_to_all(
            offered.reshape(owners, cap, width), "dom", split_axis=0, concat_axis=0, tiled=True
        ).reshape(slots, width)
        relation_span = jnp.arange(relations, dtype=jnp.int32)
        selector = (relation_ids[0, step][:, None] == relation_span[None, :]).astype(f32)
        phase_rows = jnp.dot(selector, phase, precision=lax.Precision.HIGHEST)
        padded, phase_grad = call(
            functools.partial(trainer_kernel, blocks, negatives),
            (shape((slots, wide), jnp.bfloat16), shape((triples, half), f32)),
            "trainer",
            flops=2 * slots * (9 * triples) * width,
            nbytes=2 * table_bytes,
            scratch_shapes=trainer_scratch(triples, blocks * negatives, width, wide, width),
        )(pulled, spots[step], jnp.cos(phase_rows), jnp.sin(phase_rows))
        arrived = lax.all_to_all(
            padded.reshape(owners, cap, wide), "dom", split_axis=0, concat_axis=0, tiled=True
        ).reshape(slots, wide)
        phase, phase_state = call(
            relation_kernel,
            (shape((relations, half), f32), shape((relations, 1), f32)),
            "relation",
            flops=6 * triples * relations * half,
            nbytes=4 * triples * half,
        )(spots[step], phase_grad, phase, phase_state)
        arrived_other = lax.ppermute(arrived, "rep", [(0, 1), (1, 0)])
        own = call(
            own_sum_kernel,
            shape((rows, wide), f32),
            "own_sum",
            flops=2 * slots * rows * width,
            nbytes=3 * table_bytes,
        )(ask_row[step], arrived)
        has_next = step + 1 < steps
        outputs = [
            shape((rows, width) if has_next else (width, rows), jnp.bfloat16),
            shape((rows // LANES, LANES), f32),
        ]
        operands = [ask_row_other[step], arrived_other, own, table, state]
        if has_next:
            outputs.append(shape((slots, width), jnp.bfloat16))
            operands.append(asked[step + 1])
        results = call(
            functools.partial(update_kernel, has_next),
            tuple(outputs),
            "update",
            flops=2 * slots * rows * width * (1 + has_next),
            nbytes=6 * table_bytes,
        )(*operands)
        table, state = results[:2]
        if has_next:
            offered = results[2]
    return (table.T, state.reshape(rows), phase, phase_state[:, 0])


DIRECT = 5
LINE = 4
LENT = 32
PIECES = 8


def iota(dims, axis):
    return lax.broadcasted_iota(jnp.int32, dims, axis)


def as_bf16(mask):
    return jnp.where(mask, 1.0, 0.0).astype(jnp.bfloat16)


def places(width):
    full, rest = divmod(width, LANES)
    whole = [divmod(index, full) for index in range(DIRECT * full)]
    share = LANES // rest
    groups = [list(range(first, min(first + share, DIRECT))) for first in range(0, DIRECT, share)]
    return full, rest, whole, groups


def packed_width(width):
    full, rest, whole, groups = places(width)
    return -(-(len(whole) + len(groups)) // PIECES) * LANES


def stack_tile(position):
    tile, piece = divmod(position, PIECES)
    return slice(piece * LANES, (piece + 1) * LANES), slice(tile * LANES, (tile + 1) * LANES)


def spread(width, rows_ref, stack_ref, mark):
    full, rest, whole, groups = places(width)
    for position, (row, tile) in enumerate(whole):
        stack_ref[stack_tile(position)] = rows_ref[
            row * LANES : (row + 1) * LANES, tile * LANES : (tile + 1) * LANES
        ]
    last = len(whole) + len(groups) - 1
    for index, group in enumerate(groups):
        position = len(whole) + index
        total = jnp.zeros((LANES, LANES), jnp.float32)
        for row in group:
            tail = rows_ref[row * LANES : (row + 1) * LANES, full * LANES : (full + 1) * LANES]
            tail = tail.astype(jnp.float32)
            shift = rest * (row - group[0])
            total = total + (pltpu.roll(tail, shift, 1) if shift else tail)
        if position == last and mark is not None:
            total = jnp.where(iota((LANES, LANES), 1) == LANES - 1, mark, total)
        stack_ref[stack_tile(position)] = total.astype(jnp.bfloat16)
    for position in range(last + 1, stack_ref.shape[1] // LANES * PIECES):
        stack_ref[stack_tile(position)] = jnp.zeros((LANES, LANES), jnp.bfloat16)


def gather_up(width, stack_ref, rows_ref):
    full, rest, whole, groups = places(width)
    for position, (row, tile) in enumerate(whole):
        rows_ref[row * LANES : (row + 1) * LANES, tile * LANES : (tile + 1) * LANES] = stack_ref[
            stack_tile(position)
        ]
    for index, group in enumerate(groups):
        tails = stack_ref[stack_tile(len(whole) + index)].astype(jnp.float32)
        for row in group:
            shift = rest * (row - group[0])
            tail = pltpu.roll(tails, LANES - shift, 1) if shift else tails
            tail = jnp.where(iota((LANES, LANES), 1) < rest, tail, 0.0)
            rows_ref[row * LANES : (row + 1) * LANES, full * LANES : (full + 1) * LANES] = (
                tail.astype(jnp.bfloat16)
            )


def read_mark(width, stack_ref):
    full, rest, whole, groups = places(width)
    tile = stack_ref[stack_tile(len(whole) + len(groups) - 1)].astype(jnp.float32)
    tile = jnp.where(iota((LANES, LANES), 1) == LANES - 1, tile, 0.0)
    return jnp.max(jnp.max(tile, axis=1, keepdims=True), axis=0, keepdims=True)


PART = LANES // 4


def fold(stack_ref, packed_ref):
    size = PART * PIECES
    down, across = iota((size, size), 0), iota((size, size), 1)
    turn = as_bf16(across == (down % PIECES) * PART + down // PIECES)
    for part in range(LANES // PART):
        pieces = [
            stack_ref[piece * LANES + part * PART : piece * LANES + (part + 1) * PART, :]
            for piece in range(PIECES)
        ]
        packed_ref[part * size : (part + 1) * size, :] = dot(
            turn, jnp.concatenate(pieces, axis=0)
        ).astype(jnp.bfloat16)


def unfold(packed_ref, stack_ref):
    size = PART * PIECES
    down, across = iota((size, size), 0), iota((size, size), 1)
    turn = as_bf16(across == (down % PART) * PIECES + down // PART)
    for part in range(LANES // PART):
        block = dot(turn, packed_ref[part * size : (part + 1) * size, :]).astype(jnp.bfloat16)
        for piece in range(PIECES):
            stack_ref[piece * LANES + part * PART : piece * LANES + (part + 1) * PART, :] = block[
                piece * PART : (piece + 1) * PART, :
            ]


def route_kernel(
    rows,
    want_ref,
    count_ref,
    head_ref,
    tail_ref,
    neg_ref,
    relation_ref,
    ask_ref,
    *spot_refs,
):
    steps, cap, owners = want_ref.shape
    f32 = jnp.float32
    down, across = iota((LANES, LANES), 0), iota((LANES, LANES), 1)
    same_line = down // LINE == across // LINE
    line_mat = as_bf16(same_line)
    line_before = as_bf16(same_line & (down < across))
    upto = as_bf16(down <= across)
    owner = iota((1, LANES), 1).astype(f32)
    y_at = iota((1, LANES), 1) % LINE
    slot_number = iota((cap, LANES), 0).astype(f32)
    none = jnp.zeros((cap - 3, LANES), f32)
    asks = []
    for step in range(steps):
        count = count_ref[step : step + 1, :].astype(f32)
        ends = dot(jnp.broadcast_to(count, (cap, LANES)).astype(jnp.bfloat16), upto)[0:1, :]
        begins = ends - count
        seen = jnp.zeros((cap, LANES), f32)
        uses = []
        slots = [to_column(ref[step : step + 1, :].astype(f32)) for ref in (head_ref, tail_ref)]
        slots.append(jnp.full((LANES, 1), -1.0, f32))
        blocks, negatives = neg_ref.shape[1:]
        for block in range(blocks):
            row = neg_ref[step, block : block + 1, :].astype(f32) + 1.0
            here = iota((LANES, negatives), 0) - block * negatives == iota((LANES, negatives), 1)
            slots[2] += jnp.sum(jnp.where(here, row, 0.0), axis=1, keepdims=True)
        for slot in slots:
            owned = (slot >= begins) & (slot < ends)
            within = slot - jnp.sum(jnp.where(owned, begins, 0.0), axis=1, keepdims=True)
            seen += dot(as_bf16(slot_number == to_row(within)), as_bf16(owned))
            uses.append((owned, within))
        used = seen > 0.5
        ranks = [jnp.zeros((1, LANES), f32)]
        for slot in range(cap):
            ranks.append(ranks[-1] + jnp.where(used[slot : slot + 1, :], 1.0, 0.0))
        total = ranks.pop()
        rank = jnp.concatenate(ranks, axis=0)
        over = jnp.maximum(total - DIRECT, 0.0)
        free = DIRECT - jnp.minimum(total, DIRECT)
        pair = jnp.concatenate([over, free, total, none], axis=0).astype(jnp.bfloat16)
        before = dot(pair, line_before)
        whole = dot(pair, line_mat)
        lost = jnp.max(
            jnp.where(whole[0:1, :] > whole[1:2, :], 1.0, 0.0), axis=1, keepdims=True
        )
        turn = before[0:1, :] + rank - DIRECT
        side = jnp.concatenate([before[1:2, :], free, total, none], axis=0).astype(jnp.bfloat16)
        at_slot = rank
        at_owner = jnp.broadcast_to(owner, (cap, LANES))
        code = jnp.zeros((cap, LANES), f32)
        for far in range(1, LINE):
            mover = as_bf16(same_line & (down % LINE == (across + far) % LINE))
            moved = dot(side, mover)
            hit = used & (rank >= DIRECT) & (turn >= moved[0:1, :])
            hit = hit & (turn < moved[0:1, :] + moved[1:2, :])
            slot = moved[2:3, :] + turn - moved[0:1, :]
            other = owner + ((y_at + far) % LINE - y_at).astype(f32)
            at_slot = jnp.where(hit, slot, at_slot)
            at_owner = jnp.where(hit, other, at_owner)
            code = jnp.where(hit, rows * (far * cap + slot), code)
        want = want_ref[step].astype(f32)
        for place in range(cap):
            chosen = used & (rank == place)
            value = want + 1.0 if place < DIRECT else want + code + 1.0
            row = jnp.sum(jnp.where(chosen, value, 0.0), axis=0, keepdims=True) - 1.0
            if place == cap - 1:
                row = jnp.where(lost > 0.5, -2.0, row)
            asks.append(row)
        where_at = at_slot * owners + at_owner
        spots = []
        for owned, within in uses:
            table = jnp.zeros((LANES, LANES), f32)
            for slot in range(cap):
                table = jnp.where(within == slot, where_at[slot : slot + 1, :], table)
            found = jnp.sum(jnp.where(owned, table, 0.0), axis=1, keepdims=True)
            found = jnp.where(within < 0, -1.0, found)
            spots.append(to_row(found))
        spots.append(relation_ref[step : step + 1, :].astype(f32))
        spots.append(jnp.zeros((8 - len(spots), LANES), f32))
        spot_refs[step][...] = jnp.concatenate(spots, axis=0).astype(jnp.int32)
    asks.append(jnp.zeros((LANES - len(asks), LANES), f32))
    ask_ref[...] = jnp.transpose(jnp.concatenate(asks, axis=0)).astype(jnp.int32)


def fill_lent(tag_ref, step, table_ref, lent_ref):
    rows, width = table_ref.shape
    wide = lent_ref.shape[1] - LANES
    row, slot, trainer = (tag_ref[:, 3 * step + index : 3 * step + index + 1] for index in range(3))
    chosen = one_hot_rows(row.astype(jnp.int32), rows)
    lent_ref[:, wide - LANES : wide] = jnp.zeros((LANES, LANES), jnp.bfloat16)
    lent_ref[:, :width] = dot(chosen, table_ref[...]).astype(jnp.bfloat16)
    lanes = iota((LANES, LANES), 1)
    tags = jnp.where(lanes == 0, slot, jnp.where(lanes == 1, trainer, 0.0))
    lent_ref[:, wide:] = tags.astype(jnp.bfloat16)


def collect_kernel(
    steps, cap, ask_ref, table_ref, plan_ref, tag_ref, flag_ref, lent_ref
):
    rows = table_ref.shape[0]
    f32 = jnp.float32
    asked = jnp.transpose(ask_ref[...].astype(f32))[: steps * cap, :]
    down, across = iota((LANES, LANES), 0), iota((LANES, LANES), 1)
    earlier = as_bf16(down < across)
    trainer = iota((1, LANES), 1).astype(f32)
    flag = jnp.zeros((1, 1), f32)
    tags = jnp.full((LANES, LANES), -1.0, f32)
    lent_rows = []
    extra = cap - DIRECT
    for step in range(steps):
        codes = asked[step * cap + DIRECT : (step + 1) * cap, :].astype(jnp.int32)
        flag = jnp.maximum(
            flag,
            jnp.max(
                jnp.where(codes[extra - 1 : extra, :] == -2, 1.0, 0.0), axis=1, keepdims=True
            ),
        )
        valid = codes >= 0
        row = jnp.where(valid, codes % rows, 0).astype(f32)
        place = jnp.where(valid, codes // rows, 0)
        far = place // cap
        slot = (place % cap).astype(f32)
        masks = [
            jnp.where(valid & (far == distance), 1.0, 0.0) for distance in range(1, LINE)
        ]
        stacked = jnp.concatenate(
            masks + [jnp.zeros((16 - extra * (LINE - 1), LANES), f32)], axis=0
        )
        before = dot(stacked.astype(jnp.bfloat16), earlier)
        totals = jnp.sum(stacked, axis=1, keepdims=True)
        targets = [jnp.full((1, LANES), -1.0, f32) for entry in range(extra)]
        for index in range(LINE - 1):
            offset = jnp.zeros((1, 1), f32)
            for entry in range(extra):
                line = index * extra + entry
                at = before[line : line + 1, :] + offset + index * LENT
                targets[entry] = jnp.where(masks[index][entry : entry + 1, :] > 0.5, at, targets[entry])
                offset = offset + totals[line : line + 1, :]
            flag = jnp.maximum(flag, jnp.where(offset > LENT, 1.0, 0.0))
        sums = [jnp.zeros((LANES, 1), f32) for index in range(3)]
        for entry in range(extra):
            chosen = down.astype(f32) == targets[entry]
            values = (row[entry : entry + 1, :], slot[entry : entry + 1, :], trainer)
            for index, value in enumerate(values):
                picked = jnp.where(chosen, value + 1.0, 0.0)
                sums[index] += jnp.sum(picked, axis=1, keepdims=True)
        for index in range(3):
            tags = jnp.where(across == 3 * step + index, sums[index] - 1.0, tags)
        lent_rows.append(to_row(sums[0] - 1.0))
    lent_rows.append(jnp.full((8 - steps, LANES), -1.0, f32))
    plan_ref[...] = jnp.concatenate([asked] + lent_rows, axis=0).astype(jnp.int32)
    tag_ref[...] = tags
    flag_ref[...] = jnp.broadcast_to(flag, flag_ref.shape)
    fill_lent(tag_ref, 0, table_ref, lent_ref)


def first_direct_kernel(
    cap, plan_ref, table_ref, spot_ref, phase_ref, rows_ref, cosine_ref, sine_ref
):
    put_angles(spot_ref, phase_ref[...], cosine_ref, sine_ref)
    direct_kernel(0, cap, plan_ref, table_ref, rows_ref)


def direct_kernel(step, cap, plan_ref, table_ref, rows_ref):
    rows, width = table_ref.shape
    rows_ref[:, rows_ref.shape[1] - LANES :] = jnp.zeros((rows_ref.shape[0], LANES), jnp.bfloat16)
    for first in range(0, DIRECT, 2):
        last = min(first + 2, DIRECT)
        columns = [
            to_column(plan_ref[step * cap + slot : step * cap + slot + 1, :].astype(jnp.float32))
            for slot in range(first, last)
        ]
        chosen = one_hot_rows(jnp.concatenate(columns, axis=0).astype(jnp.int32), rows)
        rows_ref[first * LANES : last * LANES, :width] = dot(chosen, table_ref[...]).astype(
            jnp.bfloat16
        )


def pack_kernel(
    width,
    rows_ref,
    flag_ref,
    one_ref,
    two_ref,
    three_ref,
    packed_ref,
    tag_ref,
    lent_ref,
    full_ref,
    stack_ref,
):
    wide = rows_ref.shape[1]
    lent_ref[3 * LENT :, :] = jnp.zeros((LANES - 3 * LENT, wide), jnp.bfloat16)
    tags = []
    for index, ref in enumerate((one_ref, two_ref, three_ref)):
        lent_ref[index * LENT : (index + 1) * LENT, :] = ref[:, :wide]
        tag = ref[:, wide : wide + LANES].astype(jnp.float32)
        tags.append(tag[:, 0:1] * LANES + tag[:, 1:2])
    tags.append(jnp.full((LANES - 3 * LENT, 1), -1.0, jnp.float32))
    tag = to_row(jnp.concatenate(tags, axis=0)).astype(jnp.int32)
    tag_ref[...] = jnp.broadcast_to(tag, tag_ref.shape)
    for slot in range(DIRECT):
        block = slice(slot * LANES, (slot + 1) * LANES)
        lent = dot(one_hot_columns(tag, slot * LANES, LANES), lent_ref[...])
        full_ref[block, :] = (rows_ref[block, :].astype(jnp.float32) + lent).astype(jnp.bfloat16)
    spread(width, full_ref, stack_ref, flag_ref[0:1, :])
    fold(stack_ref, packed_ref)


def short_trainer_kernel(
    blocks,
    negatives,
    width,
    pulled_ref,
    spot_ref,
    cosine_ref,
    sine_ref,
    packed_ref,
    phase_grad_ref,
    rows_ref,
    stack_ref,
    held_ref,
    copied,
    *scratch,
):
    unfold(pulled_ref, stack_ref)
    gather_up(width, stack_ref, rows_ref)
    mark = read_mark(width, stack_ref)
    sending = pltpu.make_async_copy(held_ref, phase_grad_ref, copied)

    def put_phase_grad(value):
        last = iota((held_ref.shape[0], LANES), 1) == LANES - 1
        held_ref[:, held_ref.shape[1] - LANES :] = jnp.where(last, mark, 0.0)
        held_ref[:, : value.shape[1]] = value
        sending.start()

    trainer_core(
        blocks,
        negatives,
        width,
        rows_ref[...],
        spot_ref,
        cosine_ref,
        sine_ref,
        rows_ref,
        put_phase_grad,
        *scratch,
    )
    spread(width, rows_ref, stack_ref, None)
    fold(stack_ref, packed_ref)
    sending.wait()


def return_kernel(width, arrived_ref, tag_ref, rows_ref, lent_ref, stack_ref):
    unfold(arrived_ref, stack_ref)
    gather_up(width, stack_ref, rows_ref)
    tag = to_column(tag_ref[0:1, :].astype(jnp.float32)).astype(jnp.int32)
    chosen = one_hot_rows(tag, rows_ref.shape[0])
    lent_ref[...] = dot(chosen, rows_ref[...]).astype(jnp.bfloat16)


def sum_kernel(
    step, cap, width, plan_ref, other_plan_ref, rows_ref, arrived_ref, total_ref, stack_ref, other_ref
):
    unfold(arrived_ref, stack_ref)
    gather_up(width, stack_ref, other_ref)

    def asked(ref):
        rows = [ref[step * cap + slot : step * cap + slot + 1, :] for slot in range(DIRECT)]
        return jnp.concatenate(rows, axis=1)

    own, other = asked(plan_ref), asked(other_plan_ref)
    for first in range(0, total_ref.shape[0], 256):
        total_ref[first : first + 256, :] = dot(
            one_hot_columns(own, first, 256), rows_ref[...]
        ) + dot(one_hot_columns(other, first, 256), other_ref[...])


def short_update_kernel(
    step,
    cap,
    has_next,
    steps,
    plan_ref,
    other_plan_ref,
    total_ref,
    back_ref,
    other_back_ref,
    table_ref,
    state_ref,
    *rest,
):
    if has_next:
        tag_ref, new_table_ref, new_state_ref, lent_ref, first_ref, second_ref = rest
    else:
        mark_ref, other_mark_ref, new_table_ref, new_state_ref, flag_ref = rest[:5]
        first_ref, second_ref = rest[5:]
        mark = jnp.max(jnp.maximum(mark_ref[...], other_mark_ref[...]))
        flag_ref[0, 0] = (mark > 0.5).astype(jnp.int32)
    rows, width = table_ref.shape
    for ref, source in ((first_ref, back_ref), (second_ref, other_back_ref)):
        ref[: 3 * LENT, :] = source[...]
        ref[3 * LENT :, :] = jnp.zeros((LANES - 3 * LENT, ref.shape[1]), jnp.bfloat16)
    line = steps * cap + step
    own, other = plan_ref[line : line + 1, :], other_plan_ref[line : line + 1, :]
    size = 256
    for first in range(0, rows, size):
        lent = dot(one_hot_columns(own, first, size), first_ref[...]) + dot(
            one_hot_columns(other, first, size), second_ref[...]
        )
        gradient = (total_ref[first : first + size, :] + lent)[:, :width]
        values = table_ref[first : first + size, :].astype(jnp.float32)
        stepped = adagrad_block(gradient, first, values, state_ref, new_state_ref)
        if has_next:
            new_table_ref[first : first + size, :] = stepped
        else:
            turn_into(stepped, new_table_ref, first)
    if has_next:
        fill_lent(tag_ref, step + 1, new_table_ref, lent_ref)


def line_pairs(owners, far):
    return [
        (owner, owner // LINE * LINE + (owner % LINE + far) % LINE) for owner in range(owners)
    ]


def short_steps(
    entity_table,
    entity_state,
    relation_phase,
    relation_state,
    want_rows,
    want_count,
    head_slot,
    tail_slot,
    negative_slot,
    relation_ids,
):
    steps, owners, cap = want_rows.shape[1:]
    rows, width = entity_table.shape
    half = width // 2
    wide = -(-width // LANES) * LANES
    blocks, negatives = negative_slot.shape[2:]
    triples = head_slot.shape[2]
    relations = relation_phase.shape[0]
    direct = DIRECT * LANES
    packed_rows = PIECES * LANES
    packed = packed_width(width)
    half_wide = -(-(half + 1) // LANES) * LANES
    f32, i32, bf16 = jnp.float32, jnp.int32, jnp.bfloat16

    asked, *spots = call(
        functools.partial(route_kernel, rows),
        (shape((LANES, LANES), i32),) + (shape((8, LANES), i32),) * steps,
        "route",
        nbytes=1 << 20,
    )(
        jnp.transpose(want_rows[0], (0, 2, 1)),
        want_count[0],
        head_slot[0],
        tail_slot[0],
        negative_slot[0],
        relation_ids[0],
    )
    asked = lax.all_to_all(asked, "dom", split_axis=0, concat_axis=0, tiled=True)
    plan, tags, flag, lent = call(
        functools.partial(collect_kernel, steps, cap),
        (
            shape((steps * cap + 8, LANES), i32),
            shape((LANES, LANES), f32),
            shape((8, LANES), f32),
            shape((LANES, wide + LANES), bf16),
        ),
        "collect",
        nbytes=4 << 20,
    )(asked, entity_table)
    swap = [(0, 1), (1, 0)]
    other_plan = lax.ppermute(plan, "rep", swap)
    forth = [line_pairs(owners, far) for far in range(1, LINE)]
    back = [[(target, source) for source, target in pairs] for pairs in forth]

    table = entity_table
    state = entity_state.reshape(rows // LANES, LANES)
    phase = relation_phase
    phase_state = relation_state[None, :]
    marks = ()
    for step in range(steps):
        has_next = step + 1 < steps
        loans = [
            lax.ppermute(lent[index * LENT : (index + 1) * LENT], "dom", forth[index])
            for index in range(LINE - 1)
        ]
        if step == 0:
            sent, cosine, sine = call(
                functools.partial(first_direct_kernel, cap),
                (shape((direct, wide), bf16),) + (shape((triples, half), f32),) * 2,
                "direct",
                flops=2 * direct * rows * width,
                nbytes=4 * rows * width,
            )(plan, table, spots[0], phase)
        else:
            sent = call(
                functools.partial(direct_kernel, step, cap),
                shape((direct, wide), bf16),
                "direct",
                flops=2 * direct * rows * width,
                nbytes=4 * rows * width,
            )(plan, table)
        offered, loan_tag = call(
            functools.partial(pack_kernel, width),
            (shape((packed_rows, packed), bf16), shape((8, LANES), i32)),
            "pack",
            nbytes=4 * rows * width,
            scratch_shapes=[
                pltpu.VMEM((LANES, wide), bf16),
                pltpu.VMEM((direct, wide), bf16),
                pltpu.VMEM((packed_rows, packed), bf16),
            ],
        )(sent, flag, *loans)
        pulled = lax.all_to_all(
            offered.reshape(owners, PIECES, packed), "dom", split_axis=0, concat_axis=0, tiled=True
        ).reshape(packed_rows, packed)
        padded, phase_grad = call(
            functools.partial(short_trainer_kernel, blocks, negatives, width),
            (shape((packed_rows, packed), bf16), shape((triples, half_wide), f32)),
            "trainer",
            flops=2 * direct * (9 * triples) * width,
            nbytes=4 * rows * width,
            out_specs=(pl.BlockSpec(memory_space=pltpu.VMEM), pl.BlockSpec(memory_space=pltpu.HBM)),
            scratch_shapes=[
                pltpu.VMEM((direct, wide), bf16),
                pltpu.VMEM((packed_rows, packed), bf16),
                pltpu.VMEM((triples, half_wide), f32),
                pltpu.SemaphoreType.DMA,
            ]
            + trainer_scratch(triples, blocks * negatives, width, wide, wide),
        )(pulled, spots[step], cosine, sine)
        arrived = lax.all_to_all(
            padded.reshape(owners, PIECES, packed), "dom", split_axis=0, concat_axis=0, tiled=True
        ).reshape(packed_rows, packed)
        arrived_other = lax.ppermute(arrived, "rep", swap)
        got, dues = call(
            functools.partial(return_kernel, width),
            (shape((direct, wide), bf16), shape((LANES, wide), bf16)),
            "give_back",
            flops=2 * LANES * direct * wide,
            nbytes=4 * rows * width,
            scratch_shapes=[pltpu.VMEM((packed_rows, packed), bf16)],
        )(arrived, loan_tag)
        dues = [
            lax.ppermute(dues[index * LENT : (index + 1) * LENT], "dom", back[index])
            for index in range(LINE - 1)
        ]
        total = call(
            functools.partial(sum_kernel, step, cap, width),
            shape((rows, wide), f32),
            "sum",
            flops=4 * direct * rows * width,
            nbytes=8 * rows * width,
            scratch_shapes=[
                pltpu.VMEM((packed_rows, packed), bf16),
                pltpu.VMEM((direct, wide), bf16),
            ],
        )(plan, other_plan, got, arrived_other)
        dues, total, marks = lax.optimization_barrier((dues, total, marks))
        dues = jnp.concatenate(dues, axis=0)
        dues_other = lax.ppermute(dues, "rep", swap)
        extras = (shape((8, LANES), f32),) + (shape((triples, half), f32),) * 2
        phase, phase_state, *extras = call(
            functools.partial(short_relation_kernel, has_next),
            (shape((relations, half), f32), shape((1, relations), f32)) + extras * has_next,
            "relation",
            flops=6 * triples * relations * half,
            nbytes=4 * triples * half,
            scratch_shapes=[pltpu.VMEM((relations, 1), f32)] * 2,
        )(spots[step], phase_grad, phase, phase_state, spots[min(step + 1, steps - 1)])
        dues_other, phase, extras = lax.optimization_barrier((dues_other, phase, extras))
        if has_next:
            seen, cosine, sine = extras
        if step == 0:
            marks = (seen, lax.ppermute(seen, "rep", swap))
        outputs = [
            shape((rows, width) if has_next else (width, rows), bf16),
            shape((rows // LANES, LANES), f32),
        ]
        vmem = pl.BlockSpec(memory_space=pltpu.VMEM)
        out_specs = [vmem, vmem]
        operands = [plan, other_plan, total, dues, dues_other, table, state]
        if has_next:
            outputs.append(shape((LANES, wide + LANES), bf16))
            out_specs.append(vmem)
            operands.append(tags)
        else:
            outputs.append(shape((1, 1), i32))
            out_specs.append(pl.BlockSpec(memory_space=pltpu.SMEM))
            operands.extend(marks)
        results = call(
            functools.partial(short_update_kernel, step, cap, has_next, steps),
            tuple(outputs),
            "update",
            flops=4 * LANES * rows * width,
            nbytes=12 * rows * width,
            out_specs=tuple(out_specs),
            scratch_shapes=[pltpu.VMEM((LANES, wide), bf16)] * 2,
        )(*operands)
        table, state = results[:2]
        if has_next:
            lent = results[2]
    spoiled = results[2][0, 0] > 0
    return (table.T, state.reshape(rows), phase, phase_state.reshape(relations)), spoiled


def local(*arrays):
    results, spoiled = short_steps(*arrays)
    return lax.cond(spoiled, lambda: full_steps(*arrays), lambda: results)


def solution(mesh):
    placed = (
        P("dom", None),
        P("dom"),
        P(("dom", "rep"), None),
        P(("dom", "rep")),
        P(("dom", "rep"), None, None, None),
        P(("dom", "rep"), None, None),
        P(("dom", "rep"), None, None),
        P(("dom", "rep"), None, None),
        P(("dom", "rep"), None, None, None),
        P(("dom", "rep"), None, None),
    )
    return jax.shard_map(
        local,
        mesh=mesh,
        in_specs=placed,
        out_specs=(P("dom", None), P("dom"), P(("dom", "rep"), None), P(("dom", "rep"))),
        check_vma=False,
    )
```

```python
import functools

import jax
import jax.numpy as jnp
from jax import lax
from jax.experimental import pallas as pl
from jax.experimental.pallas import tpu as pltpu
from jax.sharding import PartitionSpec as P

learn_rate = 0.5
smoothing = 0.25
epsilon = 1e-10
margin_rate = 0.26

LANES = 128
VMEM_LIMIT = 20 * 1024 * 1024


def slot_place(slot_ids, counts, slot_cap):
    running = jnp.cumsum(counts, dtype=jnp.int32)
    passed = (slot_ids[..., None] >= running).astype(jnp.int32)
    owner_index = jnp.sum(passed, axis=-1, dtype=jnp.int32)
    before = jnp.sum(passed * counts, axis=-1, dtype=jnp.int32)
    return owner_index * slot_cap + slot_ids - before


def call(kernel, out_shape, name, flops=0, nbytes=0, **kwargs):
    return pl.pallas_call(
        kernel,
        out_shape=out_shape,
        name=name,
        cost_estimate=pl.CostEstimate(flops=flops, bytes_accessed=nbytes, transcendentals=0),
        compiler_params=pltpu.CompilerParams(vmem_limit_bytes=VMEM_LIMIT),
        **kwargs,
    )


def diagonal():
    down = lax.broadcasted_iota(jnp.int32, (LANES, LANES), 0)
    across = lax.broadcasted_iota(jnp.int32, (LANES, LANES), 1)
    return down == across


def to_column(row):
    spread = jnp.broadcast_to(row, (LANES, LANES))
    return jnp.sum(jnp.where(diagonal(), spread, 0.0), axis=1, keepdims=True)


def to_row(column):
    spread = jnp.broadcast_to(column, (LANES, LANES))
    return jnp.sum(jnp.where(diagonal(), spread, 0.0), axis=0, keepdims=True)


def one_hot_rows(column, width):
    lanes = lax.broadcasted_iota(jnp.int32, (column.shape[0], width), 1)
    return jnp.where(lanes == column, 1.0, 0.0).astype(jnp.bfloat16)


def one_hot_columns(row, first, height):
    down = lax.broadcasted_iota(jnp.int32, (height, row.shape[1]), 0) + first
    return jnp.where(down == row, 1.0, 0.0).astype(jnp.bfloat16)


def dot(left, right):
    return jnp.dot(left, right, preferred_element_type=jnp.float32)


def turn_into(values, ref, first):
    rows, width = values.shape
    for start in range(0, width, 256):
        size = min(256, width - start)
        down = lax.broadcasted_iota(jnp.int32, (size, size), 0)
        across = lax.broadcasted_iota(jnp.int32, (size, size), 1)
        unit = jnp.where(down == across, 1.0, 0.0).astype(jnp.bfloat16)
        product = lax.dot_general(
            unit,
            values[:, start : start + size],
            (((1,), (1,)), ((), ())),
            preferred_element_type=jnp.float32,
        )
        ref[start : start + size, first : first + rows] = product.astype(jnp.bfloat16)


def split3(values):
    high = values.astype(jnp.bfloat16)
    rest = values - high.astype(jnp.float32)
    middle = rest.astype(jnp.bfloat16)
    low = (rest - middle.astype(jnp.float32)).astype(jnp.bfloat16)
    return high, middle, low


def gather_rows(wanted_ref, table_ref, offered_ref):
    table_rows = table_ref.shape[0]
    blocks = wanted_ref.shape[0]
    step = 2
    for start in range(0, blocks, step):
        columns = [
            to_column(wanted_ref[block : block + 1, :].astype(jnp.float32)).astype(jnp.int32)
            for block in range(start, start + step)
        ]
        chosen = one_hot_rows(jnp.concatenate(columns, axis=0), table_rows)
        rows = pl.ds(start * LANES, step * LANES)
        offered_ref[rows, :] = dot(chosen, table_ref[...]).astype(jnp.bfloat16)


def offer_kernel(wanted_ref, table_ref, offered_ref):
    gather_rows(wanted_ref, table_ref, offered_ref)


def own_sum_kernel(asked_ref, arrived_ref, total_ref):
    rows = total_ref.shape[0]
    step = 256
    asked = asked_ref[...]
    for first in range(0, rows, step):
        chosen = one_hot_columns(asked, first, step)
        total_ref[first : first + step, :] = dot(chosen, arrived_ref[...])


def adagrad_block(gradient, first, values, state_ref, new_state_ref):
    step, width = gradient.shape
    mean_square = jnp.sum(gradient * gradient, axis=1, keepdims=True) / width
    fresh = []
    for block in range(first // LANES, (first + step) // LANES):
        old = to_column(state_ref[block : block + 1, :])
        at = block * LANES - first
        new = old + mean_square[at : at + LANES, :]
        new_state_ref[block : block + 1, :] = to_row(new)
        fresh.append(new)
    rate = learn_rate / (jnp.sqrt(jnp.concatenate(fresh, axis=0)) + epsilon)
    return (values - gradient * rate).astype(jnp.bfloat16)


def update_kernel(
    has_next,
    asked_ref,
    arrived_ref,
    own_ref,
    table_ref,
    state_ref,
    *rest,
):
    if has_next:
        wanted_ref, new_table_ref, new_state_ref, offered_ref = rest
    else:
        new_table_ref, new_state_ref = rest
    rows, width = table_ref.shape
    step = 256
    asked = asked_ref[...]
    for first in range(0, rows, step):
        chosen = one_hot_columns(asked, first, step)
        gradient = own_ref[first : first + step, :] + dot(chosen, arrived_ref[...])
        gradient = gradient[:, :width]
        values = table_ref[first : first + step, :].astype(jnp.float32)
        stepped = adagrad_block(gradient, first, values, state_ref, new_state_ref)
        if has_next:
            new_table_ref[first : first + step, :] = stepped
        else:
            turn_into(stepped, new_table_ref, first)
    if has_next:
        gather_rows(wanted_ref, new_table_ref, offered_ref)


def sigmoid(value):
    tail = jnp.exp(-jnp.abs(value))
    return jnp.where(value >= 0, 1.0, tail) / (1.0 + tail)


def trainer_core(
    blocks,
    negatives,
    width,
    pulled,
    spot_ref,
    cosine_ref,
    sine_ref,
    padded_ref,
    put_phase_grad,
    read_ref,
    rot_real_ref,
    rot_imag_ref,
    tail_real_ref,
    tail_imag_ref,
    neg_real_ref,
    neg_imag_ref,
    rot_real_grad_ref,
    rot_imag_grad_ref,
    tail_real_grad_ref,
    tail_imag_grad_ref,
    neg_real_grad_ref,
    neg_imag_grad_ref,
    grads_ref,
):
    slots = pulled.shape[0]
    half = width // 2
    triples = cosine_ref.shape[0]
    neg_rows = blocks * negatives
    margin = margin_rate * half

    places = [
        to_column(spot_ref[index : index + 1, :].astype(jnp.float32)).astype(jnp.int32)
        for index in range(3)
    ]
    places[2] = places[2][:neg_rows]
    read_ref[...] = dot(one_hot_rows(jnp.concatenate(places, axis=0), slots), pulled)
    head_ref = read_ref.at[:triples, :]
    tail_ref = read_ref.at[triples : 2 * triples, :]
    negative_ref = read_ref.at[2 * triples :, :]

    cosine = cosine_ref[...]
    sine = sine_ref[...]
    head_real = head_ref[:, :half]
    head_imag = head_ref[:, half:width]
    rot_real_ref[...] = head_real * cosine - head_imag * sine
    rot_imag_ref[...] = head_real * sine + head_imag * cosine
    tail_real_ref[...] = tail_ref[:, :half]
    tail_imag_ref[...] = tail_ref[:, half:width]
    neg_real_ref[...] = negative_ref[:, :half]
    neg_imag_ref[...] = negative_ref[:, half:width]
    neg_real_grad_ref[...] = jnp.zeros_like(neg_real_grad_ref)
    neg_imag_grad_ref[...] = jnp.zeros_like(neg_imag_grad_ref)

    group = 8
    per_block = triples // blocks

    def pair(real, imag, other_real, other_imag):
        diff_real = real - other_real
        diff_imag = imag - other_imag
        square = diff_real * diff_real + diff_imag * diff_imag + smoothing
        inverse = lax.rsqrt(square)
        distance = jnp.sum(square * inverse, axis=1, keepdims=True)
        return distance, inverse, diff_real, diff_imag

    def chunk(index, carry):
        rows = pl.ds(pl.multiple_of(index * group, group), group)
        first = (index * group) // per_block * negatives
        real = rot_real_ref[rows, :]
        imag = rot_imag_ref[rows, :]
        distance, inverse, diff_real, diff_imag = pair(
            real, imag, tail_real_ref[rows, :], tail_imag_ref[rows, :]
        )
        scale = 0.25 * sigmoid(0.25 * distance - margin) * inverse
        total_real = scale * diff_real
        total_imag = scale * diff_imag
        tail_real_grad_ref[rows, :] = -total_real
        tail_imag_grad_ref[rows, :] = -total_imag
        for n in range(negatives):
            distance, inverse, diff_real, diff_imag = pair(
                real,
                imag,
                neg_real_ref[pl.ds(first + n, 1), :],
                neg_imag_ref[pl.ds(first + n, 1), :],
            )
            scale = (-0.25 / negatives) * sigmoid(margin - 0.25 * distance) * inverse
            part_real = scale * diff_real
            part_imag = scale * diff_imag
            total_real += part_real
            total_imag += part_imag
            neg_real_grad_ref[first + n] -= part_real
            neg_imag_grad_ref[first + n] -= part_imag
        rot_real_grad_ref[rows, :] = total_real
        rot_imag_grad_ref[rows, :] = total_imag
        return carry

    lax.fori_loop(0, triples // group, chunk, 0, unroll=4)

    real_grad = rot_real_grad_ref[...]
    imag_grad = rot_imag_grad_ref[...]
    put_phase_grad(imag_grad * rot_real_ref[...] - real_grad * rot_imag_ref[...])

    grads_ref[:, width:] = jnp.zeros_like(grads_ref[:, width:])

    def put(first, rows, real, imag):
        value = jnp.concatenate([real, imag], axis=1)
        grads_ref[first : first + rows, :width] = value.astype(jnp.bfloat16)

    put(
        0,
        triples,
        real_grad * cosine + imag_grad * sine,
        imag_grad * cosine - real_grad * sine,
    )
    put(triples, triples, tail_real_grad_ref[...], tail_imag_grad_ref[...])
    partial = neg_rows * group
    put(
        2 * triples,
        partial,
        neg_real_grad_ref[...].reshape(partial, half),
        neg_imag_grad_ref[...].reshape(partial, half),
    )
    spots = [spot_ref[index : index + 1, :] for index in range(2)]
    column = to_column(spot_ref[2:3, :].astype(jnp.float32))
    for first in range(0, partial, LANES):
        down = lax.broadcasted_iota(jnp.int32, (LANES, LANES), 0)
        across = lax.broadcasted_iota(jnp.int32, (LANES, LANES), 1) + first
        repeated = jnp.where(down == across // group, column, 0.0)
        spots.append(jnp.sum(repeated, axis=0, keepdims=True).astype(jnp.int32))
    for first in range(0, slots, 256):
        step = min(256, slots - first)
        chosen = [one_hot_columns(spot, first, step) for spot in spots]
        chosen = jnp.concatenate(chosen, axis=1)
        padded_ref[first : first + step, :] = dot(chosen, grads_ref[...]).astype(jnp.bfloat16)


def trainer_kernel(
    blocks,
    negatives,
    pulled_ref,
    spot_ref,
    cosine_ref,
    sine_ref,
    padded_ref,
    phase_grad_ref,
    *scratch,
):
    def put_phase_grad(value):
        phase_grad_ref[...] = value

    trainer_core(
        blocks,
        negatives,
        pulled_ref.shape[1],
        pulled_ref[...],
        spot_ref,
        cosine_ref,
        sine_ref,
        padded_ref,
        put_phase_grad,
        *scratch,
    )


def trainer_scratch(triples, neg_rows, width, wide, read_width):
    half = width // 2
    return (
        [pltpu.VMEM((2 * triples + neg_rows, read_width), jnp.float32)]
        + [pltpu.VMEM((triples, half), jnp.float32)] * 4
        + [pltpu.VMEM((neg_rows, half), jnp.float32)] * 2
        + [pltpu.VMEM((triples, half), jnp.float32)] * 4
        + [pltpu.VMEM((neg_rows, 8, half), jnp.float32)] * 2
        + [pltpu.VMEM((2 * triples + 8 * neg_rows, wide), jnp.bfloat16)]
    )


def relation_kernel(spot_ref, grad_ref, phase_ref, state_ref, new_phase_ref, new_state_ref):
    relations, half = phase_ref.shape
    chosen = one_hot_columns(spot_ref[3:4, :], 0, relations)
    high, middle, low = split3(grad_ref[...])
    gradient = dot(chosen, high) + dot(chosen, middle) + dot(chosen, low)
    gradient = gradient[:, :half]
    mean_square = jnp.sum(gradient * gradient, axis=1, keepdims=True) / half
    fresh = state_ref[...] + mean_square
    new_state_ref[...] = fresh
    new_phase_ref[...] = phase_ref[...] - learn_rate * gradient / (jnp.sqrt(fresh) + epsilon)


def put_angles(spot_ref, phase, cosine_ref, sine_ref):
    column = to_column(spot_ref[3:4, :].astype(jnp.float32)).astype(jnp.int32)
    chosen = one_hot_rows(column, phase.shape[0])
    for ref, values in ((cosine_ref, jnp.cos(phase)), (sine_ref, jnp.sin(phase))):
        high, middle, low = split3(values)
        ref[...] = dot(chosen, high) + dot(chosen, middle) + dot(chosen, low)


def short_relation_kernel(
    has_next,
    spot_ref,
    grad_ref,
    phase_ref,
    state_ref,
    next_spot_ref,
    new_phase_ref,
    new_state_ref,
    *rest,
):
    old_ref, column_ref = rest[-2:]
    relations = phase_ref.shape[0]
    spare = jnp.zeros((1, LANES - relations), jnp.float32)
    row = jnp.concatenate([state_ref[...], spare], axis=1)
    old_ref[...] = to_column(row)[:relations]
    relation_kernel(spot_ref, grad_ref, phase_ref, old_ref, new_phase_ref, column_ref)
    spare = jnp.zeros((LANES - relations, 1), jnp.float32)
    row = to_row(jnp.concatenate([column_ref[...], spare], axis=0))
    new_state_ref[...] = row[:, :relations]
    if has_next:
        flag_ref, cosine_ref, sine_ref = rest[:3]
        last = grad_ref.shape[1] - 1
        mark = jnp.max(grad_ref[:, last : last + 1], axis=0, keepdims=True)
        flag_ref[...] = jnp.broadcast_to(mark, flag_ref.shape)
        put_angles(next_spot_ref, new_phase_ref[...], cosine_ref, sine_ref)


def shape(dims, dtype):
    return jax.ShapeDtypeStruct(dims, dtype)


def full_steps(
    entity_table,
    entity_state,
    relation_phase,
    relation_state,
    want_rows,
    want_count,
    head_slot,
    tail_slot,
    negative_slot,
    relation_ids,
):
    steps, owners, cap = want_rows.shape[1:]
    rows, width = entity_table.shape
    half = width // 2
    wide = -(-width // LANES) * LANES
    blocks, negatives = negative_slot.shape[2:]
    triples = head_slot.shape[2]
    slots = owners * cap
    relations = relation_phase.shape[0]
    table_bytes = 2 * rows * width

    asked = jnp.transpose(want_rows[0], (1, 0, 2)).reshape(owners, steps * cap)
    asked = lax.all_to_all(asked, "dom", split_axis=0, concat_axis=0, tiled=True)
    asked = jnp.transpose(asked.reshape(owners, steps, cap), (1, 0, 2))
    asked = asked.reshape(steps, slots // LANES, LANES)
    asked_other = lax.ppermute(asked, "rep", [(0, 1), (1, 0)])
    ask_row = asked.reshape(steps, 1, slots)
    ask_row_other = asked_other.reshape(steps, 1, slots)

    spots = []
    for step in range(steps):
        counts = want_count[0, step]
        neg = slot_place(negative_slot[0, step].reshape(-1), counts, cap)
        spare = jnp.full((triples - neg.shape[0],), -1, jnp.int32)
        spots.append(
            jnp.stack(
                [
                    slot_place(head_slot[0, step], counts, cap),
                    slot_place(tail_slot[0, step], counts, cap),
                    jnp.concatenate([neg, spare]),
                    relation_ids[0, step],
                ]
            )
        )

    table = entity_table
    state = entity_state.reshape(rows // LANES, LANES)
    phase = relation_phase
    phase_state = relation_state[:, None]
    offered = call(
        offer_kernel,
        shape((slots, width), jnp.bfloat16),
        "offer",
        flops=2 * slots * rows * width,
        nbytes=2 * table_bytes,
    )(asked[0], table)
    f32 = jnp.float32
    for step in range(steps):
        pulled = lax.all_to_all(
            offered.reshape(owners, cap, width), "dom", split_axis=0, concat_axis=0, tiled=True
        ).reshape(slots, width)
        relation_span = jnp.arange(relations, dtype=jnp.int32)
        selector = (relation_ids[0, step][:, None] == relation_span[None, :]).astype(f32)
        phase_rows = jnp.dot(selector, phase, precision=lax.Precision.HIGHEST)
        padded, phase_grad = call(
            functools.partial(trainer_kernel, blocks, negatives),
            (shape((slots, wide), jnp.bfloat16), shape((triples, half), f32)),
            "trainer",
            flops=2 * slots * (9 * triples) * width,
            nbytes=2 * table_bytes,
            scratch_shapes=trainer_scratch(triples, blocks * negatives, width, wide, width),
        )(pulled, spots[step], jnp.cos(phase_rows), jnp.sin(phase_rows))
        arrived = lax.all_to_all(
            padded.reshape(owners, cap, wide), "dom", split_axis=0, concat_axis=0, tiled=True
        ).reshape(slots, wide)
        phase, phase_state = call(
            relation_kernel,
            (shape((relations, half), f32), shape((relations, 1), f32)),
            "relation",
            flops=6 * triples * relations * half,
            nbytes=4 * triples * half,
        )(spots[step], phase_grad, phase, phase_state)
        arrived_other = lax.ppermute(arrived, "rep", [(0, 1), (1, 0)])
        own = call(
            own_sum_kernel,
            shape((rows, wide), f32),
            "own_sum",
            flops=2 * slots * rows * width,
            nbytes=3 * table_bytes,
        )(ask_row[step], arrived)
        has_next = step + 1 < steps
        outputs = [
            shape((rows, width) if has_next else (width, rows), jnp.bfloat16),
            shape((rows // LANES, LANES), f32),
        ]
        operands = [ask_row_other[step], arrived_other, own, table, state]
        if has_next:
            outputs.append(shape((slots, width), jnp.bfloat16))
            operands.append(asked[step + 1])
        results = call(
            functools.partial(update_kernel, has_next),
            tuple(outputs),
            "update",
            flops=2 * slots * rows * width * (1 + has_next),
            nbytes=6 * table_bytes,
        )(*operands)
        table, state = results[:2]
        if has_next:
            offered = results[2]
    return (table.T, state.reshape(rows), phase, phase_state[:, 0])


DIRECT = 5
LINE = 4
LENT = 16
PIECES = 8


def iota(dims, axis):
    return lax.broadcasted_iota(jnp.int32, dims, axis)


def as_bf16(mask):
    return jnp.where(mask, 1.0, 0.0).astype(jnp.bfloat16)


def places(width):
    full, rest = divmod(width, LANES)
    whole = [divmod(index, full) for index in range(DIRECT * full)]
    share = LANES // rest
    groups = [list(range(first, min(first + share, DIRECT))) for first in range(0, DIRECT, share)]
    return full, rest, whole, groups


def packed_width(width):
    full, rest, whole, groups = places(width)
    return -(-(len(whole) + len(groups)) // PIECES) * LANES


def stack_tile(position):
    tile, piece = divmod(position, PIECES)
    return slice(piece * LANES, (piece + 1) * LANES), slice(tile * LANES, (tile + 1) * LANES)


def spread(width, rows_ref, stack_ref, mark):
    full, rest, whole, groups = places(width)
    for position, (row, tile) in enumerate(whole):
        stack_ref[stack_tile(position)] = rows_ref[
            row * LANES : (row + 1) * LANES, tile * LANES : (tile + 1) * LANES
        ]
    last = len(whole) + len(groups) - 1
    for index, group in enumerate(groups):
        position = len(whole) + index
        total = jnp.zeros((LANES, LANES), jnp.float32)
        for row in group:
            tail = rows_ref[row * LANES : (row + 1) * LANES, full * LANES : (full + 1) * LANES]
            tail = tail.astype(jnp.float32)
            shift = rest * (row - group[0])
            total = total + (pltpu.roll(tail, shift, 1) if shift else tail)
        if position == last and mark is not None:
            total = jnp.where(iota((LANES, LANES), 1) == LANES - 1, mark, total)
        stack_ref[stack_tile(position)] = total.astype(jnp.bfloat16)
    for position in range(last + 1, stack_ref.shape[1] // LANES * PIECES):
        stack_ref[stack_tile(position)] = jnp.zeros((LANES, LANES), jnp.bfloat16)


def gather_up(width, stack_ref, rows_ref):
    full, rest, whole, groups = places(width)
    for position, (row, tile) in enumerate(whole):
        rows_ref[row * LANES : (row + 1) * LANES, tile * LANES : (tile + 1) * LANES] = stack_ref[
            stack_tile(position)
        ]
    for index, group in enumerate(groups):
        tails = stack_ref[stack_tile(len(whole) + index)].astype(jnp.float32)
        for row in group:
            shift = rest * (row - group[0])
            tail = pltpu.roll(tails, LANES - shift, 1) if shift else tails
            tail = jnp.where(iota((LANES, LANES), 1) < rest, tail, 0.0)
            rows_ref[row * LANES : (row + 1) * LANES, full * LANES : (full + 1) * LANES] = (
                tail.astype(jnp.bfloat16)
            )


def read_mark(width, stack_ref):
    full, rest, whole, groups = places(width)
    tile = stack_ref[stack_tile(len(whole) + len(groups) - 1)].astype(jnp.float32)
    tile = jnp.where(iota((LANES, LANES), 1) == LANES - 1, tile, 0.0)
    return jnp.max(jnp.max(tile, axis=1, keepdims=True), axis=0, keepdims=True)


PART = LANES // 4


def fold(stack_ref, packed_ref):
    size = PART * PIECES
    down, across = iota((size, size), 0), iota((size, size), 1)
    turn = as_bf16(across == (down % PIECES) * PART + down // PIECES)
    for part in range(LANES // PART):
        pieces = [
            stack_ref[piece * LANES + part * PART : piece * LANES + (part + 1) * PART, :]
            for piece in range(PIECES)
        ]
        packed_ref[part * size : (part + 1) * size, :] = dot(
            turn, jnp.concatenate(pieces, axis=0)
        ).astype(jnp.bfloat16)


def unfold(packed_ref, stack_ref):
    size = PART * PIECES
    down, across = iota((size, size), 0), iota((size, size), 1)
    turn = as_bf16(across == (down % PART) * PIECES + down // PART)
    for part in range(LANES // PART):
        block = dot(turn, packed_ref[part * size : (part + 1) * size, :]).astype(jnp.bfloat16)
        for piece in range(PIECES):
            stack_ref[piece * LANES + part * PART : piece * LANES + (part + 1) * PART, :] = block[
                piece * PART : (piece + 1) * PART, :
            ]


def route_kernel(
    rows,
    want_ref,
    count_ref,
    head_ref,
    tail_ref,
    neg_ref,
    relation_ref,
    ask_ref,
    *spot_refs,
):
    steps, cap, owners = want_ref.shape
    f32 = jnp.float32
    down, across = iota((LANES, LANES), 0), iota((LANES, LANES), 1)
    same_line = down // LINE == across // LINE
    line_mat = as_bf16(same_line)
    trainer = lax.axis_index("dom")
    ahead = (down + trainer) % LINE < (across + trainer) % LINE
    behind = (down + trainer) % LINE > (across + trainer) % LINE
    ahead = jnp.where((trainer // LINE) % 2 == 0, ahead.astype(jnp.int32), behind.astype(jnp.int32))
    line_before = as_bf16(same_line & (ahead > 0))
    upto = as_bf16(down <= across)
    owner = iota((1, LANES), 1).astype(f32)
    y_at = iota((1, LANES), 1) % LINE
    slot_number = iota((cap, LANES), 0).astype(f32)
    none = jnp.zeros((cap - 3, LANES), f32)
    asks = []
    for step in range(steps):
        count = count_ref[step : step + 1, :].astype(f32)
        ends = dot(jnp.broadcast_to(count, (cap, LANES)).astype(jnp.bfloat16), upto)[0:1, :]
        begins = ends - count
        seen = jnp.zeros((cap, LANES), f32)
        uses = []
        slots = [to_column(ref[step : step + 1, :].astype(f32)) for ref in (head_ref, tail_ref)]
        slots.append(jnp.full((LANES, 1), -1.0, f32))
        blocks, negatives = neg_ref.shape[1:]
        for block in range(blocks):
            row = neg_ref[step, block : block + 1, :].astype(f32) + 1.0
            here = iota((LANES, negatives), 0) - block * negatives == iota((LANES, negatives), 1)
            slots[2] += jnp.sum(jnp.where(here, row, 0.0), axis=1, keepdims=True)
        for slot in slots:
            owned = (slot >= begins) & (slot < ends)
            within = slot - jnp.sum(jnp.where(owned, begins, 0.0), axis=1, keepdims=True)
            seen += dot(as_bf16(slot_number == to_row(within)), as_bf16(owned))
            uses.append((owned, within))
        used = seen > 0.5
        ranks = [jnp.zeros((1, LANES), f32)]
        for slot in range(cap):
            ranks.append(ranks[-1] + jnp.where(used[slot : slot + 1, :], 1.0, 0.0))
        total = ranks.pop()
        rank = jnp.concatenate(ranks, axis=0)
        over = jnp.maximum(total - DIRECT, 0.0)
        free = DIRECT - jnp.minimum(total, DIRECT)
        pair = jnp.concatenate([over, free, total, none], axis=0).astype(jnp.bfloat16)
        before = dot(pair, line_before)
        whole = dot(pair, line_mat)
        lost = jnp.max(
            jnp.where(whole[0:1, :] > whole[1:2, :], 1.0, 0.0), axis=1, keepdims=True
        )
        turn = before[0:1, :] + rank - DIRECT
        side = jnp.concatenate([before[1:2, :], free, total, none], axis=0).astype(jnp.bfloat16)
        at_slot = rank
        at_owner = jnp.broadcast_to(owner, (cap, LANES))
        code = jnp.zeros((cap, LANES), f32)
        for far in range(1, LINE):
            mover = as_bf16(same_line & (down % LINE == (across + far) % LINE))
            moved = dot(side, mover)
            hit = used & (rank >= DIRECT) & (turn >= moved[0:1, :])
            hit = hit & (turn < moved[0:1, :] + moved[1:2, :])
            slot = moved[2:3, :] + turn - moved[0:1, :]
            other = owner + ((y_at + far) % LINE - y_at).astype(f32)
            at_slot = jnp.where(hit, slot, at_slot)
            at_owner = jnp.where(hit, other, at_owner)
            code = jnp.where(hit, rows * (far * cap + slot), code)
        want = want_ref[step].astype(f32)
        for place in range(cap):
            chosen = used & (rank == place)
            value = want + 1.0 if place < DIRECT else want + code + 1.0
            row = jnp.sum(jnp.where(chosen, value, 0.0), axis=0, keepdims=True) - 1.0
            if place == cap - 1:
                row = jnp.where(lost > 0.5, -2.0, row)
            asks.append(row)
        where_at = at_slot * owners + at_owner
        spots = []
        for owned, within in uses:
            table = jnp.zeros((LANES, LANES), f32)
            for slot in range(cap):
                table = jnp.where(within == slot, where_at[slot : slot + 1, :], table)
            found = jnp.sum(jnp.where(owned, table, 0.0), axis=1, keepdims=True)
            found = jnp.where(within < 0, -1.0, found)
            spots.append(to_row(found))
        spots.append(relation_ref[step : step + 1, :].astype(f32))
        spots.append(jnp.zeros((8 - len(spots), LANES), f32))
        spot_refs[step][...] = jnp.concatenate(spots, axis=0).astype(jnp.int32)
    asks.append(jnp.zeros((LANES - len(asks), LANES), f32))
    ask_ref[...] = jnp.transpose(jnp.concatenate(asks, axis=0)).astype(jnp.int32)


def fill_lent(tag_ref, step, table_ref, lent_ref):
    rows, width = table_ref.shape
    wide = lent_ref.shape[1] - LANES
    row, slot, trainer = (tag_ref[:, 3 * step + index : 3 * step + index + 1] for index in range(3))
    chosen = one_hot_rows(row.astype(jnp.int32), rows)
    lent_ref[:, wide - LANES : wide] = jnp.zeros((LANES, LANES), jnp.bfloat16)
    lent_ref[:, :width] = dot(chosen, table_ref[...]).astype(jnp.bfloat16)
    lanes = iota((LANES, LANES), 1)
    tags = jnp.where(lanes == 0, slot, jnp.where(lanes == 1, trainer, 0.0))
    lent_ref[:, wide:] = tags.astype(jnp.bfloat16)


def collect_kernel(
    steps, cap, ask_ref, table_ref, plan_ref, tag_ref, flag_ref, lent_ref
):
    rows = table_ref.shape[0]
    f32 = jnp.float32
    asked = jnp.transpose(ask_ref[...].astype(f32))[: steps * cap, :]
    down, across = iota((LANES, LANES), 0), iota((LANES, LANES), 1)
    earlier = as_bf16(down < across)
    trainer = iota((1, LANES), 1).astype(f32)
    flag = jnp.zeros((1, 1), f32)
    tags = jnp.full((LANES, LANES), -1.0, f32)
    lent_rows = []
    extra = cap - DIRECT
    for step in range(steps):
        codes = asked[step * cap + DIRECT : (step + 1) * cap, :].astype(jnp.int32)
        flag = jnp.maximum(
            flag,
            jnp.max(
                jnp.where(codes[extra - 1 : extra, :] == -2, 1.0, 0.0), axis=1, keepdims=True
            ),
        )
        valid = codes >= 0
        row = jnp.where(valid, codes % rows, 0).astype(f32)
        place = jnp.where(valid, codes // rows, 0)
        far = place // cap
        slot = (place % cap).astype(f32)
        masks = [
            jnp.where(valid & (far == distance), 1.0, 0.0) for distance in range(1, LINE)
        ]
        stacked = jnp.concatenate(
            masks + [jnp.zeros((16 - extra * (LINE - 1), LANES), f32)], axis=0
        )
        before = dot(stacked.astype(jnp.bfloat16), earlier)
        totals = jnp.sum(stacked, axis=1, keepdims=True)
        targets = [jnp.full((1, LANES), -1.0, f32) for entry in range(extra)]
        for index in range(LINE - 1):
            offset = jnp.zeros((1, 1), f32)
            for entry in range(extra):
                line = index * extra + entry
                at = before[line : line + 1, :] + offset + index * LENT
                targets[entry] = jnp.where(masks[index][entry : entry + 1, :] > 0.5, at, targets[entry])
                offset = offset + totals[line : line + 1, :]
            flag = jnp.maximum(flag, jnp.where(offset > LENT, 1.0, 0.0))
        sums = [jnp.zeros((LANES, 1), f32) for index in range(3)]
        for entry in range(extra):
            chosen = down.astype(f32) == targets[entry]
            values = (row[entry : entry + 1, :], slot[entry : entry + 1, :], trainer)
            for index, value in enumerate(values):
                picked = jnp.where(chosen, value + 1.0, 0.0)
                sums[index] += jnp.sum(picked, axis=1, keepdims=True)
        for index in range(3):
            tags = jnp.where(across == 3 * step + index, sums[index] - 1.0, tags)
        lent_rows.append(to_row(sums[0] - 1.0))
    lent_rows.append(jnp.full((8 - steps, LANES), -1.0, f32))
    plan_ref[...] = jnp.concatenate([asked] + lent_rows, axis=0).astype(jnp.int32)
    tag_ref[...] = tags
    flag_ref[...] = jnp.broadcast_to(flag, flag_ref.shape)
    fill_lent(tag_ref, 0, table_ref, lent_ref)


def first_direct_kernel(
    cap, plan_ref, table_ref, spot_ref, phase_ref, rows_ref, cosine_ref, sine_ref
):
    put_angles(spot_ref, phase_ref[...], cosine_ref, sine_ref)
    direct_kernel(0, cap, plan_ref, table_ref, rows_ref)


def direct_kernel(step, cap, plan_ref, table_ref, rows_ref):
    rows, width = table_ref.shape
    rows_ref[:, rows_ref.shape[1] - LANES :] = jnp.zeros((rows_ref.shape[0], LANES), jnp.bfloat16)
    for first in range(0, DIRECT, 2):
        last = min(first + 2, DIRECT)
        columns = [
            to_column(plan_ref[step * cap + slot : step * cap + slot + 1, :].astype(jnp.float32))
            for slot in range(first, last)
        ]
        chosen = one_hot_rows(jnp.concatenate(columns, axis=0).astype(jnp.int32), rows)
        rows_ref[first * LANES : last * LANES, :width] = dot(chosen, table_ref[...]).astype(
            jnp.bfloat16
        )


def pack_kernel(
    width,
    rows_ref,
    flag_ref,
    one_ref,
    two_ref,
    three_ref,
    packed_ref,
    tag_ref,
    lent_ref,
    full_ref,
    stack_ref,
):
    wide = rows_ref.shape[1]
    lent_ref[3 * LENT :, :] = jnp.zeros((LANES - 3 * LENT, wide), jnp.bfloat16)
    tags = []
    for index, ref in enumerate((one_ref, two_ref, three_ref)):
        lent_ref[index * LENT : (index + 1) * LENT, :] = ref[:, :wide]
        tag = ref[:, wide : wide + LANES].astype(jnp.float32)
        tags.append(tag[:, 0:1] * LANES + tag[:, 1:2])
    tags.append(jnp.full((LANES - 3 * LENT, 1), -1.0, jnp.float32))
    tag = to_row(jnp.concatenate(tags, axis=0)).astype(jnp.int32)
    tag_ref[...] = jnp.broadcast_to(tag, tag_ref.shape)
    for slot in range(DIRECT):
        block = slice(slot * LANES, (slot + 1) * LANES)
        lent = dot(one_hot_columns(tag, slot * LANES, LANES), lent_ref[...])
        full_ref[block, :] = (rows_ref[block, :].astype(jnp.float32) + lent).astype(jnp.bfloat16)
    spread(width, full_ref, stack_ref, flag_ref[0:1, :])
    fold(stack_ref, packed_ref)


def short_trainer_kernel(
    blocks,
    negatives,
    width,
    pulled_ref,
    spot_ref,
    cosine_ref,
    sine_ref,
    packed_ref,
    phase_grad_ref,
    rows_ref,
    stack_ref,
    held_ref,
    copied,
    *scratch,
):
    unfold(pulled_ref, stack_ref)
    gather_up(width, stack_ref, rows_ref)
    mark = read_mark(width, stack_ref)
    sending = pltpu.make_async_copy(held_ref, phase_grad_ref, copied)

    def put_phase_grad(value):
        last = iota((held_ref.shape[0], LANES), 1) == LANES - 1
        held_ref[:, held_ref.shape[1] - LANES :] = jnp.where(last, mark, 0.0)
        held_ref[:, : value.shape[1]] = value
        sending.start()

    trainer_core(
        blocks,
        negatives,
        width,
        rows_ref[...],
        spot_ref,
        cosine_ref,
        sine_ref,
        rows_ref,
        put_phase_grad,
        *scratch,
    )
    spread(width, rows_ref, stack_ref, None)
    fold(stack_ref, packed_ref)
    sending.wait()


def return_kernel(width, arrived_ref, tag_ref, rows_ref, lent_ref, stack_ref):
    unfold(arrived_ref, stack_ref)
    gather_up(width, stack_ref, rows_ref)
    tag = to_column(tag_ref[0:1, :].astype(jnp.float32)).astype(jnp.int32)
    chosen = one_hot_rows(tag, rows_ref.shape[0])
    lent_ref[...] = dot(chosen, rows_ref[...]).astype(jnp.bfloat16)


def sum_kernel(
    step, cap, width, plan_ref, other_plan_ref, rows_ref, arrived_ref, total_ref, stack_ref, other_ref
):
    unfold(arrived_ref, stack_ref)
    gather_up(width, stack_ref, other_ref)

    def asked(ref):
        rows = [ref[step * cap + slot : step * cap + slot + 1, :] for slot in range(DIRECT)]
        return jnp.concatenate(rows, axis=1)

    own, other = asked(plan_ref), asked(other_plan_ref)
    for first in range(0, total_ref.shape[0], 256):
        total_ref[first : first + 256, :] = dot(
            one_hot_columns(own, first, 256), rows_ref[...]
        ) + dot(one_hot_columns(other, first, 256), other_ref[...])


def short_update_kernel(
    step,
    cap,
    has_next,
    steps,
    plan_ref,
    other_plan_ref,
    total_ref,
    back_ref,
    other_back_ref,
    table_ref,
    state_ref,
    *rest,
):
    if has_next:
        tag_ref, new_table_ref, new_state_ref, lent_ref, first_ref, second_ref = rest
    else:
        mark_ref, other_mark_ref, new_table_ref, new_state_ref, flag_ref = rest[:5]
        first_ref, second_ref, held_ref, copied = rest[5:]
        mark = jnp.max(jnp.maximum(mark_ref[...], other_mark_ref[...]))
        flag_ref[0, 0] = (mark > 0.5).astype(jnp.int32)
    rows, width = table_ref.shape
    for ref, source in ((first_ref, back_ref), (second_ref, other_back_ref)):
        ref[: 3 * LENT, :] = source[...]
        ref[3 * LENT :, :] = jnp.zeros((LANES - 3 * LENT, ref.shape[1]), jnp.bfloat16)
    line = steps * cap + step
    own, other = plan_ref[line : line + 1, :], other_plan_ref[line : line + 1, :]
    size = 256
    copies = []
    for first in range(0, rows, size):
        lent = dot(one_hot_columns(own, first, size), first_ref[...]) + dot(
            one_hot_columns(other, first, size), second_ref[...]
        )
        gradient = (total_ref[first : first + size, :] + lent)[:, :width]
        values = table_ref[first : first + size, :].astype(jnp.float32)
        stepped = adagrad_block(gradient, first, values, state_ref, new_state_ref)
        if has_next:
            new_table_ref[first : first + size, :] = stepped
        else:
            turn_into(stepped, held_ref, first)
            columns = pl.ds(first, size)
            copies.append(
                pltpu.make_async_copy(
                    held_ref.at[:, columns], new_table_ref.at[:, columns], copied.at[first // size]
                )
            )
            copies[-1].start()
    for copy in copies:
        copy.wait()
    if has_next:
        fill_lent(tag_ref, step + 1, new_table_ref, lent_ref)


def line_pairs(owners, far):
    return [
        (owner, owner // LINE * LINE + (owner % LINE + far) % LINE) for owner in range(owners)
    ]


def short_steps(
    entity_table,
    entity_state,
    relation_phase,
    relation_state,
    want_rows,
    want_count,
    head_slot,
    tail_slot,
    negative_slot,
    relation_ids,
):
    steps, owners, cap = want_rows.shape[1:]
    rows, width = entity_table.shape
    half = width // 2
    wide = -(-width // LANES) * LANES
    blocks, negatives = negative_slot.shape[2:]
    triples = head_slot.shape[2]
    relations = relation_phase.shape[0]
    direct = DIRECT * LANES
    packed_rows = PIECES * LANES
    packed = packed_width(width)
    half_wide = -(-(half + 1) // LANES) * LANES
    f32, i32, bf16 = jnp.float32, jnp.int32, jnp.bfloat16

    asked, *spots = call(
        functools.partial(route_kernel, rows),
        (shape((LANES, LANES), i32),) + (shape((8, LANES), i32),) * steps,
        "route",
        nbytes=1 << 20,
    )(
        jnp.transpose(want_rows[0], (0, 2, 1)),
        want_count[0],
        head_slot[0],
        tail_slot[0],
        negative_slot[0],
        relation_ids[0],
    )
    asked = lax.all_to_all(asked, "dom", split_axis=0, concat_axis=0, tiled=True)
    plan, tags, flag, lent = call(
        functools.partial(collect_kernel, steps, cap),
        (
            shape((steps * cap + 8, LANES), i32),
            shape((LANES, LANES), f32),
            shape((8, LANES), f32),
            shape((LANES, wide + LANES), bf16),
        ),
        "collect",
        nbytes=4 << 20,
    )(asked, entity_table)
    swap = [(0, 1), (1, 0)]
    other_plan = lax.ppermute(plan, "rep", swap)
    forth = [line_pairs(owners, far) for far in range(1, LINE)]
    back = [[(target, source) for source, target in pairs] for pairs in forth]

    table = entity_table
    state = entity_state.reshape(rows // LANES, LANES)
    phase = relation_phase
    phase_state = relation_state[None, :]
    marks = ()
    for step in range(steps):
        has_next = step + 1 < steps
        loans = [
            lax.ppermute(lent[index * LENT : (index + 1) * LENT], "dom", forth[index])
            for index in range(LINE - 1)
        ]
        if step == 0:
            sent, cosine, sine = call(
                functools.partial(first_direct_kernel, cap),
                (shape((direct, wide), bf16),) + (shape((triples, half), f32),) * 2,
                "direct",
                flops=2 * direct * rows * width,
                nbytes=4 * rows * width,
            )(plan, table, spots[0], phase)
        else:
            sent = call(
                functools.partial(direct_kernel, step, cap),
                shape((direct, wide), bf16),
                "direct",
                flops=2 * direct * rows * width,
                nbytes=4 * rows * width,
            )(plan, table)
        offered, loan_tag = call(
            functools.partial(pack_kernel, width),
            (shape((packed_rows, packed), bf16), shape((8, LANES), i32)),
            "pack",
            nbytes=4 * rows * width,
            scratch_shapes=[
                pltpu.VMEM((LANES, wide), bf16),
                pltpu.VMEM((direct, wide), bf16),
                pltpu.VMEM((packed_rows, packed), bf16),
            ],
        )(sent, flag, *loans)
        pulled = lax.all_to_all(
            offered.reshape(owners, PIECES, packed), "dom", split_axis=0, concat_axis=0, tiled=True
        ).reshape(packed_rows, packed)
        padded, phase_grad = call(
            functools.partial(short_trainer_kernel, blocks, negatives, width),
            (shape((packed_rows, packed), bf16), shape((triples, half_wide), f32)),
            "trainer",
            flops=2 * direct * (9 * triples) * width,
            nbytes=4 * rows * width,
            out_specs=(pl.BlockSpec(memory_space=pltpu.VMEM), pl.BlockSpec(memory_space=pltpu.HBM)),
            scratch_shapes=[
                pltpu.VMEM((direct, wide), bf16),
                pltpu.VMEM((packed_rows, packed), bf16),
                pltpu.VMEM((triples, half_wide), f32),
                pltpu.SemaphoreType.DMA,
            ]
            + trainer_scratch(triples, blocks * negatives, width, wide, wide),
        )(pulled, spots[step], cosine, sine)
        arrived = lax.all_to_all(
            padded.reshape(owners, PIECES, packed), "dom", split_axis=0, concat_axis=0, tiled=True
        ).reshape(packed_rows, packed)
        arrived_other = lax.ppermute(arrived, "rep", swap)
        got, dues = call(
            functools.partial(return_kernel, width),
            (shape((direct, wide), bf16), shape((LANES, wide), bf16)),
            "give_back",
            flops=2 * LANES * direct * wide,
            nbytes=4 * rows * width,
            scratch_shapes=[pltpu.VMEM((packed_rows, packed), bf16)],
        )(arrived, loan_tag)
        dues = [
            lax.ppermute(dues[index * LENT : (index + 1) * LENT], "dom", back[index])
            for index in range(LINE - 1)
        ]
        total = call(
            functools.partial(sum_kernel, step, cap, width),
            shape((rows, wide), f32),
            "sum",
            flops=4 * direct * rows * width,
            nbytes=8 * rows * width,
            scratch_shapes=[
                pltpu.VMEM((packed_rows, packed), bf16),
                pltpu.VMEM((direct, wide), bf16),
            ],
        )(plan, other_plan, got, arrived_other)
        dues, total, marks = lax.optimization_barrier((dues, total, marks))
        dues = jnp.concatenate(dues, axis=0)
        dues_other = lax.ppermute(dues, "rep", swap)
        extras = (shape((8, LANES), f32),) + (shape((triples, half), f32),) * 2
        phase, phase_state, *extras = call(
            functools.partial(short_relation_kernel, has_next),
            (shape((relations, half), f32), shape((1, relations), f32)) + extras * has_next,
            "relation",
            flops=6 * triples * relations * half,
            nbytes=4 * triples * half,
            scratch_shapes=[pltpu.VMEM((relations, 1), f32)] * 2,
        )(spots[step], phase_grad, phase, phase_state, spots[min(step + 1, steps - 1)])
        dues_other, phase, extras = lax.optimization_barrier((dues_other, phase, extras))
        if has_next:
            seen, cosine, sine = extras
        if step == 0:
            marks = (seen, lax.ppermute(seen, "rep", swap))
        outputs = [
            shape((rows, width) if has_next else (width, rows), bf16),
            shape((rows // LANES, LANES), f32),
        ]
        vmem = pl.BlockSpec(memory_space=pltpu.VMEM)
        out_specs = [vmem, vmem]
        scratch = [pltpu.VMEM((LANES, wide), bf16)] * 2
        operands = [plan, other_plan, total, dues, dues_other, table, state]
        if has_next:
            outputs.append(shape((LANES, wide + LANES), bf16))
            out_specs.append(vmem)
            operands.append(tags)
        else:
            outputs.append(shape((1, 1), i32))
            out_specs[0] = pl.BlockSpec(memory_space=pl.ANY)
            out_specs.append(pl.BlockSpec(memory_space=pltpu.SMEM))
            operands.extend(marks)
            scratch.append(pltpu.VMEM((width, rows), bf16))
            scratch.append(pltpu.SemaphoreType.DMA((rows // 256,)))
        results = call(
            functools.partial(short_update_kernel, step, cap, has_next, steps),
            tuple(outputs),
            "update",
            flops=4 * LANES * rows * width,
            nbytes=12 * rows * width,
            out_specs=tuple(out_specs),
            scratch_shapes=scratch,
        )(*operands)
        table, state = results[:2]
        if has_next:
            lent = results[2]
    spoiled = results[2][0, 0] > 0
    return (table.T, state.reshape(rows), phase, phase_state.reshape(relations)), spoiled


def local(*arrays):
    results, spoiled = short_steps(*arrays)
    return lax.cond(spoiled, lambda: full_steps(*arrays), lambda: results)


def solution(mesh):
    placed = (
        P("dom", None),
        P("dom"),
        P(("dom", "rep"), None),
        P(("dom", "rep")),
        P(("dom", "rep"), None, None, None),
        P(("dom", "rep"), None, None),
        P(("dom", "rep"), None, None),
        P(("dom", "rep"), None, None),
        P(("dom", "rep"), None, None, None),
        P(("dom", "rep"), None, None),
    )
    return jax.shard_map(
        local,
        mesh=mesh,
        in_specs=placed,
        out_specs=(P("dom", None), P("dom"), P(("dom", "rep"), None), P(("dom", "rep"))),
        check_vma=False,
    )
```

```python
import functools

import jax
import jax.numpy as jnp
from jax import lax
from jax.experimental import pallas as pl
from jax.experimental.pallas import tpu as pltpu
from jax.sharding import PartitionSpec as P

learn_rate = 0.5
smoothing = 0.25
epsilon = 1e-10
margin_rate = 0.26

LANES = 128
VMEM_LIMIT = 20 * 1024 * 1024


def slot_place(slot_ids, counts, slot_cap):
    running = jnp.cumsum(counts, dtype=jnp.int32)
    passed = (slot_ids[..., None] >= running).astype(jnp.int32)
    owner_index = jnp.sum(passed, axis=-1, dtype=jnp.int32)
    before = jnp.sum(passed * counts, axis=-1, dtype=jnp.int32)
    return owner_index * slot_cap + slot_ids - before


def call(kernel, out_shape, name, flops=0, nbytes=0, **kwargs):
    return pl.pallas_call(
        kernel,
        out_shape=out_shape,
        name=name,
        cost_estimate=pl.CostEstimate(flops=flops, bytes_accessed=nbytes, transcendentals=0),
        compiler_params=pltpu.CompilerParams(vmem_limit_bytes=VMEM_LIMIT),
        **kwargs,
    )


def diagonal():
    down = lax.broadcasted_iota(jnp.int32, (LANES, LANES), 0)
    across = lax.broadcasted_iota(jnp.int32, (LANES, LANES), 1)
    return down == across


def to_column(row):
    spread = jnp.broadcast_to(row, (LANES, LANES))
    return jnp.sum(jnp.where(diagonal(), spread, 0.0), axis=1, keepdims=True)


def to_row(column):
    spread = jnp.broadcast_to(column, (LANES, LANES))
    return jnp.sum(jnp.where(diagonal(), spread, 0.0), axis=0, keepdims=True)


def one_hot_rows(column, width):
    lanes = lax.broadcasted_iota(jnp.int32, (column.shape[0], width), 1)
    return jnp.where(lanes == column, 1.0, 0.0).astype(jnp.bfloat16)


def one_hot_columns(row, first, height):
    down = lax.broadcasted_iota(jnp.int32, (height, row.shape[1]), 0) + first
    return jnp.where(down == row, 1.0, 0.0).astype(jnp.bfloat16)


def dot(left, right):
    return jnp.dot(left, right, preferred_element_type=jnp.float32)


def turn_into(values, ref, first):
    rows, width = values.shape
    for start in range(0, width, 256):
        size = min(256, width - start)
        down = lax.broadcasted_iota(jnp.int32, (size, size), 0)
        across = lax.broadcasted_iota(jnp.int32, (size, size), 1)
        unit = jnp.where(down == across, 1.0, 0.0).astype(jnp.bfloat16)
        product = lax.dot_general(
            unit,
            values[:, start : start + size],
            (((1,), (1,)), ((), ())),
            preferred_element_type=jnp.float32,
        )
        ref[start : start + size, first : first + rows] = product.astype(jnp.bfloat16)


def split3(values):
    high = values.astype(jnp.bfloat16)
    rest = values - high.astype(jnp.float32)
    middle = rest.astype(jnp.bfloat16)
    low = (rest - middle.astype(jnp.float32)).astype(jnp.bfloat16)
    return high, middle, low


def gather_rows(wanted_ref, table_ref, offered_ref):
    table_rows = table_ref.shape[0]
    blocks = wanted_ref.shape[0]
    step = 2
    for start in range(0, blocks, step):
        columns = [
            to_column(wanted_ref[block : block + 1, :].astype(jnp.float32)).astype(jnp.int32)
            for block in range(start, start + step)
        ]
        chosen = one_hot_rows(jnp.concatenate(columns, axis=0), table_rows)
        rows = pl.ds(start * LANES, step * LANES)
        offered_ref[rows, :] = dot(chosen, table_ref[...]).astype(jnp.bfloat16)


def offer_kernel(wanted_ref, table_ref, offered_ref):
    gather_rows(wanted_ref, table_ref, offered_ref)


def own_sum_kernel(asked_ref, arrived_ref, total_ref):
    rows = total_ref.shape[0]
    step = 256
    asked = asked_ref[...]
    for first in range(0, rows, step):
        chosen = one_hot_columns(asked, first, step)
        total_ref[first : first + step, :] = dot(chosen, arrived_ref[...])


def adagrad_block(gradient, first, values, state_ref, new_state_ref):
    step, width = gradient.shape
    mean_square = jnp.sum(gradient * gradient, axis=1, keepdims=True) / width
    fresh = []
    for block in range(first // LANES, (first + step) // LANES):
        old = to_column(state_ref[block : block + 1, :])
        at = block * LANES - first
        new = old + mean_square[at : at + LANES, :]
        new_state_ref[block : block + 1, :] = to_row(new)
        fresh.append(new)
    rate = learn_rate / (jnp.sqrt(jnp.concatenate(fresh, axis=0)) + epsilon)
    return (values - gradient * rate).astype(jnp.bfloat16)


def update_kernel(
    has_next,
    asked_ref,
    arrived_ref,
    own_ref,
    table_ref,
    state_ref,
    *rest,
):
    if has_next:
        wanted_ref, new_table_ref, new_state_ref, offered_ref = rest
    else:
        new_table_ref, new_state_ref = rest
    rows, width = table_ref.shape
    step = 256
    asked = asked_ref[...]
    for first in range(0, rows, step):
        chosen = one_hot_columns(asked, first, step)
        gradient = own_ref[first : first + step, :] + dot(chosen, arrived_ref[...])
        gradient = gradient[:, :width]
        values = table_ref[first : first + step, :].astype(jnp.float32)
        stepped = adagrad_block(gradient, first, values, state_ref, new_state_ref)
        if has_next:
            new_table_ref[first : first + step, :] = stepped
        else:
            turn_into(stepped, new_table_ref, first)
    if has_next:
        gather_rows(wanted_ref, new_table_ref, offered_ref)


def sigmoid(value):
    tail = jnp.exp(-jnp.abs(value))
    return jnp.where(value >= 0, 1.0, tail) / (1.0 + tail)


def trainer_core(
    blocks,
    negatives,
    width,
    pulled,
    spot_ref,
    cosine_ref,
    sine_ref,
    padded_ref,
    put_phase_grad,
    read_ref,
    rot_real_ref,
    rot_imag_ref,
    tail_real_ref,
    tail_imag_ref,
    neg_real_ref,
    neg_imag_ref,
    rot_real_grad_ref,
    rot_imag_grad_ref,
    tail_real_grad_ref,
    tail_imag_grad_ref,
    neg_real_grad_ref,
    neg_imag_grad_ref,
    grads_ref,
):
    slots = pulled.shape[0]
    half = width // 2
    triples = cosine_ref.shape[0]
    neg_rows = blocks * negatives
    margin = margin_rate * half

    places = [
        to_column(spot_ref[index : index + 1, :].astype(jnp.float32)).astype(jnp.int32)
        for index in range(3)
    ]
    places[2] = places[2][:neg_rows]
    read_ref[...] = dot(one_hot_rows(jnp.concatenate(places, axis=0), slots), pulled)
    head_ref = read_ref.at[:triples, :]
    tail_ref = read_ref.at[triples : 2 * triples, :]
    negative_ref = read_ref.at[2 * triples :, :]

    cosine = cosine_ref[...]
    sine = sine_ref[...]
    head_real = head_ref[:, :half]
    head_imag = head_ref[:, half:width]
    rot_real_ref[...] = head_real * cosine - head_imag * sine
    rot_imag_ref[...] = head_real * sine + head_imag * cosine
    tail_real_ref[...] = tail_ref[:, :half]
    tail_imag_ref[...] = tail_ref[:, half:width]
    neg_real_ref[...] = negative_ref[:, :half]
    neg_imag_ref[...] = negative_ref[:, half:width]
    neg_real_grad_ref[...] = jnp.zeros_like(neg_real_grad_ref)
    neg_imag_grad_ref[...] = jnp.zeros_like(neg_imag_grad_ref)

    group = 8
    per_block = triples // blocks

    def pair(real, imag, other_real, other_imag):
        diff_real = real - other_real
        diff_imag = imag - other_imag
        square = diff_real * diff_real + diff_imag * diff_imag + smoothing
        inverse = lax.rsqrt(square)
        distance = jnp.sum(square * inverse, axis=1, keepdims=True)
        return distance, inverse, diff_real, diff_imag

    def chunk(index, carry):
        rows = pl.ds(pl.multiple_of(index * group, group), group)
        first = (index * group) // per_block * negatives
        real = rot_real_ref[rows, :]
        imag = rot_imag_ref[rows, :]
        distance, inverse, diff_real, diff_imag = pair(
            real, imag, tail_real_ref[rows, :], tail_imag_ref[rows, :]
        )
        scale = 0.25 * sigmoid(0.25 * distance - margin) * inverse
        total_real = scale * diff_real
        total_imag = scale * diff_imag
        tail_real_grad_ref[rows, :] = -total_real
        tail_imag_grad_ref[rows, :] = -total_imag
        for n in range(negatives):
            distance, inverse, diff_real, diff_imag = pair(
                real,
                imag,
                neg_real_ref[pl.ds(first + n, 1), :],
                neg_imag_ref[pl.ds(first + n, 1), :],
            )
            scale = (-0.25 / negatives) * sigmoid(margin - 0.25 * distance) * inverse
            part_real = scale * diff_real
            part_imag = scale * diff_imag
            total_real += part_real
            total_imag += part_imag
            neg_real_grad_ref[first + n] -= part_real
            neg_imag_grad_ref[first + n] -= part_imag
        rot_real_grad_ref[rows, :] = total_real
        rot_imag_grad_ref[rows, :] = total_imag
        return carry

    lax.fori_loop(0, triples // group, chunk, 0, unroll=4)

    real_grad = rot_real_grad_ref[...]
    imag_grad = rot_imag_grad_ref[...]
    put_phase_grad(imag_grad * rot_real_ref[...] - real_grad * rot_imag_ref[...])

    grads_ref[:, width:] = jnp.zeros_like(grads_ref[:, width:])

    def put(first, rows, real, imag):
        value = jnp.concatenate([real, imag], axis=1)
        grads_ref[first : first + rows, :width] = value.astype(jnp.bfloat16)

    put(
        0,
        triples,
        real_grad * cosine + imag_grad * sine,
        imag_grad * cosine - real_grad * sine,
    )
    put(triples, triples, tail_real_grad_ref[...], tail_imag_grad_ref[...])
    partial = neg_rows * group
    put(
        2 * triples,
        partial,
        neg_real_grad_ref[...].reshape(partial, half),
        neg_imag_grad_ref[...].reshape(partial, half),
    )
    spots = [spot_ref[index : index + 1, :] for index in range(2)]
    column = to_column(spot_ref[2:3, :].astype(jnp.float32))
    for first in range(0, partial, LANES):
        down = lax.broadcasted_iota(jnp.int32, (LANES, LANES), 0)
        across = lax.broadcasted_iota(jnp.int32, (LANES, LANES), 1) + first
        repeated = jnp.where(down == across // group, column, 0.0)
        spots.append(jnp.sum(repeated, axis=0, keepdims=True).astype(jnp.int32))
    for first in range(0, slots, 256):
        step = min(256, slots - first)
        chosen = [one_hot_columns(spot, first, step) for spot in spots]
        chosen = jnp.concatenate(chosen, axis=1)
        padded_ref[first : first + step, :] = dot(chosen, grads_ref[...]).astype(jnp.bfloat16)


def trainer_kernel(
    blocks,
    negatives,
    pulled_ref,
    spot_ref,
    cosine_ref,
    sine_ref,
    padded_ref,
    phase_grad_ref,
    *scratch,
):
    def put_phase_grad(value):
        phase_grad_ref[...] = value

    trainer_core(
        blocks,
        negatives,
        pulled_ref.shape[1],
        pulled_ref[...],
        spot_ref,
        cosine_ref,
        sine_ref,
        padded_ref,
        put_phase_grad,
        *scratch,
    )


def trainer_scratch(triples, neg_rows, width, wide, read_width):
    half = width // 2
    return (
        [pltpu.VMEM((2 * triples + neg_rows, read_width), jnp.float32)]
        + [pltpu.VMEM((triples, half), jnp.float32)] * 4
        + [pltpu.VMEM((neg_rows, half), jnp.float32)] * 2
        + [pltpu.VMEM((triples, half), jnp.float32)] * 4
        + [pltpu.VMEM((neg_rows, 8, half), jnp.float32)] * 2
        + [pltpu.VMEM((2 * triples + 8 * neg_rows, wide), jnp.bfloat16)]
    )


def relation_kernel(spot_ref, grad_ref, phase_ref, state_ref, new_phase_ref, new_state_ref):
    relations, half = phase_ref.shape
    chosen = one_hot_columns(spot_ref[3:4, :], 0, relations)
    high, middle, low = split3(grad_ref[...])
    gradient = dot(chosen, high) + dot(chosen, middle) + dot(chosen, low)
    gradient = gradient[:, :half]
    mean_square = jnp.sum(gradient * gradient, axis=1, keepdims=True) / half
    fresh = state_ref[...] + mean_square
    new_state_ref[...] = fresh
    new_phase_ref[...] = phase_ref[...] - learn_rate * gradient / (jnp.sqrt(fresh) + epsilon)


def put_angles(spot_ref, phase, cosine_ref, sine_ref):
    column = to_column(spot_ref[3:4, :].astype(jnp.float32)).astype(jnp.int32)
    chosen = one_hot_rows(column, phase.shape[0])
    for ref, values in ((cosine_ref, jnp.cos(phase)), (sine_ref, jnp.sin(phase))):
        high, middle, low = split3(values)
        ref[...] = dot(chosen, high) + dot(chosen, middle) + dot(chosen, low)


def short_relation_kernel(
    has_next,
    spot_ref,
    grad_ref,
    phase_ref,
    state_ref,
    next_spot_ref,
    new_phase_ref,
    new_state_ref,
    *rest,
):
    old_ref, column_ref = rest[-2:]
    relations = phase_ref.shape[0]
    spare = jnp.zeros((1, LANES - relations), jnp.float32)
    row = jnp.concatenate([state_ref[...], spare], axis=1)
    old_ref[...] = to_column(row)[:relations]
    relation_kernel(spot_ref, grad_ref, phase_ref, old_ref, new_phase_ref, column_ref)
    spare = jnp.zeros((LANES - relations, 1), jnp.float32)
    row = to_row(jnp.concatenate([column_ref[...], spare], axis=0))
    new_state_ref[...] = row[:, :relations]
    if has_next:
        flag_ref, cosine_ref, sine_ref = rest[:3]
        last = grad_ref.shape[1] - 1
        mark = jnp.max(grad_ref[:, last : last + 1], axis=0, keepdims=True)
        flag_ref[...] = jnp.broadcast_to(mark, flag_ref.shape)
        put_angles(next_spot_ref, new_phase_ref[...], cosine_ref, sine_ref)


def shape(dims, dtype):
    return jax.ShapeDtypeStruct(dims, dtype)


def full_steps(
    entity_table,
    entity_state,
    relation_phase,
    relation_state,
    want_rows,
    want_count,
    head_slot,
    tail_slot,
    negative_slot,
    relation_ids,
):
    steps, owners, cap = want_rows.shape[1:]
    rows, width = entity_table.shape
    half = width // 2
    wide = -(-width // LANES) * LANES
    blocks, negatives = negative_slot.shape[2:]
    triples = head_slot.shape[2]
    slots = owners * cap
    relations = relation_phase.shape[0]
    table_bytes = 2 * rows * width

    asked = jnp.transpose(want_rows[0], (1, 0, 2)).reshape(owners, steps * cap)
    asked = lax.all_to_all(asked, "dom", split_axis=0, concat_axis=0, tiled=True)
    asked = jnp.transpose(asked.reshape(owners, steps, cap), (1, 0, 2))
    asked = asked.reshape(steps, slots // LANES, LANES)
    asked_other = lax.ppermute(asked, "rep", [(0, 1), (1, 0)])
    ask_row = asked.reshape(steps, 1, slots)
    ask_row_other = asked_other.reshape(steps, 1, slots)

    spots = []
    for step in range(steps):
        counts = want_count[0, step]
        neg = slot_place(negative_slot[0, step].reshape(-1), counts, cap)
        spare = jnp.full((triples - neg.shape[0],), -1, jnp.int32)
        spots.append(
            jnp.stack(
                [
                    slot_place(head_slot[0, step], counts, cap),
                    slot_place(tail_slot[0, step], counts, cap),
                    jnp.concatenate([neg, spare]),
                    relation_ids[0, step],
                ]
            )
        )

    table = entity_table
    state = entity_state.reshape(rows // LANES, LANES)
    phase = relation_phase
    phase_state = relation_state[:, None]
    offered = call(
        offer_kernel,
        shape((slots, width), jnp.bfloat16),
        "offer",
        flops=2 * slots * rows * width,
        nbytes=2 * table_bytes,
    )(asked[0], table)
    f32 = jnp.float32
    for step in range(steps):
        pulled = lax.all_to_all(
            offered.reshape(owners, cap, width), "dom", split_axis=0, concat_axis=0, tiled=True
        ).reshape(slots, width)
        relation_span = jnp.arange(relations, dtype=jnp.int32)
        selector = (relation_ids[0, step][:, None] == relation_span[None, :]).astype(f32)
        phase_rows = jnp.dot(selector, phase, precision=lax.Precision.HIGHEST)
        padded, phase_grad = call(
            functools.partial(trainer_kernel, blocks, negatives),
            (shape((slots, wide), jnp.bfloat16), shape((triples, half), f32)),
            "trainer",
            flops=2 * slots * (9 * triples) * width,
            nbytes=2 * table_bytes,
            scratch_shapes=trainer_scratch(triples, blocks * negatives, width, wide, width),
        )(pulled, spots[step], jnp.cos(phase_rows), jnp.sin(phase_rows))
        arrived = lax.all_to_all(
            padded.reshape(owners, cap, wide), "dom", split_axis=0, concat_axis=0, tiled=True
        ).reshape(slots, wide)
        phase, phase_state = call(
            relation_kernel,
            (shape((relations, half), f32), shape((relations, 1), f32)),
            "relation",
            flops=6 * triples * relations * half,
            nbytes=4 * triples * half,
        )(spots[step], phase_grad, phase, phase_state)
        arrived_other = lax.ppermute(arrived, "rep", [(0, 1), (1, 0)])
        own = call(
            own_sum_kernel,
            shape((rows, wide), f32),
            "own_sum",
            flops=2 * slots * rows * width,
            nbytes=3 * table_bytes,
        )(ask_row[step], arrived)
        has_next = step + 1 < steps
        outputs = [
            shape((rows, width) if has_next else (width, rows), jnp.bfloat16),
            shape((rows // LANES, LANES), f32),
        ]
        operands = [ask_row_other[step], arrived_other, own, table, state]
        if has_next:
            outputs.append(shape((slots, width), jnp.bfloat16))
            operands.append(asked[step + 1])
        results = call(
            functools.partial(update_kernel, has_next),
            tuple(outputs),
            "update",
            flops=2 * slots * rows * width * (1 + has_next),
            nbytes=6 * table_bytes,
        )(*operands)
        table, state = results[:2]
        if has_next:
            offered = results[2]
    return (table.T, state.reshape(rows), phase, phase_state[:, 0])


DIRECT = 5
LINE = 4
LENT = 16
PIECES = 8


def iota(dims, axis):
    return lax.broadcasted_iota(jnp.int32, dims, axis)


def as_bf16(mask):
    return jnp.where(mask, 1.0, 0.0).astype(jnp.bfloat16)


def places(width):
    full, rest = divmod(width, LANES)
    whole = [divmod(index, full) for index in range(DIRECT * full)]
    share = LANES // rest
    groups = [list(range(first, min(first + share, DIRECT))) for first in range(0, DIRECT, share)]
    return full, rest, whole, groups


def packed_width(width):
    full, rest, whole, groups = places(width)
    return -(-(len(whole) + len(groups)) // PIECES) * LANES


def stack_tile(position):
    tile, piece = divmod(position, PIECES)
    return slice(piece * LANES, (piece + 1) * LANES), slice(tile * LANES, (tile + 1) * LANES)


def spread(width, rows_ref, stack_ref, mark):
    full, rest, whole, groups = places(width)
    for position, (row, tile) in enumerate(whole):
        stack_ref[stack_tile(position)] = rows_ref[
            row * LANES : (row + 1) * LANES, tile * LANES : (tile + 1) * LANES
        ]
    last = len(whole) + len(groups) - 1
    for index, group in enumerate(groups):
        position = len(whole) + index
        total = jnp.zeros((LANES, LANES), jnp.float32)
        for row in group:
            tail = rows_ref[row * LANES : (row + 1) * LANES, full * LANES : (full + 1) * LANES]
            tail = tail.astype(jnp.float32)
            shift = rest * (row - group[0])
            total = total + (pltpu.roll(tail, shift, 1) if shift else tail)
        if position == last and mark is not None:
            total = jnp.where(iota((LANES, LANES), 1) == LANES - 1, mark, total)
        stack_ref[stack_tile(position)] = total.astype(jnp.bfloat16)
    for position in range(last + 1, stack_ref.shape[1] // LANES * PIECES):
        stack_ref[stack_tile(position)] = jnp.zeros((LANES, LANES), jnp.bfloat16)


def gather_up(width, stack_ref, rows_ref):
    full, rest, whole, groups = places(width)
    for position, (row, tile) in enumerate(whole):
        rows_ref[row * LANES : (row + 1) * LANES, tile * LANES : (tile + 1) * LANES] = stack_ref[
            stack_tile(position)
        ]
    for index, group in enumerate(groups):
        tails = stack_ref[stack_tile(len(whole) + index)].astype(jnp.float32)
        for row in group:
            shift = rest * (row - group[0])
            tail = pltpu.roll(tails, LANES - shift, 1) if shift else tails
            tail = jnp.where(iota((LANES, LANES), 1) < rest, tail, 0.0)
            rows_ref[row * LANES : (row + 1) * LANES, full * LANES : (full + 1) * LANES] = (
                tail.astype(jnp.bfloat16)
            )


def read_mark(width, stack_ref):
    full, rest, whole, groups = places(width)
    tile = stack_ref[stack_tile(len(whole) + len(groups) - 1)].astype(jnp.float32)
    tile = jnp.where(iota((LANES, LANES), 1) == LANES - 1, tile, 0.0)
    return jnp.max(jnp.max(tile, axis=1, keepdims=True), axis=0, keepdims=True)


PART = LANES // 4


def fold(stack_ref, packed_ref):
    size = PART * PIECES
    down, across = iota((size, size), 0), iota((size, size), 1)
    turn = as_bf16(across == (down % PIECES) * PART + down // PIECES)
    for part in range(LANES // PART):
        pieces = [
            stack_ref[piece * LANES + part * PART : piece * LANES + (part + 1) * PART, :]
            for piece in range(PIECES)
        ]
        packed_ref[part * size : (part + 1) * size, :] = dot(
            turn, jnp.concatenate(pieces, axis=0)
        ).astype(jnp.bfloat16)


def unfold(packed_ref, stack_ref):
    size = PART * PIECES
    down, across = iota((size, size), 0), iota((size, size), 1)
    turn = as_bf16(across == (down % PART) * PIECES + down // PART)
    for part in range(LANES // PART):
        block = dot(turn, packed_ref[part * size : (part + 1) * size, :]).astype(jnp.bfloat16)
        for piece in range(PIECES):
            stack_ref[piece * LANES + part * PART : piece * LANES + (part + 1) * PART, :] = block[
                piece * PART : (piece + 1) * PART, :
            ]


def route_kernel(
    rows,
    want_ref,
    count_ref,
    head_ref,
    tail_ref,
    neg_ref,
    relation_ref,
    ask_ref,
    *spot_refs,
):
    steps, cap, owners = want_ref.shape
    f32 = jnp.float32
    down, across = iota((LANES, LANES), 0), iota((LANES, LANES), 1)
    same_line = down // LINE == across // LINE
    line_mat = as_bf16(same_line)
    trainer = lax.axis_index("dom")
    ahead = (down + trainer) % LINE < (across + trainer) % LINE
    behind = (down + trainer) % LINE > (across + trainer) % LINE
    ahead = jnp.where((trainer // LINE) % 2 == 0, ahead.astype(jnp.int32), behind.astype(jnp.int32))
    line_before = as_bf16(same_line & (ahead > 0))
    upto = as_bf16(down <= across)
    owner = iota((1, LANES), 1).astype(f32)
    y_at = iota((1, LANES), 1) % LINE
    slot_number = iota((cap, LANES), 0).astype(f32)
    none = jnp.zeros((cap - 3, LANES), f32)
    asks = []
    for step in range(steps):
        count = count_ref[step : step + 1, :].astype(f32)
        ends = dot(jnp.broadcast_to(count, (cap, LANES)).astype(jnp.bfloat16), upto)[0:1, :]
        begins = ends - count
        seen = jnp.zeros((cap, LANES), f32)
        uses = []
        slots = [to_column(ref[step : step + 1, :].astype(f32)) for ref in (head_ref, tail_ref)]
        slots.append(jnp.full((LANES, 1), -1.0, f32))
        blocks, negatives = neg_ref.shape[1:]
        for block in range(blocks):
            row = neg_ref[step, block : block + 1, :].astype(f32) + 1.0
            here = iota((LANES, negatives), 0) - block * negatives == iota((LANES, negatives), 1)
            slots[2] += jnp.sum(jnp.where(here, row, 0.0), axis=1, keepdims=True)
        for slot in slots:
            owned = (slot >= begins) & (slot < ends)
            within = slot - jnp.sum(jnp.where(owned, begins, 0.0), axis=1, keepdims=True)
            seen += dot(as_bf16(slot_number == to_row(within)), as_bf16(owned))
            uses.append((owned, within))
        used = seen > 0.5
        ranks = [jnp.zeros((1, LANES), f32)]
        for slot in range(cap):
            ranks.append(ranks[-1] + jnp.where(used[slot : slot + 1, :], 1.0, 0.0))
        total = ranks.pop()
        rank = jnp.concatenate(ranks, axis=0)
        over = jnp.maximum(total - DIRECT, 0.0)
        free = DIRECT - jnp.minimum(total, DIRECT)
        pair = jnp.concatenate([over, free, total, none], axis=0).astype(jnp.bfloat16)
        before = dot(pair, line_before)
        whole = dot(pair, line_mat)
        lost = jnp.max(
            jnp.where(whole[0:1, :] > whole[1:2, :], 1.0, 0.0), axis=1, keepdims=True
        )
        turn = before[0:1, :] + rank - DIRECT
        side = jnp.concatenate([before[1:2, :], free, total, none], axis=0).astype(jnp.bfloat16)
        at_slot = rank
        at_owner = jnp.broadcast_to(owner, (cap, LANES))
        code = jnp.zeros((cap, LANES), f32)
        for far in range(1, LINE):
            mover = as_bf16(same_line & (down % LINE == (across + far) % LINE))
            moved = dot(side, mover)
            hit = used & (rank >= DIRECT) & (turn >= moved[0:1, :])
            hit = hit & (turn < moved[0:1, :] + moved[1:2, :])
            slot = moved[2:3, :] + turn - moved[0:1, :]
            other = owner + ((y_at + far) % LINE - y_at).astype(f32)
            at_slot = jnp.where(hit, slot, at_slot)
            at_owner = jnp.where(hit, other, at_owner)
            code = jnp.where(hit, rows * (far * cap + slot), code)
        want = want_ref[step].astype(f32)
        for place in range(cap):
            chosen = used & (rank == place)
            value = want + 1.0 if place < DIRECT else want + code + 1.0
            row = jnp.sum(jnp.where(chosen, value, 0.0), axis=0, keepdims=True) - 1.0
            if place == cap - 1:
                row = jnp.where(lost > 0.5, -2.0, row)
            asks.append(row)
        where_at = at_slot * owners + at_owner
        spots = []
        for owned, within in uses:
            table = jnp.zeros((LANES, LANES), f32)
            for slot in range(cap):
                table = jnp.where(within == slot, where_at[slot : slot + 1, :], table)
            found = jnp.sum(jnp.where(owned, table, 0.0), axis=1, keepdims=True)
            found = jnp.where(within < 0, -1.0, found)
            spots.append(to_row(found))
        spots.append(relation_ref[step : step + 1, :].astype(f32))
        spots.append(jnp.zeros((8 - len(spots), LANES), f32))
        spot_refs[step][...] = jnp.concatenate(spots, axis=0).astype(jnp.int32)
    asks.append(jnp.zeros((LANES - len(asks), LANES), f32))
    ask_ref[...] = jnp.transpose(jnp.concatenate(asks, axis=0)).astype(jnp.int32)


def fill_lent(tag_ref, step, table_ref, lent_ref):
    rows, width = table_ref.shape
    wide = lent_ref.shape[1] - LANES
    row, slot, trainer = (tag_ref[:, 3 * step + index : 3 * step + index + 1] for index in range(3))
    chosen = one_hot_rows(row.astype(jnp.int32), rows)
    lent_ref[:, wide - LANES : wide] = jnp.zeros((LANES, LANES), jnp.bfloat16)
    lent_ref[:, :width] = dot(chosen, table_ref[...]).astype(jnp.bfloat16)
    lanes = iota((LANES, LANES), 1)
    tags = jnp.where(lanes == 0, slot, jnp.where(lanes == 1, trainer, 0.0))
    lent_ref[:, wide:] = tags.astype(jnp.bfloat16)


def collect_kernel(
    steps, cap, ask_ref, table_ref, plan_ref, tag_ref, flag_ref, lent_ref
):
    rows = table_ref.shape[0]
    f32 = jnp.float32
    asked = jnp.transpose(ask_ref[...].astype(f32))[: steps * cap, :]
    down, across = iota((LANES, LANES), 0), iota((LANES, LANES), 1)
    earlier = as_bf16(down < across)
    trainer = iota((1, LANES), 1).astype(f32)
    flag = jnp.zeros((1, 1), f32)
    tags = jnp.full((LANES, LANES), -1.0, f32)
    lent_rows = []
    extra = cap - DIRECT
    for step in range(steps):
        codes = asked[step * cap + DIRECT : (step + 1) * cap, :].astype(jnp.int32)
        flag = jnp.maximum(
            flag,
            jnp.max(
                jnp.where(codes[extra - 1 : extra, :] == -2, 1.0, 0.0), axis=1, keepdims=True
            ),
        )
        valid = codes >= 0
        row = jnp.where(valid, codes % rows, 0).astype(f32)
        place = jnp.where(valid, codes // rows, 0)
        far = place // cap
        slot = (place % cap).astype(f32)
        masks = [
            jnp.where(valid & (far == distance), 1.0, 0.0) for distance in range(1, LINE)
        ]
        stacked = jnp.concatenate(
            masks + [jnp.zeros((16 - extra * (LINE - 1), LANES), f32)], axis=0
        )
        before = dot(stacked.astype(jnp.bfloat16), earlier)
        totals = jnp.sum(stacked, axis=1, keepdims=True)
        targets = [jnp.full((1, LANES), -1.0, f32) for entry in range(extra)]
        for index in range(LINE - 1):
            offset = jnp.zeros((1, 1), f32)
            for entry in range(extra):
                line = index * extra + entry
                at = before[line : line + 1, :] + offset + index * LENT
                targets[entry] = jnp.where(masks[index][entry : entry + 1, :] > 0.5, at, targets[entry])
                offset = offset + totals[line : line + 1, :]
            flag = jnp.maximum(flag, jnp.where(offset > LENT, 1.0, 0.0))
        sums = [jnp.zeros((LANES, 1), f32) for index in range(3)]
        for entry in range(extra):
            chosen = down.astype(f32) == targets[entry]
            values = (row[entry : entry + 1, :], slot[entry : entry + 1, :], trainer)
            for index, value in enumerate(values):
                picked = jnp.where(chosen, value + 1.0, 0.0)
                sums[index] += jnp.sum(picked, axis=1, keepdims=True)
        for index in range(3):
            tags = jnp.where(across == 3 * step + index, sums[index] - 1.0, tags)
        lent_rows.append(to_row(sums[0] - 1.0))
    lent_rows.append(jnp.full((8 - steps, LANES), -1.0, f32))
    plan_ref[...] = jnp.concatenate([asked] + lent_rows, axis=0).astype(jnp.int32)
    tag_ref[...] = tags
    flag_ref[...] = jnp.broadcast_to(flag, flag_ref.shape)
    fill_lent(tag_ref, 0, table_ref, lent_ref)


def first_direct_kernel(
    cap, plan_ref, table_ref, spot_ref, phase_ref, rows_ref, cosine_ref, sine_ref
):
    put_angles(spot_ref, phase_ref[...], cosine_ref, sine_ref)
    direct_kernel(0, cap, plan_ref, table_ref, rows_ref)


def direct_kernel(step, cap, plan_ref, table_ref, rows_ref):
    rows, width = table_ref.shape
    rows_ref[:, rows_ref.shape[1] - LANES :] = jnp.zeros((rows_ref.shape[0], LANES), jnp.bfloat16)
    for first in range(0, DIRECT, 2):
        last = min(first + 2, DIRECT)
        columns = [
            to_column(plan_ref[step * cap + slot : step * cap + slot + 1, :].astype(jnp.float32))
            for slot in range(first, last)
        ]
        chosen = one_hot_rows(jnp.concatenate(columns, axis=0).astype(jnp.int32), rows)
        rows_ref[first * LANES : last * LANES, :width] = dot(chosen, table_ref[...]).astype(
            jnp.bfloat16
        )


def pack_kernel(
    width,
    rows_ref,
    flag_ref,
    one_ref,
    two_ref,
    three_ref,
    packed_ref,
    tag_ref,
    lent_ref,
    full_ref,
    stack_ref,
):
    wide = rows_ref.shape[1]
    lent_ref[3 * LENT :, :] = jnp.zeros((LANES - 3 * LENT, wide), jnp.bfloat16)
    tags = []
    for index, ref in enumerate((one_ref, two_ref, three_ref)):
        lent_ref[index * LENT : (index + 1) * LENT, :] = ref[:, :wide]
        tag = ref[:, wide : wide + LANES].astype(jnp.float32)
        tags.append(tag[:, 0:1] * LANES + tag[:, 1:2])
    tags.append(jnp.full((LANES - 3 * LENT, 1), -1.0, jnp.float32))
    tag = to_row(jnp.concatenate(tags, axis=0)).astype(jnp.int32)
    tag_ref[...] = jnp.broadcast_to(tag, tag_ref.shape)
    for slot in range(DIRECT):
        block = slice(slot * LANES, (slot + 1) * LANES)
        lent = dot(one_hot_columns(tag, slot * LANES, LANES), lent_ref[...])
        full_ref[block, :] = (rows_ref[block, :].astype(jnp.float32) + lent).astype(jnp.bfloat16)
    spread(width, full_ref, stack_ref, flag_ref[0:1, :])
    fold(stack_ref, packed_ref)


def short_trainer_kernel(
    blocks,
    negatives,
    width,
    pulled_ref,
    spot_ref,
    cosine_ref,
    sine_ref,
    packed_ref,
    phase_grad_ref,
    rows_ref,
    stack_ref,
    held_ref,
    copied,
    *scratch,
):
    unfold(pulled_ref, stack_ref)
    gather_up(width, stack_ref, rows_ref)
    mark = read_mark(width, stack_ref)
    sending = pltpu.make_async_copy(held_ref, phase_grad_ref, copied)

    def put_phase_grad(value):
        last = iota((held_ref.shape[0], LANES), 1) == LANES - 1
        held_ref[:, held_ref.shape[1] - LANES :] = jnp.where(last, mark, 0.0)
        held_ref[:, : value.shape[1]] = value
        sending.start()

    trainer_core(
        blocks,
        negatives,
        width,
        rows_ref[...],
        spot_ref,
        cosine_ref,
        sine_ref,
        rows_ref,
        put_phase_grad,
        *scratch,
    )
    spread(width, rows_ref, stack_ref, None)
    fold(stack_ref, packed_ref)
    sending.wait()


def return_kernel(width, arrived_ref, tag_ref, rows_ref, lent_ref, stack_ref):
    unfold(arrived_ref, stack_ref)
    gather_up(width, stack_ref, rows_ref)
    tag = to_column(tag_ref[0:1, :].astype(jnp.float32)).astype(jnp.int32)
    chosen = one_hot_rows(tag, rows_ref.shape[0])
    lent_ref[...] = dot(chosen, rows_ref[...]).astype(jnp.bfloat16)


def sum_kernel(
    step, cap, width, plan_ref, other_plan_ref, rows_ref, arrived_ref, total_ref, stack_ref, other_ref
):
    unfold(arrived_ref, stack_ref)
    gather_up(width, stack_ref, other_ref)

    def asked(ref):
        rows = [ref[step * cap + slot : step * cap + slot + 1, :] for slot in range(DIRECT)]
        return jnp.concatenate(rows, axis=1)

    own, other = asked(plan_ref), asked(other_plan_ref)
    for first in range(0, total_ref.shape[0], 256):
        total_ref[first : first + 256, :] = dot(
            one_hot_columns(own, first, 256), rows_ref[...]
        ) + dot(one_hot_columns(other, first, 256), other_ref[...])


def short_update_kernel(
    step,
    cap,
    has_next,
    steps,
    plan_ref,
    other_plan_ref,
    total_ref,
    back_ref,
    other_back_ref,
    table_ref,
    state_ref,
    *rest,
):
    if has_next:
        tag_ref, new_table_ref, new_state_ref, lent_ref, first_ref, second_ref = rest
    else:
        mark_ref, other_mark_ref, new_table_ref, new_state_ref, flag_ref = rest[:5]
        first_ref, second_ref, held_ref, copied = rest[5:]
        mark = jnp.max(jnp.maximum(mark_ref[...], other_mark_ref[...]))
        flag_ref[0, 0] = (mark > 0.5).astype(jnp.int32)
    rows, width = table_ref.shape
    for ref, source in ((first_ref, back_ref), (second_ref, other_back_ref)):
        ref[: 3 * LENT, :] = source[...]
        ref[3 * LENT :, :] = jnp.zeros((LANES - 3 * LENT, ref.shape[1]), jnp.bfloat16)
    line = steps * cap + step
    own, other = plan_ref[line : line + 1, :], other_plan_ref[line : line + 1, :]
    size = 256
    copies = []
    for first in range(0, rows, size):
        lent = dot(one_hot_columns(own, first, size), first_ref[...]) + dot(
            one_hot_columns(other, first, size), second_ref[...]
        )
        gradient = (total_ref[first : first + size, :] + lent)[:, :width]
        values = table_ref[first : first + size, :].astype(jnp.float32)
        stepped = adagrad_block(gradient, first, values, state_ref, new_state_ref)
        if has_next:
            new_table_ref[first : first + size, :] = stepped
        else:
            turn_into(stepped, held_ref, first)
            columns = pl.ds(first, size)
            copies.append(
                pltpu.make_async_copy(
                    held_ref.at[:, columns], new_table_ref.at[:, columns], copied.at[first // size]
                )
            )
            copies[-1].start()
    for copy in copies:
        copy.wait()
    if has_next:
        fill_lent(tag_ref, step + 1, new_table_ref, lent_ref)


def line_pairs(owners, far):
    return [
        (owner, owner // LINE * LINE + (owner % LINE + far) % LINE) for owner in range(owners)
    ]


def short_steps(
    entity_table,
    entity_state,
    relation_phase,
    relation_state,
    want_rows,
    want_count,
    head_slot,
    tail_slot,
    negative_slot,
    relation_ids,
):
    steps, owners, cap = want_rows.shape[1:]
    rows, width = entity_table.shape
    half = width // 2
    wide = -(-width // LANES) * LANES
    blocks, negatives = negative_slot.shape[2:]
    triples = head_slot.shape[2]
    relations = relation_phase.shape[0]
    direct = DIRECT * LANES
    packed_rows = PIECES * LANES
    packed = packed_width(width)
    half_wide = -(-(half + 1) // LANES) * LANES
    f32, i32, bf16 = jnp.float32, jnp.int32, jnp.bfloat16

    asked, *spots = call(
        functools.partial(route_kernel, rows),
        (shape((LANES, LANES), i32),) + (shape((8, LANES), i32),) * steps,
        "route",
        nbytes=1 << 20,
    )(
        jnp.transpose(want_rows[0], (0, 2, 1)),
        want_count[0],
        head_slot[0],
        tail_slot[0],
        negative_slot[0],
        relation_ids[0],
    )
    asked = lax.all_to_all(asked, "dom", split_axis=0, concat_axis=0, tiled=True)
    plan, tags, flag, lent = call(
        functools.partial(collect_kernel, steps, cap),
        (
            shape((steps * cap + 8, LANES), i32),
            shape((LANES, LANES), f32),
            shape((8, LANES), f32),
            shape((LANES, wide + LANES), bf16),
        ),
        "collect",
        nbytes=4 << 20,
    )(asked, entity_table)
    swap = [(0, 1), (1, 0)]
    forth = [line_pairs(owners, far) for far in range(1, LINE)]
    back = [[(target, source) for source, target in pairs] for pairs in forth]

    table = entity_table
    state = entity_state.reshape(rows // LANES, LANES)
    phase = relation_phase
    phase_state = relation_state[None, :]
    marks = ()
    for step in range(steps):
        has_next = step + 1 < steps
        loans = [
            lax.ppermute(lent[index * LENT : (index + 1) * LENT], "dom", forth[index])
            for index in range(LINE - 1)
        ]
        if step == 0:
            sent, cosine, sine = call(
                functools.partial(first_direct_kernel, cap),
                (shape((direct, wide), bf16),) + (shape((triples, half), f32),) * 2,
                "direct",
                flops=2 * direct * rows * width,
                nbytes=4 * rows * width,
            )(plan, table, spots[0], phase)
        else:
            sent = call(
                functools.partial(direct_kernel, step, cap),
                shape((direct, wide), bf16),
                "direct",
                flops=2 * direct * rows * width,
                nbytes=4 * rows * width,
            )(plan, table)
        offered, loan_tag = call(
            functools.partial(pack_kernel, width),
            (shape((packed_rows, packed), bf16), shape((8, LANES), i32)),
            "pack",
            nbytes=4 * rows * width,
            scratch_shapes=[
                pltpu.VMEM((LANES, wide), bf16),
                pltpu.VMEM((direct, wide), bf16),
                pltpu.VMEM((packed_rows, packed), bf16),
            ],
        )(sent, flag, *loans)
        pulled = lax.all_to_all(
            offered.reshape(owners, PIECES, packed), "dom", split_axis=0, concat_axis=0, tiled=True
        ).reshape(packed_rows, packed)
        padded, phase_grad = call(
            functools.partial(short_trainer_kernel, blocks, negatives, width),
            (shape((packed_rows, packed), bf16), shape((triples, half_wide), f32)),
            "trainer",
            flops=2 * direct * (9 * triples) * width,
            nbytes=4 * rows * width,
            out_specs=(pl.BlockSpec(memory_space=pltpu.VMEM), pl.BlockSpec(memory_space=pltpu.HBM)),
            scratch_shapes=[
                pltpu.VMEM((direct, wide), bf16),
                pltpu.VMEM((packed_rows, packed), bf16),
                pltpu.VMEM((triples, half_wide), f32),
                pltpu.SemaphoreType.DMA,
            ]
            + trainer_scratch(triples, blocks * negatives, width, wide, wide),
        )(pulled, spots[step], cosine, sine)
        arrived = lax.all_to_all(
            padded.reshape(owners, PIECES, packed), "dom", split_axis=0, concat_axis=0, tiled=True
        ).reshape(packed_rows, packed)
        got, dues = call(
            functools.partial(return_kernel, width),
            (shape((direct, wide), bf16), shape((LANES, wide), bf16)),
            "give_back",
            flops=2 * LANES * direct * wide,
            nbytes=4 * rows * width,
            scratch_shapes=[pltpu.VMEM((packed_rows, packed), bf16)],
        )(arrived, loan_tag)
        arrived, dues, plan = lax.optimization_barrier((arrived, dues, plan))
        arrived_other = lax.ppermute(arrived, "rep", swap)
        if step == 0:
            other_plan = lax.ppermute(plan, "rep", swap)
        dues = [
            lax.ppermute(dues[index * LENT : (index + 1) * LENT], "dom", back[index])
            for index in range(LINE - 1)
        ]
        total = call(
            functools.partial(sum_kernel, step, cap, width),
            shape((rows, wide), f32),
            "sum",
            flops=4 * direct * rows * width,
            nbytes=8 * rows * width,
            scratch_shapes=[
                pltpu.VMEM((packed_rows, packed), bf16),
                pltpu.VMEM((direct, wide), bf16),
            ],
        )(plan, other_plan, got, arrived_other)
        dues, total, marks = lax.optimization_barrier((dues, total, marks))
        dues = jnp.concatenate(dues, axis=0)
        dues_other = lax.ppermute(dues, "rep", swap)
        extras = (shape((8, LANES), f32),) + (shape((triples, half), f32),) * 2
        phase, phase_state, *extras = call(
            functools.partial(short_relation_kernel, has_next),
            (shape((relations, half), f32), shape((1, relations), f32)) + extras * has_next,
            "relation",
            flops=6 * triples * relations * half,
            nbytes=4 * triples * half,
            scratch_shapes=[pltpu.VMEM((relations, 1), f32)] * 2,
        )(spots[step], phase_grad, phase, phase_state, spots[min(step + 1, steps - 1)])
        dues_other, phase, extras = lax.optimization_barrier((dues_other, phase, extras))
        if has_next:
            seen, cosine, sine = extras
        if step == 0:
            marks = (seen, lax.ppermute(seen, "rep", swap))
        outputs = [
            shape((rows, width) if has_next else (width, rows), bf16),
            shape((rows // LANES, LANES), f32),
        ]
        vmem = pl.BlockSpec(memory_space=pltpu.VMEM)
        out_specs = [vmem, vmem]
        scratch = [pltpu.VMEM((LANES, wide), bf16)] * 2
        operands = [plan, other_plan, total, dues, dues_other, table, state]
        if has_next:
            outputs.append(shape((LANES, wide + LANES), bf16))
            out_specs.append(vmem)
            operands.append(tags)
        else:
            outputs.append(shape((1, 1), i32))
            out_specs[0] = pl.BlockSpec(memory_space=pl.ANY)
            out_specs.append(pl.BlockSpec(memory_space=pltpu.SMEM))
            operands.extend(marks)
            scratch.append(pltpu.VMEM((width, rows), bf16))
            scratch.append(pltpu.SemaphoreType.DMA((rows // 256,)))
        results = call(
            functools.partial(short_update_kernel, step, cap, has_next, steps),
            tuple(outputs),
            "update",
            flops=4 * LANES * rows * width,
            nbytes=12 * rows * width,
            out_specs=tuple(out_specs),
            scratch_shapes=scratch,
        )(*operands)
        table, state = results[:2]
        if has_next:
            lent = results[2]
    spoiled = results[2][0, 0] > 0
    return (table.T, state.reshape(rows), phase, phase_state.reshape(relations)), spoiled


def local(*arrays):
    results, spoiled = short_steps(*arrays)
    return lax.cond(spoiled, lambda: full_steps(*arrays), lambda: results)


def solution(mesh):
    placed = (
        P("dom", None),
        P("dom"),
        P(("dom", "rep"), None),
        P(("dom", "rep")),
        P(("dom", "rep"), None, None, None),
        P(("dom", "rep"), None, None),
        P(("dom", "rep"), None, None),
        P(("dom", "rep"), None, None),
        P(("dom", "rep"), None, None, None),
        P(("dom", "rep"), None, None),
    )
    return jax.shard_map(
        local,
        mesh=mesh,
        in_specs=placed,
        out_specs=(P("dom", None), P("dom"), P(("dom", "rep"), None), P(("dom", "rep"))),
        check_vma=False,
    )
```
